32 devices in a mesh: groups: 2 (over y), dp: 4 (over z), tensor: 4 (over x, core).
Axes of the slice: x: 2, y: 2, z: 4, core: 2. Of those that a mesh axis runs over, the one named last changes fastest.
Arguments:
- hidden: bfloat16 [16, 4, 8192], P(('groups', 'dp'), None, 'tensor'), parts along dimension 0, may hold values from -6 to 6
- norm_gain: bfloat16 [8192], P('tensor'), may hold values from 0.099609375 to 1.8984375
- queries: bfloat16 [16, 4, 8192], P(('groups', 'dp')), parts along dimension 0, may hold values from -150 to 150
- key_weight: bfloat16 [8192, 1024], P('tensor'), may hold values from -0.0625 to 0.0625
- value_weight: bfloat16 [8192, 1024], P('tensor'), may hold values from -0.0625 to 0.0625
- key_down: float32 [128, 8192], P(('groups', 'dp'), 'tensor'), parts along dimension 0, may hold values from -0.0625 to 0.0625
- key_up: float32 [2048, 64], P(('groups', 'dp')), parts along dimension 0, may hold values from -0.75 to 0.75
- value_down: float32 [128, 8192], P(('groups', 'dp'), 'tensor'), parts along dimension 0, may hold values from -0.0625 to 0.0625
- value_up: float32 [2048, 64], P(('groups', 'dp')), parts along dimension 0, may hold values from -0.75 to 0.75
- key_cache: bfloat16 [16, 2048, 1024], P(('groups', 'dp'), 'tensor'), parts along dimension 0, may hold values from -6 to 6
- value_cache: bfloat16 [16, 2048, 1024], P(('groups', 'dp'), 'tensor'), parts along dimension 0, may hold values from -6 to 6
- lengths: int32 [16], P(('groups', 'dp')), parts along dimension 0, may hold values from 1 to 2048, as said below
Outputs:
- new_keys: bfloat16 [16, 4, 1024], P(('groups', 'dp')), parts along dimension 0
- new_values: bfloat16 [16, 4, 1024], P(('groups', 'dp')), parts along dimension 0
- attended: bfloat16 [16, 4, 8192], P(('groups', 'dp')), parts along dimension 0
The draws below stay inside these ranges and needn't reach their ends.
There are 2 independent parts, one for each index of `groups`. The reference program is written for one: setup_inputs(seed, part) draws one part's arguments, and reference() takes and returns one part's arrays. A program takes and returns all parts, laid end to end along the dimension named above; an argument that names none is the same for every part. Nothing has to cross between parts.
Inputs may be any that keep to these rules, and one draw needn't show every extreme that they name: `lengths`: some sequence fills all 2048 cache positions.
All inputs are finite; a program needn't handle non-finite values.
Results may differ from the reference program's by a relative error of at most 0.0078.
Values may be sent and summed in bfloat16 or wider, within the bound.
No kernel may reach another device: no remote copies, remote signals or barrier semaphores. Data moves between devices by JAX's collectives and lax.ppermute only.
A program may use at most 64 MiB of HBM per device.

```python
import math
import jax
import jax.numpy as jnp
from jax import lax

D = 8192
H = 64
KVH = 8
HD = 128
R = 64
STEPS = 4
L_CACHE = 2048
SEQS = 8


def draw_lengths(key, part):
    key = jax.random.fold_in(key, 11)
    first_key, second_key = jax.random.split(key)
    drawn = jax.random.randint(first_key, (SEQS,), 1, L_CACHE + 1, dtype=jnp.int32)
    fullest = jax.random.randint(second_key, (), 0, SEQS, dtype=jnp.int32)
    return jnp.where(jnp.arange(SEQS, dtype=jnp.int32) == fullest, L_CACHE, drawn).astype(jnp.int32)


def draw_queries(key, part):
    key = jax.random.fold_in(key, 5)
    noise_key = jax.random.fold_in(key, 0)
    sample = jnp.clip(jax.random.normal(noise_key, (SEQS, STEPS, H, HD), jnp.float32), -6.0, 6.0)
    return sample.reshape(SEQS, STEPS, H * HD).astype(jnp.bfloat16)


def draw_key_cache(key, part):
    key = jax.random.fold_in(key, 13)
    sample = jnp.clip(jax.random.normal(key, (SEQS, L_CACHE, KVH * HD), jnp.float32), -6.0, 6.0)
    return sample.astype(jnp.bfloat16)


def block_levels(own_key, dims, shards, low, high):
    level, own = 1.0, jax.random.fold_in(own_key, 6)
    for position, shards_of in shards:
        steps = jnp.exp(jax.random.uniform(jax.random.fold_in(own, position), (shards_of,), jnp.float32, low / len(shards), high / len(shards)))
        level = level * jnp.repeat(steps, dims[position] // shards_of).reshape([-1 if axis == position else 1 for axis in range(len(dims))])
    return level


def noise(own_key, shape, spread, bound, cuts=(), kind=jnp.bfloat16):
    result = spread * jax.random.normal(own_key, shape, jnp.float32)
    if cuts:
        result = result * block_levels(own_key, shape, cuts, -0.22, 0.18)
    return jnp.clip(result, -bound, bound).astype(kind)


def setup_inputs(seed: int = 0, part: int = 0) -> dict:
    keys = jax.random.split(jax.random.key(seed), 13)
    part_splits = jax.random.split(jax.random.fold_in(keys[12], part), 13)
    hidden = noise(part_splits[0], (SEQS, STEPS, D), 1.0, 6.0, ((0, 4), (2, 4)))
    norm_gain = jnp.clip(1.0 + 0.18 * jax.random.normal(keys[1], (D,), jnp.float32), 0.099609375, 1.8984375).astype(jnp.bfloat16)
    queries = draw_queries(jax.random.fold_in(jax.random.fold_in(keys[12], part), 71), part)
    key_weight = noise(keys[3], (D, KVH * HD), D ** -0.5, 0.0625, ((0, 4),))
    value_weight = noise(keys[4], (D, KVH * HD), D ** -0.5, 0.0625, ((0, 4),))
    key_down = noise(part_splits[5], (R, D), D ** -0.5, 0.0625, ((0, 4), (1, 4)), jnp.float32)
    key_up = noise(part_splits[6], (KVH * HD, R), R ** -0.5, 0.75, ((0, 4),), jnp.float32)
    value_down = noise(part_splits[7], (R, D), D ** -0.5, 0.0625, ((0, 4), (1, 4)), jnp.float32)
    value_up = noise(part_splits[8], (KVH * HD, R), R ** -0.5, 0.75, ((0, 4),), jnp.float32)
    key_cache = draw_key_cache(jax.random.fold_in(jax.random.fold_in(keys[12], part), 71), part)
    value_cache = noise(part_splits[10], (SEQS, L_CACHE, KVH * HD), 1.0, 6.0, ((0, 4), (1, 4)))
    lengths = draw_lengths(jax.random.fold_in(jax.random.fold_in(keys[12], part), 71), part)
    return dict(hidden=hidden, norm_gain=norm_gain, queries=queries, key_weight=key_weight, value_weight=value_weight, key_down=key_down, key_up=key_up, value_down=value_down, value_up=value_up, key_cache=key_cache, value_cache=value_cache, lengths=lengths)


EPSILON = 1e-05
ROPE_BASE = 500000.0
MASKED_SCORE = -1e+30

def rotate(vectors, positions):
    half_size = vectors.shape[-1] // 2
    frequency = ROPE_BASE ** (-(2.0 * jnp.arange(half_size, dtype=jnp.float32)) / vectors.shape[-1])
    angles = positions.astype(jnp.float32)[..., None, None] * frequency
    cosine = jnp.cos(angles)
    sine_part = jnp.sin(angles)
    front = vectors[..., :half_size]
    back = vectors[..., half_size:]
    return jnp.concatenate([front * cosine - back * sine_part, back * cosine + front * sine_part], -1)

def reference(hidden, norm_gain, queries, key_weight, value_weight, key_down, key_up, value_down, value_up, key_cache, value_cache, lengths):
    highest = lax.Precision.HIGHEST
    group_size = H // KVH
    rows_flat = hidden.reshape(SEQS * STEPS, D).astype(jnp.float32)
    mean_square = lax.optimization_barrier(jnp.sum(rows_flat * rows_flat, axis=1, keepdims=True)) / D
    normed = (rows_flat * lax.rsqrt(mean_square + EPSILON) * norm_gain.astype(jnp.float32)).astype(jnp.bfloat16)
    normed_wide = normed.astype(jnp.float32)
    merged_key = key_weight.astype(jnp.float32) + jnp.dot(key_down.T, key_up.T, precision=highest)
    merged_value = value_weight.astype(jnp.float32) + jnp.dot(value_down.T, value_up.T, precision=highest)
    raw_key = jnp.dot(normed_wide, merged_key, precision=highest).reshape(SEQS, STEPS, KVH, HD)
    raw_value = jnp.dot(normed_wide, merged_value, precision=highest).reshape(SEQS, STEPS, KVH, HD)
    positions = lengths[:, None] + jnp.arange(STEPS, dtype=jnp.int32)[None, :]
    new_keys = rotate(raw_key, positions).astype(jnp.bfloat16).reshape(SEQS, STEPS, KVH * HD)
    new_values = raw_value.astype(jnp.bfloat16).reshape(SEQS, STEPS, KVH * HD)
    rotated_queries = rotate(queries.astype(jnp.float32).reshape(SEQS, STEPS, H, HD), positions).astype(jnp.bfloat16)

    def per_sequence(bundle):
        query_rows, cached_keys, cached_values, fresh_keys, fresh_values, length = bundle
        grouped = query_rows.astype(jnp.float32).reshape(STEPS, KVH, group_size, HD)
        keys_all = jnp.concatenate([cached_keys, fresh_keys], 0).astype(jnp.float32).reshape(L_CACHE + STEPS, KVH, HD)
        values_all = jnp.concatenate([cached_values, fresh_values], 0).astype(jnp.float32).reshape(L_CACHE + STEPS, KVH, HD)
        scores = jnp.einsum('ikgd,tkd->ikgt', grouped, keys_all, precision=highest) / math.sqrt(HD)
        slot_index = jnp.arange(L_CACHE + STEPS, dtype=jnp.int32)[None, :]
        step_index = jnp.arange(STEPS, dtype=jnp.int32)[:, None]
        valid_mask = jnp.where(slot_index < L_CACHE, slot_index < length, slot_index - L_CACHE <= step_index)
        valid_mask = valid_mask[:, None, None, :]
        masked = jnp.where(valid_mask, scores, MASKED_SCORE)
        row_max = lax.optimization_barrier(jnp.max(masked, axis=-1, keepdims=True))
        rounded = jnp.where(valid_mask, jnp.exp(masked - row_max), 0.0).astype(jnp.bfloat16)
        weights = lax.optimization_barrier(rounded).astype(jnp.float32)
        weight_sum = lax.optimization_barrier(jnp.sum(weights, axis=-1))
        numerator = jnp.einsum('ikgt,tkd->ikgd', weights, values_all, precision=highest)
        return (numerator / weight_sum[..., None]).reshape(STEPS, H * HD).astype(jnp.bfloat16)
    attended = lax.map(per_sequence, (rotated_queries, key_cache, value_cache, new_keys, new_values, lengths))
    return (new_keys, new_values, attended)
```

```python
import functools
import math

import jax
import jax.numpy as jnp
from jax import lax
from jax.experimental import pallas as pl
from jax.experimental.pallas import tpu as pltpu
from jax.sharding import PartitionSpec as P

HD = 128
GROUP = 8
STEPS = 4
EPSILON = 1e-05
ROPE_BASE = 500000.0
MASKED_SCORE = -1e30
SCALE = 1.0 / math.sqrt(HD)
PAIR = GROUP * HD + 128

F32 = jnp.float32
BF16 = jnp.bfloat16
NT = (((1,), (1,)), ((), ()))


def rotated(tile, cosine, sine):
    return tile * cosine + pltpu.roll(tile, HD // 2, 1) * sine


def tokens(ref):
    return jnp.concatenate([ref[0].astype(F32), ref[1].astype(F32)], 0)


def rounded(value):
    return value.astype(BF16).astype(F32)


def cache_kernel(limit_ref, q_ref, k_ref, v_ref, cos_ref, sin_ref, out_ref, qrot_ref):
    cosine, sine = cos_ref[...], sin_ref[...]
    q = tokens(q_ref)
    rows = [[], []]
    for g in range(GROUP):
        for e in range(2):
            at = (e * GROUP + g) * HD
            rows[e].append(rotated(q[:, at : at + HD], cosine, sine))
        qrot_ref[:, g * HD : (g + 1) * HD] = jnp.concatenate([rows[0][g], rows[1][g]], 0).astype(BF16)
    zero = jnp.zeros((GROUP * 8, HD), F32)
    upper = jnp.concatenate([jnp.concatenate(rows[0], 0), zero], 1)
    lower = jnp.concatenate([zero, jnp.concatenate(rows[1], 0)], 1)
    queries = jnp.concatenate([upper, lower], 0).astype(BF16)
    scores = [
        lax.dot_general(queries, k_ref[s], NT, preferred_element_type=F32) for s in range(2)
    ]
    shape = scores[0].shape
    first = lax.broadcasted_iota(jnp.int32, shape, 0) % 8 < STEPS
    place = lax.broadcasted_iota(jnp.int32, shape, 1)
    valid = place < jnp.where(first, limit_ref[0], limit_ref[1])
    masked = jnp.where(valid, jnp.where(first, scores[0], scores[1]) * SCALE, MASKED_SCORE)
    top = rounded(jnp.max(masked, 1, keepdims=True))
    weights = rounded(jnp.where(valid, jnp.exp(masked - top), 0.0))
    total = jnp.sum(weights, 1, keepdims=True)
    numer = jnp.dot(
        jnp.where(first, weights, 0.0).astype(BF16), v_ref[0], preferred_element_type=F32
    ) + jnp.dot(jnp.where(first, 0.0, weights).astype(BF16), v_ref[1], preferred_element_type=F32)
    high = rounded(total)
    low = total - high
    lane = lax.broadcasted_iota(jnp.int32, (16, 128), 1)
    stats = jnp.zeros((16, 128), F32)
    for g in range(GROUP):
        a, b = slice(g * 8, g * 8 + 8), slice(64 + g * 8, 64 + g * 8 + 8)
        out_ref[:, g * HD : (g + 1) * HD] = jnp.concatenate(
            [numer[a, :HD], numer[b, HD:]], 0
        ).astype(BF16)
        for slot, value in enumerate((top, high, low)):
            column = jnp.concatenate([value[a], value[b]], 0)
            stats = jnp.where(lane == slot * GROUP + g, column, stats)
    out_ref[:, GROUP * HD :] = stats.astype(BF16)


def cache_attention(limits, queries, key_cache, value_cache, cosine, sine):
    seqs, length, width = key_cache.shape
    pairs = width // (2 * HD)
    table = pl.BlockSpec((8, HD), lambda p: (0, 0))
    cache = pl.BlockSpec((seqs, length, 2 * HD), lambda p: (0, 0, p))
    return pl.pallas_call(
        cache_kernel,
        grid=(pairs,),
        in_specs=[
            pl.BlockSpec(memory_space=pltpu.SMEM),
            pl.BlockSpec((seqs, STEPS, 2 * GROUP * HD), lambda p: (0, 0, p)),
            cache,
            cache,
            table,
            table,
        ],
        out_specs=[
            pl.BlockSpec((16, PAIR), lambda p: (0, p)),
            pl.BlockSpec((16, GROUP * HD), lambda p: (0, p)),
        ],
        out_shape=[
            jax.ShapeDtypeStruct((16, pairs * PAIR), BF16),
            jax.ShapeDtypeStruct((16, pairs * GROUP * HD), BF16),
        ],
        compiler_params=pltpu.CompilerParams(vmem_limit_bytes=32 * 2**20),
        cost_estimate=pl.CostEstimate(
            flops=4 * 128 * 256 * seqs * length * pairs,
            bytes_accessed=4 * seqs * length * width,
            transcendentals=128 * length * pairs,
        ),
        name="cache_attention",
    )(limits, queries, key_cache, value_cache, cosine, sine)


def base_kernel(x_ref, gain_ref, wk_ref, wv_ref, out_ref, acc_ref, sq_ref):
    step = pl.program_id(0)
    x = tokens(x_ref)
    scaled = (x * gain_ref[...].astype(F32)).astype(BF16)
    part = jnp.concatenate(
        [
            jnp.dot(scaled, wk_ref[...], preferred_element_type=F32),
            jnp.dot(scaled, wv_ref[...], preferred_element_type=F32),
        ],
        0,
    )
    squares = jnp.broadcast_to(jnp.sum(x * x, 1, keepdims=True), (8, 128))

    @pl.when(step == 0)
    def _():
        acc_ref[...] = part
        sq_ref[...] = squares

    @pl.when(step > 0)
    def _():
        acc_ref[...] += part
        sq_ref[...] += squares

    @pl.when(step == pl.num_programs(0) - 1)
    def _():
        width = acc_ref.shape[1]
        out_ref[:, :width] = acc_ref[...].astype(BF16)
        total = sq_ref[...]
        high = rounded(total)
        out_ref[:, width:] = jnp.concatenate([high, total - high], 0).astype(BF16)


def base_projection(hidden, gain, key_weight, value_weight):
    depth, width = key_weight.shape
    chunk = 512
    weight = pl.BlockSpec((chunk, width), lambda c: (c, 0))
    return pl.pallas_call(
        base_kernel,
        grid=(depth // chunk,),
        in_specs=[
            pl.BlockSpec((2, STEPS, chunk), lambda c: (0, 0, c)),
            pl.BlockSpec((1, chunk), lambda c: (0, c)),
            weight,
            weight,
        ],
        out_specs=pl.BlockSpec((16, width + 128), lambda c: (0, 0)),
        out_shape=jax.ShapeDtypeStruct((16, width + 128), BF16),
        scratch_shapes=[pltpu.VMEM((16, width), F32), pltpu.VMEM((8, 128), F32)],
        compiler_params=pltpu.CompilerParams(vmem_limit_bytes=32 * 2**20),
        cost_estimate=pl.CostEstimate(
            flops=4 * 16 * depth * width, bytes_accessed=4 * depth * width, transcendentals=0
        ),
        name="base_projection",
    )(hidden, gain, key_weight, value_weight)


def rank_kernel(n, place_ref, gain_ref, kd_ref, vd_ref, *refs):
    gain = gain_ref[...].astype(F32)
    x = jnp.concatenate([tokens(ref) for ref in refs[:n]], 0)
    own = kd_ref.shape[0]
    fill = jnp.zeros((64 - own, x.shape[1]), F32)
    down = jnp.concatenate([kd_ref[...], fill, vd_ref[...], fill], 0).astype(BF16)
    z = lax.dot_general((x * gain).astype(BF16), down, NT, preferred_element_type=F32)
    z = pltpu.roll(z, place_ref[0] * own, 1)
    for i in range(n):
        refs[n + i][...] = z[8 * i : 8 * i + 8]


def rank_products(place, gain, key_down, value_down, hiddens):
    n = len(hiddens)
    whole = pl.BlockSpec(memory_space=pltpu.VMEM)
    return pl.pallas_call(
        functools.partial(rank_kernel, n),
        in_specs=[pl.BlockSpec(memory_space=pltpu.SMEM)] + [whole] * (3 + n),
        out_specs=[whole] * n,
        out_shape=[jax.ShapeDtypeStruct((8, 128), F32)] * n,
        compiler_params=pltpu.CompilerParams(vmem_limit_bytes=32 * 2**20),
        cost_estimate=pl.CostEstimate(
            flops=2 * 8 * n * 128 * key_down.shape[1],
            bytes_accessed=8 * key_down.size + 2 * n * hiddens[0].size,
            transcendentals=0,
        ),
        name="rank_products",
    )(place, gain, key_down, value_down, *hiddens)


def final_kernel(counts, width_all, place_ref, cos_ref, sin_ref, qrot_ref, *refs):
    nz, nu, nt = counts
    zs, refs = refs[:nz], refs[nz:]
    ups, refs = refs[:nu], refs[nu:]
    bases, refs = refs[:nt], refs[nt:]
    caches, refs = refs[:nt], refs[nt:]
    keys_out, values_out, out_ref, kv_ref = refs
    width = kv_ref.shape[1]
    cosine, sine = cos_ref[...], sin_ref[...]
    z = zs[0][...]
    for ref in zs[1:]:
        z = z + ref[...]
    lane8 = lax.broadcasted_iota(jnp.int32, (8, 128), 1)
    z = jnp.concatenate([jnp.where(lane8 < 64, z, 0.0), jnp.where(lane8 < 64, 0.0, z)], 0).astype(BF16)
    for d, ref in enumerate(ups):
        rows = ref.shape[0]
        at = pl.multiple_of((place_ref[0] ^ d) * rows, rows) if nu > 1 else 0
        kv_ref[:, pl.ds(at, rows)] = lax.dot_general(z, ref[...], NT, preferred_element_type=F32)
    total = kv_ref[...]
    squares = jnp.zeros((8, 128), F32)
    for ref in bases:
        total = total + ref[:, :width].astype(F32)
        tail = ref[:, width:].astype(F32)
        squares = squares + tail[:8] + tail[8:]
    scale = lax.rsqrt(squares / width_all + EPSILON)
    row16 = lax.broadcasted_iota(jnp.int32, (16, 128), 0)
    row8 = lax.broadcasted_iota(jnp.int32, (8, 128), 0)
    lane = lax.broadcasted_iota(jnp.int32, (16, 128), 1)
    step = row16 % STEPS

    def of_step(tile, j):
        return jnp.where(row8 < STEPS, tile[j : j + 1], tile[STEPS + j : STEPS + j + 1])

    for p in range(width // (2 * HD)):
        new_keys, new_values = [], []
        for e in range(2):
            at = slice((2 * p + e) * HD, (2 * p + e + 1) * HD)
            new_keys.append(rounded(rotated(total[:8, at] * scale, cosine, sine)))
            new_values.append(rounded(total[8:, at] * scale))
        at = slice(2 * p * HD, 2 * (p + 1) * HD)
        for out, parts in ((keys_out, new_keys), (values_out, new_values)):
            both = jnp.concatenate(parts, 1).astype(BF16)
            out[0, :, at] = both[:STEPS]
            out[1, :, at] = both[STEPS:]
        keys = [
            jnp.concatenate([of_step(new_keys[0], j), of_step(new_keys[1], j)], 0)
            for j in range(STEPS)
        ]
        values = [
            jnp.concatenate([of_step(new_values[0], j), of_step(new_values[1], j)], 0)
            for j in range(STEPS)
        ]
        scores = [jnp.zeros((16, 128), F32) for _ in range(STEPS)]
        for g in range(GROUP):
            q = qrot_ref[:, (p * GROUP + g) * HD : (p * GROUP + g + 1) * HD].astype(F32)
            for j in range(STEPS):
                dot = jnp.sum(q * keys[j], 1, keepdims=True) * SCALE
                scores[j] = jnp.where(lane == g, dot, scores[j])
        scores = [jnp.where(j <= step, scores[j], MASKED_SCORE) for j in range(STEPS)]
        stats = [
            ref[:, p * PAIR + GROUP * HD : (p + 1) * PAIR].astype(F32) for ref in caches
        ]
        top = functools.reduce(jnp.maximum, scores + stats)
        fresh = [rounded(jnp.where(j <= step, jnp.exp(scores[j] - top), 0.0)) for j in range(STEPS)]
        factors = [jnp.exp(jnp.minimum(s - top, 0.0)) for s in stats]
        denom = functools.reduce(jnp.add, fresh)
        for factor, s in zip(factors, stats):
            denom = denom + factor * (
                pltpu.roll(s, 128 - GROUP, 1) + pltpu.roll(s, 128 - 2 * GROUP, 1)
            )
        inverse = 1.0 / denom
        coefficients = [c * inverse for c in fresh + factors]
        tiles = []
        for g in range(GROUP):
            at = slice(p * PAIR + g * HD, p * PAIR + (g + 1) * HD)
            terms = values + [ref[:, at].astype(F32) for ref in caches]
            tile = jnp.zeros((16, 128), F32)
            for c, term in zip(coefficients, terms):
                tile = tile + c[:, g : g + 1] * term
            tiles.append(tile)
        both = jnp.concatenate(tiles, 1)
        for e in range(2):
            at = slice((2 * p + e) * GROUP * HD, (2 * p + e + 1) * GROUP * HD)
            for s in range(2):
                out_ref[s, :, at] = both[8 * e + 4 * s : 8 * e + 4 * s + 4].astype(BF16)


def final(place, cosine, sine, qrot, zs, ups, bases, caches, width_all):
    width = bases[0].shape[1] - 128
    whole = pl.BlockSpec(memory_space=pltpu.VMEM)
    operands = [cosine, sine, qrot, *zs, *ups, *bases, *caches]
    return pl.pallas_call(
        functools.partial(final_kernel, (len(zs), len(ups), len(bases)), width_all),
        in_specs=[pl.BlockSpec(memory_space=pltpu.SMEM)] + [whole] * len(operands),
        out_specs=[whole] * 3,
        out_shape=[
            jax.ShapeDtypeStruct((2, STEPS, width), BF16),
            jax.ShapeDtypeStruct((2, STEPS, width), BF16),
            jax.ShapeDtypeStruct((2, STEPS, GROUP * width), BF16),
        ],
        scratch_shapes=[pltpu.VMEM((16, width), F32)],
        compiler_params=pltpu.CompilerParams(vmem_limit_bytes=32 * 2**20),
        name="final",
    )(place, *operands)


def swaps(value, axis, n):
    return [value] + [
        lax.ppermute(value, axis, [(i, i ^ d) for i in range(n)]) for d in range(1, n)
    ]


def shards(
    n_dp,
    n_tensor,
    hidden,
    norm_gain,
    queries,
    key_weight,
    value_weight,
    key_down,
    key_up,
    value_down,
    value_up,
    key_cache,
    value_cache,
    lengths,
):
    dp_place = lax.axis_index("dp").astype(jnp.int32).reshape(1)
    tensor_place = lax.axis_index("tensor").astype(jnp.int32)
    gain = norm_gain.reshape(1, -1)
    hiddens = swaps(hidden, "dp", n_dp)
    ups = jnp.concatenate([key_up, value_up], 1).astype(BF16)
    if n_dp <= 4:
        ups = swaps(ups, "dp", n_dp)
    else:
        ups = [lax.all_gather(ups, "dp", axis=0, tiled=True)]

    positions = (lengths[:, None] + jnp.arange(STEPS, dtype=jnp.int32)[None, :]).reshape(-1, 1)
    half = HD // 2
    frequency = ROPE_BASE ** (-(2.0 * jnp.arange(half, dtype=F32)) / HD)
    angles = positions.astype(F32) * frequency
    cosine = jnp.cos(angles)
    sine = jnp.sin(angles)
    cosine = jnp.concatenate([cosine, cosine], 1)
    sine = jnp.concatenate([-sine, sine], 1)
    limits = lengths - tensor_place * key_cache.shape[1]

    base = base_projection(hidden, gain, key_weight, value_weight)
    bases = swaps(base, "tensor", n_tensor)
    cache, qrot = cache_attention(limits, queries, key_cache, value_cache, cosine, sine)
    caches = swaps(cache, "tensor", n_tensor)

    ranks = rank_products(dp_place, gain, key_down, value_down, hiddens)
    if n_dp <= 4:
        zs = []
        for d in range(n_dp):
            for e in range(n_tensor):
                if d == 0 and e == 0:
                    zs.append(ranks[0])
                    continue
                perm = [
                    (a * n_tensor + b, (a ^ d) * n_tensor + (b ^ e))
                    for a in range(n_dp)
                    for b in range(n_tensor)
                ]
                zs.append(lax.ppermute(ranks[d], ("dp", "tensor"), perm))
    else:
        total = ranks[0]
        for d in range(1, n_dp):
            total = total + lax.ppermute(ranks[d], "dp", [(i, i ^ d) for i in range(n_dp)])
        zs = [lax.psum(total, "tensor")]
    return final(
        dp_place, cosine, sine, qrot, zs, ups, bases, caches, float(hidden.shape[2] * n_tensor)
    )


def solution(mesh):
    body = functools.partial(shards, mesh.shape["dp"], mesh.shape["tensor"])
    return jax.shard_map(
        body,
        mesh=mesh,
        in_specs=(
            P(("groups", "dp"), None, "tensor"),
            P("tensor"),
            P(("groups", "dp"), None, None),
            P("tensor", None),
            P("tensor", None),
            P(("groups", "dp"), "tensor"),
            P(("groups", "dp"), None),
            P(("groups", "dp"), "tensor"),
            P(("groups", "dp"), None),
            P(("groups", "dp"), "tensor", None),
            P(("groups", "dp"), "tensor", None),
            P(("groups", "dp")),
        ),
        out_specs=(
            P(("groups", "dp"), None, None),
            P(("groups", "dp"), None, None),
            P(("groups", "dp"), None, None),
        ),
        check_vma=False,
    )
```

```python
import functools
import math

import jax
import jax.numpy as jnp
from jax import lax
from jax.experimental import pallas as pl
from jax.experimental.pallas import tpu as pltpu
from jax.sharding import PartitionSpec as P

HD = 128
GROUP = 8
STEPS = 4
RANK = 64
EPSILON = 1e-05
ROPE_BASE = 500000.0
MASKED_SCORE = -1e30
LOWEST_TOP = -1e20
EXPONENT = math.log2(math.e) / math.sqrt(HD)
PAIR = GROUP * HD + 128
CHUNK = 512

F32 = jnp.float32
BF16 = jnp.bfloat16
NT = (((1,), (1,)), ((), ()))
VMEM = pl.BlockSpec(memory_space=pltpu.VMEM)
HBM = pl.BlockSpec(memory_space=pltpu.HBM)
MEBI = 2**20
WHOLE_VMEM = 65000 * 1024
HINT = 40 * MEBI


def rounded(value):
    return value.astype(BF16).astype(F32)


def split(value):
    high = rounded(value)
    return jnp.concatenate([high, value - high], 0).astype(BF16)


def joined(tile):
    wide = tile.astype(F32)
    return wide[:8] + wide[8:]


def rotated(tile, cosine, sine):
    return tile * cosine + pltpu.roll(tile, HD // 2, 1) * sine


def first_rows(shape):
    return lax.broadcasted_iota(jnp.int32, shape, 0) % 8 < STEPS


def exchanged(a, b):
    first = first_rows(a.shape)
    return (
        jnp.where(first, a, pltpu.roll(b, STEPS, 0)),
        jnp.where(first, pltpu.roll(a, STEPS, 0), b),
    )


def flat(matrix):
    return jnp.concatenate([matrix[i : i + 16] for i in range(0, matrix.shape[0], 16)], 1)


def pack_kernel(*refs):
    sources, (a_ref, b_ref, sq_ref), held, sems = refs[:6], refs[6:9], refs[9:15], refs[15]
    copies = [
        pltpu.make_async_copy(source, target, sems.at[i])
        for i, (source, target) in enumerate(zip(sources, held))
    ]
    for copy in copies:
        copy.start()
    x_ref, gain_ref, kd_ref, vd_ref, ku_ref, vu_ref = held
    for copy in copies:
        copy.wait()
    x = jnp.concatenate([x_ref[0].astype(F32), x_ref[1].astype(F32)], 0)
    depth = x.shape[1]
    sq_ref[...] = jnp.broadcast_to(jnp.sum(x * x, 1, keepdims=True), sq_ref.shape)
    scaled = x * gain_ref[...].astype(F32).reshape(1, depth)
    b_ref[:, : depth // 2] = jnp.concatenate(
        [scaled[:, : depth // 2], scaled[:, depth // 2 :]], 0
    ).astype(BF16)
    ups = flat(jnp.concatenate([ku_ref[...], vu_ref[...]], 0).T.astype(BF16))
    b_ref[:, depth // 2 :] = ups
    own = kd_ref.shape[0]
    for slot, ref in enumerate((kd_ref, vd_ref)):
        down = ref[...]
        if own < 16:
            down = jnp.concatenate([down, jnp.zeros((16 - own, depth), F32)], 0)
        a_ref[:, slot * depth : (slot + 1) * depth] = down.astype(BF16)
    a_ref[:, 2 * depth :] = ups


def pack(hidden, gain, key_down, value_down, key_up, value_up):
    operands = [hidden, gain, key_down, value_down, key_up.T, value_up.T]
    depth = hidden.shape[2]
    ups = key_up.shape[0] * 8
    return pl.pallas_call(
        pack_kernel,
        in_specs=[HBM] * len(operands),
        out_specs=[VMEM] * 3,
        out_shape=[
            jax.ShapeDtypeStruct((16, 2 * depth + ups), BF16),
            jax.ShapeDtypeStruct((16, depth // 2 + ups), BF16),
            jax.ShapeDtypeStruct((8, 128), F32),
        ],
        scratch_shapes=[pltpu.VMEM(o.shape, o.dtype) for o in operands]
        + [pltpu.SemaphoreType.DMA((len(operands),))],
        compiler_params=pltpu.CompilerParams(vmem_limit_bytes=WHOLE_VMEM),
        name="pack",
    )(*operands)


def tables(lengths_ref):
    shape = (8, HD)
    row = lax.broadcasted_iota(jnp.int32, shape, 0)
    lane = lax.broadcasted_iota(jnp.int32, shape, 1)
    step = row % STEPS
    position = (jnp.where(row < STEPS, lengths_ref[0], lengths_ref[1]) + step).astype(F32)
    pair = lane % (HD // 2)
    frequency = jnp.ones(shape, F32)
    for bit in range(6):
        factor = ROPE_BASE ** (-(2.0 * 2**bit) / HD)
        frequency = jnp.where((pair >> bit) & 1 == 1, frequency * factor, frequency)
    angle = position * frequency
    sine = jnp.sin(angle)
    return jnp.cos(angle), jnp.where(lane < HD // 2, -sine, sine)


def attend(p, limits, cosine, sine, q_ref, k_ref, v_ref, out_ref, qrot_ref):
    halves = [[], []]
    for e in range(2):
        tiles = []
        for g in range(GROUP):
            at = slice(((2 * p + e) * GROUP + g) * HD, ((2 * p + e) * GROUP + g + 1) * HD)
            q = jnp.concatenate([q_ref[0, :, at].astype(F32), q_ref[1, :, at].astype(F32)], 0)
            tiles.append(rotated(q, cosine, sine))
        halves[e] = tiles
    for g in range(GROUP):
        at = slice((p * GROUP + g) * HD, (p * GROUP + g + 1) * HD)
        qrot_ref[:, at] = jnp.concatenate([halves[0][g], halves[1][g]], 0).astype(BF16)
    mixed = [[exchanged(halves[e][g], halves[e][g + 4]) for g in range(4)] for e in range(2)]
    zero = jnp.zeros((32, HD), F32)
    numers, stats = [], []
    lane8 = lax.broadcasted_iota(jnp.int32, (8, 128), 1)
    pair = slice(2 * p * HD, 2 * (p + 1) * HD)
    for s in range(2):
        rows = [jnp.concatenate([mixed[e][g][s] for g in range(4)], 0) for e in range(2)]
        queries = jnp.concatenate(
            [jnp.concatenate([rows[0], zero], 1), jnp.concatenate([zero, rows[1]], 1)], 0
        ).astype(BF16)
        scores = lax.dot_general(queries, k_ref[s, :, pair], NT, preferred_element_type=F32)
        place = lax.broadcasted_iota(jnp.int32, scores.shape, 1)
        masked = jnp.where(place < limits[s], scores, MASKED_SCORE)
        top = rounded(jnp.maximum(jnp.max(masked, 1, keepdims=True), LOWEST_TOP))
        weights = jnp.exp2((masked - top) * EXPONENT).astype(BF16)
        total = jnp.sum(weights.astype(F32), 1, keepdims=True)
        numers.append(jnp.dot(weights, v_ref[s, :, pair], preferred_element_type=F32))
        high = rounded(total)
        compact = []
        for e in range(2):
            tile = jnp.zeros((8, 128), F32)
            for g in range(4):
                at = slice(32 * e + 8 * g, 32 * e + 8 * g + 8)
                for slot, value in enumerate((top, high, total - high)):
                    tile = jnp.where(lane8 == slot * GROUP + g, value[at], tile)
            compact.append(tile)
        stats.append(compact)
    outs, ends = [[], []], []
    for e in range(2):
        back = []
        for g in range(4):
            at = slice(32 * e + 8 * g, 32 * e + 8 * g + 8)
            cols = slice(e * HD, (e + 1) * HD)
            back.append(exchanged(numers[0][at, cols], numers[1][at, cols]))
        outs[e] = [b[0] for b in back] + [b[1] for b in back]
        a, b = exchanged(stats[0][e], stats[1][e])
        ends.append(jnp.where(lane8 % 8 < 4, a, pltpu.roll(b, 4, 1)))
    for g in range(GROUP):
        at = slice(p * PAIR + g * HD, p * PAIR + (g + 1) * HD)
        out_ref[:, at] = jnp.concatenate([outs[0][g], outs[1][g]], 0).astype(BF16)
    out_ref[:, p * PAIR + GROUP * HD : (p + 1) * PAIR] = jnp.concatenate(ends, 0).astype(BF16)


def local_kernel(
    x_ref, lengths_hbm, q_hbm, k_hbm, v_hbm, wk_hbm, wv_hbm,
    out_ref, qrot_ref, base_ref, trig_ref,
    lengths_ref, q_ref, k_ref, v_ref, wk_ref, wv_ref, length_sem, q_sem, cache_sem, weight_sem,
):
    pairs = k_hbm.shape[2] // (2 * HD)
    chunks = wk_hbm.shape[0] // CHUNK
    length_copy = pltpu.make_async_copy(lengths_hbm, lengths_ref, length_sem)
    length_copy.start()
    q_copy = pltpu.make_async_copy(q_hbm, q_ref, q_sem)
    q_copy.start()
    cache_copies, weight_copies = [], []
    for p in range(pairs):
        at = (slice(None), slice(None), pl.ds(2 * p * HD, 2 * HD))
        for i, (source, target) in enumerate(((k_hbm, k_ref), (v_hbm, v_ref))):
            copy = pltpu.make_async_copy(source.at[at], target.at[at], cache_sem.at[p, i])
            copy.start()
            cache_copies.append(copy)
    for c in range(chunks):
        at = pl.ds(c * CHUNK, CHUNK)
        for i, (source, target) in enumerate(((wk_hbm, wk_ref), (wv_hbm, wv_ref))):
            copy = pltpu.make_async_copy(source.at[at], target.at[at], weight_sem.at[c, i])
            copy.start()
            weight_copies.append(copy)
    length_copy.wait()
    cosine, sine = tables(lengths_ref)
    trig_ref[...] = jnp.concatenate([cosine, sine], 0)
    start = lax.axis_index("tensor") * k_hbm.shape[1]
    limits = [lengths_ref[s] - start for s in range(2)]
    q_copy.wait()
    for p in range(pairs):
        cache_copies[2 * p].wait()
        cache_copies[2 * p + 1].wait()
        attend(p, limits, cosine, sine, q_ref, k_ref, v_ref, out_ref, qrot_ref)
    half = wk_hbm.shape[0] // 2
    x = x_ref[:, :half].astype(F32)
    x = jnp.concatenate([x[:8], x[8:]], 1).astype(BF16)
    total = None
    for c in range(chunks):
        weight_copies[2 * c].wait()
        weight_copies[2 * c + 1].wait()
        rows = x[:, c * CHUNK : (c + 1) * CHUNK]
        part = jnp.concatenate(
            [
                jnp.dot(rows, ref[c * CHUNK : (c + 1) * CHUNK], preferred_element_type=F32)
                for ref in (wk_ref, wv_ref)
            ],
            0,
        )
        total = part if total is None else total + part
    base_ref[...] = total


def local(lengths, message, queries, key_cache, value_cache, key_weight, value_weight):
    seqs, length, width = key_cache.shape
    depth = key_weight.shape[0]
    pairs = width // (2 * HD)
    return pl.pallas_call(
        local_kernel,
        in_specs=[VMEM] + [HBM] * 6,
        out_specs=[VMEM] * 4,
        out_shape=[
            jax.ShapeDtypeStruct((16, pairs * PAIR), BF16),
            jax.ShapeDtypeStruct((16, pairs * GROUP * HD), BF16),
            jax.ShapeDtypeStruct((16, width), F32),
            jax.ShapeDtypeStruct((16, HD), F32),
        ],
        scratch_shapes=[
            pltpu.SMEM(lengths.shape, jnp.int32),
            pltpu.VMEM(queries.shape, BF16),
            pltpu.VMEM(key_cache.shape, BF16),
            pltpu.VMEM(value_cache.shape, BF16),
            pltpu.VMEM(key_weight.shape, BF16),
            pltpu.VMEM(value_weight.shape, BF16),
            pltpu.SemaphoreType.DMA,
            pltpu.SemaphoreType.DMA,
            pltpu.SemaphoreType.DMA((pairs, 2)),
            pltpu.SemaphoreType.DMA((depth // CHUNK, 2)),
        ],
        compiler_params=pltpu.CompilerParams(vmem_limit_bytes=WHOLE_VMEM),
        cost_estimate=pl.CostEstimate(
            flops=4 * 64 * 256 * seqs * length * pairs + 4 * 16 * depth * width,
            bytes_accessed=4 * seqs * length * width + 4 * depth * width,
            transcendentals=64 * seqs * length * pairs,
        ),
        name="local",
    )(message, lengths, queries, key_cache, value_cache, key_weight, value_weight)


def rank_kernel(n, rows, depth, *refs):
    base_ref, sq_ref, own_ref, near_ref = refs[:4]
    tokens, out_ref = refs[4 : 4 + n], refs[4 + n]
    width = base_ref.shape[1]
    place = lax.axis_index("dp")
    x = []
    for ref in tokens:
        part = ref[:, : depth // 2].astype(F32)
        x.append(jnp.concatenate([part[:8], part[8:]], 1))
    x = jnp.concatenate(x, 0).astype(BF16)
    fill = jnp.zeros((RANK - 16, depth), BF16)
    z = None
    for ref, at in ((own_ref, place), (near_ref, place ^ 1)):
        down = jnp.concatenate([ref[:, :depth], fill, ref[:, depth : 2 * depth], fill], 0)
        part = lax.dot_general(x, down, NT, preferred_element_type=F32)
        part = pltpu.roll(part, at * rows, 1)
        z = part if z is None else z + part
    out_ref[:, :width] = base_ref[...].astype(BF16)
    out_ref[:, width : width + 128] = split(sq_ref[...])
    for i in range(n):
        at = width + 128 * (i + 1)
        out_ref[:, at : at + 128] = split(z[8 * i : 8 * i + 8])


def rank_products(rows, depth, base, squares, own, near, tokens):
    n = len(tokens)
    return pl.pallas_call(
        functools.partial(rank_kernel, n, rows, depth),
        in_specs=[VMEM] * (4 + n),
        out_specs=VMEM,
        out_shape=jax.ShapeDtypeStruct((16, base.shape[1] + 128 * (n + 1)), BF16),
        compiler_params=pltpu.CompilerParams(vmem_limit_bytes=32 * MEBI),
        cost_estimate=pl.CostEstimate(flops=0, bytes_accessed=HINT, transcendentals=0),
        name="rank_products",
    )(base, squares, own, near, *tokens)


def broadcast_lane(tile, lane):
    return jnp.broadcast_to(tile[:, lane : lane + 1], tile.shape)


def combine_kernel(ca_ref, cb_ref, pa_ref, pb_ref, c_ref, p_ref):
    width = p_ref.shape[1]
    sums = pa_ref[...].astype(F32) + pb_ref[...].astype(F32)
    tail = c_ref.shape[1] // PAIR * 2 * HD
    p_ref[:, :tail] = sums[:, :tail].astype(BF16)
    p_ref[:, tail:] = split(sums[:8, tail:] + sums[8:, tail:])
    lane = lax.broadcasted_iota(jnp.int32, (16, 128), 1)
    for p in range(c_ref.shape[1] // PAIR):
        end = slice(p * PAIR + GROUP * HD, (p + 1) * PAIR)
        a, b = ca_ref[:, end].astype(F32), cb_ref[:, end].astype(F32)
        top = jnp.maximum(a, b)
        fa = jnp.exp2(jnp.minimum(a - top, 0.0) * EXPONENT)
        fb = jnp.exp2(jnp.minimum(b - top, 0.0) * EXPONENT)
        total = fa * totals(a) + fb * totals(b)
        high = rounded(total)
        stats = jnp.where(lane < GROUP, top, 0.0)
        stats = jnp.where(lane // GROUP == 1, pltpu.roll(high, GROUP, 1), stats)
        stats = jnp.where(lane // GROUP == 2, pltpu.roll(total - high, 2 * GROUP, 1), stats)
        c_ref[:, end] = stats.astype(BF16)
        for g in range(GROUP):
            at = slice(p * PAIR + g * HD, p * PAIR + (g + 1) * HD)
            c_ref[:, at] = (
                broadcast_lane(fa, g) * ca_ref[:, at].astype(F32)
                + broadcast_lane(fb, g) * cb_ref[:, at].astype(F32)
            ).astype(BF16)


def totals(stats):
    return pltpu.roll(stats, 128 - GROUP, 1) + pltpu.roll(stats, 128 - 2 * GROUP, 1)


def combine(cache_a, cache_b, part_a, part_b):
    return pl.pallas_call(
        combine_kernel,
        in_specs=[VMEM] * 4,
        out_specs=[VMEM] * 2,
        out_shape=[
            jax.ShapeDtypeStruct(cache_a.shape, BF16),
            jax.ShapeDtypeStruct(part_a.shape, BF16),
        ],
        compiler_params=pltpu.CompilerParams(vmem_limit_bytes=32 * MEBI),
        name="combine",
    )(cache_a, cache_b, part_a, part_b)


def answer_kernel(n, at, pa_ref, pb_ref, near_ref, *outs):
    ups = near_ref.shape[1] - outs[0].shape[1] + 128
    z = pa_ref[:, at:].astype(F32) + pb_ref[:, at:].astype(F32)
    for i, ref in enumerate(outs):
        part = z[:, 128 * (i + 1) : 128 * (i + 2)]
        ref[:, :128] = split(part[:8] + part[8:])
        ref[:, 128:] = near_ref[:, ups:]


def answers(n, part_a, part_b, near, up_columns):
    at = part_a.shape[1] - 128 * (n + 1)
    return pl.pallas_call(
        functools.partial(answer_kernel, n, at),
        in_specs=[VMEM] * 3,
        out_specs=[VMEM] * n,
        out_shape=[jax.ShapeDtypeStruct((16, 128 + up_columns), BF16)] * n,
        compiler_params=pltpu.CompilerParams(vmem_limit_bytes=32 * MEBI),
        name="answers",
    )(part_a, part_b, near)


def final_kernel(n, width_all, trig_ref, qrot_ref, ca_ref, cb_ref, pa_ref, pb_ref, *refs):
    own_ref, near_ref = refs[:2]
    sent, back = refs[2 : 2 + n], refs[2 + n : 2 + 2 * n]
    keys_out, values_out, out_ref, up_ref = refs[2 + 2 * n :]
    width = keys_out.shape[2]
    place = lax.axis_index("dp")
    columns = back[0].shape[1] - 128
    rows = columns // 8
    blocks = [(own_ref, 0), (near_ref, 1)]
    for i in range(n):
        blocks += [(sent[i], 2 * i + 2), (back[i], 2 * i + 3)]
    for ref, distance in blocks:
        start = ref.shape[1] - columns
        at = (place ^ distance) * rows
        for i in range(rows // 16):
            up_ref[pl.ds(pl.multiple_of(at + 16 * i, 16), 16), :] = ref[
                :, start + 128 * i : start + 128 * (i + 1)
            ]
    cosine, sine = trig_ref[:8], trig_ref[8:]
    sums = pa_ref[...].astype(F32) + pb_ref[...].astype(F32)
    tail = sums[:8, width : width + 256] + sums[8:, width : width + 256]
    squares, z = tail[:, :128], tail[:, 128:]
    for ref in back:
        z = z + joined(ref[:, :128])
    lane8 = lax.broadcasted_iota(jnp.int32, (8, 128), 1)
    z = jnp.concatenate(
        [jnp.where(lane8 < RANK, z, 0.0), jnp.where(lane8 < RANK, 0.0, z)], 0
    ).astype(BF16)
    total = sums[:, :width] + lax.dot_general(z, up_ref[...], NT, preferred_element_type=F32)
    scale = lax.rsqrt(squares / width_all + EPSILON)
    lane = lax.broadcasted_iota(jnp.int32, (16, 128), 1)
    step = lax.broadcasted_iota(jnp.int32, (16, 128), 0) % STEPS
    first = first_rows((8, 128))

    def of_step(tiles, j):
        return jnp.concatenate(
            [
                jnp.where(first, tile[j : j + 1], tile[STEPS + j : STEPS + j + 1])
                for tile in tiles
            ],
            0,
        )

    for p in range(width // (2 * HD)):
        new_keys, new_values = [], []
        for e in range(2):
            at = slice((2 * p + e) * HD, (2 * p + e + 1) * HD)
            new_keys.append(rounded(rotated(total[:8, at] * scale, cosine, sine)))
            new_values.append(rounded(total[8:, at] * scale))
        at = slice(2 * p * HD, 2 * (p + 1) * HD)
        for out, parts in ((keys_out, new_keys), (values_out, new_values)):
            both = jnp.concatenate(parts, 1).astype(BF16)
            out[0, :, at] = both[:STEPS]
            out[1, :, at] = both[STEPS:]
        keys = [of_step(new_keys, j) for j in range(STEPS)]
        values = [of_step(new_values, j) for j in range(STEPS)]
        scores = [jnp.zeros((16, 128), F32) for _ in range(STEPS)]
        for g in range(GROUP):
            q = qrot_ref[:, (p * GROUP + g) * HD : (p * GROUP + g + 1) * HD].astype(F32)
            for j in range(STEPS):
                dot = jnp.sum(q * keys[j], 1, keepdims=True)
                scores[j] = jnp.where(lane == g, dot, scores[j])
        scores = [jnp.where(j <= step, scores[j], MASKED_SCORE) for j in range(STEPS)]
        end = slice(p * PAIR + GROUP * HD, (p + 1) * PAIR)
        stats = [ref[:, end].astype(F32) for ref in (ca_ref, cb_ref)]
        top = functools.reduce(jnp.maximum, scores + stats)
        fresh = [rounded(jnp.exp2((scores[j] - top) * EXPONENT)) for j in range(STEPS)]
        factors = [jnp.exp2(jnp.minimum(s - top, 0.0) * EXPONENT) for s in stats]
        denom = functools.reduce(jnp.add, fresh)
        for factor, s in zip(factors, stats):
            denom = denom + factor * totals(s)
        inverse = 1.0 / denom
        coefficients = [c * inverse for c in fresh + factors]
        tiles = []
        for g in range(GROUP):
            at = slice(p * PAIR + g * HD, p * PAIR + (g + 1) * HD)
            terms = values + [ref[:, at].astype(F32) for ref in (ca_ref, cb_ref)]
            tile = jnp.zeros((16, 128), F32)
            for c, term in zip(coefficients, terms):
                tile = tile + broadcast_lane(c, g) * term
            tiles.append(tile)
        both = jnp.concatenate(tiles, 1)
        for e in range(2):
            at = slice((2 * p + e) * GROUP * HD, (2 * p + e + 1) * GROUP * HD)
            for s in range(2):
                out_ref[s, :, at] = both[8 * e + 4 * s : 8 * e + 4 * s + 4].astype(BF16)


def final(width, width_all, trig, qrot, caches, parts, own, near, sent, back):
    n = len(sent)
    operands = [trig, qrot, *caches, *parts, own, near, *sent, *back]
    return pl.pallas_call(
        functools.partial(final_kernel, n, width_all),
        in_specs=[VMEM] * len(operands),
        out_specs=[VMEM] * 3,
        out_shape=[
            jax.ShapeDtypeStruct((2, STEPS, width), BF16),
            jax.ShapeDtypeStruct((2, STEPS, width), BF16),
            jax.ShapeDtypeStruct((2, STEPS, GROUP * width), BF16),
        ],
        scratch_shapes=[pltpu.VMEM((width, 128), BF16)],
        compiler_params=pltpu.CompilerParams(vmem_limit_bytes=32 * MEBI),
        name="final",
    )(*operands)


def swap(value, axis, n, distance):
    return lax.ppermute(value, axis, [(i, i ^ distance) for i in range(n)])


def shards(
    n_dp,
    n_tensor,
    hidden,
    norm_gain,
    queries,
    key_weight,
    value_weight,
    key_down,
    key_up,
    value_down,
    value_up,
    key_cache,
    value_cache,
    lengths,
):
    depth, width = key_weight.shape
    rows, up_columns = key_down.shape[0], key_up.shape[0] * 8
    to_dp = lambda value, distance: swap(value, "dp", n_dp, distance)
    to_tensor = lambda value, distance: swap(value, "tensor", n_tensor, distance)
    partners = range(2, n_dp, 2)

    own, tokens, squares = pack(
        hidden, norm_gain, key_down, value_down, key_up, value_up
    )
    near = to_dp(own, 1)
    sent = [to_dp(tokens, d) for d in partners]
    cache, qrot, base, trig = local(
        lengths, tokens, queries, key_cache, value_cache, key_weight, value_weight
    )
    part = rank_products(rows, depth, base, squares, own, near, [tokens, *sent])
    cache, part = combine(cache, to_tensor(cache, 1), part, to_tensor(part, 1))
    part_far = to_tensor(part, 2)
    cache_far = to_tensor(cache, 2)
    replies = answers(len(sent), part, part_far, near, up_columns)
    back = [to_dp(reply, d) for reply, d in zip(replies, partners)]
    return final(
        width,
        float(depth * n_tensor),
        trig,
        qrot,
        (cache, cache_far),
        (part, part_far),
        own,
        near,
        sent,
        back,
    )


def solution(mesh):
    body = functools.partial(shards, mesh.shape["dp"], mesh.shape["tensor"])
    return jax.shard_map(
        body,
        mesh=mesh,
        in_specs=(
            P(("groups", "dp"), None, "tensor"),
            P("tensor"),
            P(("groups", "dp"), None, None),
            P("tensor", None),
            P("tensor", None),
            P(("groups", "dp"), "tensor"),
            P(("groups", "dp"), None),
            P(("groups", "dp"), "tensor"),
            P(("groups", "dp"), None),
            P(("groups", "dp"), "tensor", None),
            P(("groups", "dp"), "tensor", None),
            P(("groups", "dp")),
        ),
        out_specs=(
            P(("groups", "dp"), None, None),
            P(("groups", "dp"), None, None),
            P(("groups", "dp"), None, None),
        ),
        check_vma=False,
    )
```

```python
import functools
import math

import jax
import jax.numpy as jnp
from jax import lax
from jax.experimental import pallas as pl
from jax.experimental.pallas import tpu as pltpu
from jax.sharding import PartitionSpec as P

HD = 128
GROUP = 8
STEPS = 4
RANK = 64
EPSILON = 1e-05
ROPE_BASE = 500000.0
MASKED_SCORE = -1e30
LOWEST_TOP = -1e20
EXPONENT = math.log2(math.e) / math.sqrt(HD)
PAIR = GROUP * HD + 128
CHUNK = 512
AHEAD = 3

F32 = jnp.float32
BF16 = jnp.bfloat16
NT = (((1,), (1,)), ((), ()))
VMEM = pl.BlockSpec(memory_space=pltpu.VMEM)
HBM = pl.BlockSpec(memory_space=pltpu.HBM)
MEBI = 2**20
WHOLE_VMEM = 65000 * 1024
LOCAL_VMEM = 54900 * 1024


def rounded(value):
    return value.astype(BF16).astype(F32)


def split(value):
    high = rounded(value)
    return jnp.concatenate([high, value - high], 0).astype(BF16)


def joined(tile):
    wide = tile.astype(F32)
    return wide[:8] + wide[8:]


def rotated(tile, cosine, sine):
    return tile * cosine + pltpu.roll(tile, HD // 2, 1) * sine


def first_rows(shape):
    return lax.broadcasted_iota(jnp.int32, shape, 0) % 8 < STEPS


def exchanged(a, b):
    first = first_rows(a.shape)
    return (
        jnp.where(first, a, pltpu.roll(b, STEPS, 0)),
        jnp.where(first, pltpu.roll(a, STEPS, 0), b),
    )


def flat(matrix):
    return jnp.concatenate([matrix[i : i + 16] for i in range(0, matrix.shape[0], 16)], 1)


def pack_kernel(*refs):
    sources, (a_ref, b_ref, up_ref, qrot_ref, table_ref) = refs[:8], refs[8:13]
    held, rows_ref, sems = refs[13:21], refs[21], refs[22]
    copies = [
        pltpu.make_async_copy(source, target, sems.at[i])
        for i, (source, target) in enumerate(zip(sources, held))
    ]
    for copy in copies:
        copy.start()
    lengths_ref, x_ref, gain_ref, kd_ref, vd_ref, ku_ref, vu_ref, q_ref = held
    for copy in copies:
        copy.wait()
    x = jnp.concatenate([x_ref[0].astype(F32), x_ref[1].astype(F32)], 0)
    depth = x.shape[1]
    scaled = x * gain_ref[...].astype(F32).reshape(1, depth)
    b_ref[:, : depth // 2] = jnp.concatenate(
        [scaled[:, : depth // 2], scaled[:, depth // 2 :]], 0
    ).astype(BF16)
    row = lax.broadcasted_iota(jnp.int32, (16, 128), 0)
    length = jnp.where(row % 8 < STEPS, lengths_ref[0], lengths_ref[1])
    length = jnp.where(row < 8, length // 64 * 64, length % 64)
    b_ref[:, depth // 2 : depth // 2 + 128] = length.astype(F32).astype(BF16)
    ups = jnp.concatenate([ku_ref[...], vu_ref[...]], 0).T.astype(BF16)
    half = ups.shape[0] // 2
    rows_ref[...] = ups
    up_ref[...] = flat(ups)
    start = pl.multiple_of(lax.axis_index("tensor") % 2 * half, half)
    b_ref[:, depth // 2 + 128 :] = flat(rows_ref[pl.ds(start, half), :])
    own = kd_ref.shape[0]
    for slot, ref in enumerate((kd_ref, vd_ref)):
        down = ref[...]
        if own < 16:
            down = jnp.concatenate([down, jnp.zeros((16 - own, depth), F32)], 0)
        a_ref[:, slot * depth : (slot + 1) * depth] = down.astype(BF16)
    cosine, sine = tables(lengths_ref)
    squares = jnp.broadcast_to(jnp.sum(x * x, 1, keepdims=True), (8, 128))
    table_ref[...] = jnp.concatenate([squares, cosine, sine], 0)
    size = 2 * GROUP * HD
    for p in range(q_ref.shape[2] // size):
        at = pl.ds(pl.multiple_of(pair_at(p) * size, size), size)
        q = jnp.concatenate([q_ref[0, :, at].astype(F32), q_ref[1, :, at].astype(F32)], 0)
        for g in range(GROUP):
            tiles = [
                rotated(q[:, (e * GROUP + g) * HD : (e * GROUP + g + 1) * HD], cosine, sine)
                for e in range(2)
            ]
            at = slice((p * GROUP + g) * HD, (p * GROUP + g + 1) * HD)
            qrot_ref[:, at] = jnp.concatenate(tiles, 0).astype(BF16)


def pack(lengths, hidden, gain, key_down, value_down, key_up, value_up, queries):
    operands = [lengths, hidden, gain, key_down, value_down, key_up.T, value_up.T, queries]
    depth = hidden.shape[2]
    ups = key_up.shape[0] * 8
    return pl.pallas_call(
        pack_kernel,
        in_specs=[HBM] * len(operands),
        out_specs=[VMEM] * 5,
        out_shape=[
            jax.ShapeDtypeStruct((16, 2 * depth), BF16),
            jax.ShapeDtypeStruct((16, depth // 2 + 128 + ups // 2), BF16),
            jax.ShapeDtypeStruct((16, ups), BF16),
            jax.ShapeDtypeStruct((16, queries.shape[2] // 2), BF16),
            jax.ShapeDtypeStruct((24, 128), F32),
        ],
        scratch_shapes=[pltpu.SMEM(lengths.shape, jnp.int32)]
        + [pltpu.VMEM(o.shape, o.dtype) for o in operands[1:]]
        + [
            pltpu.VMEM((key_up.shape[0], 128), BF16),
            pltpu.SemaphoreType.DMA((len(operands),)),
        ],
        compiler_params=pltpu.CompilerParams(vmem_limit_bytes=WHOLE_VMEM),
        name="pack",
    )(*operands)


def tables(lengths_ref):
    shape = (8, HD)
    row = lax.broadcasted_iota(jnp.int32, shape, 0)
    lane = lax.broadcasted_iota(jnp.int32, shape, 1)
    step = row % STEPS
    position = (jnp.where(row < STEPS, lengths_ref[0], lengths_ref[1]) + step).astype(F32)
    pair = lane % (HD // 2)
    frequency = jnp.ones(shape, F32)
    for bit in range(6):
        factor = ROPE_BASE ** (-(2.0 * 2**bit) / HD)
        frequency = jnp.where((pair >> bit) & 1 == 1, frequency * factor, frequency)
    angle = position * frequency
    sine = jnp.sin(angle)
    return jnp.cos(angle), jnp.where(lane < HD // 2, -sine, sine)


def attend(p, limit, q_ref, k_ref, v_ref, out_ref):
    halves = [[], []]
    for g in range(GROUP):
        tile = q_ref[:, (p * GROUP + g) * HD : (p * GROUP + g + 1) * HD].astype(F32)
        halves[0].append(tile[:8])
        halves[1].append(tile[8:])
    mixed = [[exchanged(halves[e][g], halves[e][g + 4]) for g in range(4)] for e in range(2)]
    zero = jnp.zeros((32, HD), F32)
    numers, stats = [], []
    lane8 = lax.broadcasted_iota(jnp.int32, (8, 128), 1)
    pair = slice(2 * p * HD, 2 * (p + 1) * HD)
    for s in range(2):
        rows = [jnp.concatenate([mixed[e][g][s] for g in range(4)], 0) for e in range(2)]
        queries = jnp.concatenate(
            [jnp.concatenate([rows[0], zero], 1), jnp.concatenate([zero, rows[1]], 1)], 0
        ).astype(BF16)
        scores = lax.dot_general(queries, k_ref[s, :, pair], NT, preferred_element_type=F32)
        place = lax.broadcasted_iota(jnp.int32, scores.shape, 1)
        bound = limit[STEPS * s : STEPS * s + 1, :1].astype(jnp.int32)
        masked = jnp.where(place < bound, scores, MASKED_SCORE)
        top = rounded(jnp.maximum(jnp.max(masked, 1, keepdims=True), LOWEST_TOP))
        weights = jnp.exp2((masked - top) * EXPONENT).astype(BF16)
        total = jnp.sum(weights.astype(F32), 1, keepdims=True)
        numers.append(jnp.dot(weights, v_ref[s, :, pair], preferred_element_type=F32))
        high = rounded(total)
        compact = []
        for e in range(2):
            tile = jnp.zeros((8, 128), F32)
            for g in range(4):
                at = slice(32 * e + 8 * g, 32 * e + 8 * g + 8)
                for slot, value in enumerate((top, high, total - high)):
                    tile = jnp.where(lane8 == slot * GROUP + g, value[at], tile)
            compact.append(tile)
        stats.append(compact)
    outs, ends = [[], []], []
    for e in range(2):
        back = []
        for g in range(4):
            at = slice(32 * e + 8 * g, 32 * e + 8 * g + 8)
            cols = slice(e * HD, (e + 1) * HD)
            back.append(exchanged(numers[0][at, cols], numers[1][at, cols]))
        outs[e] = [b[0] for b in back] + [b[1] for b in back]
        a, b = exchanged(stats[0][e], stats[1][e])
        ends.append(jnp.where(lane8 % 8 < 4, a, pltpu.roll(b, 4, 1)))
    p = p % (out_ref.shape[1] // PAIR)
    for g in range(GROUP):
        at = slice(p * PAIR + g * HD, p * PAIR + (g + 1) * HD)
        out_ref[:, at] = jnp.concatenate([outs[0][g], outs[1][g]], 0).astype(BF16)
    out_ref[:, p * PAIR + GROUP * HD : (p + 1) * PAIR] = jnp.concatenate(ends, 0).astype(BF16)


def pair_at(i):
    return i ^ (lax.axis_index("tensor") % 2 * 2)


def local_kernel(
    x_hbm, q_hbm, k_hbm, v_hbm, wk_hbm, wv_hbm,
    keep_ref, send_ref, base_ref,
    x_ref, q_ref, k_ref, v_ref, wk_ref, wv_ref, x_sem, q_sem, cache_sem, weight_sem,
):
    pairs = k_hbm.shape[2] // (2 * HD)
    chunks = wk_hbm.shape[0] // CHUNK
    width = wk_hbm.shape[1]
    x_copy = pltpu.make_async_copy(x_hbm, x_ref, x_sem)
    x_copy.start()
    q_copy = pltpu.make_async_copy(q_hbm, q_ref, q_sem)
    q_copy.start()
    steps = []
    for p in range(pairs):
        size = 2 * HD
        start = pl.multiple_of(pair_at(p) * size, size)
        steps.append(
            [
                pltpu.make_async_copy(
                    source.at[:, :, pl.ds(start, size)],
                    target.at[:, :, pl.ds(p * size, size)],
                    cache_sem.at[p, i],
                )
                for i, (source, target) in enumerate(((k_hbm, k_ref), (v_hbm, v_ref)))
            ]
        )
    core = lax.axis_index("tensor") % 2
    for c in range(chunks):
        copies = []
        for i, (source, target) in enumerate(((wk_hbm, wk_ref), (wv_hbm, wv_ref))):
            for h in range(2):
                start = pl.multiple_of((core ^ h) * (width // 2), width // 2)
                copies.append(
                    pltpu.make_async_copy(
                        source.at[pl.ds(c * CHUNK, CHUNK), pl.ds(start, width // 2)],
                        target.at[pl.ds(c * CHUNK, CHUNK), pl.ds(h * (width // 2), width // 2)],
                        weight_sem.at[c, 2 * i + h],
                    )
                )
        steps.append(copies)
    for copies in steps[:AHEAD]:
        for copy in copies:
            copy.start()

    def arrive(i):
        for copy in steps[i]:
            copy.wait()
        if i + AHEAD < len(steps):
            for copy in steps[i + AHEAD]:
                copy.start()

    x_copy.wait()
    half = wk_hbm.shape[0] // 2
    x = x_ref[:, :half].astype(F32)
    x = jnp.concatenate([x[:8], x[8:]], 1).astype(BF16)
    first = lax.axis_index("tensor") * k_hbm.shape[1]
    limit = joined(x_ref[:, half : half + 128]) - first.astype(F32)
    q_copy.wait()
    for p in range(pairs):
        arrive(p)
        attend(p, limit, q_ref, k_ref, v_ref, keep_ref if p < pairs // 2 else send_ref)
    total = None
    for c in range(chunks):
        arrive(pairs + c)
        rows = x[:, c * CHUNK : (c + 1) * CHUNK]
        part = jnp.concatenate(
            [
                jnp.dot(rows, ref[c * CHUNK : (c + 1) * CHUNK], preferred_element_type=F32)
                for ref in (wk_ref, wv_ref)
            ],
            0,
        )
        total = part if total is None else total + part
    base_ref[...] = total


def local(message, queries, key_cache, value_cache, key_weight, value_weight):
    seqs, length, width = key_cache.shape
    depth = key_weight.shape[0]
    pairs = width // (2 * HD)
    operands = [message, queries, key_cache, value_cache, key_weight, value_weight]
    return pl.pallas_call(
        local_kernel,
        in_specs=[HBM] * 6,
        out_specs=[VMEM] * 3,
        out_shape=[
            jax.ShapeDtypeStruct((16, pairs // 2 * PAIR), BF16),
            jax.ShapeDtypeStruct((16, pairs // 2 * PAIR), BF16),
            jax.ShapeDtypeStruct((16, width), F32),
        ],
        scratch_shapes=[pltpu.VMEM(o.shape, BF16) for o in operands]
        + [
            pltpu.SemaphoreType.DMA,
            pltpu.SemaphoreType.DMA,
            pltpu.SemaphoreType.DMA((pairs, 2)),
            pltpu.SemaphoreType.DMA((depth // CHUNK, 4)),
        ],
        compiler_params=pltpu.CompilerParams(vmem_limit_bytes=LOCAL_VMEM),
        cost_estimate=pl.CostEstimate(
            flops=4 * 64 * 256 * seqs * length * pairs + 4 * 16 * depth * width,
            bytes_accessed=4 * seqs * length * width + 4 * depth * width,
            transcendentals=64 * seqs * length * pairs,
        ),
        name="local",
    )(*operands)


def rank_kernel(n, rows, depth, columns, *refs):
    base_ref, table_ref, own_ref, near_ref = refs[:4]
    tokens, out_ref = refs[4 : 4 + n], refs[4 + n]
    half = base_ref.shape[1] // 2
    place = lax.axis_index("dp")
    x = []
    for ref in tokens:
        part = ref[:, : depth // 2].astype(F32)
        x.append(jnp.concatenate([part[:8], part[8:]], 1))
    x = jnp.concatenate(x, 0).astype(BF16)
    fill = jnp.zeros((RANK - 16, depth), BF16)
    z = None
    for ref, at in ((own_ref, place), (near_ref, place ^ 1)):
        down = jnp.concatenate([ref[:, :depth], fill, ref[:, depth:], fill], 0)
        part = lax.dot_general(x, down, NT, preferred_element_type=F32)
        part = pltpu.roll(part, at * rows, 1)
        z = part if z is None else z + part
    out_ref[:, :half] = base_ref[:, half:].astype(BF16)
    out_ref[:, half : half + 128] = split(table_ref[:8])
    for i in range(n):
        at = half + 128 * (i + 1)
        out_ref[:, at : at + 128] = split(z[8 * i : 8 * i + 8])
    if columns:
        out_ref[:, half + 128 * (n + 1) :] = tokens[1][:, depth // 2 + 128 :]


def rank_products(rows, depth, columns, base, table, own, near, tokens):
    n = len(tokens)
    return pl.pallas_call(
        functools.partial(rank_kernel, n, rows, depth, columns),
        in_specs=[VMEM] * (4 + n),
        out_specs=VMEM,
        out_shape=jax.ShapeDtypeStruct((16, base.shape[1] // 2 + 128 * (n + 1) + columns), BF16),
        compiler_params=pltpu.CompilerParams(vmem_limit_bytes=32 * MEBI),
        name="rank_products",
    )(base, table, own, near, *tokens)


def broadcast_lane(tile, lane):
    return jnp.broadcast_to(tile[:, lane : lane + 1], tile.shape)


def combine_part_kernel(n, *refs):
    base_ref, mine_ref, theirs_ref, out_ref = (*refs[:3], refs[-1])
    if len(refs) > 4:
        up_ref, sent_ref, out_ref, has_ref = refs[3:]
        core = lax.axis_index("tensor") % 2
        columns = up_ref.shape[1] // 2
        mine = sent_ref[:, sent_ref.shape[1] - columns :].astype(F32)
        theirs = theirs_ref[:, theirs_ref.shape[1] - columns :].astype(F32)
        here = lax.axis_index("dp") // 2 == core
        for h in range(2):
            at = slice(h * columns, (h + 1) * columns)
            far = jnp.where(core == h, mine, theirs)
            has_ref[:, at] = jnp.where(here, up_ref[:, at].astype(F32), far).astype(BF16)
    half = base_ref.shape[1] // 2
    own = base_ref[:, :half] + theirs_ref[:, :half].astype(F32)
    out_ref[:, :half] = own.astype(BF16)
    at = slice(half, half + 128 * (n + 2))
    sums = mine_ref[:, at].astype(F32) + theirs_ref[:, at].astype(F32)
    out_ref[:, half:] = split(sums[:8] + sums[8:])


def combine_part(n, base, mine, theirs, extra):
    half = base.shape[1] // 2
    out_shape = [jax.ShapeDtypeStruct((16, half + 128 * (n + 2)), BF16)]
    if extra:
        out_shape.append(jax.ShapeDtypeStruct(extra[0].shape, BF16))
    return pl.pallas_call(
        functools.partial(combine_part_kernel, n),
        in_specs=[VMEM] * (3 + len(extra)),
        out_specs=[VMEM] * len(out_shape),
        out_shape=out_shape,
        compiler_params=pltpu.CompilerParams(vmem_limit_bytes=32 * MEBI),
        name="combine_part",
    )(base, mine, theirs, *extra)


def combine_cache_kernel(a_ref, b_ref, out_ref):
    lane = lax.broadcasted_iota(jnp.int32, (16, 128), 1)
    for p in range(out_ref.shape[1] // PAIR):
        end = slice(p * PAIR + GROUP * HD, (p + 1) * PAIR)
        a, b = a_ref[:, end].astype(F32), b_ref[:, end].astype(F32)
        top = jnp.maximum(a, b)
        fa = jnp.exp2(jnp.minimum(a - top, 0.0) * EXPONENT)
        fb = jnp.exp2(jnp.minimum(b - top, 0.0) * EXPONENT)
        total = fa * totals(a) + fb * totals(b)
        high = rounded(total)
        stats = jnp.where(lane < GROUP, top, 0.0)
        stats = jnp.where(lane // GROUP == 1, pltpu.roll(high, GROUP, 1), stats)
        stats = jnp.where(lane // GROUP == 2, pltpu.roll(total - high, 2 * GROUP, 1), stats)
        out_ref[:, end] = stats.astype(BF16)
        for g in range(GROUP):
            at = slice(p * PAIR + g * HD, p * PAIR + (g + 1) * HD)
            out_ref[:, at] = (
                broadcast_lane(fa, g) * a_ref[:, at].astype(F32)
                + broadcast_lane(fb, g) * b_ref[:, at].astype(F32)
            ).astype(BF16)


def totals(stats):
    return pltpu.roll(stats, 128 - GROUP, 1) + pltpu.roll(stats, 128 - 2 * GROUP, 1)


def combine_cache(a, b):
    return pl.pallas_call(
        combine_cache_kernel,
        in_specs=[VMEM] * 2,
        out_specs=VMEM,
        out_shape=jax.ShapeDtypeStruct(a.shape, BF16),
        compiler_params=pltpu.CompilerParams(vmem_limit_bytes=32 * MEBI),
        name="combine_cache",
    )(a, b)


def answer_kernel(at, pa_ref, pb_ref, *outs):
    z = pa_ref[:, at:].astype(F32) + pb_ref[:, at:].astype(F32)
    for i, ref in enumerate(outs):
        part = z[:, 128 * (i + 1) : 128 * (i + 2)]
        ref[...] = split(part[:8] + part[8:])


def answers(n, part_a, part_b):
    at = part_a.shape[1] - 128 * (n + 1)
    return pl.pallas_call(
        functools.partial(answer_kernel, at),
        in_specs=[VMEM] * 2,
        out_specs=[VMEM] * n,
        out_shape=[jax.ShapeDtypeStruct((16, 128), BF16)] * n,
        compiler_params=pltpu.CompilerParams(vmem_limit_bytes=32 * MEBI),
        name="answers",
    )(part_a, part_b)


def merge_kernel(n, paired, width_all, *refs):
    table_ref, qrot_ref, pa_ref, pb_ref, ca_ref, cb_ref = refs[:6]
    backs, (ua_ref, ub_ref, out_ref) = refs[6 : 6 + n], refs[6 + n :]
    pairs = ca_ref.shape[1] // PAIR
    width = pairs * 2 * HD
    cosine, sine = table_ref[8:16], table_ref[16:]
    sums = pa_ref[...].astype(F32) + pb_ref[...].astype(F32)
    tail = sums[:8, width : width + 256] + sums[8:, width : width + 256]
    squares, z = tail[:, :128], tail[:, 128:]
    for ref in backs:
        z = z + joined(ref[...])
    lane8 = lax.broadcasted_iota(jnp.int32, (8, 128), 1)
    z = jnp.concatenate(
        [jnp.where(lane8 < RANK, z, 0.0), jnp.where(lane8 < RANK, 0.0, z)], 0
    ).astype(BF16)
    adapted = []
    for ref in (ua_ref, ub_ref):
        ups = jnp.concatenate([ref[:, i : i + 128] for i in range(0, ref.shape[1], 128)], 0)
        adapted.append(lax.dot_general(z, ups, NT, preferred_element_type=F32))
    if paired:
        even = lax.axis_index("dp") % 2 == 0
        a, b = adapted
        adapted = [jnp.where(even, a, b), jnp.where(even, b, a)]
    total = sums[:, :width] + jnp.concatenate(adapted, 1)
    scale = lax.rsqrt(squares / width_all + EPSILON)
    lane = lax.broadcasted_iota(jnp.int32, (16, 128), 1)
    step = lax.broadcasted_iota(jnp.int32, (16, 128), 0) % STEPS
    first = first_rows((8, 128))

    def of_step(tiles, j):
        return jnp.concatenate(
            [
                jnp.where(first, tile[j : j + 1], tile[STEPS + j : STEPS + j + 1])
                for tile in tiles
            ],
            0,
        )

    for p in range(pairs):
        new_keys, new_values = [], []
        for e in range(2):
            at = slice((2 * p + e) * HD, (2 * p + e + 1) * HD)
            new_keys.append(rounded(rotated(total[:8, at] * scale, cosine, sine)))
            new_values.append(rounded(total[8:, at] * scale))
            fresh = jnp.concatenate([new_keys[e], new_values[e]], 0)
            start = pairs * GROUP * HD + (2 * p + e) * HD
            out_ref[:, start : start + HD] = fresh.astype(BF16)
        keys = [of_step(new_keys, j) for j in range(STEPS)]
        values = [of_step(new_values, j) for j in range(STEPS)]
        scores = [jnp.zeros((16, 128), F32) for _ in range(STEPS)]
        for g in range(GROUP):
            q = qrot_ref[:, (p * GROUP + g) * HD : (p * GROUP + g + 1) * HD].astype(F32)
            for j in range(STEPS):
                dot = jnp.sum(q * keys[j], 1, keepdims=True)
                scores[j] = jnp.where(lane == g, dot, scores[j])
        scores = [jnp.where(j <= step, scores[j], MASKED_SCORE) for j in range(STEPS)]
        end = slice(p * PAIR + GROUP * HD, (p + 1) * PAIR)
        stats = [ref[:, end].astype(F32) for ref in (ca_ref, cb_ref)]
        top = functools.reduce(jnp.maximum, scores + stats)
        fresh = [rounded(jnp.exp2((scores[j] - top) * EXPONENT)) for j in range(STEPS)]
        factors = [jnp.exp2(jnp.minimum(s - top, 0.0) * EXPONENT) for s in stats]
        denom = functools.reduce(jnp.add, fresh)
        for factor, s in zip(factors, stats):
            denom = denom + factor * totals(s)
        inverse = 1.0 / denom
        coefficients = [c * inverse for c in fresh + factors]
        for g in range(GROUP):
            at = slice(p * PAIR + g * HD, p * PAIR + (g + 1) * HD)
            terms = values + [ref[:, at].astype(F32) for ref in (ca_ref, cb_ref)]
            tile = jnp.zeros((16, 128), F32)
            for c, term in zip(coefficients, terms):
                tile = tile + broadcast_lane(c, g) * term
            out_ref[:, (p * GROUP + g) * HD : (p * GROUP + g + 1) * HD] = tile.astype(BF16)


def merge(paired, width_all, table, qrot, parts, caches, backs, ups):
    operands = [table, qrot, *parts, *caches, *backs, *ups]
    pairs = caches[0].shape[1] // PAIR
    return pl.pallas_call(
        functools.partial(merge_kernel, len(backs), paired, width_all),
        in_specs=[VMEM] * len(operands),
        out_specs=VMEM,
        out_shape=jax.ShapeDtypeStruct((16, pairs * (GROUP + 2) * HD), BF16),
        compiler_params=pltpu.CompilerParams(vmem_limit_bytes=32 * MEBI),
        name="merge",
    )(*operands)


def place_kernel(mine_ref, theirs_ref, keys_out, values_out, out_ref):
    pairs = mine_ref.shape[1] // ((GROUP + 2) * HD)
    for c, ref in enumerate((mine_ref, theirs_ref)):
        for p in range(pairs):
            pair = pair_at(c * pairs + p)
            tiles = ref[:, p * GROUP * HD : (p + 1) * GROUP * HD].astype(F32)
            size = GROUP * HD
            for e in range(2):
                at = pl.ds(pl.multiple_of((2 * pair + e) * size, size), size)
                for s in range(2):
                    rows = slice(8 * e + 4 * s, 8 * e + 4 * s + 4)
                    out_ref[s, :, at] = tiles[rows].astype(BF16)
            start = pairs * GROUP * HD + p * 2 * HD
            fresh = ref[:, start : start + 2 * HD].astype(F32)
            at = pl.ds(pl.multiple_of(pair * 2 * HD, 2 * HD), 2 * HD)
            for i, out in enumerate((keys_out, values_out)):
                for s in range(2):
                    rows = slice(8 * i + 4 * s, 8 * i + 4 * s + 4)
                    out[s, :, at] = fresh[rows].astype(BF16)


def place(width, mine, theirs):
    return pl.pallas_call(
        place_kernel,
        in_specs=[VMEM] * 2,
        out_specs=[VMEM] * 3,
        out_shape=[
            jax.ShapeDtypeStruct((2, STEPS, width), BF16),
            jax.ShapeDtypeStruct((2, STEPS, width), BF16),
            jax.ShapeDtypeStruct((2, STEPS, GROUP * width), BF16),
        ],
        compiler_params=pltpu.CompilerParams(vmem_limit_bytes=32 * MEBI),
        name="place",
    )(mine, theirs)


def swap(value, axis, n, distance):
    return lax.ppermute(value, axis, [(i, i ^ distance) for i in range(n)])


def shards(
    n_dp,
    n_tensor,
    hidden,
    norm_gain,
    queries,
    key_weight,
    value_weight,
    key_down,
    key_up,
    value_down,
    value_up,
    key_cache,
    value_cache,
    lengths,
):
    depth, width = key_weight.shape
    rows = key_down.shape[0]
    to_dp = lambda value, distance: swap(value, "dp", n_dp, distance)
    to_tensor = lambda value, distance: swap(value, "tensor", n_tensor, distance)
    partners = range(2, n_dp, 2)
    n = len(partners)
    paired = n_dp == 4

    own, tokens, ups, qrot, table = pack(
        lengths, hidden, norm_gain, key_down, value_down, key_up, value_up, queries
    )
    near = to_dp(own, 1)
    sent = [to_dp(tokens, d) for d in partners]
    keep, send, base = local(tokens, qrot, key_cache, value_cache, key_weight, value_weight)
    received = to_tensor(send, 1)
    columns = ups.shape[1] // 2 if paired else 0
    part = rank_products(rows, depth, columns, base, table, own, near, [tokens, *sent])
    extra = [ups, sent[0]] if paired else []
    part, *has = combine_part(n, base, part, to_tensor(part, 1), extra)
    if paired:
        ups = [has[0], to_dp(has[0], 1)]
    else:
        ups = lax.all_gather(ups, "dp").reshape(n_dp, 16, -1, 128).transpose(0, 2, 1, 3)
        ups = ups.reshape(2, 2, 16, 16, 128).transpose(0, 1, 3, 2, 4).reshape(2, 2, 16, -1)
        ups = lax.dynamic_index_in_dim(ups, lax.axis_index("tensor") % 2, 0, keepdims=False)
        ups = [ups[0], ups[1]]
    cache = combine_cache(keep, received)
    part_far = to_tensor(part, 2)
    cache_far = to_tensor(cache, 2)
    backs = [to_dp(reply, d) for reply, d in zip(answers(n, part, part_far), partners)]
    merged = merge(
        paired,
        float(depth * n_tensor),
        table,
        qrot,
        (part, part_far),
        (cache, cache_far),
        backs,
        ups,
    )
    return place(width, merged, to_tensor(merged, 1))


def solution(mesh):
    body = functools.partial(shards, mesh.shape["dp"], mesh.shape["tensor"])
    return jax.shard_map(
        body,
        mesh=mesh,
        in_specs=(
            P(("groups", "dp"), None, "tensor"),
            P("tensor"),
            P(("groups", "dp"), None, None),
            P("tensor", None),
            P("tensor", None),
            P(("groups", "dp"), "tensor"),
            P(("groups", "dp"), None),
            P(("groups", "dp"), "tensor"),
            P(("groups", "dp"), None),
            P(("groups", "dp"), "tensor", None),
            P(("groups", "dp"), "tensor", None),
            P(("groups", "dp")),
        ),
        out_specs=(
            P(("groups", "dp"), None, None),
            P(("groups", "dp"), None, None),
            P(("groups", "dp"), None, None),
        ),
        check_vma=False,
    )
```

```python
import functools
import math

import jax
import jax.numpy as jnp
from jax import lax
from jax.experimental import pallas as pl
from jax.experimental.pallas import tpu as pltpu
from jax.sharding import PartitionSpec as P

HD = 128
GROUP = 8
STEPS = 4
RANK = 64
EPSILON = 1e-05
ROPE_BASE = 500000.0
MASKED_SCORE = -1e30
LOWEST_TOP = -1e20
EXPONENT = math.log2(math.e) / math.sqrt(HD)
PAIR = GROUP * HD + 128
CHUNK = 512
AHEAD = 3

F32 = jnp.float32
BF16 = jnp.bfloat16
NT = (((1,), (1,)), ((), ()))
VMEM = pl.BlockSpec(memory_space=pltpu.VMEM)
HBM = pl.BlockSpec(memory_space=pltpu.HBM)
MEBI = 2**20
WHOLE_VMEM = 65000 * 1024
LOCAL_VMEM = 54800 * 1024


def rounded(value):
    return value.astype(BF16).astype(F32)


def split(value):
    high = rounded(value)
    return jnp.concatenate([high, value - high], 0).astype(BF16)


def joined(tile):
    wide = tile.astype(F32)
    return wide[:8] + wide[8:]


def rotated(tile, cosine, sine):
    return tile * cosine + pltpu.roll(tile, HD // 2, 1) * sine


def first_rows(shape):
    return lax.broadcasted_iota(jnp.int32, shape, 0) % 8 < STEPS


def exchanged(a, b):
    first = first_rows(a.shape)
    return (
        jnp.where(first, a, pltpu.roll(b, STEPS, 0)),
        jnp.where(first, pltpu.roll(a, STEPS, 0), b),
    )


def flat(matrix):
    return jnp.concatenate([matrix[i : i + 16] for i in range(0, matrix.shape[0], 16)], 1)


def pack_kernel(*refs):
    sources, (a_ref, b_ref), held, sems = refs[:7], refs[7:9], refs[9:16], refs[16]
    copies = [
        pltpu.make_async_copy(source, target, sems.at[i])
        for i, (source, target) in enumerate(zip(sources, held))
    ]
    for copy in copies:
        copy.start()
    lengths_ref, x_ref, gain_ref, kd_ref, vd_ref, ku_ref, vu_ref = held
    for copy in copies:
        copy.wait()
    x = jnp.concatenate([x_ref[0].astype(F32), x_ref[1].astype(F32)], 0)
    depth = x.shape[1]
    scaled = x * gain_ref[...].astype(F32).reshape(1, depth)
    b_ref[:, : depth // 2] = jnp.concatenate(
        [scaled[:, : depth // 2], scaled[:, depth // 2 :]], 0
    ).astype(BF16)
    row = lax.broadcasted_iota(jnp.int32, (16, 128), 0)
    length = jnp.where(row % 8 < STEPS, lengths_ref[0], lengths_ref[1])
    length = jnp.where(row < 8, length // 64 * 64, length % 64)
    b_ref[:, depth // 2 : depth // 2 + 128] = length.astype(F32).astype(BF16)
    squares = jnp.broadcast_to(jnp.sum(x * x, 1, keepdims=True), (8, 128))
    b_ref[:, depth // 2 + 128 : depth // 2 + 256] = split(squares)
    ups = jnp.concatenate([ku_ref[...], vu_ref[...]], 0).T.astype(BF16)
    b_ref[:, depth // 2 + 256 :] = flat(ups)
    own = kd_ref.shape[0]
    for slot, ref in enumerate((kd_ref, vd_ref)):
        down = ref[...]
        if own < 16:
            down = jnp.concatenate([down, jnp.zeros((16 - own, depth), F32)], 0)
        a_ref[:, slot * depth : (slot + 1) * depth] = down.astype(BF16)


def pack(lengths, hidden, gain, key_down, value_down, key_up, value_up):
    operands = [lengths, hidden, gain, key_down, value_down, key_up.T, value_up.T]
    depth = hidden.shape[2]
    ups = key_up.shape[0] * 8
    return pl.pallas_call(
        pack_kernel,
        in_specs=[HBM] * len(operands),
        out_specs=[VMEM] * 2,
        out_shape=[
            jax.ShapeDtypeStruct((16, 2 * depth), BF16),
            jax.ShapeDtypeStruct((16, depth // 2 + 256 + ups), BF16),
        ],
        scratch_shapes=[pltpu.SMEM(lengths.shape, jnp.int32)]
        + [pltpu.VMEM(o.shape, o.dtype) for o in operands[1:]]
        + [pltpu.SemaphoreType.DMA((len(operands),))],
        compiler_params=pltpu.CompilerParams(vmem_limit_bytes=WHOLE_VMEM),
        name="pack",
    )(*operands)


def tables(length):
    shape = length.shape
    row = lax.broadcasted_iota(jnp.int32, shape, 0)
    lane = lax.broadcasted_iota(jnp.int32, shape, 1)
    position = length + (row % STEPS).astype(F32)
    pair = lane % (HD // 2)
    frequency = jnp.ones(shape, F32)
    for bit in range(6):
        factor = ROPE_BASE ** (-(2.0 * 2**bit) / HD)
        frequency = jnp.where((pair >> bit) & 1 == 1, frequency * factor, frequency)
    angle = position * frequency
    sine = jnp.sin(angle)
    return jnp.cos(angle), jnp.where(lane < HD // 2, -sine, sine)


def attend(p, limit, cosine, sine, q_ref, k_ref, v_ref, out_ref, qrot_ref):
    halves = [[], []]
    for e in range(2):
        for g in range(GROUP):
            at = slice(((2 * p + e) * GROUP + g) * HD, ((2 * p + e) * GROUP + g + 1) * HD)
            q = jnp.concatenate([q_ref[0, :, at].astype(F32), q_ref[1, :, at].astype(F32)], 0)
            halves[e].append(rotated(q, cosine, sine))
    if qrot_ref is not None:
        for g in range(GROUP):
            at = slice((p * GROUP + g) * HD, (p * GROUP + g + 1) * HD)
            qrot_ref[:, at] = jnp.concatenate([halves[0][g], halves[1][g]], 0).astype(BF16)
    mixed = [[exchanged(halves[e][g], halves[e][g + 4]) for g in range(4)] for e in range(2)]
    zero = jnp.zeros((32, HD), F32)
    numers, stats = [], []
    lane8 = lax.broadcasted_iota(jnp.int32, (8, 128), 1)
    pair = slice(2 * p * HD, 2 * (p + 1) * HD)
    for s in range(2):
        rows = [jnp.concatenate([mixed[e][g][s] for g in range(4)], 0) for e in range(2)]
        queries = jnp.concatenate(
            [jnp.concatenate([rows[0], zero], 1), jnp.concatenate([zero, rows[1]], 1)], 0
        ).astype(BF16)
        scores = lax.dot_general(queries, k_ref[s, :, pair], NT, preferred_element_type=F32)
        place = lax.broadcasted_iota(jnp.int32, scores.shape, 1)
        bound = limit[STEPS * s : STEPS * s + 1, :1].astype(jnp.int32)
        masked = jnp.where(place < bound, scores, MASKED_SCORE)
        top = rounded(jnp.maximum(jnp.max(masked, 1, keepdims=True), LOWEST_TOP))
        weights = jnp.exp2((masked - top) * EXPONENT).astype(BF16)
        total = jnp.sum(weights.astype(F32), 1, keepdims=True)
        numers.append(jnp.dot(weights, v_ref[s, :, pair], preferred_element_type=F32))
        high = rounded(total)
        compact = []
        for e in range(2):
            tile = jnp.zeros((8, 128), F32)
            for g in range(4):
                at = slice(32 * e + 8 * g, 32 * e + 8 * g + 8)
                for slot, value in enumerate((top, high, total - high)):
                    tile = jnp.where(lane8 == slot * GROUP + g, value[at], tile)
            compact.append(tile)
        stats.append(compact)
    outs, ends = [[], []], []
    for e in range(2):
        back = []
        for g in range(4):
            at = slice(32 * e + 8 * g, 32 * e + 8 * g + 8)
            cols = slice(e * HD, (e + 1) * HD)
            back.append(exchanged(numers[0][at, cols], numers[1][at, cols]))
        outs[e] = [b[0] for b in back] + [b[1] for b in back]
        a, b = exchanged(stats[0][e], stats[1][e])
        ends.append(jnp.where(lane8 % 8 < 4, a, pltpu.roll(b, 4, 1)))
    p = p % (out_ref.shape[1] // PAIR)
    for g in range(GROUP):
        at = slice(p * PAIR + g * HD, p * PAIR + (g + 1) * HD)
        out_ref[:, at] = jnp.concatenate([outs[0][g], outs[1][g]], 0).astype(BF16)
    out_ref[:, p * PAIR + GROUP * HD : (p + 1) * PAIR] = jnp.concatenate(ends, 0).astype(BF16)


def pair_at(i):
    return i ^ (lax.axis_index("tensor") % 2 * 2)


def local_kernel(
    x_hbm, q_hbm, k_hbm, v_hbm, wk_hbm, wv_hbm,
    keep_ref, send_ref, base_ref, qrot_ref, table_ref,
    x_ref, q_ref, k_ref, v_ref, wk_ref, wv_ref, x_sem, q_sem, cache_sem, weight_sem,
):
    pairs = k_hbm.shape[2] // (2 * HD)
    chunks = wk_hbm.shape[0] // CHUNK
    width = wk_hbm.shape[1]
    x_copy = pltpu.make_async_copy(x_hbm, x_ref, x_sem)
    x_copy.start()
    q_copies = []
    for p in range(pairs):
        size = 2 * GROUP * HD
        start = pl.multiple_of(pair_at(p) * size, size)
        q_copies.append(
            pltpu.make_async_copy(
                q_hbm.at[:, :, pl.ds(start, size)],
                q_ref.at[:, :, pl.ds(p * size, size)],
                q_sem.at[p],
            )
        )
        q_copies[p].start()
    caches, weights = [], []
    for p in range(pairs):
        size = 2 * HD
        start = pl.multiple_of(pair_at(p) * size, size)
        caches.append(
            [
                pltpu.make_async_copy(
                    source.at[:, :, pl.ds(start, size)],
                    target.at[:, :, pl.ds(p * size, size)],
                    cache_sem.at[p, i],
                )
                for i, (source, target) in enumerate(((k_hbm, k_ref), (v_hbm, v_ref)))
            ]
        )
    core = lax.axis_index("tensor") % 2
    for c in range(chunks):
        copies = []
        for i, (source, target) in enumerate(((wk_hbm, wk_ref), (wv_hbm, wv_ref))):
            for h in range(2):
                start = pl.multiple_of((core ^ h) * (width // 2), width // 2)
                copies.append(
                    pltpu.make_async_copy(
                        source.at[pl.ds(c * CHUNK, CHUNK), pl.ds(start, width // 2)],
                        target.at[pl.ds(c * CHUNK, CHUNK), pl.ds(h * (width // 2), width // 2)],
                        weight_sem.at[c, 2 * i + h],
                    )
                )
        weights.append(copies)
    steps = caches[:1] + [k + w for k, w in zip(caches[1:], weights)] + weights[pairs - 1 :]
    for copies in steps[:AHEAD]:
        for copy in copies:
            copy.start()

    x_copy.wait()
    half = wk_hbm.shape[0] // 2
    x = x_ref[:, :half].astype(F32)
    x = jnp.concatenate([x[:8], x[8:]], 1).astype(BF16)
    length = joined(x_ref[:, half : half + 128])
    cosine, sine = tables(length)
    table_ref[...] = jnp.concatenate([joined(x_ref[:, half + 128 : half + 256]), cosine, sine], 0)
    limit = length - (lax.axis_index("tensor") * k_hbm.shape[1]).astype(F32)
    for copy in q_copies:
        copy.wait()
    total = None
    for i, copies in enumerate(steps):
        for copy in copies:
            copy.wait()
        if i + AHEAD < len(steps):
            for copy in steps[i + AHEAD]:
                copy.start()
        if i >= 1:
            at = slice((i - 1) * CHUNK, i * CHUNK)
            part = jnp.concatenate(
                [
                    jnp.dot(x[:, at], ref[at], preferred_element_type=F32)
                    for ref in (wk_ref, wv_ref)
                ],
                0,
            )
            total = part if total is None else total + part
        if i < pairs:
            kept = i < pairs // 2
            out_ref = keep_ref if kept else send_ref
            attend(
                i, limit, cosine, sine, q_ref, k_ref, v_ref, out_ref, qrot_ref if kept else None
            )
    base_ref[...] = total


def local(message, queries, key_cache, value_cache, key_weight, value_weight):
    seqs, length, width = key_cache.shape
    depth = key_weight.shape[0]
    pairs = width // (2 * HD)
    operands = [message, queries, key_cache, value_cache, key_weight, value_weight]
    return pl.pallas_call(
        local_kernel,
        in_specs=[HBM] * 6,
        out_specs=[VMEM] * 5,
        out_shape=[
            jax.ShapeDtypeStruct((16, pairs // 2 * PAIR), BF16),
            jax.ShapeDtypeStruct((16, pairs // 2 * PAIR), BF16),
            jax.ShapeDtypeStruct((16, width), F32),
            jax.ShapeDtypeStruct((16, pairs // 2 * GROUP * HD), BF16),
            jax.ShapeDtypeStruct((24, 128), F32),
        ],
        scratch_shapes=[pltpu.VMEM(o.shape, BF16) for o in operands]
        + [
            pltpu.SemaphoreType.DMA,
            pltpu.SemaphoreType.DMA((pairs,)),
            pltpu.SemaphoreType.DMA((pairs, 2)),
            pltpu.SemaphoreType.DMA((depth // CHUNK, 4)),
        ],
        compiler_params=pltpu.CompilerParams(vmem_limit_bytes=LOCAL_VMEM),
        cost_estimate=pl.CostEstimate(
            flops=4 * 64 * 256 * seqs * length * pairs + 4 * 16 * depth * width,
            bytes_accessed=4 * seqs * length * width + 4 * depth * width,
            transcendentals=64 * seqs * length * pairs,
        ),
        name="local",
    )(*operands)


def rank_kernel(n, rows, depth, *refs):
    base_ref, table_ref, own_ref, near_ref = refs[:4]
    tokens, (out_ref, *has) = refs[4 : 4 + n], refs[4 + n :]
    half = base_ref.shape[1] // 2
    place = lax.axis_index("dp")
    x = []
    for ref in tokens:
        part = ref[:, : depth // 2].astype(F32)
        x.append(jnp.concatenate([part[:8], part[8:]], 1))
    x = jnp.concatenate(x, 0).astype(BF16)
    fill = jnp.zeros((RANK - 16, depth), BF16)
    z = None
    for ref, at in ((own_ref, place), (near_ref, place ^ 1)):
        down = jnp.concatenate([ref[:, :depth], fill, ref[:, depth:], fill], 0)
        part = lax.dot_general(x, down, NT, preferred_element_type=F32)
        part = pltpu.roll(part, at * rows, 1)
        z = part if z is None else z + part
    out_ref[:, :half] = base_ref[:, half:].astype(BF16)
    out_ref[:, half : half + 128] = split(table_ref[:8])
    for i in range(n):
        at = half + 128 * (i + 1)
        out_ref[:, at : at + 128] = split(z[8 * i : 8 * i + 8])
    for ref in has:
        here = place // 2 == lax.axis_index("tensor") % 2
        mine, far = (token[:, depth // 2 + 256 :].astype(F32) for token in tokens[:2])
        ref[...] = jnp.where(here, mine, far).astype(BF16)


def rank_products(rows, depth, columns, base, table, own, near, tokens):
    n = len(tokens)
    out_shape = [jax.ShapeDtypeStruct((16, base.shape[1] // 2 + 128 * (n + 1)), BF16)]
    if columns:
        out_shape.append(jax.ShapeDtypeStruct((16, columns), BF16))
    return pl.pallas_call(
        functools.partial(rank_kernel, n, rows, depth),
        in_specs=[VMEM] * (4 + n),
        out_specs=[VMEM] * len(out_shape),
        out_shape=out_shape,
        compiler_params=pltpu.CompilerParams(vmem_limit_bytes=32 * MEBI),
        name="rank_products",
    )(base, table, own, near, *tokens)


def broadcast_lane(tile, lane):
    return jnp.broadcast_to(tile[:, lane : lane + 1], tile.shape)


def combine_part_kernel(base_ref, mine_ref, theirs_ref, out_ref):
    half = base_ref.shape[1] // 2
    own = base_ref[:, :half] + theirs_ref[:, :half].astype(F32)
    out_ref[:, :half] = own.astype(BF16)
    sums = mine_ref[:, half:].astype(F32) + theirs_ref[:, half:].astype(F32)
    out_ref[:, half:] = split(sums[:8] + sums[8:])


def combine_part(base, mine, theirs):
    return pl.pallas_call(
        combine_part_kernel,
        in_specs=[VMEM] * 3,
        out_specs=VMEM,
        out_shape=jax.ShapeDtypeStruct(mine.shape, BF16),
        compiler_params=pltpu.CompilerParams(vmem_limit_bytes=32 * MEBI),
        name="combine_part",
    )(base, mine, theirs)


def combine_cache_kernel(a_ref, b_ref, *refs):
    out_ref = refs[-1]
    lane = lax.broadcasted_iota(jnp.int32, (16, 128), 1)
    for p in range(out_ref.shape[1] // PAIR):
        end = slice(p * PAIR + GROUP * HD, (p + 1) * PAIR)
        a, b = a_ref[:, end].astype(F32), b_ref[:, end].astype(F32)
        top = jnp.maximum(a, b)
        fa = jnp.exp2(jnp.minimum(a - top, 0.0) * EXPONENT)
        fb = jnp.exp2(jnp.minimum(b - top, 0.0) * EXPONENT)
        total = fa * totals(a) + fb * totals(b)
        high = rounded(total)
        stats = jnp.where(lane < GROUP, top, 0.0)
        stats = jnp.where(lane // GROUP == 1, pltpu.roll(high, GROUP, 1), stats)
        stats = jnp.where(lane // GROUP == 2, pltpu.roll(total - high, 2 * GROUP, 1), stats)
        out_ref[:, end] = stats.astype(BF16)
        for g in range(GROUP):
            at = slice(p * PAIR + g * HD, p * PAIR + (g + 1) * HD)
            out_ref[:, at] = (
                broadcast_lane(fa, g) * a_ref[:, at].astype(F32)
                + broadcast_lane(fb, g) * b_ref[:, at].astype(F32)
            ).astype(BF16)


def totals(stats):
    return pltpu.roll(stats, 128 - GROUP, 1) + pltpu.roll(stats, 128 - 2 * GROUP, 1)


def combine_cache(a, b, *earlier):
    return pl.pallas_call(
        combine_cache_kernel,
        in_specs=[VMEM] * (2 + len(earlier)),
        out_specs=VMEM,
        out_shape=jax.ShapeDtypeStruct(a.shape, BF16),
        compiler_params=pltpu.CompilerParams(vmem_limit_bytes=32 * MEBI),
        name="combine_cache",
    )(a, b, *earlier)


def answer_kernel(at, pa_ref, pb_ref, *outs):
    z = pa_ref[:, at:].astype(F32) + pb_ref[:, at:].astype(F32)
    for i, ref in enumerate(outs):
        part = z[:, 128 * (i + 1) : 128 * (i + 2)]
        ref[...] = split(part[:8] + part[8:])


def answers(n, part_a, part_b):
    at = part_a.shape[1] - 128 * (n + 1)
    return pl.pallas_call(
        functools.partial(answer_kernel, at),
        in_specs=[VMEM] * 2,
        out_specs=[VMEM] * n,
        out_shape=[jax.ShapeDtypeStruct((16, 128), BF16)] * n,
        compiler_params=pltpu.CompilerParams(vmem_limit_bytes=32 * MEBI),
        name="answers",
    )(part_a, part_b)


def merge_kernel(n, paired, width_all, *refs):
    table_ref, qrot_ref, pa_ref, pb_ref, ca_ref, cb_ref = refs[:6]
    backs, (ua_ref, ub_ref, out_ref) = refs[6 : 6 + n], refs[6 + n :]
    pairs = ca_ref.shape[1] // PAIR
    width = pairs * 2 * HD
    cosine, sine = table_ref[8:16], table_ref[16:]
    sums = pa_ref[...].astype(F32) + pb_ref[...].astype(F32)
    tail = sums[:8, width : width + 256] + sums[8:, width : width + 256]
    squares, z = tail[:, :128], tail[:, 128:]
    for ref in backs:
        z = z + joined(ref[...])
    lane8 = lax.broadcasted_iota(jnp.int32, (8, 128), 1)
    z = jnp.concatenate(
        [jnp.where(lane8 < RANK, z, 0.0), jnp.where(lane8 < RANK, 0.0, z)], 0
    ).astype(BF16)
    adapted = []
    for ref in (ua_ref, ub_ref):
        ups = jnp.concatenate([ref[:, i : i + 128] for i in range(0, ref.shape[1], 128)], 0)
        adapted.append(lax.dot_general(z, ups, NT, preferred_element_type=F32))
    if paired:
        even = lax.axis_index("dp") % 2 == 0
        a, b = adapted
        adapted = [jnp.where(even, a, b), jnp.where(even, b, a)]
    total = sums[:, :width] + jnp.concatenate(adapted, 1)
    scale = lax.rsqrt(squares / width_all + EPSILON)
    lane = lax.broadcasted_iota(jnp.int32, (16, 128), 1)
    step = lax.broadcasted_iota(jnp.int32, (16, 128), 0) % STEPS
    first = first_rows((8, 128))

    def of_step(tiles, j):
        return jnp.concatenate(
            [
                jnp.where(first, tile[j : j + 1], tile[STEPS + j : STEPS + j + 1])
                for tile in tiles
            ],
            0,
        )

    for p in range(pairs):
        new_keys, new_values = [], []
        for e in range(2):
            at = slice((2 * p + e) * HD, (2 * p + e + 1) * HD)
            new_keys.append(rounded(rotated(total[:8, at] * scale, cosine, sine)))
            new_values.append(rounded(total[8:, at] * scale))
            fresh = jnp.concatenate([new_keys[e], new_values[e]], 0)
            start = pairs * GROUP * HD + (2 * p + e) * HD
            out_ref[:, start : start + HD] = fresh.astype(BF16)
        keys = [of_step(new_keys, j) for j in range(STEPS)]
        values = [of_step(new_values, j) for j in range(STEPS)]
        scores = [jnp.zeros((16, 128), F32) for _ in range(STEPS)]
        for g in range(GROUP):
            q = qrot_ref[:, (p * GROUP + g) * HD : (p * GROUP + g + 1) * HD].astype(F32)
            for j in range(STEPS):
                dot = jnp.sum(q * keys[j], 1, keepdims=True)
                scores[j] = jnp.where(lane == g, dot, scores[j])
        scores = [jnp.where(j <= step, scores[j], MASKED_SCORE) for j in range(STEPS)]
        end = slice(p * PAIR + GROUP * HD, (p + 1) * PAIR)
        stats = [ref[:, end].astype(F32) for ref in (ca_ref, cb_ref)]
        top = functools.reduce(jnp.maximum, scores + stats)
        fresh = [rounded(jnp.exp2((scores[j] - top) * EXPONENT)) for j in range(STEPS)]
        factors = [jnp.exp2(jnp.minimum(s - top, 0.0) * EXPONENT) for s in stats]
        denom = functools.reduce(jnp.add, fresh)
        for factor, s in zip(factors, stats):
            denom = denom + factor * totals(s)
        inverse = 1.0 / denom
        coefficients = [c * inverse for c in fresh + factors]
        for g in range(GROUP):
            at = slice(p * PAIR + g * HD, p * PAIR + (g + 1) * HD)
            terms = values + [ref[:, at].astype(F32) for ref in (ca_ref, cb_ref)]
            tile = jnp.zeros((16, 128), F32)
            for c, term in zip(coefficients, terms):
                tile = tile + broadcast_lane(c, g) * term
            out_ref[:, (p * GROUP + g) * HD : (p * GROUP + g + 1) * HD] = tile.astype(BF16)


def merge(paired, width_all, table, qrot, parts, caches, backs, ups):
    operands = [table, qrot, *parts, *caches, *backs, *ups]
    pairs = caches[0].shape[1] // PAIR
    return pl.pallas_call(
        functools.partial(merge_kernel, len(backs), paired, width_all),
        in_specs=[VMEM] * len(operands),
        out_specs=VMEM,
        out_shape=jax.ShapeDtypeStruct((16, pairs * (GROUP + 2) * HD), BF16),
        compiler_params=pltpu.CompilerParams(vmem_limit_bytes=32 * MEBI),
        name="merge",
    )(*operands)


def place_kernel(mine_ref, theirs_ref, keys_out, values_out, out_ref):
    pairs = mine_ref.shape[1] // ((GROUP + 2) * HD)
    for c, ref in enumerate((mine_ref, theirs_ref)):
        for p in range(pairs):
            pair = pair_at(c * pairs + p)
            tiles = ref[:, p * GROUP * HD : (p + 1) * GROUP * HD].astype(F32)
            size = GROUP * HD
            for e in range(2):
                at = pl.ds(pl.multiple_of((2 * pair + e) * size, size), size)
                for s in range(2):
                    rows = slice(8 * e + 4 * s, 8 * e + 4 * s + 4)
                    out_ref[s, :, at] = tiles[rows].astype(BF16)
            start = pairs * GROUP * HD + p * 2 * HD
            fresh = ref[:, start : start + 2 * HD].astype(F32)
            at = pl.ds(pl.multiple_of(pair * 2 * HD, 2 * HD), 2 * HD)
            for i, out in enumerate((keys_out, values_out)):
                for s in range(2):
                    rows = slice(8 * i + 4 * s, 8 * i + 4 * s + 4)
                    out[s, :, at] = fresh[rows].astype(BF16)


def place(width, mine, theirs):
    return pl.pallas_call(
        place_kernel,
        in_specs=[VMEM] * 2,
        out_specs=[VMEM] * 3,
        out_shape=[
            jax.ShapeDtypeStruct((2, STEPS, width), BF16),
            jax.ShapeDtypeStruct((2, STEPS, width), BF16),
            jax.ShapeDtypeStruct((2, STEPS, GROUP * width), BF16),
        ],
        compiler_params=pltpu.CompilerParams(vmem_limit_bytes=32 * MEBI),
        name="place",
    )(mine, theirs)


def swap(value, axis, n, distance):
    return lax.ppermute(value, axis, [(i, i ^ distance) for i in range(n)])


def shards(
    n_dp,
    n_tensor,
    hidden,
    norm_gain,
    queries,
    key_weight,
    value_weight,
    key_down,
    key_up,
    value_down,
    value_up,
    key_cache,
    value_cache,
    lengths,
):
    depth, width = key_weight.shape
    rows = key_down.shape[0]
    to_dp = lambda value, distance: swap(value, "dp", n_dp, distance)
    to_tensor = lambda value, distance: swap(value, "tensor", n_tensor, distance)
    partners = range(2, n_dp, 2)
    n = len(partners)
    paired = n_dp == 4

    own, tokens = pack(lengths, hidden, norm_gain, key_down, value_down, key_up, value_up)
    near = to_dp(own, 1)
    sent = [to_dp(tokens, d) for d in partners]
    keep, send, base, qrot, table = local(
        tokens, queries, key_cache, value_cache, key_weight, value_weight
    )
    received = to_tensor(send, 1)
    columns = key_up.shape[0] * 8 if paired else 0
    part, *has = rank_products(rows, depth, columns, base, table, own, near, [tokens, *sent])
    if paired:
        ups = [has[0], to_dp(has[0], 1)]
    else:
        ups = lax.all_gather(tokens[:, depth // 2 + 256 :], "dp")
        ups = ups.reshape(n_dp, 16, -1, 128).transpose(0, 2, 1, 3)
        ups = ups.reshape(2, 2, 16, 16, 128).transpose(0, 1, 3, 2, 4).reshape(2, 2, 16, -1)
        ups = lax.dynamic_index_in_dim(ups, lax.axis_index("tensor") % 2, 0, keepdims=False)
        ups = [ups[0], ups[1]]
    part = combine_part(base, part, to_tensor(part, 1))
    part_far = to_tensor(part, 2)
    cache = combine_cache(keep, received, part_far, ups[1])
    cache_far = to_tensor(cache, 2)
    replies = answers(n, part, part_far)
    backs = [to_dp(reply, d) for reply, d in zip(replies, partners)]
    merged = merge(
        paired,
        float(depth * n_tensor),
        table,
        qrot,
        (part, part_far),
        (cache, cache_far),
        backs,
        ups,
    )
    return place(width, merged, to_tensor(merged, 1))


def solution(mesh):
    body = functools.partial(shards, mesh.shape["dp"], mesh.shape["tensor"])
    return jax.shard_map(
        body,
        mesh=mesh,
        in_specs=(
            P(("groups", "dp"), None, "tensor"),
            P("tensor"),
            P(("groups", "dp"), None, None),
            P("tensor", None),
            P("tensor", None),
            P(("groups", "dp"), "tensor"),
            P(("groups", "dp"), None),
            P(("groups", "dp"), "tensor"),
            P(("groups", "dp"), None),
            P(("groups", "dp"), "tensor", None),
            P(("groups", "dp"), "tensor", None),
            P(("groups", "dp")),
        ),
        out_specs=(
            P(("groups", "dp"), None, None),
            P(("groups", "dp"), None, None),
            P(("groups", "dp"), None, None),
        ),
        check_vma=False,
    )
```

```python
import functools
import math

import jax
import jax.numpy as jnp
from jax import lax
from jax.experimental import pallas as pl
from jax.experimental.pallas import tpu as pltpu
from jax.sharding import PartitionSpec as P

HD = 128
GROUP = 8
STEPS = 4
RANK = 64
EPSILON = 1e-05
ROPE_BASE = 500000.0
MASKED_SCORE = -1e30
LOWEST_TOP = -1e20
EXPONENT = math.log2(math.e) / math.sqrt(HD)
PAIR = GROUP * HD + 128
CHUNK = 512

F32 = jnp.float32
BF16 = jnp.bfloat16
NT = (((1,), (1,)), ((), ()))
VMEM = pl.BlockSpec(memory_space=pltpu.VMEM)
HBM = pl.BlockSpec(memory_space=pltpu.HBM)
MEBI = 2**20
WHOLE_VMEM = 65000 * 1024
LOCAL_VMEM = 54900 * 1024


def rounded(value):
    return value.astype(BF16).astype(F32)


def split(value):
    high = rounded(value)
    return jnp.concatenate([high, value - high], 0).astype(BF16)


def joined(tile):
    wide = tile.astype(F32)
    return wide[:8] + wide[8:]


def rotated(tile, cosine, sine):
    return tile * cosine + pltpu.roll(tile, HD // 2, 1) * sine


def first_rows(shape):
    return lax.broadcasted_iota(jnp.int32, shape, 0) % 8 < STEPS


def exchanged(a, b):
    first = first_rows(a.shape)
    return (
        jnp.where(first, a, pltpu.roll(b, STEPS, 0)),
        jnp.where(first, pltpu.roll(a, STEPS, 0), b),
    )


def flat(matrix):
    return jnp.concatenate([matrix[i : i + 16] for i in range(0, matrix.shape[0], 16)], 1)


def pack_kernel(*refs):
    sources, (a_ref, b_ref, up_ref), held, sems = refs[:7], refs[7:10], refs[10:17], refs[17]
    copies = [
        pltpu.make_async_copy(source, target, sems.at[i])
        for i, (source, target) in enumerate(zip(sources, held))
    ]
    for copy in copies:
        copy.start()
    lengths_ref, x_ref, gain_ref, kd_ref, vd_ref, ku_ref, vu_ref = held
    for copy in copies:
        copy.wait()
    x = jnp.concatenate([x_ref[0].astype(F32), x_ref[1].astype(F32)], 0)
    depth = x.shape[1]
    scaled = x * gain_ref[...].astype(F32).reshape(1, depth)
    b_ref[:, : depth // 2] = jnp.concatenate(
        [scaled[:, : depth // 2], scaled[:, depth // 2 :]], 0
    ).astype(BF16)
    row = lax.broadcasted_iota(jnp.int32, (16, 128), 0)
    length = jnp.where(row % 8 < STEPS, lengths_ref[0], lengths_ref[1])
    length = jnp.where(row < 8, length // 64 * 64, length % 64)
    b_ref[:, depth // 2 : depth // 2 + 128] = length.astype(F32).astype(BF16)
    squares = jnp.broadcast_to(jnp.sum(x * x, 1, keepdims=True), (8, 128))
    b_ref[:, depth // 2 + 128 : depth // 2 + 256] = split(squares)
    ups = jnp.concatenate([ku_ref[...], vu_ref[...]], 0).T.astype(BF16)
    b_ref[:, depth // 2 + 256 :] = flat(ups)
    up_ref[...] = flat(ups)
    own = kd_ref.shape[0]
    for slot, ref in enumerate((kd_ref, vd_ref)):
        down = ref[...]
        if own < 16:
            down = jnp.concatenate([down, jnp.zeros((16 - own, depth), F32)], 0)
        a_ref[:, slot * depth : (slot + 1) * depth] = down.astype(BF16)


def pack(lengths, hidden, gain, key_down, value_down, key_up, value_up):
    operands = [lengths, hidden, gain, key_down, value_down, key_up.T, value_up.T]
    depth = hidden.shape[2]
    ups = key_up.shape[0] * 8
    return pl.pallas_call(
        pack_kernel,
        in_specs=[HBM] * len(operands),
        out_specs=[VMEM] * 3,
        out_shape=[
            jax.ShapeDtypeStruct((16, 2 * depth), BF16),
            jax.ShapeDtypeStruct((16, depth // 2 + 256 + ups), BF16),
            jax.ShapeDtypeStruct((16, ups), BF16),
        ],
        scratch_shapes=[pltpu.SMEM(lengths.shape, jnp.int32)]
        + [pltpu.VMEM(o.shape, o.dtype) for o in operands[1:]]
        + [pltpu.SemaphoreType.DMA((len(operands),))],
        compiler_params=pltpu.CompilerParams(vmem_limit_bytes=WHOLE_VMEM),
        name="pack",
    )(*operands)


def tables(length):
    shape = length.shape
    row = lax.broadcasted_iota(jnp.int32, shape, 0)
    lane = lax.broadcasted_iota(jnp.int32, shape, 1)
    position = length + (row % STEPS).astype(F32)
    pair = lane % (HD // 2)
    frequency = jnp.ones(shape, F32)
    for bit in range(6):
        factor = ROPE_BASE ** (-(2.0 * 2**bit) / HD)
        frequency = jnp.where((pair >> bit) & 1 == 1, frequency * factor, frequency)
    angle = position * frequency
    sine = jnp.sin(angle)
    return jnp.cos(angle), jnp.where(lane < HD // 2, -sine, sine)


def attend(p, limit, cosine, sine, q_ref, k_ref, v_ref, out_ref, qrot_ref):
    halves = [[], []]
    for e in range(2):
        for g in range(GROUP):
            at = slice(((2 * p + e) * GROUP + g) * HD, ((2 * p + e) * GROUP + g + 1) * HD)
            q = jnp.concatenate([q_ref[0, :, at].astype(F32), q_ref[1, :, at].astype(F32)], 0)
            halves[e].append(rotated(q, cosine, sine))
    if qrot_ref is not None:
        for g in range(GROUP):
            at = slice((p * GROUP + g) * HD, (p * GROUP + g + 1) * HD)
            qrot_ref[:, at] = jnp.concatenate([halves[0][g], halves[1][g]], 0).astype(BF16)
    mixed = [[exchanged(halves[e][g], halves[e][g + 4]) for g in range(4)] for e in range(2)]
    zero = jnp.zeros((32, HD), F32)
    numers, stats = [], []
    lane8 = lax.broadcasted_iota(jnp.int32, (8, 128), 1)
    pair = slice(2 * p * HD, 2 * (p + 1) * HD)
    for s in range(2):
        rows = [jnp.concatenate([mixed[e][g][s] for g in range(4)], 0) for e in range(2)]
        queries = jnp.concatenate(
            [jnp.concatenate([rows[0], zero], 1), jnp.concatenate([zero, rows[1]], 1)], 0
        ).astype(BF16)
        scores = lax.dot_general(queries, k_ref[s, :, pair], NT, preferred_element_type=F32)
        place = lax.broadcasted_iota(jnp.int32, scores.shape, 1)
        bound = limit[STEPS * s : STEPS * s + 1, :1].astype(jnp.int32)
        masked = jnp.where(place < bound, scores, MASKED_SCORE)
        top = rounded(jnp.maximum(jnp.max(masked, 1, keepdims=True), LOWEST_TOP))
        weights = jnp.exp2((masked - top) * EXPONENT).astype(BF16)
        total = jnp.sum(weights.astype(F32), 1, keepdims=True)
        numers.append(jnp.dot(weights, v_ref[s, :, pair], preferred_element_type=F32))
        high = rounded(total)
        compact = []
        for e in range(2):
            tile = jnp.zeros((8, 128), F32)
            for g in range(4):
                at = slice(32 * e + 8 * g, 32 * e + 8 * g + 8)
                for slot, value in enumerate((top, high, total - high)):
                    tile = jnp.where(lane8 == slot * GROUP + g, value[at], tile)
            compact.append(tile)
        stats.append(compact)
    outs, ends = [[], []], []
    for e in range(2):
        back = []
        for g in range(4):
            at = slice(32 * e + 8 * g, 32 * e + 8 * g + 8)
            cols = slice(e * HD, (e + 1) * HD)
            back.append(exchanged(numers[0][at, cols], numers[1][at, cols]))
        outs[e] = [b[0] for b in back] + [b[1] for b in back]
        a, b = exchanged(stats[0][e], stats[1][e])
        ends.append(jnp.where(lane8 % 8 < 4, a, pltpu.roll(b, 4, 1)))
    p = p % (out_ref.shape[1] // PAIR)
    for g in range(GROUP):
        at = slice(p * PAIR + g * HD, p * PAIR + (g + 1) * HD)
        out_ref[:, at] = jnp.concatenate([outs[0][g], outs[1][g]], 0).astype(BF16)
    out_ref[:, p * PAIR + GROUP * HD : (p + 1) * PAIR] = jnp.concatenate(ends, 0).astype(BF16)


def pair_at(i):
    return i ^ (lax.axis_index("tensor") % 2 * 2)


def local_kernel(
    x_hbm, q_hbm, k_hbm, v_hbm, wk_hbm, wv_hbm,
    keep_ref, send_ref, base_ref, qrot_ref, table_ref,
    x_ref, q_ref, k_ref, v_ref, wk_ref, wv_ref, x_sem, q_sem, cache_sem, weight_sem,
):
    pairs = k_hbm.shape[2] // (2 * HD)
    chunks = wk_hbm.shape[0] // CHUNK
    width = wk_hbm.shape[1]
    core = lax.axis_index("tensor") % 2
    x_copy = pltpu.make_async_copy(x_hbm, x_ref, x_sem)
    x_copy.start()
    groups = []
    for h in range(2):
        copies = []
        trio = ((q_hbm, q_ref, q_sem.at[h]), (k_hbm, k_ref, cache_sem.at[h, 0]))
        for source, target, sem in (*trio, (v_hbm, v_ref, cache_sem.at[h, 1])):
            size = source.shape[2] // 2
            start = pl.multiple_of((core ^ h) * size, size)
            copies.append(
                pltpu.make_async_copy(
                    source.at[:, :, pl.ds(start, size)],
                    target.at[:, :, pl.ds(h * size, size)],
                    sem,
                )
            )
        groups.append(copies)
    weights = []
    for c in range(chunks):
        at = pl.ds(c * CHUNK, CHUNK)
        weights.append(
            [
                pltpu.make_async_copy(source.at[at], target.at[at], weight_sem.at[c, i])
                for i, (source, target) in enumerate(((wk_hbm, wk_ref), (wv_hbm, wv_ref)))
            ]
        )
    steps = groups + weights
    later = [[] for _ in steps]
    later[0] = weights[:1]
    later[1] = weights[1:3]
    for c in range(3, chunks):
        later[c - 1].append(weights[c])

    def start(copies):
        for copy in copies:
            copy.start()

    start(groups[0])
    start(groups[1])
    x_copy.wait()
    half = wk_hbm.shape[0] // 2
    x = x_ref[:, :half].astype(F32)
    x = jnp.concatenate([x[:8], x[8:]], 1).astype(BF16)
    length = joined(x_ref[:, half : half + 128])
    cosine, sine = tables(length)
    table_ref[...] = jnp.concatenate([joined(x_ref[:, half + 128 : half + 256]), cosine, sine], 0)
    limit = length - (lax.axis_index("tensor") * k_hbm.shape[1]).astype(F32)
    total = None
    for i, copies in enumerate(steps):
        for copy in copies:
            copy.wait()
        for ahead in later[i]:
            start(ahead)
        if i < 2:
            for p in range(i * pairs // 2, (i + 1) * pairs // 2):
                attend(
                    p, limit, cosine, sine, q_ref, k_ref, v_ref,
                    send_ref if i else keep_ref, None if i else qrot_ref,
                )
        else:
            at = slice((i - 2) * CHUNK, (i - 1) * CHUNK)
            part = jnp.concatenate(
                [
                    jnp.dot(x[:, at], ref[at], preferred_element_type=F32)
                    for ref in (wk_ref, wv_ref)
                ],
                0,
            )
            total = part if total is None else total + part
    lower, upper = total[:, : width // 2], total[:, width // 2 :]
    base_ref[:, : width // 2] = jnp.where(core == 0, lower, upper)
    base_ref[:, width // 2 :] = jnp.where(core == 0, upper, lower)


def local(message, queries, key_cache, value_cache, key_weight, value_weight):
    seqs, length, width = key_cache.shape
    depth = key_weight.shape[0]
    pairs = width // (2 * HD)
    operands = [message, queries, key_cache, value_cache, key_weight, value_weight]
    return pl.pallas_call(
        local_kernel,
        in_specs=[HBM] * 6,
        out_specs=[VMEM] * 5,
        out_shape=[
            jax.ShapeDtypeStruct((16, pairs // 2 * PAIR), BF16),
            jax.ShapeDtypeStruct((16, pairs // 2 * PAIR), BF16),
            jax.ShapeDtypeStruct((16, width), F32),
            jax.ShapeDtypeStruct((16, pairs // 2 * GROUP * HD), BF16),
            jax.ShapeDtypeStruct((24, 128), F32),
        ],
        scratch_shapes=[pltpu.VMEM(o.shape, BF16) for o in operands]
        + [
            pltpu.SemaphoreType.DMA,
            pltpu.SemaphoreType.DMA((2,)),
            pltpu.SemaphoreType.DMA((2, 2)),
            pltpu.SemaphoreType.DMA((depth // CHUNK, 2)),
        ],
        compiler_params=pltpu.CompilerParams(vmem_limit_bytes=LOCAL_VMEM),
        cost_estimate=pl.CostEstimate(
            flops=4 * 64 * 256 * seqs * length * pairs + 4 * 16 * depth * width,
            bytes_accessed=4 * seqs * length * width + 4 * depth * width,
            transcendentals=64 * seqs * length * pairs,
        ),
        name="local",
    )(*operands)


def rank_kernel(n, rows, depth, *refs):
    base_ref, table_ref, own_ref, near_ref = refs[:4]
    tokens, (out_ref, *has) = refs[4 : 4 + n], refs[4 + n :]
    half = base_ref.shape[1] // 2
    place = lax.axis_index("dp")
    x = []
    for ref in tokens:
        part = ref[:, : depth // 2].astype(F32)
        x.append(jnp.concatenate([part[:8], part[8:]], 1))
    x = jnp.concatenate(x, 0).astype(BF16)
    fill = jnp.zeros((RANK - 16, depth), BF16)
    z = None
    for ref, at in ((own_ref, place), (near_ref, place ^ 1)):
        down = jnp.concatenate([ref[:, :depth], fill, ref[:, depth:], fill], 0)
        part = lax.dot_general(x, down, NT, preferred_element_type=F32)
        part = pltpu.roll(part, at * rows, 1)
        z = part if z is None else z + part
    out_ref[:, :half] = base_ref[:, half:].astype(BF16)
    out_ref[:, half : half + 128] = split(table_ref[:8])
    for i in range(n):
        at = half + 128 * (i + 1)
        out_ref[:, at : at + 128] = split(z[8 * i : 8 * i + 8])
    for ref in has:
        here = place // 2 == lax.axis_index("tensor") % 2
        mine, far = (token[:, depth // 2 + 256 :].astype(F32) for token in tokens[:2])
        ref[...] = jnp.where(here, mine, far).astype(BF16)


def rank_products(rows, depth, columns, base, table, own, near, tokens):
    n = len(tokens)
    out_shape = [jax.ShapeDtypeStruct((16, base.shape[1] // 2 + 128 * (n + 1)), BF16)]
    if columns:
        out_shape.append(jax.ShapeDtypeStruct((16, columns), BF16))
    return pl.pallas_call(
        functools.partial(rank_kernel, n, rows, depth),
        in_specs=[VMEM] * (4 + n),
        out_specs=[VMEM] * len(out_shape),
        out_shape=out_shape,
        compiler_params=pltpu.CompilerParams(vmem_limit_bytes=32 * MEBI),
        name="rank_products",
    )(base, table, own, near, *tokens)


def broadcast_lane(tile, lane):
    return jnp.broadcast_to(tile[:, lane : lane + 1], tile.shape)


def combine_part_kernel(base_ref, mine_ref, theirs_ref, _, out_ref):
    half = base_ref.shape[1] // 2
    own = base_ref[:, :half] + theirs_ref[:, :half].astype(F32)
    out_ref[:, :half] = own.astype(BF16)
    sums = mine_ref[:, half:].astype(F32) + theirs_ref[:, half:].astype(F32)
    out_ref[:, half:] = split(sums[:8] + sums[8:])


def combine_part(base, mine, theirs, earlier):
    return pl.pallas_call(
        combine_part_kernel,
        in_specs=[VMEM] * 4,
        out_specs=VMEM,
        out_shape=jax.ShapeDtypeStruct(mine.shape, BF16),
        compiler_params=pltpu.CompilerParams(vmem_limit_bytes=32 * MEBI),
        name="combine_part",
    )(base, mine, theirs, earlier)


def combine_cache_kernel(a_ref, b_ref, out_ref):
    lane = lax.broadcasted_iota(jnp.int32, (16, 128), 1)
    for p in range(out_ref.shape[1] // PAIR):
        end = slice(p * PAIR + GROUP * HD, (p + 1) * PAIR)
        a, b = a_ref[:, end].astype(F32), b_ref[:, end].astype(F32)
        top = jnp.maximum(a, b)
        fa = jnp.exp2(jnp.minimum(a - top, 0.0) * EXPONENT)
        fb = jnp.exp2(jnp.minimum(b - top, 0.0) * EXPONENT)
        total = fa * totals(a) + fb * totals(b)
        high = rounded(total)
        stats = jnp.where(lane < GROUP, top, 0.0)
        stats = jnp.where(lane // GROUP == 1, pltpu.roll(high, GROUP, 1), stats)
        stats = jnp.where(lane // GROUP == 2, pltpu.roll(total - high, 2 * GROUP, 1), stats)
        out_ref[:, end] = stats.astype(BF16)
        for g in range(GROUP):
            at = slice(p * PAIR + g * HD, p * PAIR + (g + 1) * HD)
            out_ref[:, at] = (
                broadcast_lane(fa, g) * a_ref[:, at].astype(F32)
                + broadcast_lane(fb, g) * b_ref[:, at].astype(F32)
            ).astype(BF16)


def totals(stats):
    return pltpu.roll(stats, 128 - GROUP, 1) + pltpu.roll(stats, 128 - 2 * GROUP, 1)


def combine_cache(a, b):
    return pl.pallas_call(
        combine_cache_kernel,
        in_specs=[VMEM] * 2,
        out_specs=VMEM,
        out_shape=jax.ShapeDtypeStruct(a.shape, BF16),
        compiler_params=pltpu.CompilerParams(vmem_limit_bytes=32 * MEBI),
        name="combine_cache",
    )(a, b)


def answer_kernel(at, pa_ref, pb_ref, *outs):
    z = pa_ref[:, at:].astype(F32) + pb_ref[:, at:].astype(F32)
    for i, ref in enumerate(outs):
        part = z[:, 128 * (i + 1) : 128 * (i + 2)]
        ref[...] = split(part[:8] + part[8:])


def answers(n, part_a, part_b):
    at = part_a.shape[1] - 128 * (n + 1)
    return pl.pallas_call(
        functools.partial(answer_kernel, at),
        in_specs=[VMEM] * 2,
        out_specs=[VMEM] * n,
        out_shape=[jax.ShapeDtypeStruct((16, 128), BF16)] * n,
        compiler_params=pltpu.CompilerParams(vmem_limit_bytes=32 * MEBI),
        name="answers",
    )(part_a, part_b)


def merge_kernel(n, paired, width_all, *refs):
    table_ref, qrot_ref, pa_ref, pb_ref, ca_ref, cb_ref = refs[:6]
    backs, (ua_ref, ub_ref, out_ref) = refs[6 : 6 + n], refs[6 + n :]
    pairs = ca_ref.shape[1] // PAIR
    width = pairs * 2 * HD
    cosine, sine = table_ref[8:16], table_ref[16:]
    sums = pa_ref[...].astype(F32) + pb_ref[...].astype(F32)
    tail = sums[:8, width : width + 256] + sums[8:, width : width + 256]
    squares, z = tail[:, :128], tail[:, 128:]
    for ref in backs:
        z = z + joined(ref[...])
    lane8 = lax.broadcasted_iota(jnp.int32, (8, 128), 1)
    z = jnp.concatenate(
        [jnp.where(lane8 < RANK, z, 0.0), jnp.where(lane8 < RANK, 0.0, z)], 0
    ).astype(BF16)
    adapted = []
    for ref in (ua_ref, ub_ref):
        ups = jnp.concatenate([ref[:, i : i + 128] for i in range(0, ref.shape[1], 128)], 0)
        adapted.append(lax.dot_general(z, ups, NT, preferred_element_type=F32))
    if paired:
        even = lax.axis_index("dp") % 2 == 0
        a, b = adapted
        adapted = [jnp.where(even, a, b), jnp.where(even, b, a)]
    total = sums[:, :width] + jnp.concatenate(adapted, 1)
    scale = lax.rsqrt(squares / width_all + EPSILON)
    lane = lax.broadcasted_iota(jnp.int32, (16, 128), 1)
    step = lax.broadcasted_iota(jnp.int32, (16, 128), 0) % STEPS
    first = first_rows((8, 128))

    def of_step(tiles, j):
        return jnp.concatenate(
            [
                jnp.where(first, tile[j : j + 1], tile[STEPS + j : STEPS + j + 1])
                for tile in tiles
            ],
            0,
        )

    for p in range(pairs):
        new_keys, new_values = [], []
        for e in range(2):
            at = slice((2 * p + e) * HD, (2 * p + e + 1) * HD)
            new_keys.append(rounded(rotated(total[:8, at] * scale, cosine, sine)))
            new_values.append(rounded(total[8:, at] * scale))
            fresh = jnp.concatenate([new_keys[e], new_values[e]], 0)
            start = pairs * GROUP * HD + (2 * p + e) * HD
            out_ref[:, start : start + HD] = fresh.astype(BF16)
        keys = [of_step(new_keys, j) for j in range(STEPS)]
        values = [of_step(new_values, j) for j in range(STEPS)]
        scores = [jnp.zeros((16, 128), F32) for _ in range(STEPS)]
        for g in range(GROUP):
            q = qrot_ref[:, (p * GROUP + g) * HD : (p * GROUP + g + 1) * HD].astype(F32)
            for j in range(STEPS):
                dot = jnp.sum(q * keys[j], 1, keepdims=True)
                scores[j] = jnp.where(lane == g, dot, scores[j])
        scores = [jnp.where(j <= step, scores[j], MASKED_SCORE) for j in range(STEPS)]
        end = slice(p * PAIR + GROUP * HD, (p + 1) * PAIR)
        stats = [ref[:, end].astype(F32) for ref in (ca_ref, cb_ref)]
        top = functools.reduce(jnp.maximum, scores + stats)
        fresh = [rounded(jnp.exp2((scores[j] - top) * EXPONENT)) for j in range(STEPS)]
        factors = [jnp.exp2(jnp.minimum(s - top, 0.0) * EXPONENT) for s in stats]
        denom = functools.reduce(jnp.add, fresh)
        for factor, s in zip(factors, stats):
            denom = denom + factor * totals(s)
        inverse = 1.0 / denom
        coefficients = [c * inverse for c in fresh + factors]
        for g in range(GROUP):
            at = slice(p * PAIR + g * HD, p * PAIR + (g + 1) * HD)
            terms = values + [ref[:, at].astype(F32) for ref in (ca_ref, cb_ref)]
            tile = jnp.zeros((16, 128), F32)
            for c, term in zip(coefficients, terms):
                tile = tile + broadcast_lane(c, g) * term
            out_ref[:, (p * GROUP + g) * HD : (p * GROUP + g + 1) * HD] = tile.astype(BF16)


def merge(paired, width_all, table, qrot, parts, caches, backs, ups):
    operands = [table, qrot, *parts, *caches, *backs, *ups]
    pairs = caches[0].shape[1] // PAIR
    return pl.pallas_call(
        functools.partial(merge_kernel, len(backs), paired, width_all),
        in_specs=[VMEM] * len(operands),
        out_specs=VMEM,
        out_shape=jax.ShapeDtypeStruct((16, pairs * (GROUP + 2) * HD), BF16),
        compiler_params=pltpu.CompilerParams(vmem_limit_bytes=32 * MEBI),
        name="merge",
    )(*operands)


def place_kernel(mine_ref, theirs_ref, keys_out, values_out, out_ref):
    pairs = mine_ref.shape[1] // ((GROUP + 2) * HD)
    for c, ref in enumerate((mine_ref, theirs_ref)):
        for p in range(pairs):
            pair = pair_at(c * pairs + p)
            tiles = ref[:, p * GROUP * HD : (p + 1) * GROUP * HD].astype(F32)
            size = GROUP * HD
            for e in range(2):
                at = pl.ds(pl.multiple_of((2 * pair + e) * size, size), size)
                for s in range(2):
                    rows = slice(8 * e + 4 * s, 8 * e + 4 * s + 4)
                    out_ref[s, :, at] = tiles[rows].astype(BF16)
            start = pairs * GROUP * HD + p * 2 * HD
            fresh = ref[:, start : start + 2 * HD].astype(F32)
            at = pl.ds(pl.multiple_of(pair * 2 * HD, 2 * HD), 2 * HD)
            for i, out in enumerate((keys_out, values_out)):
                for s in range(2):
                    rows = slice(8 * i + 4 * s, 8 * i + 4 * s + 4)
                    out[s, :, at] = fresh[rows].astype(BF16)


def place(width, mine, theirs):
    return pl.pallas_call(
        place_kernel,
        in_specs=[VMEM] * 2,
        out_specs=[VMEM] * 3,
        out_shape=[
            jax.ShapeDtypeStruct((2, STEPS, width), BF16),
            jax.ShapeDtypeStruct((2, STEPS, width), BF16),
            jax.ShapeDtypeStruct((2, STEPS, GROUP * width), BF16),
        ],
        compiler_params=pltpu.CompilerParams(vmem_limit_bytes=32 * MEBI),
        name="place",
    )(mine, theirs)


def swap(value, axis, n, distance):
    return lax.ppermute(value, axis, [(i, i ^ distance) for i in range(n)])


def shards(
    n_dp,
    n_tensor,
    hidden,
    norm_gain,
    queries,
    key_weight,
    value_weight,
    key_down,
    key_up,
    value_down,
    value_up,
    key_cache,
    value_cache,
    lengths,
):
    depth, width = key_weight.shape
    rows = key_down.shape[0]
    to_dp = lambda value, distance: swap(value, "dp", n_dp, distance)
    to_tensor = lambda value, distance: swap(value, "tensor", n_tensor, distance)
    partners = range(2, n_dp, 2)
    n = len(partners)
    paired = n_dp == 4

    own, tokens, own_ups = pack(lengths, hidden, norm_gain, key_down, value_down, key_up, value_up)
    near = to_dp(own, 1)
    sent = [to_dp(tokens, d) for d in partners]
    keep, send, base, qrot, table = local(
        tokens, queries, key_cache, value_cache, key_weight, value_weight
    )
    received = to_tensor(send, 1)
    columns = key_up.shape[0] * 8 if paired else 0
    part, *has = rank_products(rows, depth, columns, base, table, own, near, [tokens, *sent])
    if paired:
        places = [(s, t) for s in range(n_dp) for t in range(n_tensor)]
        perm = [
            (s * n_tensor + t, (s ^ 1) * n_tensor + t if t % 2 == s // 2 else (s ^ 3) * n_tensor + (t ^ 1))
            for s, t in places
        ]
        ups = [has[0], lax.ppermute(own_ups, ("dp", "tensor"), perm)]
    else:
        ups = lax.all_gather(own_ups, "dp")
        ups = ups.reshape(n_dp, 16, -1, 128).transpose(0, 2, 1, 3)
        ups = ups.reshape(2, 2, 16, 16, 128).transpose(0, 1, 3, 2, 4).reshape(2, 2, 16, -1)
        ups = lax.dynamic_index_in_dim(ups, lax.axis_index("tensor") % 2, 0, keepdims=False)
        ups = [ups[0], ups[1]]
    part = combine_part(base, part, to_tensor(part, 1), ups[1])
    part_far = to_tensor(part, 2)
    cache = combine_cache(keep, received)
    cache_far = to_tensor(cache, 2)
    replies = answers(n, part, part_far)
    backs = [to_dp(reply, d) for reply, d in zip(replies, partners)]
    merged = merge(
        paired,
        float(depth * n_tensor),
        table,
        qrot,
        (part, part_far),
        (cache, cache_far),
        backs,
        ups,
    )
    return place(width, merged, to_tensor(merged, 1))


def solution(mesh):
    body = functools.partial(shards, mesh.shape["dp"], mesh.shape["tensor"])
    return jax.shard_map(
        body,
        mesh=mesh,
        in_specs=(
            P(("groups", "dp"), None, "tensor"),
            P("tensor"),
            P(("groups", "dp"), None, None),
            P("tensor", None),
            P("tensor", None),
            P(("groups", "dp"), "tensor"),
            P(("groups", "dp"), None),
            P(("groups", "dp"), "tensor"),
            P(("groups", "dp"), None),
            P(("groups", "dp"), "tensor", None),
            P(("groups", "dp"), "tensor", None),
            P(("groups", "dp")),
        ),
        out_specs=(
            P(("groups", "dp"), None, None),
            P(("groups", "dp"), None, None),
            P(("groups", "dp"), None, None),
        ),
        check_vma=False,
    )
```

```python
import functools
import math

import jax
import jax.numpy as jnp
from jax import lax
from jax.experimental import pallas as pl
from jax.experimental.pallas import tpu as pltpu
from jax.sharding import PartitionSpec as P

HD = 128
GROUP = 8
STEPS = 4
RANK = 64
EPSILON = 1e-05
ROPE_BASE = 500000.0
MASKED_SCORE = -1e30
LOWEST_TOP = -1e20
EXPONENT = math.log2(math.e) / math.sqrt(HD)
PAIR = GROUP * HD + 128
CHUNK = 512

F32 = jnp.float32
BF16 = jnp.bfloat16
NT = (((1,), (1,)), ((), ()))
VMEM = pl.BlockSpec(memory_space=pltpu.VMEM)
HBM = pl.BlockSpec(memory_space=pltpu.HBM)
MEBI = 2**20
WHOLE_VMEM = 65000 * 1024
LOCAL_VMEM = 54900 * 1024


def rounded(value):
    return value.astype(BF16).astype(F32)


def split(value):
    high = rounded(value)
    return jnp.concatenate([high, value - high], 0).astype(BF16)


def joined(tile):
    wide = tile.astype(F32)
    return wide[:8] + wide[8:]


def rotated(tile, cosine, sine):
    return tile * cosine + pltpu.roll(tile, HD // 2, 1) * sine


def first_rows(shape):
    return lax.broadcasted_iota(jnp.int32, shape, 0) % 8 < STEPS


def exchanged(a, b):
    first = first_rows(a.shape)
    return (
        jnp.where(first, a, pltpu.roll(b, STEPS, 0)),
        jnp.where(first, pltpu.roll(a, STEPS, 0), b),
    )


def flat(matrix):
    return jnp.concatenate([matrix[i : i + 16] for i in range(0, matrix.shape[0], 16)], 1)


def pack_kernel(*refs):
    sources, (a_ref, b_ref, up_ref), held, sems = refs[:7], refs[7:10], refs[10:17], refs[17]
    copies = [
        pltpu.make_async_copy(source, target, sems.at[i])
        for i, (source, target) in enumerate(zip(sources, held))
    ]
    for copy in copies:
        copy.start()
    lengths_ref, x_ref, gain_ref, kd_ref, vd_ref, ku_ref, vu_ref = held
    for copy in copies:
        copy.wait()
    x = jnp.concatenate([x_ref[0].astype(F32), x_ref[1].astype(F32)], 0)
    depth = x.shape[1]
    scaled = x * gain_ref[...].astype(F32).reshape(1, depth)
    b_ref[:, : depth // 2] = jnp.concatenate(
        [scaled[:, : depth // 2], scaled[:, depth // 2 :]], 0
    ).astype(BF16)
    row = lax.broadcasted_iota(jnp.int32, (16, 128), 0)
    length = jnp.where(row % 8 < STEPS, lengths_ref[0], lengths_ref[1])
    length = jnp.where(row < 8, length // 64 * 64, length % 64)
    b_ref[:, depth // 2 : depth // 2 + 128] = length.astype(F32).astype(BF16)
    squares = jnp.broadcast_to(jnp.sum(x * x, 1, keepdims=True), (8, 128))
    b_ref[:, depth // 2 + 128 : depth // 2 + 256] = split(squares)
    ups = jnp.concatenate([ku_ref[...], vu_ref[...]], 0).T.astype(BF16)
    b_ref[:, depth // 2 + 256 :] = flat(ups)
    up_ref[...] = flat(ups)
    own = kd_ref.shape[0]
    for slot, ref in enumerate((kd_ref, vd_ref)):
        down = ref[...]
        if own < 16:
            down = jnp.concatenate([down, jnp.zeros((16 - own, depth), F32)], 0)
        a_ref[:, slot * depth : (slot + 1) * depth] = down.astype(BF16)


def pack(lengths, hidden, gain, key_down, value_down, key_up, value_up):
    operands = [lengths, hidden, gain, key_down, value_down, key_up.T, value_up.T]
    depth = hidden.shape[2]
    ups = key_up.shape[0] * 8
    return pl.pallas_call(
        pack_kernel,
        in_specs=[HBM] * len(operands),
        out_specs=[VMEM] * 3,
        out_shape=[
            jax.ShapeDtypeStruct((16, 2 * depth), BF16),
            jax.ShapeDtypeStruct((16, depth // 2 + 256 + ups), BF16),
            jax.ShapeDtypeStruct((16, ups), BF16),
        ],
        scratch_shapes=[pltpu.SMEM(lengths.shape, jnp.int32)]
        + [pltpu.VMEM(o.shape, o.dtype) for o in operands[1:]]
        + [pltpu.SemaphoreType.DMA((len(operands),))],
        compiler_params=pltpu.CompilerParams(vmem_limit_bytes=WHOLE_VMEM),
        name="pack",
    )(*operands)


def tables(length):
    shape = length.shape
    row = lax.broadcasted_iota(jnp.int32, shape, 0)
    lane = lax.broadcasted_iota(jnp.int32, shape, 1)
    position = length + (row % STEPS).astype(F32)
    pair = lane % (HD // 2)
    frequency = jnp.ones(shape, F32)
    for bit in range(6):
        factor = ROPE_BASE ** (-(2.0 * 2**bit) / HD)
        frequency = jnp.where((pair >> bit) & 1 == 1, frequency * factor, frequency)
    angle = position * frequency
    sine = jnp.sin(angle)
    return jnp.cos(angle), jnp.where(lane < HD // 2, -sine, sine)


def attend(pairs, limit, cosine, sine, q_ref, k_ref, v_ref, out_ref, qrot_ref):
    zero = jnp.zeros((32, HD), F32)
    scores = []
    for p in pairs:
        halves = [[], []]
        for e in range(2):
            for g in range(GROUP):
                at = slice(((2 * p + e) * GROUP + g) * HD, ((2 * p + e) * GROUP + g + 1) * HD)
                q = jnp.concatenate([q_ref[0, :, at].astype(F32), q_ref[1, :, at].astype(F32)], 0)
                halves[e].append(rotated(q, cosine, sine))
        if qrot_ref is not None:
            for g in range(GROUP):
                at = slice((p * GROUP + g) * HD, (p * GROUP + g + 1) * HD)
                qrot_ref[:, at] = jnp.concatenate([halves[0][g], halves[1][g]], 0).astype(BF16)
        mixed = [[exchanged(halves[e][g], halves[e][g + 4]) for g in range(4)] for e in range(2)]
        for s in range(2):
            rows = [jnp.concatenate([mixed[e][g][s] for g in range(4)], 0) for e in range(2)]
            queries = jnp.concatenate(
                [jnp.concatenate([rows[0], zero], 1), jnp.concatenate([zero, rows[1]], 1)], 0
            ).astype(BF16)
            keys = k_ref[s, :, 2 * p * HD : 2 * (p + 1) * HD]
            score = lax.dot_general(queries, keys, NT, preferred_element_type=F32)
            place = lax.broadcasted_iota(jnp.int32, score.shape, 1)
            bound = limit[STEPS * s : STEPS * s + 1, :1].astype(jnp.int32)
            scores.append(jnp.where(place < bound, score, MASKED_SCORE))
    scores = jnp.concatenate(scores, 0)
    top = rounded(jnp.maximum(jnp.max(scores, 1, keepdims=True), LOWEST_TOP))
    weights = jnp.exp2((scores - top) * EXPONENT).astype(BF16)
    total = jnp.sum(weights.astype(F32), 1, keepdims=True)
    high = rounded(total)
    columns = (top, high, total - high)
    lane8 = lax.broadcasted_iota(jnp.int32, (8, 128), 1)
    numers = []
    for i, p in enumerate(pairs):
        for s in range(2):
            at = slice(64 * (2 * i + s), 64 * (2 * i + s + 1))
            values = v_ref[s, :, 2 * p * HD : 2 * (p + 1) * HD]
            numers.append(jnp.dot(weights[at], values, preferred_element_type=F32))
    for i, p in enumerate(pairs):
        outs, ends = [[], []], []
        for e in range(2):
            back, stats = [], []
            for s in range(2):
                tile = jnp.zeros((8, 128), F32)
                for g in range(4):
                    row = 64 * (2 * i + s) + 32 * e + 8 * g
                    for slot, value in enumerate(columns):
                        tile = jnp.where(lane8 == slot * GROUP + g, value[row : row + 8], tile)
                stats.append(tile)
            for g in range(4):
                at = slice(32 * e + 8 * g, 32 * e + 8 * g + 8)
                cols = slice(e * HD, (e + 1) * HD)
                back.append(exchanged(numers[2 * i][at, cols], numers[2 * i + 1][at, cols]))
            outs[e] = [b[0] for b in back] + [b[1] for b in back]
            a, b = exchanged(*stats)
            ends.append(jnp.where(lane8 % 8 < 4, a, pltpu.roll(b, 4, 1)))
        for g in range(GROUP):
            at = slice(i * PAIR + g * HD, i * PAIR + (g + 1) * HD)
            out_ref[:, at] = jnp.concatenate([outs[0][g], outs[1][g]], 0).astype(BF16)
        out_ref[:, i * PAIR + GROUP * HD : (i + 1) * PAIR] = jnp.concatenate(ends, 0).astype(BF16)


def pair_at(i):
    return i ^ (lax.axis_index("tensor") % 2 * 2)


def local_kernel(
    x_hbm, q_hbm, k_hbm, v_hbm, wk_hbm, wv_hbm,
    keep_ref, send_ref, base_ref, qrot_ref, table_ref,
    x_ref, q_ref, k_ref, v_ref, wk_ref, wv_ref, x_sem, q_sem, cache_sem, weight_sem,
):
    pairs = k_hbm.shape[2] // (2 * HD)
    chunks = wk_hbm.shape[0] // CHUNK
    width = wk_hbm.shape[1]
    core = lax.axis_index("tensor") % 2
    x_copy = pltpu.make_async_copy(x_hbm, x_ref, x_sem)
    x_copy.start()
    groups = []
    for h in range(2):
        copies = []
        trio = ((q_hbm, q_ref, q_sem.at[h]), (k_hbm, k_ref, cache_sem.at[h, 0]))
        for source, target, sem in (*trio, (v_hbm, v_ref, cache_sem.at[h, 1])):
            size = source.shape[2] // 2
            start = pl.multiple_of((core ^ h) * size, size)
            copies.append(
                pltpu.make_async_copy(
                    source.at[:, :, pl.ds(start, size)],
                    target.at[:, :, pl.ds(h * size, size)],
                    sem,
                )
            )
        groups.append(copies)
    weights = []
    for c in range(chunks):
        at = pl.ds(c * CHUNK, CHUNK)
        weights.append(
            [
                pltpu.make_async_copy(source.at[at], target.at[at], weight_sem.at[c, i])
                for i, (source, target) in enumerate(((wk_hbm, wk_ref), (wv_hbm, wv_ref)))
            ]
        )
    steps = groups + weights
    later = [[] for _ in steps]
    later[0] = weights[:1]
    later[1] = weights[1:3]
    for c in range(3, chunks):
        later[c - 1].append(weights[c])

    def start(copies):
        for copy in copies:
            copy.start()

    start(groups[0])
    start(groups[1])
    x_copy.wait()
    half = wk_hbm.shape[0] // 2
    x = x_ref[:, :half].astype(F32)
    x = jnp.concatenate([x[:8], x[8:]], 1).astype(BF16)
    length = joined(x_ref[:, half : half + 128])
    cosine, sine = tables(length)
    table_ref[...] = jnp.concatenate([joined(x_ref[:, half + 128 : half + 256]), cosine, sine], 0)
    limit = length - (lax.axis_index("tensor") * k_hbm.shape[1]).astype(F32)
    total = None
    for i, copies in enumerate(steps):
        for copy in copies:
            copy.wait()
        for ahead in later[i]:
            start(ahead)
        if i < 2:
            attend(
                range(i * pairs // 2, (i + 1) * pairs // 2), limit, cosine, sine,
                q_ref, k_ref, v_ref, send_ref if i else keep_ref, None if i else qrot_ref,
            )
        else:
            at = slice((i - 2) * CHUNK, (i - 1) * CHUNK)
            part = jnp.concatenate(
                [
                    jnp.dot(x[:, at], ref[at], preferred_element_type=F32)
                    for ref in (wk_ref, wv_ref)
                ],
                0,
            )
            total = part if total is None else total + part
    lower, upper = total[:, : width // 2], total[:, width // 2 :]
    base_ref[:, : width // 2] = jnp.where(core == 0, lower, upper)
    base_ref[:, width // 2 :] = jnp.where(core == 0, upper, lower)


def local(message, queries, key_cache, value_cache, key_weight, value_weight):
    seqs, length, width = key_cache.shape
    depth = key_weight.shape[0]
    pairs = width // (2 * HD)
    operands = [message, queries, key_cache, value_cache, key_weight, value_weight]
    return pl.pallas_call(
        local_kernel,
        in_specs=[HBM] * 6,
        out_specs=[VMEM] * 5,
        out_shape=[
            jax.ShapeDtypeStruct((16, pairs // 2 * PAIR), BF16),
            jax.ShapeDtypeStruct((16, pairs // 2 * PAIR), BF16),
            jax.ShapeDtypeStruct((16, width), F32),
            jax.ShapeDtypeStruct((16, pairs // 2 * GROUP * HD), BF16),
            jax.ShapeDtypeStruct((24, 128), F32),
        ],
        scratch_shapes=[pltpu.VMEM(o.shape, BF16) for o in operands]
        + [
            pltpu.SemaphoreType.DMA,
            pltpu.SemaphoreType.DMA((2,)),
            pltpu.SemaphoreType.DMA((2, 2)),
            pltpu.SemaphoreType.DMA((depth // CHUNK, 2)),
        ],
        compiler_params=pltpu.CompilerParams(vmem_limit_bytes=LOCAL_VMEM),
        cost_estimate=pl.CostEstimate(
            flops=4 * 64 * 256 * seqs * length * pairs + 4 * 16 * depth * width,
            bytes_accessed=4 * seqs * length * width + 4 * depth * width,
            transcendentals=64 * seqs * length * pairs,
        ),
        name="local",
    )(*operands)


def rank_kernel(n, rows, depth, *refs):
    base_ref, table_ref, own_ref, near_ref = refs[:4]
    tokens, (out_ref, *has) = refs[4 : 4 + n], refs[4 + n :]
    half = base_ref.shape[1] // 2
    place = lax.axis_index("dp")
    x = []
    for ref in tokens:
        part = ref[:, : depth // 2].astype(F32)
        x.append(jnp.concatenate([part[:8], part[8:]], 1))
    x = jnp.concatenate(x, 0).astype(BF16)
    fill = jnp.zeros((RANK - 16, depth), BF16)
    z = None
    for ref, at in ((own_ref, place), (near_ref, place ^ 1)):
        down = jnp.concatenate([ref[:, :depth], fill, ref[:, depth:], fill], 0)
        part = lax.dot_general(x, down, NT, preferred_element_type=F32)
        part = pltpu.roll(part, at * rows, 1)
        z = part if z is None else z + part
    out_ref[:, :half] = base_ref[:, half:].astype(BF16)
    out_ref[:, half : half + 128] = split(table_ref[:8])
    for i in range(n):
        at = half + 128 * (i + 1)
        out_ref[:, at : at + 128] = split(z[8 * i : 8 * i + 8])
    for ref in has:
        here = place // 2 == lax.axis_index("tensor") % 2
        mine, far = (token[:, depth // 2 + 256 :].astype(F32) for token in tokens[:2])
        ref[...] = jnp.where(here, mine, far).astype(BF16)


def rank_products(rows, depth, columns, base, table, own, near, tokens):
    n = len(tokens)
    out_shape = [jax.ShapeDtypeStruct((16, base.shape[1] // 2 + 128 * (n + 1)), BF16)]
    if columns:
        out_shape.append(jax.ShapeDtypeStruct((16, columns), BF16))
    return pl.pallas_call(
        functools.partial(rank_kernel, n, rows, depth),
        in_specs=[VMEM] * (4 + n),
        out_specs=[VMEM] * len(out_shape),
        out_shape=out_shape,
        compiler_params=pltpu.CompilerParams(vmem_limit_bytes=32 * MEBI),
        name="rank_products",
    )(base, table, own, near, *tokens)


def broadcast_lane(tile, lane):
    return jnp.broadcast_to(tile[:, lane : lane + 1], tile.shape)


def combine_part_kernel(base_ref, mine_ref, theirs_ref, *refs):
    (*passed, out_ref), through = refs[: len(refs) // 2 + 1], refs[len(refs) // 2 + 1 :]
    for source, target in zip(passed, through):
        target[...] = source[...]
    half = base_ref.shape[1] // 2
    own = base_ref[:, :half] + theirs_ref[:, :half].astype(F32)
    out_ref[:, :half] = own.astype(BF16)
    sums = mine_ref[:, half:].astype(F32) + theirs_ref[:, half:].astype(F32)
    out_ref[:, half:] = split(sums[:8] + sums[8:])


def combine_part(base, mine, theirs, *passed):
    shapes = [mine.shape] + [p.shape for p in passed]
    return pl.pallas_call(
        combine_part_kernel,
        in_specs=[VMEM] * (3 + len(passed)),
        out_specs=[VMEM] * len(shapes),
        out_shape=[jax.ShapeDtypeStruct(shape, BF16) for shape in shapes],
        compiler_params=pltpu.CompilerParams(vmem_limit_bytes=32 * MEBI),
        name="combine_part",
    )(base, mine, theirs, *passed)


def combine_cache_kernel(a_ref, b_ref, _, out_ref):
    lane = lax.broadcasted_iota(jnp.int32, (16, 128), 1)
    for p in range(out_ref.shape[1] // PAIR):
        end = slice(p * PAIR + GROUP * HD, (p + 1) * PAIR)
        a, b = a_ref[:, end].astype(F32), b_ref[:, end].astype(F32)
        top = jnp.maximum(a, b)
        fa = jnp.exp2(jnp.minimum(a - top, 0.0) * EXPONENT)
        fb = jnp.exp2(jnp.minimum(b - top, 0.0) * EXPONENT)
        total = fa * totals(a) + fb * totals(b)
        high = rounded(total)
        stats = jnp.where(lane < GROUP, top, 0.0)
        stats = jnp.where(lane // GROUP == 1, pltpu.roll(high, GROUP, 1), stats)
        stats = jnp.where(lane // GROUP == 2, pltpu.roll(total - high, 2 * GROUP, 1), stats)
        out_ref[:, end] = stats.astype(BF16)
        for g in range(GROUP):
            at = slice(p * PAIR + g * HD, p * PAIR + (g + 1) * HD)
            out_ref[:, at] = (
                broadcast_lane(fa, g) * a_ref[:, at].astype(F32)
                + broadcast_lane(fb, g) * b_ref[:, at].astype(F32)
            ).astype(BF16)


def totals(stats):
    return pltpu.roll(stats, 128 - GROUP, 1) + pltpu.roll(stats, 128 - 2 * GROUP, 1)


def combine_cache(a, b, earlier):
    return pl.pallas_call(
        combine_cache_kernel,
        in_specs=[VMEM] * 3,
        out_specs=VMEM,
        out_shape=jax.ShapeDtypeStruct(a.shape, BF16),
        compiler_params=pltpu.CompilerParams(vmem_limit_bytes=32 * MEBI),
        name="combine_cache",
    )(a, b, earlier)


def answer_kernel(at, pa_ref, pb_ref, *outs):
    z = pa_ref[:, at:].astype(F32) + pb_ref[:, at:].astype(F32)
    for i, ref in enumerate(outs):
        part = z[:, 128 * (i + 1) : 128 * (i + 2)]
        ref[...] = split(part[:8] + part[8:])


def answers(n, part_a, part_b):
    at = part_a.shape[1] - 128 * (n + 1)
    return pl.pallas_call(
        functools.partial(answer_kernel, at),
        in_specs=[VMEM] * 2,
        out_specs=[VMEM] * n,
        out_shape=[jax.ShapeDtypeStruct((16, 128), BF16)] * n,
        compiler_params=pltpu.CompilerParams(vmem_limit_bytes=32 * MEBI),
        name="answers",
    )(part_a, part_b)


def merge_kernel(n, paired, width_all, *refs):
    table_ref, qrot_ref, pa_ref, pb_ref, ca_ref, cb_ref = refs[:6]
    backs, (ua_ref, ub_ref, out_ref) = refs[6 : 6 + n], refs[6 + n :]
    pairs = ca_ref.shape[1] // PAIR
    width = pairs * 2 * HD
    cosine, sine = table_ref[8:16], table_ref[16:]
    sums = pa_ref[...].astype(F32) + pb_ref[...].astype(F32)
    tail = sums[:8, width : width + 256] + sums[8:, width : width + 256]
    squares, z = tail[:, :128], tail[:, 128:]
    for ref in backs:
        z = z + joined(ref[...])
    lane8 = lax.broadcasted_iota(jnp.int32, (8, 128), 1)
    z = jnp.concatenate(
        [jnp.where(lane8 < RANK, z, 0.0), jnp.where(lane8 < RANK, 0.0, z)], 0
    ).astype(BF16)
    adapted = []
    for ref in (ua_ref, ub_ref):
        ups = jnp.concatenate([ref[:, i : i + 128] for i in range(0, ref.shape[1], 128)], 0)
        adapted.append(lax.dot_general(z, ups, NT, preferred_element_type=F32))
    if paired:
        even = lax.axis_index("dp") % 2 == 0
        a, b = adapted
        adapted = [jnp.where(even, a, b), jnp.where(even, b, a)]
    total = sums[:, :width] + jnp.concatenate(adapted, 1)
    scale = lax.rsqrt(squares / width_all + EPSILON)
    lane = lax.broadcasted_iota(jnp.int32, (16, 128), 1)
    step = lax.broadcasted_iota(jnp.int32, (16, 128), 0) % STEPS
    first = first_rows((8, 128))

    def of_step(tiles, j):
        return jnp.concatenate(
            [
                jnp.where(first, tile[j : j + 1], tile[STEPS + j : STEPS + j + 1])
                for tile in tiles
            ],
            0,
        )

    for p in range(pairs):
        new_keys, new_values = [], []
        for e in range(2):
            at = slice((2 * p + e) * HD, (2 * p + e + 1) * HD)
            new_keys.append(rounded(rotated(total[:8, at] * scale, cosine, sine)))
            new_values.append(rounded(total[8:, at] * scale))
            fresh = jnp.concatenate([new_keys[e], new_values[e]], 0)
            start = pairs * GROUP * HD + (2 * p + e) * HD
            out_ref[:, start : start + HD] = fresh.astype(BF16)
        keys = [of_step(new_keys, j) for j in range(STEPS)]
        values = [of_step(new_values, j) for j in range(STEPS)]
        scores = [jnp.zeros((16, 128), F32) for _ in range(STEPS)]
        for g in range(GROUP):
            q = qrot_ref[:, (p * GROUP + g) * HD : (p * GROUP + g + 1) * HD].astype(F32)
            for j in range(STEPS):
                dot = jnp.sum(q * keys[j], 1, keepdims=True)
                scores[j] = jnp.where(lane == g, dot, scores[j])
        scores = [jnp.where(j <= step, scores[j], MASKED_SCORE) for j in range(STEPS)]
        end = slice(p * PAIR + GROUP * HD, (p + 1) * PAIR)
        stats = [ref[:, end].astype(F32) for ref in (ca_ref, cb_ref)]
        top = functools.reduce(jnp.maximum, scores + stats)
        fresh = [rounded(jnp.exp2((scores[j] - top) * EXPONENT)) for j in range(STEPS)]
        factors = [jnp.exp2(jnp.minimum(s - top, 0.0) * EXPONENT) for s in stats]
        denom = functools.reduce(jnp.add, fresh)
        for factor, s in zip(factors, stats):
            denom = denom + factor * totals(s)
        inverse = 1.0 / denom
        coefficients = [c * inverse for c in fresh + factors]
        for g in range(GROUP):
            at = slice(p * PAIR + g * HD, p * PAIR + (g + 1) * HD)
            terms = values + [ref[:, at].astype(F32) for ref in (ca_ref, cb_ref)]
            tile = jnp.zeros((16, 128), F32)
            for c, term in zip(coefficients, terms):
                tile = tile + broadcast_lane(c, g) * term
            out_ref[:, (p * GROUP + g) * HD : (p * GROUP + g + 1) * HD] = tile.astype(BF16)


def merge(paired, width_all, table, qrot, parts, caches, backs, ups):
    operands = [table, qrot, *parts, *caches, *backs, *ups]
    pairs = caches[0].shape[1] // PAIR
    return pl.pallas_call(
        functools.partial(merge_kernel, len(backs), paired, width_all),
        in_specs=[VMEM] * len(operands),
        out_specs=VMEM,
        out_shape=jax.ShapeDtypeStruct((16, pairs * (GROUP + 2) * HD), BF16),
        compiler_params=pltpu.CompilerParams(vmem_limit_bytes=32 * MEBI),
        name="merge",
    )(*operands)


def place_kernel(mine_ref, theirs_ref, keys_out, values_out, out_ref):
    pairs = mine_ref.shape[1] // ((GROUP + 2) * HD)
    for c, ref in enumerate((mine_ref, theirs_ref)):
        for p in range(pairs):
            pair = pair_at(c * pairs + p)
            tiles = ref[:, p * GROUP * HD : (p + 1) * GROUP * HD].astype(F32)
            size = GROUP * HD
            for e in range(2):
                at = pl.ds(pl.multiple_of((2 * pair + e) * size, size), size)
                for s in range(2):
                    rows = slice(8 * e + 4 * s, 8 * e + 4 * s + 4)
                    out_ref[s, :, at] = tiles[rows].astype(BF16)
            start = pairs * GROUP * HD + p * 2 * HD
            fresh = ref[:, start : start + 2 * HD].astype(F32)
            at = pl.ds(pl.multiple_of(pair * 2 * HD, 2 * HD), 2 * HD)
            for i, out in enumerate((keys_out, values_out)):
                for s in range(2):
                    rows = slice(8 * i + 4 * s, 8 * i + 4 * s + 4)
                    out[s, :, at] = fresh[rows].astype(BF16)


def place(width, mine, theirs):
    return pl.pallas_call(
        place_kernel,
        in_specs=[VMEM] * 2,
        out_specs=[VMEM] * 3,
        out_shape=[
            jax.ShapeDtypeStruct((2, STEPS, width), BF16),
            jax.ShapeDtypeStruct((2, STEPS, width), BF16),
            jax.ShapeDtypeStruct((2, STEPS, GROUP * width), BF16),
        ],
        compiler_params=pltpu.CompilerParams(vmem_limit_bytes=32 * MEBI),
        name="place",
    )(mine, theirs)


def swap(value, axis, n, distance):
    return lax.ppermute(value, axis, [(i, i ^ distance) for i in range(n)])


def shards(
    n_dp,
    n_tensor,
    hidden,
    norm_gain,
    queries,
    key_weight,
    value_weight,
    key_down,
    key_up,
    value_down,
    value_up,
    key_cache,
    value_cache,
    lengths,
):
    depth, width = key_weight.shape
    rows = key_down.shape[0]
    to_dp = lambda value, distance: swap(value, "dp", n_dp, distance)
    to_tensor = lambda value, distance: swap(value, "tensor", n_tensor, distance)
    partners = range(2, n_dp, 2)
    n = len(partners)
    paired = n_dp == 4

    own, tokens, own_ups = pack(lengths, hidden, norm_gain, key_down, value_down, key_up, value_up)
    near = to_dp(own, 1)
    sent = [to_dp(tokens, d) for d in partners]
    keep, send, base, qrot, table = local(
        tokens, queries, key_cache, value_cache, key_weight, value_weight
    )
    received = to_tensor(send, 1)
    columns = key_up.shape[0] * 8 if paired else 0
    message, *has = rank_products(rows, depth, columns, base, table, own, near, [tokens, *sent])
    part, own_ups = combine_part(base, message, to_tensor(message, 1), own_ups)
    if paired:
        places = [(s, t) for s in range(n_dp) for t in range(n_tensor)]
        perm = [
            (s * n_tensor + t, (s ^ 1) * n_tensor + t if t % 2 == s // 2 else (s ^ 3) * n_tensor + (t ^ 1))
            for s, t in places
        ]
        ups = [has[0], lax.ppermute(own_ups, ("dp", "tensor"), perm)]
    else:
        ups = lax.all_gather(own_ups, "dp")
        ups = ups.reshape(n_dp, 16, -1, 128).transpose(0, 2, 1, 3)
        ups = ups.reshape(2, 2, 16, 16, 128).transpose(0, 1, 3, 2, 4).reshape(2, 2, 16, -1)
        ups = lax.dynamic_index_in_dim(ups, lax.axis_index("tensor") % 2, 0, keepdims=False)
        ups = [ups[0], ups[1]]
    part_far = to_tensor(part, 2)
    cache = combine_cache(keep, received, message)
    cache_far = to_tensor(cache, 2)
    replies = answers(n, part, part_far)
    backs = [to_dp(reply, d) for reply, d in zip(replies, partners)]
    merged = merge(
        paired,
        float(depth * n_tensor),
        table,
        qrot,
        (part, part_far),
        (cache, cache_far),
        backs,
        ups,
    )
    return place(width, merged, to_tensor(merged, 1))


def solution(mesh):
    body = functools.partial(shards, mesh.shape["dp"], mesh.shape["tensor"])
    return jax.shard_map(
        body,
        mesh=mesh,
        in_specs=(
            P(("groups", "dp"), None, "tensor"),
            P("tensor"),
            P(("groups", "dp"), None, None),
            P("tensor", None),
            P("tensor", None),
            P(("groups", "dp"), "tensor"),
            P(("groups", "dp"), None),
            P(("groups", "dp"), "tensor"),
            P(("groups", "dp"), None),
            P(("groups", "dp"), "tensor", None),
            P(("groups", "dp"), "tensor", None),
            P(("groups", "dp")),
        ),
        out_specs=(
            P(("groups", "dp"), None, None),
            P(("groups", "dp"), None, None),
            P(("groups", "dp"), None, None),
        ),
        check_vma=False,
    )
```

```python
import functools
import math

import jax
import jax.numpy as jnp
from jax import lax
from jax.experimental import pallas as pl
from jax.experimental.pallas import tpu as pltpu
from jax.sharding import PartitionSpec as P

HD = 128
GROUP = 8
STEPS = 4
RANK = 64
EPSILON = 1e-05
ROPE_BASE = 500000.0
MASKED_SCORE = -1e30
LOWEST_TOP = -1e20
EXPONENT = math.log2(math.e) / math.sqrt(HD)
PAIR = GROUP * HD + 128
CHUNK = 512

F32 = jnp.float32
BF16 = jnp.bfloat16
NT = (((1,), (1,)), ((), ()))
VMEM = pl.BlockSpec(memory_space=pltpu.VMEM)
HBM = pl.BlockSpec(memory_space=pltpu.HBM)
MEBI = 2**20
WHOLE_VMEM = 65000 * 1024
LOCAL_VMEM = 54900 * 1024


def rounded(value):
    return value.astype(BF16).astype(F32)


def split(value):
    high = rounded(value)
    return jnp.concatenate([high, value - high], 0).astype(BF16)


def joined(tile):
    wide = tile.astype(F32)
    return wide[:8] + wide[8:]


def rotated(tile, cosine, sine):
    return tile * cosine + pltpu.roll(tile, HD // 2, 1) * sine


def first_rows(shape):
    return lax.broadcasted_iota(jnp.int32, shape, 0) % 8 < STEPS


def exchanged(a, b):
    first = first_rows(a.shape)
    return (
        jnp.where(first, a, pltpu.roll(b, STEPS, 0)),
        jnp.where(first, pltpu.roll(a, STEPS, 0), b),
    )


def flat(matrix):
    return jnp.concatenate([matrix[i : i + 16] for i in range(0, matrix.shape[0], 16)], 1)


def pack_kernel(*refs):
    sources, (a_ref, b_ref), held, sems = refs[:7], refs[7:9], refs[9:16], refs[16]
    copies = [
        pltpu.make_async_copy(source, target, sems.at[i])
        for i, (source, target) in enumerate(zip(sources, held))
    ]
    for copy in copies:
        copy.start()
    lengths_ref, x_ref, gain_ref, kd_ref, vd_ref, ku_ref, vu_ref = held
    for copy in copies:
        copy.wait()
    x = jnp.concatenate([x_ref[0].astype(F32), x_ref[1].astype(F32)], 0)
    depth = x.shape[1]
    scaled = x * gain_ref[...].astype(F32).reshape(1, depth)
    b_ref[:, : depth // 2] = jnp.concatenate(
        [scaled[:, : depth // 2], scaled[:, depth // 2 :]], 0
    ).astype(BF16)
    row = lax.broadcasted_iota(jnp.int32, (16, 128), 0)
    length = jnp.where(row % 8 < STEPS, lengths_ref[0], lengths_ref[1])
    length = jnp.where(row < 8, length // 64 * 64, length % 64)
    b_ref[:, depth // 2 : depth // 2 + 128] = length.astype(F32).astype(BF16)
    squares = jnp.broadcast_to(jnp.sum(x * x, 1, keepdims=True), (8, 128))
    b_ref[:, depth // 2 + 128 : depth // 2 + 256] = split(squares)
    ups = jnp.concatenate([ku_ref[...], vu_ref[...]], 0).T.astype(BF16)
    b_ref[:, depth // 2 + 256 :] = flat(ups)
    own = kd_ref.shape[0]
    for slot, ref in enumerate((kd_ref, vd_ref)):
        down = ref[...]
        if own < 16:
            down = jnp.concatenate([down, jnp.zeros((16 - own, depth), F32)], 0)
        a_ref[:, slot * depth : (slot + 1) * depth] = down.astype(BF16)


def pack(lengths, hidden, gain, key_down, value_down, key_up, value_up):
    operands = [lengths, hidden, gain, key_down, value_down, key_up.T, value_up.T]
    depth = hidden.shape[2]
    ups = key_up.shape[0] * 8
    return pl.pallas_call(
        pack_kernel,
        in_specs=[HBM] * len(operands),
        out_specs=[VMEM] * 2,
        out_shape=[
            jax.ShapeDtypeStruct((16, 2 * depth), BF16),
            jax.ShapeDtypeStruct((16, depth // 2 + 256 + ups), BF16),
        ],
        scratch_shapes=[pltpu.SMEM(lengths.shape, jnp.int32)]
        + [pltpu.VMEM(o.shape, o.dtype) for o in operands[1:]]
        + [pltpu.SemaphoreType.DMA((len(operands),))],
        compiler_params=pltpu.CompilerParams(vmem_limit_bytes=WHOLE_VMEM),
        name="pack",
    )(*operands)


def tables(length):
    shape = length.shape
    row = lax.broadcasted_iota(jnp.int32, shape, 0)
    lane = lax.broadcasted_iota(jnp.int32, shape, 1)
    position = length + (row % STEPS).astype(F32)
    pair = lane % (HD // 2)
    frequency = jnp.ones(shape, F32)
    for bit in range(6):
        factor = ROPE_BASE ** (-(2.0 * 2**bit) / HD)
        frequency = jnp.where((pair >> bit) & 1 == 1, frequency * factor, frequency)
    angle = position * frequency
    sine = jnp.sin(angle)
    return jnp.cos(angle), jnp.where(lane < HD // 2, -sine, sine)


def attend(pairs, limit, cosine, sine, q_ref, k_ref, v_ref, out_ref, qrot_ref):
    zero = jnp.zeros((32, HD), F32)
    scores = []
    for p in pairs:
        halves = [[], []]
        for e in range(2):
            for g in range(GROUP):
                at = slice(((2 * p + e) * GROUP + g) * HD, ((2 * p + e) * GROUP + g + 1) * HD)
                q = jnp.concatenate([q_ref[0, :, at].astype(F32), q_ref[1, :, at].astype(F32)], 0)
                halves[e].append(rotated(q, cosine, sine))
        if qrot_ref is not None:
            for g in range(GROUP):
                at = slice((p * GROUP + g) * HD, (p * GROUP + g + 1) * HD)
                qrot_ref[:, at] = jnp.concatenate([halves[0][g], halves[1][g]], 0).astype(BF16)
        mixed = [[exchanged(halves[e][g], halves[e][g + 4]) for g in range(4)] for e in range(2)]
        for s in range(2):
            rows = [jnp.concatenate([mixed[e][g][s] for g in range(4)], 0) for e in range(2)]
            queries = jnp.concatenate(
                [jnp.concatenate([rows[0], zero], 1), jnp.concatenate([zero, rows[1]], 1)], 0
            ).astype(BF16)
            keys = k_ref[s, :, 2 * p * HD : 2 * (p + 1) * HD]
            score = lax.dot_general(queries, keys, NT, preferred_element_type=F32)
            place = lax.broadcasted_iota(jnp.int32, score.shape, 1)
            bound = limit[STEPS * s : STEPS * s + 1, :1].astype(jnp.int32)
            scores.append(jnp.where(place < bound, score, MASKED_SCORE))
    scores = jnp.concatenate(scores, 0)
    top = rounded(jnp.maximum(jnp.max(scores, 1, keepdims=True), LOWEST_TOP))
    weights = jnp.exp2((scores - top) * EXPONENT).astype(BF16)
    total = jnp.sum(weights.astype(F32), 1, keepdims=True)
    high = rounded(total)
    columns = (top, high, total - high)
    lane8 = lax.broadcasted_iota(jnp.int32, (8, 128), 1)
    numers = []
    for i, p in enumerate(pairs):
        for s in range(2):
            at = slice(64 * (2 * i + s), 64 * (2 * i + s + 1))
            values = v_ref[s, :, 2 * p * HD : 2 * (p + 1) * HD]
            numers.append(jnp.dot(weights[at], values, preferred_element_type=F32))
    for i, p in enumerate(pairs):
        outs, ends = [[], []], []
        for e in range(2):
            back, stats = [], []
            for s in range(2):
                tile = jnp.zeros((8, 128), F32)
                for g in range(4):
                    row = 64 * (2 * i + s) + 32 * e + 8 * g
                    for slot, value in enumerate(columns):
                        tile = jnp.where(lane8 == slot * GROUP + g, value[row : row + 8], tile)
                stats.append(tile)
            for g in range(4):
                at = slice(32 * e + 8 * g, 32 * e + 8 * g + 8)
                cols = slice(e * HD, (e + 1) * HD)
                back.append(exchanged(numers[2 * i][at, cols], numers[2 * i + 1][at, cols]))
            outs[e] = [b[0] for b in back] + [b[1] for b in back]
            a, b = exchanged(*stats)
            ends.append(jnp.where(lane8 % 8 < 4, a, pltpu.roll(b, 4, 1)))
        for g in range(GROUP):
            at = slice(i * PAIR + g * HD, i * PAIR + (g + 1) * HD)
            out_ref[:, at] = jnp.concatenate([outs[0][g], outs[1][g]], 0).astype(BF16)
        out_ref[:, i * PAIR + GROUP * HD : (i + 1) * PAIR] = jnp.concatenate(ends, 0).astype(BF16)


def pair_at(i):
    return i ^ (lax.axis_index("tensor") % 2 * 2)


def local_kernel(
    x_hbm, q_hbm, k_hbm, v_hbm, wk_hbm, wv_hbm,
    keep_ref, send_ref, base_ref, qrot_ref, table_ref,
    x_ref, q_ref, k_ref, v_ref, wk_ref, wv_ref, x_sem, q_sem, cache_sem, weight_sem,
):
    pairs = k_hbm.shape[2] // (2 * HD)
    chunks = wk_hbm.shape[0] // CHUNK
    width = wk_hbm.shape[1]
    core = lax.axis_index("tensor") % 2
    x_copy = pltpu.make_async_copy(x_hbm, x_ref, x_sem)
    x_copy.start()
    groups = []
    for h in range(2):
        copies = []
        trio = ((q_hbm, q_ref, q_sem.at[h]), (k_hbm, k_ref, cache_sem.at[h, 0]))
        for source, target, sem in (*trio, (v_hbm, v_ref, cache_sem.at[h, 1])):
            size = source.shape[2] // 2
            start = pl.multiple_of((core ^ h) * size, size)
            copies.append(
                pltpu.make_async_copy(
                    source.at[:, :, pl.ds(start, size)],
                    target.at[:, :, pl.ds(h * size, size)],
                    sem,
                )
            )
        groups.append(copies)
    weights = []
    for c in range(chunks):
        at = pl.ds(c * CHUNK, CHUNK)
        weights.append(
            [
                pltpu.make_async_copy(source.at[at], target.at[at], weight_sem.at[c, i])
                for i, (source, target) in enumerate(((wk_hbm, wk_ref), (wv_hbm, wv_ref)))
            ]
        )
    steps = [groups[0], groups[1] + weights[0], *weights[1:]]
    later = [[] for _ in steps]
    later[0] = weights[1:2]
    later[1] = weights[2:4]
    for c in range(4, chunks):
        later[c - 2].append(weights[c])

    def start(copies):
        for copy in copies:
            copy.start()

    start(groups[0])
    start(groups[1])
    start(weights[0])
    x_copy.wait()
    half = wk_hbm.shape[0] // 2
    x = x_ref[:, :half].astype(F32)
    x = jnp.concatenate([x[:8], x[8:]], 1).astype(BF16)
    length = joined(x_ref[:, half : half + 128])
    cosine, sine = tables(length)
    table_ref[...] = jnp.concatenate([joined(x_ref[:, half + 128 : half + 256]), cosine, sine], 0)
    limit = length - (lax.axis_index("tensor") * k_hbm.shape[1]).astype(F32)
    total = None
    for i, copies in enumerate(steps):
        for copy in copies:
            copy.wait()
        for ahead in later[i]:
            start(ahead)
        if i >= 1:
            at = slice((i - 1) * CHUNK, i * CHUNK)
            part = jnp.concatenate(
                [
                    jnp.dot(x[:, at], ref[at], preferred_element_type=F32)
                    for ref in (wk_ref, wv_ref)
                ],
                0,
            )
            total = part if total is None else total + part
        if i < 2:
            attend(
                range(i * pairs // 2, (i + 1) * pairs // 2), limit, cosine, sine,
                q_ref, k_ref, v_ref, send_ref if i else keep_ref, None if i else qrot_ref,
            )
    lower, upper = total[:, : width // 2], total[:, width // 2 :]
    base_ref[:, : width // 2] = jnp.where(core == 0, lower, upper)
    base_ref[:, width // 2 :] = jnp.where(core == 0, upper, lower)


def local(message, queries, key_cache, value_cache, key_weight, value_weight):
    seqs, length, width = key_cache.shape
    depth = key_weight.shape[0]
    pairs = width // (2 * HD)
    operands = [message, queries, key_cache, value_cache, key_weight, value_weight]
    return pl.pallas_call(
        local_kernel,
        in_specs=[HBM] * 6,
        out_specs=[VMEM] * 5,
        out_shape=[
            jax.ShapeDtypeStruct((16, pairs // 2 * PAIR), BF16),
            jax.ShapeDtypeStruct((16, pairs // 2 * PAIR), BF16),
            jax.ShapeDtypeStruct((16, width), F32),
            jax.ShapeDtypeStruct((16, pairs // 2 * GROUP * HD), BF16),
            jax.ShapeDtypeStruct((24, 128), F32),
        ],
        scratch_shapes=[pltpu.VMEM(o.shape, BF16) for o in operands]
        + [
            pltpu.SemaphoreType.DMA,
            pltpu.SemaphoreType.DMA((2,)),
            pltpu.SemaphoreType.DMA((2, 2)),
            pltpu.SemaphoreType.DMA((depth // CHUNK, 2)),
        ],
        compiler_params=pltpu.CompilerParams(vmem_limit_bytes=LOCAL_VMEM),
        cost_estimate=pl.CostEstimate(
            flops=4 * 64 * 256 * seqs * length * pairs + 4 * 16 * depth * width,
            bytes_accessed=4 * seqs * length * width + 4 * depth * width,
            transcendentals=64 * seqs * length * pairs,
        ),
        name="local",
    )(*operands)


def rank_kernel(n, rows, depth, *refs):
    base_ref, table_ref, own_ref, near_ref = refs[:4]
    tokens, (out_ref, *has) = refs[4 : 4 + n], refs[4 + n :]
    half = base_ref.shape[1] // 2
    place = lax.axis_index("dp")
    x = []
    for ref in tokens:
        part = ref[:, : depth // 2].astype(F32)
        x.append(jnp.concatenate([part[:8], part[8:]], 1))
    x = jnp.concatenate(x, 0).astype(BF16)
    fill = jnp.zeros((RANK - 16, depth), BF16)
    z = None
    for ref, at in ((own_ref, place), (near_ref, place ^ 1)):
        down = jnp.concatenate([ref[:, :depth], fill, ref[:, depth:], fill], 0)
        part = lax.dot_general(x, down, NT, preferred_element_type=F32)
        part = pltpu.roll(part, at * rows, 1)
        z = part if z is None else z + part
    out_ref[:, :half] = base_ref[:, half:].astype(BF16)
    out_ref[:, half : half + 128] = split(table_ref[:8])
    for i in range(n):
        at = half + 128 * (i + 1)
        out_ref[:, at : at + 128] = split(z[8 * i : 8 * i + 8])
    for ref in has:
        here = place // 2 == lax.axis_index("tensor") % 2
        mine, far = (token[:, depth // 2 + 256 :].astype(F32) for token in tokens[:2])
        ref[...] = jnp.where(here, mine, far).astype(BF16)


def rank_products(rows, depth, columns, base, table, own, near, tokens):
    n = len(tokens)
    out_shape = [jax.ShapeDtypeStruct((16, base.shape[1] // 2 + 128 * (n + 1)), BF16)]
    if columns:
        out_shape.append(jax.ShapeDtypeStruct((16, columns), BF16))
    return pl.pallas_call(
        functools.partial(rank_kernel, n, rows, depth),
        in_specs=[VMEM] * (4 + n),
        out_specs=[VMEM] * len(out_shape),
        out_shape=out_shape,
        compiler_params=pltpu.CompilerParams(vmem_limit_bytes=32 * MEBI),
        name="rank_products",
    )(base, table, own, near, *tokens)


def broadcast_lane(tile, lane):
    return jnp.broadcast_to(tile[:, lane : lane + 1], tile.shape)


def combine_part_kernel(n, base_ref, mine_ref, theirs_ref, *refs):
    passed, refs = refs[: (len(refs) - n) // 2], refs[(len(refs) - n) // 2 :]
    out_ref, replies, through = refs[0], refs[1:n], refs[n:]
    half = base_ref.shape[1] // 2
    own = base_ref[:, :half] + theirs_ref[:, :half].astype(F32)
    out_ref[:, :half] = own.astype(BF16)
    sums = mine_ref[:, half:].astype(F32) + theirs_ref[:, half:].astype(F32)
    sums = split(sums[:8] + sums[8:])
    out_ref[:, half:] = sums[:, :256]
    for i, ref in enumerate(replies):
        ref[...] = sums[:, 128 * (i + 2) : 128 * (i + 3)]
    for source, target in zip(passed, through):
        target[...] = source[...]


def combine_part(n, base, mine, theirs, passed):
    shapes = [(16, base.shape[1] // 2 + 256)] + [(16, 128)] * (n - 1) + [p.shape for p in passed]
    return pl.pallas_call(
        functools.partial(combine_part_kernel, n),
        in_specs=[VMEM] * (3 + len(passed)),
        out_specs=[VMEM] * len(shapes),
        out_shape=[jax.ShapeDtypeStruct(shape, BF16) for shape in shapes],
        compiler_params=pltpu.CompilerParams(vmem_limit_bytes=32 * MEBI),
        name="combine_part",
    )(base, mine, theirs, *passed)


def combine_cache_kernel(a_ref, b_ref, _, out_ref):
    lane = lax.broadcasted_iota(jnp.int32, (16, 128), 1)
    for p in range(out_ref.shape[1] // PAIR):
        end = slice(p * PAIR + GROUP * HD, (p + 1) * PAIR)
        a, b = a_ref[:, end].astype(F32), b_ref[:, end].astype(F32)
        top = jnp.maximum(a, b)
        fa = jnp.exp2(jnp.minimum(a - top, 0.0) * EXPONENT)
        fb = jnp.exp2(jnp.minimum(b - top, 0.0) * EXPONENT)
        total = fa * totals(a) + fb * totals(b)
        high = rounded(total)
        stats = jnp.where(lane < GROUP, top, 0.0)
        stats = jnp.where(lane // GROUP == 1, pltpu.roll(high, GROUP, 1), stats)
        stats = jnp.where(lane // GROUP == 2, pltpu.roll(total - high, 2 * GROUP, 1), stats)
        out_ref[:, end] = stats.astype(BF16)
        for g in range(GROUP):
            at = slice(p * PAIR + g * HD, p * PAIR + (g + 1) * HD)
            out_ref[:, at] = (
                broadcast_lane(fa, g) * a_ref[:, at].astype(F32)
                + broadcast_lane(fb, g) * b_ref[:, at].astype(F32)
            ).astype(BF16)


def totals(stats):
    return pltpu.roll(stats, 128 - GROUP, 1) + pltpu.roll(stats, 128 - 2 * GROUP, 1)


def combine_cache(a, b, earlier):
    return pl.pallas_call(
        combine_cache_kernel,
        in_specs=[VMEM] * 3,
        out_specs=VMEM,
        out_shape=jax.ShapeDtypeStruct(a.shape, BF16),
        compiler_params=pltpu.CompilerParams(vmem_limit_bytes=32 * MEBI),
        name="combine_cache",
    )(a, b, earlier)


def merge_kernel(n, paired, width_all, *refs):
    table_ref, qrot_ref, pa_ref, pb_ref, ca_ref, cb_ref = refs[:6]
    backs, (ua_ref, ub_ref, out_ref) = refs[6 : 6 + n], refs[6 + n :]
    pairs = ca_ref.shape[1] // PAIR
    width = pairs * 2 * HD
    cosine, sine = table_ref[8:16], table_ref[16:]
    sums = pa_ref[...].astype(F32) + pb_ref[...].astype(F32)
    tail = sums[:8, width : width + 256] + sums[8:, width : width + 256]
    squares, z = tail[:, :128], tail[:, 128:]
    for ref in backs:
        z = z + joined(ref[...])
    lane8 = lax.broadcasted_iota(jnp.int32, (8, 128), 1)
    z = jnp.concatenate(
        [jnp.where(lane8 < RANK, z, 0.0), jnp.where(lane8 < RANK, 0.0, z)], 0
    ).astype(BF16)
    adapted = []
    for ref in (ua_ref, ub_ref):
        ups = jnp.concatenate([ref[:, i : i + 128] for i in range(0, ref.shape[1], 128)], 0)
        adapted.append(lax.dot_general(z, ups, NT, preferred_element_type=F32))
    if paired:
        even = lax.axis_index("dp") % 2 == 0
        a, b = adapted
        adapted = [jnp.where(even, a, b), jnp.where(even, b, a)]
    total = sums[:, :width] + jnp.concatenate(adapted, 1)
    scale = lax.rsqrt(squares / width_all + EPSILON)
    lane = lax.broadcasted_iota(jnp.int32, (16, 128), 1)
    step = lax.broadcasted_iota(jnp.int32, (16, 128), 0) % STEPS
    first = first_rows((8, 128))

    def of_step(tiles, j):
        return jnp.concatenate(
            [
                jnp.where(first, tile[j : j + 1], tile[STEPS + j : STEPS + j + 1])
                for tile in tiles
            ],
            0,
        )

    for p in range(pairs):
        new_keys, new_values = [], []
        for e in range(2):
            at = slice((2 * p + e) * HD, (2 * p + e + 1) * HD)
            new_keys.append(rounded(rotated(total[:8, at] * scale, cosine, sine)))
            new_values.append(rounded(total[8:, at] * scale))
            fresh = jnp.concatenate([new_keys[e], new_values[e]], 0)
            start = pairs * GROUP * HD + (2 * p + e) * HD
            out_ref[:, start : start + HD] = fresh.astype(BF16)
        keys = [of_step(new_keys, j) for j in range(STEPS)]
        values = [of_step(new_values, j) for j in range(STEPS)]
        scores = [jnp.zeros((16, 128), F32) for _ in range(STEPS)]
        for g in range(GROUP):
            q = qrot_ref[:, (p * GROUP + g) * HD : (p * GROUP + g + 1) * HD].astype(F32)
            for j in range(STEPS):
                dot = jnp.sum(q * keys[j], 1, keepdims=True)
                scores[j] = jnp.where(lane == g, dot, scores[j])
        scores = [jnp.where(j <= step, scores[j], MASKED_SCORE) for j in range(STEPS)]
        end = slice(p * PAIR + GROUP * HD, (p + 1) * PAIR)
        stats = [ref[:, end].astype(F32) for ref in (ca_ref, cb_ref)]
        top = functools.reduce(jnp.maximum, scores + stats)
        fresh = [rounded(jnp.exp2((scores[j] - top) * EXPONENT)) for j in range(STEPS)]
        factors = [jnp.exp2(jnp.minimum(s - top, 0.0) * EXPONENT) for s in stats]
        denom = functools.reduce(jnp.add, fresh)
        for factor, s in zip(factors, stats):
            denom = denom + factor * totals(s)
        inverse = 1.0 / denom
        coefficients = [c * inverse for c in fresh + factors]
        for g in range(GROUP):
            at = slice(p * PAIR + g * HD, p * PAIR + (g + 1) * HD)
            terms = values + [ref[:, at].astype(F32) for ref in (ca_ref, cb_ref)]
            tile = jnp.zeros((16, 128), F32)
            for c, term in zip(coefficients, terms):
                tile = tile + broadcast_lane(c, g) * term
            out_ref[:, (p * GROUP + g) * HD : (p * GROUP + g + 1) * HD] = tile.astype(BF16)


def merge(paired, width_all, table, qrot, parts, caches, backs, ups):
    operands = [table, qrot, *parts, *caches, *backs, *ups]
    pairs = caches[0].shape[1] // PAIR
    return pl.pallas_call(
        functools.partial(merge_kernel, len(backs), paired, width_all),
        in_specs=[VMEM] * len(operands),
        out_specs=VMEM,
        out_shape=jax.ShapeDtypeStruct((16, pairs * (GROUP + 2) * HD), BF16),
        compiler_params=pltpu.CompilerParams(vmem_limit_bytes=32 * MEBI),
        name="merge",
    )(*operands)


def place_kernel(mine_ref, theirs_ref, keys_out, values_out, out_ref):
    pairs = mine_ref.shape[1] // ((GROUP + 2) * HD)
    for c, ref in enumerate((mine_ref, theirs_ref)):
        for p in range(pairs):
            pair = pair_at(c * pairs + p)
            tiles = ref[:, p * GROUP * HD : (p + 1) * GROUP * HD].astype(F32)
            size = GROUP * HD
            for e in range(2):
                at = pl.ds(pl.multiple_of((2 * pair + e) * size, size), size)
                for s in range(2):
                    rows = slice(8 * e + 4 * s, 8 * e + 4 * s + 4)
                    out_ref[s, :, at] = tiles[rows].astype(BF16)
            start = pairs * GROUP * HD + p * 2 * HD
            fresh = ref[:, start : start + 2 * HD].astype(F32)
            at = pl.ds(pl.multiple_of(pair * 2 * HD, 2 * HD), 2 * HD)
            for i, out in enumerate((keys_out, values_out)):
                for s in range(2):
                    rows = slice(8 * i + 4 * s, 8 * i + 4 * s + 4)
                    out[s, :, at] = fresh[rows].astype(BF16)


def place(width, mine, theirs):
    return pl.pallas_call(
        place_kernel,
        in_specs=[VMEM] * 2,
        out_specs=[VMEM] * 3,
        out_shape=[
            jax.ShapeDtypeStruct((2, STEPS, width), BF16),
            jax.ShapeDtypeStruct((2, STEPS, width), BF16),
            jax.ShapeDtypeStruct((2, STEPS, GROUP * width), BF16),
        ],
        compiler_params=pltpu.CompilerParams(vmem_limit_bytes=32 * MEBI),
        name="place",
    )(mine, theirs)


def swap(value, axis, n, distance):
    return lax.ppermute(value, axis, [(i, i ^ distance) for i in range(n)])


def shards(
    n_dp,
    n_tensor,
    hidden,
    norm_gain,
    queries,
    key_weight,
    value_weight,
    key_down,
    key_up,
    value_down,
    value_up,
    key_cache,
    value_cache,
    lengths,
):
    depth, width = key_weight.shape
    rows = key_down.shape[0]
    to_dp = lambda value, distance: swap(value, "dp", n_dp, distance)
    to_tensor = lambda value, distance: swap(value, "tensor", n_tensor, distance)
    partners = range(2, n_dp, 2)
    n = len(partners)
    paired = n_dp == 4

    own, tokens = pack(lengths, hidden, norm_gain, key_down, value_down, key_up, value_up)
    near = to_dp(own, 1)
    sent = [to_dp(tokens, d) for d in partners]
    keep, send, base, qrot, table = local(
        tokens, queries, key_cache, value_cache, key_weight, value_weight
    )
    received = to_tensor(send, 1)
    columns = key_up.shape[0] * 8 if paired else 0
    message, *has = rank_products(rows, depth, columns, base, table, own, near, [tokens, *sent])
    part, *rest = combine_part(n + 1, base, message, to_tensor(message, 1), has)
    replies, has = rest[:n], rest[n:]
    if paired:
        ups = [has[0], to_dp(has[0], 1)]
    else:
        ups = lax.all_gather(tokens[:, depth // 2 + 256 :], "dp")
        ups = ups.reshape(n_dp, 16, -1, 128).transpose(0, 2, 1, 3)
        ups = ups.reshape(2, 2, 16, 16, 128).transpose(0, 1, 3, 2, 4).reshape(2, 2, 16, -1)
        ups = lax.dynamic_index_in_dim(ups, lax.axis_index("tensor") % 2, 0, keepdims=False)
        ups = [ups[0], ups[1]]
    cache = combine_cache(keep, received, message)
    cache_far = to_tensor(cache, 2)
    part_far = to_tensor(part, 2)
    places = [(s, t) for s in range(n_dp) for t in range(n_tensor)]
    backs = []
    for reply, d in zip(replies, partners):
        for e in (0, 2):
            perm = [(s * n_tensor + t, (s ^ d) * n_tensor + (t ^ e)) for s, t in places]
            backs.append(lax.ppermute(reply, ("dp", "tensor"), perm))
    merged = merge(
        paired,
        float(depth * n_tensor),
        table,
        qrot,
        (part, part_far),
        (cache, cache_far),
        backs,
        ups,
    )
    return place(width, merged, to_tensor(merged, 1))


def solution(mesh):
    body = functools.partial(shards, mesh.shape["dp"], mesh.shape["tensor"])
    return jax.shard_map(
        body,
        mesh=mesh,
        in_specs=(
            P(("groups", "dp"), None, "tensor"),
            P("tensor"),
            P(("groups", "dp"), None, None),
            P("tensor", None),
            P("tensor", None),
            P(("groups", "dp"), "tensor"),
            P(("groups", "dp"), None),
            P(("groups", "dp"), "tensor"),
            P(("groups", "dp"), None),
            P(("groups", "dp"), "tensor", None),
            P(("groups", "dp"), "tensor", None),
            P(("groups", "dp")),
        ),
        out_specs=(
            P(("groups", "dp"), None, None),
            P(("groups", "dp"), None, None),
            P(("groups", "dp"), None, None),
        ),
        check_vma=False,
    )
```

```python
import functools
import math

import jax
import jax.numpy as jnp
from jax import lax
from jax.experimental import pallas as pl
from jax.experimental.pallas import tpu as pltpu
from jax.sharding import PartitionSpec as P

HD = 128
GROUP = 8
STEPS = 4
RANK = 64
EPSILON = 1e-05
ROPE_BASE = 500000.0
MASKED_SCORE = -1e30
LOWEST_TOP = -1e20
EXPONENT = math.log2(math.e) / math.sqrt(HD)
PAIR = GROUP * HD + 128
UP_COLUMNS = 3584
CHUNK = 512

F32 = jnp.float32
BF16 = jnp.bfloat16
NT = (((1,), (1,)), ((), ()))
VMEM = pl.BlockSpec(memory_space=pltpu.VMEM)
HBM = pl.BlockSpec(memory_space=pltpu.HBM)
MEBI = 2**20
WHOLE_VMEM = 65000 * 1024
LOCAL_VMEM = 54900 * 1024


def rounded(value):
    return value.astype(BF16).astype(F32)


def split(value):
    high = rounded(value)
    return jnp.concatenate([high, value - high], 0).astype(BF16)


def joined(tile):
    wide = tile.astype(F32)
    return wide[:8] + wide[8:]


def rotated(tile, cosine, sine):
    return tile * cosine + pltpu.roll(tile, HD // 2, 1) * sine


def first_rows(shape):
    return lax.broadcasted_iota(jnp.int32, shape, 0) % 8 < STEPS


def exchanged(a, b):
    first = first_rows(a.shape)
    return (
        jnp.where(first, a, pltpu.roll(b, STEPS, 0)),
        jnp.where(first, pltpu.roll(a, STEPS, 0), b),
    )


def flat(matrix):
    return jnp.concatenate([matrix[i : i + 16] for i in range(0, matrix.shape[0], 16)], 1)


def pack_kernel(*refs):
    sources, (a_ref, b_ref), held, sems = refs[:7], refs[7:9], refs[9:16], refs[16]
    copies = [
        pltpu.make_async_copy(source, target, sems.at[i])
        for i, (source, target) in enumerate(zip(sources, held))
    ]
    for copy in copies:
        copy.start()
    lengths_ref, x_ref, gain_ref, kd_ref, vd_ref, ku_ref, vu_ref = held
    for copy in copies:
        copy.wait()
    x = jnp.concatenate([x_ref[0].astype(F32), x_ref[1].astype(F32)], 0)
    depth = x.shape[1]
    scaled = x * gain_ref[...].astype(F32).reshape(1, depth)
    b_ref[:, : depth // 2] = jnp.concatenate(
        [scaled[:, : depth // 2], scaled[:, depth // 2 :]], 0
    ).astype(BF16)
    row = lax.broadcasted_iota(jnp.int32, (16, 128), 0)
    length = jnp.where(row % 8 < STEPS, lengths_ref[0], lengths_ref[1])
    length = jnp.where(row < 8, length // 64 * 64, length % 64)
    b_ref[:, depth // 2 : depth // 2 + 128] = length.astype(F32).astype(BF16)
    squares = jnp.broadcast_to(jnp.sum(x * x, 1, keepdims=True), (8, 128))
    b_ref[:, depth // 2 + 128 : depth // 2 + 256] = split(squares)
    ups = jnp.concatenate([ku_ref[...], vu_ref[...]], 0).T.astype(BF16)
    b_ref[:, depth // 2 + 256 :] = flat(ups)
    own = kd_ref.shape[0]
    for slot, ref in enumerate((kd_ref, vd_ref)):
        down = ref[...]
        if own < 16:
            down = jnp.concatenate([down, jnp.zeros((16 - own, depth), F32)], 0)
        a_ref[:, slot * depth : (slot + 1) * depth] = down.astype(BF16)


def pack(lengths, hidden, gain, key_down, value_down, key_up, value_up):
    operands = [lengths, hidden, gain, key_down, value_down, key_up.T, value_up.T]
    depth = hidden.shape[2]
    ups = key_up.shape[0] * 8
    return pl.pallas_call(
        pack_kernel,
        in_specs=[HBM] * len(operands),
        out_specs=[VMEM] * 2,
        out_shape=[
            jax.ShapeDtypeStruct((16, 2 * depth), BF16),
            jax.ShapeDtypeStruct((16, depth // 2 + 256 + ups), BF16),
        ],
        scratch_shapes=[pltpu.SMEM(lengths.shape, jnp.int32)]
        + [pltpu.VMEM(o.shape, o.dtype) for o in operands[1:]]
        + [pltpu.SemaphoreType.DMA((len(operands),))],
        compiler_params=pltpu.CompilerParams(vmem_limit_bytes=WHOLE_VMEM),
        name="pack",
    )(*operands)


def tables(length):
    shape = length.shape
    row = lax.broadcasted_iota(jnp.int32, shape, 0)
    lane = lax.broadcasted_iota(jnp.int32, shape, 1)
    position = length + (row % STEPS).astype(F32)
    pair = lane % (HD // 2)
    frequency = jnp.ones(shape, F32)
    for bit in range(6):
        factor = ROPE_BASE ** (-(2.0 * 2**bit) / HD)
        frequency = jnp.where((pair >> bit) & 1 == 1, frequency * factor, frequency)
    angle = position * frequency
    sine = jnp.sin(angle)
    return jnp.cos(angle), jnp.where(lane < HD // 2, -sine, sine)


def rotated_rows(pairs, cosine, sine, q_ref, qrot_ref):
    zero = jnp.zeros((32, HD), F32)
    result = []
    for p in pairs:
        halves = [[], []]
        for e in range(2):
            for g in range(GROUP):
                at = slice(((2 * p + e) * GROUP + g) * HD, ((2 * p + e) * GROUP + g + 1) * HD)
                q = jnp.concatenate([q_ref[0, :, at].astype(F32), q_ref[1, :, at].astype(F32)], 0)
                halves[e].append(rotated(q, cosine, sine))
        if qrot_ref is not None:
            for g in range(GROUP):
                at = slice((p * GROUP + g) * HD, (p * GROUP + g + 1) * HD)
                qrot_ref[:, at] = jnp.concatenate([halves[0][g], halves[1][g]], 0).astype(BF16)
        mixed = [[exchanged(halves[e][g], halves[e][g + 4]) for g in range(4)] for e in range(2)]
        for s in range(2):
            rows = [jnp.concatenate([mixed[e][g][s] for g in range(4)], 0) for e in range(2)]
            result.append(
                jnp.concatenate(
                    [jnp.concatenate([rows[0], zero], 1), jnp.concatenate([zero, rows[1]], 1)], 0
                ).astype(BF16)
            )
    return result


def attend(pairs, limit, queries, k_ref, v_ref, wait_values, out_ref):
    scores = []
    for i, p in enumerate(pairs):
        for s in range(2):
            keys = k_ref[s, :, 2 * p * HD : 2 * (p + 1) * HD]
            score = lax.dot_general(queries[2 * i + s], keys, NT, preferred_element_type=F32)
            place = lax.broadcasted_iota(jnp.int32, score.shape, 1)
            bound = limit[STEPS * s : STEPS * s + 1, :1].astype(jnp.int32)
            scores.append(jnp.where(place < bound, score, MASKED_SCORE))
    scores = jnp.concatenate(scores, 0)
    top = rounded(jnp.maximum(jnp.max(scores, 1, keepdims=True), LOWEST_TOP))
    weights = jnp.exp2((scores - top) * EXPONENT).astype(BF16)
    total = jnp.sum(weights.astype(F32), 1, keepdims=True)
    high = rounded(total)
    columns = (top, high, total - high)
    lane8 = lax.broadcasted_iota(jnp.int32, (8, 128), 1)
    numers = []
    wait_values()
    for i, p in enumerate(pairs):
        for s in range(2):
            at = slice(64 * (2 * i + s), 64 * (2 * i + s + 1))
            values = v_ref[s, :, 2 * p * HD : 2 * (p + 1) * HD]
            numers.append(jnp.dot(weights[at], values, preferred_element_type=F32))
    for i, p in enumerate(pairs):
        outs, ends = [[], []], []
        for e in range(2):
            back, stats = [], []
            for s in range(2):
                tile = jnp.zeros((8, 128), F32)
                for g in range(4):
                    row = 64 * (2 * i + s) + 32 * e + 8 * g
                    for slot, value in enumerate(columns):
                        tile = jnp.where(lane8 == slot * GROUP + g, value[row : row + 8], tile)
                stats.append(tile)
            for g in range(4):
                at = slice(32 * e + 8 * g, 32 * e + 8 * g + 8)
                cols = slice(e * HD, (e + 1) * HD)
                back.append(exchanged(numers[2 * i][at, cols], numers[2 * i + 1][at, cols]))
            outs[e] = [b[0] for b in back] + [b[1] for b in back]
            a, b = exchanged(*stats)
            ends.append(jnp.where(lane8 % 8 < 4, a, pltpu.roll(b, 4, 1)))
        for g in range(GROUP):
            at = slice(i * PAIR + g * HD, i * PAIR + (g + 1) * HD)
            out_ref[:, at] = jnp.concatenate([outs[0][g], outs[1][g]], 0).astype(BF16)
        out_ref[:, i * PAIR + GROUP * HD : (i + 1) * PAIR] = jnp.concatenate(ends, 0).astype(BF16)


def pair_at(i):
    return i ^ (lax.axis_index("tensor") % 2 * 2)


def local_kernel(
    x_hbm, q_hbm, k_hbm, v_hbm, wk_hbm, wv_hbm,
    keep_ref, send_ref, base_ref, qrot_ref, table_ref,
    x_ref, q_ref, k_ref, v_ref, wk_ref, wv_ref, x_sem, q_sem, cache_sem, weight_sem,
):
    pairs = k_hbm.shape[2] // (2 * HD)
    chunks = wk_hbm.shape[0] // CHUNK
    width = wk_hbm.shape[1]
    core = lax.axis_index("tensor") % 2
    x_copy = pltpu.make_async_copy(x_hbm, x_ref, x_sem)
    x_copy.start()
    groups = []
    for h in range(2):
        copies = []
        trio = ((q_hbm, q_ref, q_sem.at[h]), (k_hbm, k_ref, cache_sem.at[h, 0]))
        for source, target, sem in (*trio, (v_hbm, v_ref, cache_sem.at[h, 1])):
            size = source.shape[2] // 2
            start = pl.multiple_of((core ^ h) * size, size)
            copies.append(
                pltpu.make_async_copy(
                    source.at[:, :, pl.ds(start, size)],
                    target.at[:, :, pl.ds(h * size, size)],
                    sem,
                )
            )
        groups.append(copies)
    for h in range(2):
        groups[h][0].start()
    for copy in groups[0][1:]:
        copy.start()
    weights = []
    for c in range(chunks):
        at = pl.ds(c * CHUNK, CHUNK)
        weights.append(
            [
                pltpu.make_async_copy(source.at[at], target.at[at], weight_sem.at[c, i])
                for i, (source, target) in enumerate(((wk_hbm, wk_ref), (wv_hbm, wv_ref)))
            ]
        )
    def start(copies):
        for copy in copies:
            copy.start()

    x_copy.wait()
    start(groups[1][1:])
    start(weights[0])
    half = wk_hbm.shape[0] // 2
    x = x_ref[:, :half].astype(F32)
    x = jnp.concatenate([x[:8], x[8:]], 1).astype(BF16)
    length = joined(x_ref[:, half : half + 128])
    cosine, sine = tables(length)
    table_ref[...] = jnp.concatenate([joined(x_ref[:, half + 128 : half + 256]), cosine, sine], 0)
    limit = length - (lax.axis_index("tensor") * k_hbm.shape[1]).astype(F32)
    queries = []
    for h in range(2):
        groups[h][0].wait()
        own = range(h * pairs // 2, (h + 1) * pairs // 2)
        queries.append(rotated_rows(own, cosine, sine, q_ref, None if h else qrot_ref))
    for h, out_ref in enumerate((keep_ref, send_ref)):
        groups[h][1].wait()
        for copies in weights[1:2] if h == 0 else weights[2:]:
            start(copies)
        attend(
            range(h * pairs // 2, (h + 1) * pairs // 2),
            limit, queries[h], k_ref, v_ref, groups[h][2].wait, out_ref,
        )
    total = None
    for c in range(chunks):
        for copy in weights[c]:
            copy.wait()
        at = slice(c * CHUNK, (c + 1) * CHUNK)
        part = jnp.concatenate(
            [jnp.dot(x[:, at], ref[at], preferred_element_type=F32) for ref in (wk_ref, wv_ref)],
            0,
        )
        total = part if total is None else total + part
    lower, upper = total[:, : width // 2], total[:, width // 2 :]
    base_ref[:, : width // 2] = jnp.where(core == 0, lower, upper)
    base_ref[:, width // 2 :] = jnp.where(core == 0, upper, lower)


def local(message, queries, key_cache, value_cache, key_weight, value_weight):
    seqs, length, width = key_cache.shape
    depth = key_weight.shape[0]
    pairs = width // (2 * HD)
    operands = [message, queries, key_cache, value_cache, key_weight, value_weight]
    return pl.pallas_call(
        local_kernel,
        in_specs=[HBM] * 6,
        out_specs=[VMEM] * 5,
        out_shape=[
            jax.ShapeDtypeStruct((16, pairs // 2 * PAIR), BF16),
            jax.ShapeDtypeStruct((16, pairs // 2 * PAIR), BF16),
            jax.ShapeDtypeStruct((16, width), F32),
            jax.ShapeDtypeStruct((16, pairs // 2 * GROUP * HD), BF16),
            jax.ShapeDtypeStruct((24, 128), F32),
        ],
        scratch_shapes=[pltpu.VMEM(o.shape, BF16) for o in operands]
        + [
            pltpu.SemaphoreType.DMA,
            pltpu.SemaphoreType.DMA((2,)),
            pltpu.SemaphoreType.DMA((2, 2)),
            pltpu.SemaphoreType.DMA((depth // CHUNK, 2)),
        ],
        compiler_params=pltpu.CompilerParams(vmem_limit_bytes=LOCAL_VMEM),
        cost_estimate=pl.CostEstimate(
            flops=4 * 64 * 256 * seqs * length * pairs + 4 * 16 * depth * width,
            bytes_accessed=4 * seqs * length * width + 4 * depth * width,
            transcendentals=64 * seqs * length * pairs,
        ),
        name="local",
    )(*operands)


def rank_kernel(n, rows, depth, *refs):
    base_ref, table_ref, own_ref, near_ref = refs[:4]
    tokens, (out_ref, *has) = refs[4 : 4 + n], refs[4 + n :]
    half = base_ref.shape[1] // 2
    place = lax.axis_index("dp")
    x = []
    for ref in tokens:
        part = ref[:, : depth // 2].astype(F32)
        x.append(jnp.concatenate([part[:8], part[8:]], 1))
    x = jnp.concatenate(x, 0).astype(BF16)
    fill = jnp.zeros((RANK - 16, depth), BF16)
    z = None
    for ref, at in ((own_ref, place), (near_ref, place ^ 1)):
        down = jnp.concatenate([ref[:, :depth], fill, ref[:, depth:], fill], 0)
        part = lax.dot_general(x, down, NT, preferred_element_type=F32)
        part = pltpu.roll(part, at * rows, 1)
        z = part if z is None else z + part
    out_ref[:, :half] = base_ref[:, half:].astype(BF16)
    out_ref[:, half : half + 128] = split(table_ref[:8])
    for i in range(n):
        at = half + 128 * (i + 1)
        out_ref[:, at : at + 128] = split(z[8 * i : 8 * i + 8])
    for ref in has:
        here = place // 2 == lax.axis_index("tensor") % 2
        mine, far = (token[:, depth // 2 + 256 :].astype(F32) for token in tokens[:2])
        ref[:, : mine.shape[1]] = jnp.where(here, mine, far).astype(BF16)
        ref[:, mine.shape[1] :] = jnp.zeros((16, ref.shape[1] - mine.shape[1]), BF16)


def rank_products(rows, depth, columns, base, table, own, near, tokens):
    n = len(tokens)
    out_shape = [jax.ShapeDtypeStruct((16, base.shape[1] // 2 + 128 * (n + 1)), BF16)]
    if columns:
        out_shape.append(jax.ShapeDtypeStruct((16, columns), BF16))
    return pl.pallas_call(
        functools.partial(rank_kernel, n, rows, depth),
        in_specs=[VMEM] * (4 + n),
        out_specs=[VMEM] * len(out_shape),
        out_shape=out_shape,
        compiler_params=pltpu.CompilerParams(vmem_limit_bytes=32 * MEBI),
        name="rank_products",
    )(base, table, own, near, *tokens)


def broadcast_lane(tile, lane):
    return jnp.broadcast_to(tile[:, lane : lane + 1], tile.shape)


def combine_part_kernel(base_ref, mine_ref, theirs_ref, cache_ref, out_ref, *replies):
    half = base_ref.shape[1] // 2
    own = base_ref[:, :half] + theirs_ref[:, :half].astype(F32)
    out_ref[:, :half] = own.astype(BF16)
    sums = mine_ref[:, half:].astype(F32) + theirs_ref[:, half:].astype(F32)
    sums = split(sums[:8] + sums[8:])
    out_ref[:, half : half + 256] = sums[:, :256]
    out_ref[:, half + 256 :] = cache_ref[...]
    for i, ref in enumerate(replies):
        ref[...] = sums[:, 128 * (i + 2) : 128 * (i + 3)]


def combine_part(n, base, mine, theirs, cache):
    shapes = [(16, base.shape[1] // 2 + 256 + cache.shape[1])] + [(16, 128)] * n
    return pl.pallas_call(
        combine_part_kernel,
        in_specs=[VMEM] * 4,
        out_specs=[VMEM] * len(shapes),
        out_shape=[jax.ShapeDtypeStruct(shape, BF16) for shape in shapes],
        compiler_params=pltpu.CompilerParams(vmem_limit_bytes=32 * MEBI),
        name="combine_part",
    )(base, mine, theirs, cache)


def combine_cache_kernel(a_ref, b_ref, _, out_ref):
    lane = lax.broadcasted_iota(jnp.int32, (16, 128), 1)
    for p in range(out_ref.shape[1] // PAIR):
        end = slice(p * PAIR + GROUP * HD, (p + 1) * PAIR)
        a, b = a_ref[:, end].astype(F32), b_ref[:, end].astype(F32)
        top = jnp.maximum(a, b)
        fa = jnp.exp2(jnp.minimum(a - top, 0.0) * EXPONENT)
        fb = jnp.exp2(jnp.minimum(b - top, 0.0) * EXPONENT)
        total = fa * totals(a) + fb * totals(b)
        high = rounded(total)
        stats = jnp.where(lane < GROUP, top, 0.0)
        stats = jnp.where(lane // GROUP == 1, pltpu.roll(high, GROUP, 1), stats)
        stats = jnp.where(lane // GROUP == 2, pltpu.roll(total - high, 2 * GROUP, 1), stats)
        out_ref[:, end] = stats.astype(BF16)
        for g in range(GROUP):
            at = slice(p * PAIR + g * HD, p * PAIR + (g + 1) * HD)
            out_ref[:, at] = (
                broadcast_lane(fa, g) * a_ref[:, at].astype(F32)
                + broadcast_lane(fb, g) * b_ref[:, at].astype(F32)
            ).astype(BF16)


def totals(stats):
    return pltpu.roll(stats, 128 - GROUP, 1) + pltpu.roll(stats, 128 - 2 * GROUP, 1)


def combine_cache(a, b, earlier):
    return pl.pallas_call(
        combine_cache_kernel,
        in_specs=[VMEM] * 3,
        out_specs=VMEM,
        out_shape=jax.ShapeDtypeStruct(a.shape, BF16),
        compiler_params=pltpu.CompilerParams(vmem_limit_bytes=32 * MEBI),
        name="combine_cache",
    )(a, b, earlier)


def merge_kernel(n, paired, width_all, *refs):
    table_ref, qrot_ref, pa_ref, pb_ref = refs[:4]
    backs, (ua_ref, ub_ref, out_ref) = refs[4 : 4 + n], refs[4 + n :]
    pairs = qrot_ref.shape[1] // (GROUP * HD)
    width = pairs * 2 * HD
    cosine, sine = table_ref[8:16], table_ref[16:]
    head = width + 256
    sums = pa_ref[:, :head].astype(F32) + pb_ref[:, :head].astype(F32)
    tail = sums[:8, width : width + 256] + sums[8:, width : width + 256]
    squares, z = tail[:, :128], tail[:, 128:]
    for ref in backs:
        z = z + joined(ref[...])
    lane8 = lax.broadcasted_iota(jnp.int32, (8, 128), 1)
    z = jnp.concatenate(
        [jnp.where(lane8 < RANK, z, 0.0), jnp.where(lane8 < RANK, 0.0, z)], 0
    ).astype(BF16)
    adapted = []
    for ref in (ua_ref, ub_ref):
        ups = jnp.concatenate([ref[:, i : i + 128] for i in range(0, 16 * HD, 128)], 0)
        adapted.append(lax.dot_general(z, ups, NT, preferred_element_type=F32))
    if paired:
        even = lax.axis_index("dp") % 2 == 0
        a, b = adapted
        adapted = [jnp.where(even, a, b), jnp.where(even, b, a)]
    total = sums[:, :width] + jnp.concatenate(adapted, 1)
    scale = lax.rsqrt(squares / width_all + EPSILON)
    lane = lax.broadcasted_iota(jnp.int32, (16, 128), 1)
    step = lax.broadcasted_iota(jnp.int32, (16, 128), 0) % STEPS
    first = first_rows((8, 128))

    def of_step(tiles, j):
        return jnp.concatenate(
            [
                jnp.where(first, tile[j : j + 1], tile[STEPS + j : STEPS + j + 1])
                for tile in tiles
            ],
            0,
        )

    for p in range(pairs):
        new_keys, new_values = [], []
        for e in range(2):
            at = slice((2 * p + e) * HD, (2 * p + e + 1) * HD)
            new_keys.append(rounded(rotated(total[:8, at] * scale, cosine, sine)))
            new_values.append(rounded(total[8:, at] * scale))
            fresh = jnp.concatenate([new_keys[e], new_values[e]], 0)
            start = pairs * GROUP * HD + (2 * p + e) * HD
            out_ref[:, start : start + HD] = fresh.astype(BF16)
        keys = [of_step(new_keys, j) for j in range(STEPS)]
        values = [of_step(new_values, j) for j in range(STEPS)]
        scores = [jnp.zeros((16, 128), F32) for _ in range(STEPS)]
        for g in range(GROUP):
            q = qrot_ref[:, (p * GROUP + g) * HD : (p * GROUP + g + 1) * HD].astype(F32)
            for j in range(STEPS):
                dot = jnp.sum(q * keys[j], 1, keepdims=True)
                scores[j] = jnp.where(lane == g, dot, scores[j])
        scores = [jnp.where(j <= step, scores[j], MASKED_SCORE) for j in range(STEPS)]
        end = slice(head + p * PAIR + GROUP * HD, head + (p + 1) * PAIR)
        stats = [ref[:, end].astype(F32) for ref in (pa_ref, pb_ref)]
        top = functools.reduce(jnp.maximum, scores + stats)
        fresh = [rounded(jnp.exp2((scores[j] - top) * EXPONENT)) for j in range(STEPS)]
        factors = [jnp.exp2(jnp.minimum(s - top, 0.0) * EXPONENT) for s in stats]
        denom = functools.reduce(jnp.add, fresh)
        for factor, s in zip(factors, stats):
            denom = denom + factor * totals(s)
        inverse = 1.0 / denom
        coefficients = [c * inverse for c in fresh + factors]
        for g in range(GROUP):
            at = slice(head + p * PAIR + g * HD, head + p * PAIR + (g + 1) * HD)
            terms = values + [ref[:, at].astype(F32) for ref in (pa_ref, pb_ref)]
            tile = jnp.zeros((16, 128), F32)
            for c, term in zip(coefficients, terms):
                tile = tile + broadcast_lane(c, g) * term
            out_ref[:, (p * GROUP + g) * HD : (p * GROUP + g + 1) * HD] = tile.astype(BF16)


def merge(paired, width_all, table, qrot, parts, backs, ups):
    operands = [table, qrot, *parts, *backs, *ups]
    pairs = qrot.shape[1] // (GROUP * HD)
    return pl.pallas_call(
        functools.partial(merge_kernel, len(backs), paired, width_all),
        in_specs=[VMEM] * len(operands),
        out_specs=VMEM,
        out_shape=jax.ShapeDtypeStruct((16, pairs * (GROUP + 2) * HD), BF16),
        compiler_params=pltpu.CompilerParams(vmem_limit_bytes=32 * MEBI),
        name="merge",
    )(*operands)


def place_kernel(mine_ref, theirs_ref, keys_out, values_out, out_ref):
    pairs = mine_ref.shape[1] // ((GROUP + 2) * HD)
    for c, ref in enumerate((mine_ref, theirs_ref)):
        for p in range(pairs):
            pair = pair_at(c * pairs + p)
            tiles = ref[:, p * GROUP * HD : (p + 1) * GROUP * HD].astype(F32)
            size = GROUP * HD
            for e in range(2):
                at = pl.ds(pl.multiple_of((2 * pair + e) * size, size), size)
                for s in range(2):
                    rows = slice(8 * e + 4 * s, 8 * e + 4 * s + 4)
                    out_ref[s, :, at] = tiles[rows].astype(BF16)
            start = pairs * GROUP * HD + p * 2 * HD
            fresh = ref[:, start : start + 2 * HD].astype(F32)
            at = pl.ds(pl.multiple_of(pair * 2 * HD, 2 * HD), 2 * HD)
            for i, out in enumerate((keys_out, values_out)):
                for s in range(2):
                    rows = slice(8 * i + 4 * s, 8 * i + 4 * s + 4)
                    out[s, :, at] = fresh[rows].astype(BF16)


def place(width, mine, theirs):
    return pl.pallas_call(
        place_kernel,
        in_specs=[VMEM] * 2,
        out_specs=[VMEM] * 3,
        out_shape=[
            jax.ShapeDtypeStruct((2, STEPS, width), BF16),
            jax.ShapeDtypeStruct((2, STEPS, width), BF16),
            jax.ShapeDtypeStruct((2, STEPS, GROUP * width), BF16),
        ],
        compiler_params=pltpu.CompilerParams(vmem_limit_bytes=32 * MEBI),
        name="place",
    )(mine, theirs)


def swap(value, axis, n, distance):
    return lax.ppermute(value, axis, [(i, i ^ distance) for i in range(n)])


def shards(
    n_dp,
    n_tensor,
    hidden,
    norm_gain,
    queries,
    key_weight,
    value_weight,
    key_down,
    key_up,
    value_down,
    value_up,
    key_cache,
    value_cache,
    lengths,
):
    depth, width = key_weight.shape
    rows = key_down.shape[0]
    to_dp = lambda value, distance: swap(value, "dp", n_dp, distance)
    to_tensor = lambda value, distance: swap(value, "tensor", n_tensor, distance)
    partners = range(2, n_dp, 2)
    n = len(partners)
    paired = n_dp == 4

    own, tokens = pack(lengths, hidden, norm_gain, key_down, value_down, key_up, value_up)
    near = to_dp(own, 1)
    sent = [to_dp(tokens, d) for d in partners]
    keep, send, base, qrot, table = local(
        tokens, queries, key_cache, value_cache, key_weight, value_weight
    )
    received = to_tensor(send, 1)
    columns = UP_COLUMNS if paired else 0
    message, *has = rank_products(rows, depth, columns, base, table, own, near, [tokens, *sent])
    if paired:
        ups = [has[0], to_dp(has[0], 1)]
    else:
        ups = lax.all_gather(tokens[:, depth // 2 + 256 :], "dp")
        ups = ups.reshape(n_dp, 16, -1, 128).transpose(0, 2, 1, 3)
        ups = ups.reshape(2, 2, 16, 16, 128).transpose(0, 1, 3, 2, 4).reshape(2, 2, 16, -1)
        ups = lax.dynamic_index_in_dim(ups, lax.axis_index("tensor") % 2, 0, keepdims=False)
        ups = [ups[0], ups[1]]
    cache = combine_cache(keep, received, message)
    part, *replies = combine_part(n, base, message, to_tensor(message, 1), cache)
    part_far = to_tensor(part, 2)
    places = [(s, t) for s in range(n_dp) for t in range(n_tensor)]
    backs = []
    for reply, d in zip(replies, partners):
        for e in (0, 2):
            perm = [(s * n_tensor + t, (s ^ d) * n_tensor + (t ^ e)) for s, t in places]
            backs.append(lax.ppermute(reply, ("dp", "tensor"), perm))
    merged = merge(
        paired,
        float(depth * n_tensor),
        table,
        qrot,
        (part, part_far),
        backs,
        ups,
    )
    return place(width, merged, to_tensor(merged, 1))


def solution(mesh):
    body = functools.partial(shards, mesh.shape["dp"], mesh.shape["tensor"])
    return jax.shard_map(
        body,
        mesh=mesh,
        in_specs=(
            P(("groups", "dp"), None, "tensor"),
            P("tensor"),
            P(("groups", "dp"), None, None),
            P("tensor", None),
            P("tensor", None),
            P(("groups", "dp"), "tensor"),
            P(("groups", "dp"), None),
            P(("groups", "dp"), "tensor"),
            P(("groups", "dp"), None),
            P(("groups", "dp"), "tensor", None),
            P(("groups", "dp"), "tensor", None),
            P(("groups", "dp")),
        ),
        out_specs=(
            P(("groups", "dp"), None, None),
            P(("groups", "dp"), None, None),
            P(("groups", "dp"), None, None),
        ),
        check_vma=False,
    )
```

```python
import functools
import math

import jax
import jax.numpy as jnp
from jax import lax
from jax.experimental import pallas as pl
from jax.experimental.pallas import tpu as pltpu
from jax.sharding import PartitionSpec as P

HD = 128
GROUP = 8
STEPS = 4
RANK = 64
EPSILON = 1e-05
ROPE_BASE = 500000.0
MASKED_SCORE = -1e30
LOWEST_TOP = -1e20
EXPONENT = math.log2(math.e) / math.sqrt(HD)
PAIR = GROUP * HD + 128
UP_COLUMNS = 3584
CHUNK = 512

F32 = jnp.float32
BF16 = jnp.bfloat16
NT = (((1,), (1,)), ((), ()))
VMEM = pl.BlockSpec(memory_space=pltpu.VMEM)
HBM = pl.BlockSpec(memory_space=pltpu.HBM)
MEBI = 2**20
WHOLE_VMEM = 65000 * 1024
LOCAL_VMEM = 54900 * 1024


def rounded(value):
    return value.astype(BF16).astype(F32)


def split(value):
    high = rounded(value)
    return jnp.concatenate([high, value - high], 0).astype(BF16)


def joined(tile):
    wide = tile.astype(F32)
    return wide[:8] + wide[8:]


def rotated(tile, cosine, sine):
    return tile * cosine + pltpu.roll(tile, HD // 2, 1) * sine


def first_rows(shape):
    return lax.broadcasted_iota(jnp.int32, shape, 0) % 8 < STEPS


def exchanged(a, b):
    first = first_rows(a.shape)
    return (
        jnp.where(first, a, pltpu.roll(b, STEPS, 0)),
        jnp.where(first, pltpu.roll(a, STEPS, 0), b),
    )


def flat(matrix):
    return jnp.concatenate([matrix[i : i + 16] for i in range(0, matrix.shape[0], 16)], 1)


def pack_kernel(*refs):
    sources, outs, held = refs[:7], refs[7:9], refs[9:16]
    (a_ref, b_ref), sems, out_sems = refs[16:18], refs[18], refs[19]
    copies = [
        pltpu.make_async_copy(source, target, sems.at[i])
        for i, (source, target) in enumerate(zip(sources, held))
    ]
    for copy in copies:
        copy.start()
    backs = [
        pltpu.make_async_copy(source, target, out_sems.at[i])
        for i, (source, target) in enumerate(zip((a_ref, b_ref), outs))
    ]
    kd_ref, vd_ref, x_ref, gain_ref, lengths_ref, ku_ref, vu_ref = held
    own, depth = kd_ref.shape
    for slot, ref in enumerate((kd_ref, vd_ref)):
        copies[slot].wait()
        down = ref[...]
        if own < 16:
            down = jnp.concatenate([down, jnp.zeros((16 - own, depth), F32)], 0)
        a_ref[:, slot * depth : (slot + 1) * depth] = down.astype(BF16)
    backs[0].start()
    for copy in copies[2:]:
        copy.wait()
    x = jnp.concatenate([x_ref[0].astype(F32), x_ref[1].astype(F32)], 0)
    gain = gain_ref[...].astype(F32)
    scaled = jnp.concatenate(
        [x[:, i * 128 : (i + 1) * 128] * gain[i : i + 1] for i in range(depth // 128)], 1
    )
    b_ref[:, : depth // 2] = jnp.concatenate(
        [scaled[:, : depth // 2], scaled[:, depth // 2 :]], 0
    ).astype(BF16)
    row = lax.broadcasted_iota(jnp.int32, (16, 128), 0)
    lengths = lengths_ref[...]
    length = jnp.where(row % 8 < STEPS, lengths[:, :1], lengths[:, 1:])
    length = jnp.where(row < 8, length // 64 * 64, length % 64)
    b_ref[:, depth // 2 : depth // 2 + 128] = length.astype(F32).astype(BF16)
    squares = jnp.broadcast_to(jnp.sum(x * x, 1, keepdims=True), (8, 128))
    b_ref[:, depth // 2 + 128 : depth // 2 + 256] = split(squares)
    ups = jnp.concatenate([ku_ref[...], vu_ref[...]], 0).T.astype(BF16)
    b_ref[:, depth // 2 + 256 :] = flat(ups)
    backs[1].start()
    for copy in backs:
        copy.wait()


def pack(lengths, hidden, gain, key_down, value_down, key_up, value_up):
    operands = [key_down, value_down, hidden, gain.reshape(-1, 128), lengths.reshape(1, 2)]
    operands += [key_up.T, value_up.T]
    depth = hidden.shape[2]
    ups = key_up.shape[0] * 8
    outs = [
        jax.ShapeDtypeStruct((16, 2 * depth), BF16),
        jax.ShapeDtypeStruct((16, depth // 2 + 256 + ups), BF16),
    ]
    return pl.pallas_call(
        pack_kernel,
        in_specs=[HBM] * len(operands),
        out_specs=[HBM] * len(outs),
        out_shape=outs,
        scratch_shapes=[pltpu.VMEM(o.shape, o.dtype) for o in operands + outs]
        + [pltpu.SemaphoreType.DMA((len(operands),)), pltpu.SemaphoreType.DMA((len(outs),))],
        compiler_params=pltpu.CompilerParams(vmem_limit_bytes=WHOLE_VMEM),
        name="pack",
    )(*operands)


def tables(length):
    shape = length.shape
    row = lax.broadcasted_iota(jnp.int32, shape, 0)
    lane = lax.broadcasted_iota(jnp.int32, shape, 1)
    position = length + (row % STEPS).astype(F32)
    pair = lane % (HD // 2)
    frequency = jnp.ones(shape, F32)
    for bit in range(6):
        factor = ROPE_BASE ** (-(2.0 * 2**bit) / HD)
        frequency = jnp.where((pair >> bit) & 1 == 1, frequency * factor, frequency)
    angle = position * frequency
    sine = jnp.sin(angle)
    return jnp.cos(angle), jnp.where(lane < HD // 2, -sine, sine)


def rotated_rows(pairs, cosine, sine, q_ref, qrot_ref):
    zero = jnp.zeros((32, HD), F32)
    result = []
    for p in pairs:
        halves = [[], []]
        for e in range(2):
            for g in range(GROUP):
                at = slice(((2 * p + e) * GROUP + g) * HD, ((2 * p + e) * GROUP + g + 1) * HD)
                q = jnp.concatenate([q_ref[0, :, at].astype(F32), q_ref[1, :, at].astype(F32)], 0)
                halves[e].append(rotated(q, cosine, sine))
        if qrot_ref is not None:
            for g in range(GROUP):
                at = slice((p * GROUP + g) * HD, (p * GROUP + g + 1) * HD)
                qrot_ref[:, at] = jnp.concatenate([halves[0][g], halves[1][g]], 0).astype(BF16)
        mixed = [[exchanged(halves[e][g], halves[e][g + 4]) for g in range(4)] for e in range(2)]
        for s in range(2):
            rows = [jnp.concatenate([mixed[e][g][s] for g in range(4)], 0) for e in range(2)]
            result.append(
                jnp.concatenate(
                    [jnp.concatenate([rows[0], zero], 1), jnp.concatenate([zero, rows[1]], 1)], 0
                ).astype(BF16)
            )
    return result


def attend(pairs, limit, queries, k_ref, v_ref, wait_values, out_ref):
    scores = []
    for i, p in enumerate(pairs):
        for s in range(2):
            keys = k_ref[s, :, 2 * p * HD : 2 * (p + 1) * HD]
            score = lax.dot_general(queries[2 * i + s], keys, NT, preferred_element_type=F32)
            place = lax.broadcasted_iota(jnp.int32, score.shape, 1)
            bound = limit[STEPS * s : STEPS * s + 1, :1].astype(jnp.int32)
            scores.append(jnp.where(place < bound, score, MASKED_SCORE))
    scores = jnp.concatenate(scores, 0)
    top = rounded(jnp.maximum(jnp.max(scores, 1, keepdims=True), LOWEST_TOP))
    weights = jnp.exp2((scores - top) * EXPONENT).astype(BF16)
    total = jnp.sum(weights.astype(F32), 1, keepdims=True)
    high = rounded(total)
    columns = (top, high, total - high)
    lane8 = lax.broadcasted_iota(jnp.int32, (8, 128), 1)
    numers = []
    wait_values()
    for i, p in enumerate(pairs):
        for s in range(2):
            at = slice(64 * (2 * i + s), 64 * (2 * i + s + 1))
            values = v_ref[s, :, 2 * p * HD : 2 * (p + 1) * HD]
            numers.append(jnp.dot(weights[at], values, preferred_element_type=F32))
    for i, p in enumerate(pairs):
        outs, ends = [[], []], []
        for e in range(2):
            back, stats = [], []
            for s in range(2):
                tile = jnp.zeros((8, 128), F32)
                for g in range(4):
                    row = 64 * (2 * i + s) + 32 * e + 8 * g
                    for slot, value in enumerate(columns):
                        tile = jnp.where(lane8 == slot * GROUP + g, value[row : row + 8], tile)
                stats.append(tile)
            for g in range(4):
                at = slice(32 * e + 8 * g, 32 * e + 8 * g + 8)
                cols = slice(e * HD, (e + 1) * HD)
                back.append(exchanged(numers[2 * i][at, cols], numers[2 * i + 1][at, cols]))
            outs[e] = [b[0] for b in back] + [b[1] for b in back]
            a, b = exchanged(*stats)
            ends.append(jnp.where(lane8 % 8 < 4, a, pltpu.roll(b, 4, 1)))
        for g in range(GROUP):
            at = slice(i * PAIR + g * HD, i * PAIR + (g + 1) * HD)
            out_ref[:, at] = jnp.concatenate([outs[0][g], outs[1][g]], 0).astype(BF16)
        out_ref[:, i * PAIR + GROUP * HD : (i + 1) * PAIR] = jnp.concatenate(ends, 0).astype(BF16)


def pair_at(i):
    return i ^ (lax.axis_index("tensor") % 2 * 2)


def local_kernel(
    x_hbm, q_hbm, k_hbm, v_hbm, wk_hbm, wv_hbm,
    keep_ref, send_ref, base_ref, qrot_ref, table_ref,
    x_ref, q_ref, k_ref, v_ref, wk_ref, wv_ref, x_sem, q_sem, cache_sem, weight_sem,
):
    pairs = k_hbm.shape[2] // (2 * HD)
    chunks = wk_hbm.shape[0] // CHUNK
    width = wk_hbm.shape[1]
    core = lax.axis_index("tensor") % 2
    x_copy = pltpu.make_async_copy(x_hbm, x_ref, x_sem)
    x_copy.start()
    groups = []
    for h in range(2):
        copies = []
        trio = ((q_hbm, q_ref, q_sem.at[h]), (k_hbm, k_ref, cache_sem.at[h, 0]))
        for source, target, sem in (*trio, (v_hbm, v_ref, cache_sem.at[h, 1])):
            size = source.shape[2] // 2
            start = pl.multiple_of((core ^ h) * size, size)
            copies.append(
                pltpu.make_async_copy(
                    source.at[:, :, pl.ds(start, size)],
                    target.at[:, :, pl.ds(h * size, size)],
                    sem,
                )
            )
        groups.append(copies)
    for h in range(2):
        groups[h][0].start()
    for copy in groups[0][1:]:
        copy.start()
    weights = []
    for c in range(chunks):
        at = pl.ds(c * CHUNK, CHUNK)
        weights.append(
            [
                pltpu.make_async_copy(source.at[at], target.at[at], weight_sem.at[c, i])
                for i, (source, target) in enumerate(((wk_hbm, wk_ref), (wv_hbm, wv_ref)))
            ]
        )
    def start(copies):
        for copy in copies:
            copy.start()

    x_copy.wait()
    start(groups[1][1:])
    start(weights[0])
    half = wk_hbm.shape[0] // 2
    x = x_ref[:, :half].astype(F32)
    x = jnp.concatenate([x[:8], x[8:]], 1).astype(BF16)
    length = joined(x_ref[:, half : half + 128])
    cosine, sine = tables(length)
    table_ref[...] = jnp.concatenate([joined(x_ref[:, half + 128 : half + 256]), cosine, sine], 0)
    limit = length - (lax.axis_index("tensor") * k_hbm.shape[1]).astype(F32)
    queries = []
    for h in range(2):
        groups[h][0].wait()
        own = range(h * pairs // 2, (h + 1) * pairs // 2)
        queries.append(rotated_rows(own, cosine, sine, q_ref, None if h else qrot_ref))
    for h, out_ref in enumerate((keep_ref, send_ref)):
        groups[h][1].wait()
        for copies in weights[1:2] if h == 0 else weights[2:]:
            start(copies)
        attend(
            range(h * pairs // 2, (h + 1) * pairs // 2),
            limit, queries[h], k_ref, v_ref, groups[h][2].wait, out_ref,
        )
    total = None
    for c in range(chunks):
        for copy in weights[c]:
            copy.wait()
        at = slice(c * CHUNK, (c + 1) * CHUNK)
        part = jnp.concatenate(
            [jnp.dot(x[:, at], ref[at], preferred_element_type=F32) for ref in (wk_ref, wv_ref)],
            0,
        )
        total = part if total is None else total + part
    lower, upper = total[:, : width // 2], total[:, width // 2 :]
    base_ref[:, : width // 2] = jnp.where(core == 0, lower, upper)
    base_ref[:, width // 2 :] = jnp.where(core == 0, upper, lower)


def local(message, queries, key_cache, value_cache, key_weight, value_weight):
    seqs, length, width = key_cache.shape
    depth = key_weight.shape[0]
    pairs = width // (2 * HD)
    operands = [message, queries, key_cache, value_cache, key_weight, value_weight]
    return pl.pallas_call(
        local_kernel,
        in_specs=[HBM] * 6,
        out_specs=[VMEM] * 5,
        out_shape=[
            jax.ShapeDtypeStruct((16, pairs // 2 * PAIR), BF16),
            jax.ShapeDtypeStruct((16, pairs // 2 * PAIR), BF16),
            jax.ShapeDtypeStruct((16, width), F32),
            jax.ShapeDtypeStruct((16, pairs // 2 * GROUP * HD), BF16),
            jax.ShapeDtypeStruct((24, 128), F32),
        ],
        scratch_shapes=[pltpu.VMEM(o.shape, BF16) for o in operands]
        + [
            pltpu.SemaphoreType.DMA,
            pltpu.SemaphoreType.DMA((2,)),
            pltpu.SemaphoreType.DMA((2, 2)),
            pltpu.SemaphoreType.DMA((depth // CHUNK, 2)),
        ],
        compiler_params=pltpu.CompilerParams(vmem_limit_bytes=LOCAL_VMEM),
        cost_estimate=pl.CostEstimate(
            flops=4 * 64 * 256 * seqs * length * pairs + 4 * 16 * depth * width,
            bytes_accessed=4 * seqs * length * width + 4 * depth * width,
            transcendentals=64 * seqs * length * pairs,
        ),
        name="local",
    )(*operands)


def rank_kernel(n, rows, depth, *refs):
    base_ref, table_ref, own_ref, near_ref = refs[:4]
    tokens, (out_ref, *has) = refs[4 : 4 + n], refs[4 + n :]
    half = base_ref.shape[1] // 2
    place = lax.axis_index("dp")
    x = []
    for ref in tokens:
        part = ref[:, : depth // 2].astype(F32)
        x.append(jnp.concatenate([part[:8], part[8:]], 1))
    x = jnp.concatenate(x, 0).astype(BF16)
    fill = jnp.zeros((RANK - 16, depth), BF16)
    z = None
    for ref, at in ((own_ref, place), (near_ref, place ^ 1)):
        down = jnp.concatenate([ref[:, :depth], fill, ref[:, depth:], fill], 0)
        part = lax.dot_general(x, down, NT, preferred_element_type=F32)
        part = pltpu.roll(part, at * rows, 1)
        z = part if z is None else z + part
    out_ref[:, :half] = base_ref[:, half:].astype(BF16)
    out_ref[:, half : half + 128] = split(table_ref[:8])
    for i in range(n):
        at = half + 128 * (i + 1)
        out_ref[:, at : at + 128] = split(z[8 * i : 8 * i + 8])
    for ref in has:
        here = place // 2 == lax.axis_index("tensor") % 2
        mine, far = (token[:, depth // 2 + 256 :].astype(F32) for token in tokens[:2])
        ref[:, : mine.shape[1]] = jnp.where(here, mine, far).astype(BF16)
        ref[:, mine.shape[1] :] = jnp.zeros((16, ref.shape[1] - mine.shape[1]), BF16)


def rank_products(rows, depth, columns, base, table, own, near, tokens):
    n = len(tokens)
    out_shape = [jax.ShapeDtypeStruct((16, base.shape[1] // 2 + 128 * (n + 1)), BF16)]
    if columns:
        out_shape.append(jax.ShapeDtypeStruct((16, columns), BF16))
    return pl.pallas_call(
        functools.partial(rank_kernel, n, rows, depth),
        in_specs=[VMEM] * (4 + n),
        out_specs=[VMEM] * len(out_shape),
        out_shape=out_shape,
        compiler_params=pltpu.CompilerParams(vmem_limit_bytes=32 * MEBI),
        name="rank_products",
    )(base, table, own, near, *tokens)


def broadcast_lane(tile, lane):
    return jnp.broadcast_to(tile[:, lane : lane + 1], tile.shape)


def combine_part_kernel(base_ref, mine_ref, theirs_ref, cache_ref, out_ref, *replies):
    half = base_ref.shape[1] // 2
    own = base_ref[:, :half] + theirs_ref[:, :half].astype(F32)
    out_ref[:, :half] = own.astype(BF16)
    sums = mine_ref[:, half:].astype(F32) + theirs_ref[:, half:].astype(F32)
    sums = split(sums[:8] + sums[8:])
    out_ref[:, half : half + 256] = sums[:, :256]
    out_ref[:, half + 256 :] = cache_ref[...]
    for i, ref in enumerate(replies):
        ref[...] = sums[:, 128 * (i + 2) : 128 * (i + 3)]


def combine_part(n, base, mine, theirs, cache):
    shapes = [(16, base.shape[1] // 2 + 256 + cache.shape[1])] + [(16, 128)] * n
    return pl.pallas_call(
        combine_part_kernel,
        in_specs=[VMEM] * 4,
        out_specs=[VMEM] * len(shapes),
        out_shape=[jax.ShapeDtypeStruct(shape, BF16) for shape in shapes],
        compiler_params=pltpu.CompilerParams(vmem_limit_bytes=32 * MEBI),
        name="combine_part",
    )(base, mine, theirs, cache)


def combine_cache_kernel(a_ref, b_ref, _, out_ref):
    lane = lax.broadcasted_iota(jnp.int32, (16, 128), 1)
    for p in range(out_ref.shape[1] // PAIR):
        end = slice(p * PAIR + GROUP * HD, (p + 1) * PAIR)
        a, b = a_ref[:, end].astype(F32), b_ref[:, end].astype(F32)
        top = jnp.maximum(a, b)
        fa = jnp.exp2(jnp.minimum(a - top, 0.0) * EXPONENT)
        fb = jnp.exp2(jnp.minimum(b - top, 0.0) * EXPONENT)
        total = fa * totals(a) + fb * totals(b)
        high = rounded(total)
        stats = jnp.where(lane < GROUP, top, 0.0)
        stats = jnp.where(lane // GROUP == 1, pltpu.roll(high, GROUP, 1), stats)
        stats = jnp.where(lane // GROUP == 2, pltpu.roll(total - high, 2 * GROUP, 1), stats)
        out_ref[:, end] = stats.astype(BF16)
        for g in range(GROUP):
            at = slice(p * PAIR + g * HD, p * PAIR + (g + 1) * HD)
            out_ref[:, at] = (
                broadcast_lane(fa, g) * a_ref[:, at].astype(F32)
                + broadcast_lane(fb, g) * b_ref[:, at].astype(F32)
            ).astype(BF16)


def totals(stats):
    return pltpu.roll(stats, 128 - GROUP, 1) + pltpu.roll(stats, 128 - 2 * GROUP, 1)


def combine_cache(a, b, earlier):
    return pl.pallas_call(
        combine_cache_kernel,
        in_specs=[VMEM] * 3,
        out_specs=VMEM,
        out_shape=jax.ShapeDtypeStruct(a.shape, BF16),
        compiler_params=pltpu.CompilerParams(vmem_limit_bytes=32 * MEBI),
        name="combine_cache",
    )(a, b, earlier)


def merge_kernel(n, paired, width_all, *refs):
    table_ref, qrot_ref, pa_ref, pb_ref = refs[:4]
    backs, (ua_ref, ub_ref, out_ref) = refs[4 : 4 + n], refs[4 + n :]
    pairs = qrot_ref.shape[1] // (GROUP * HD)
    width = pairs * 2 * HD
    cosine, sine = table_ref[8:16], table_ref[16:]
    head = width + 256
    sums = pa_ref[:, :head].astype(F32) + pb_ref[:, :head].astype(F32)
    tail = sums[:8, width : width + 256] + sums[8:, width : width + 256]
    squares, z = tail[:, :128], tail[:, 128:]
    for ref in backs:
        z = z + joined(ref[...])
    lane8 = lax.broadcasted_iota(jnp.int32, (8, 128), 1)
    z = jnp.concatenate(
        [jnp.where(lane8 < RANK, z, 0.0), jnp.where(lane8 < RANK, 0.0, z)], 0
    ).astype(BF16)
    adapted = []
    for ref in (ua_ref, ub_ref):
        ups = jnp.concatenate([ref[:, i : i + 128] for i in range(0, 16 * HD, 128)], 0)
        adapted.append(lax.dot_general(z, ups, NT, preferred_element_type=F32))
    if paired:
        even = lax.axis_index("dp") % 2 == 0
        a, b = adapted
        adapted = [jnp.where(even, a, b), jnp.where(even, b, a)]
    total = sums[:, :width] + jnp.concatenate(adapted, 1)
    scale = lax.rsqrt(squares / width_all + EPSILON)
    lane = lax.broadcasted_iota(jnp.int32, (16, 128), 1)
    step = lax.broadcasted_iota(jnp.int32, (16, 128), 0) % STEPS
    first = first_rows((8, 128))

    def of_step(tiles, j):
        return jnp.concatenate(
            [
                jnp.where(first, tile[j : j + 1], tile[STEPS + j : STEPS + j + 1])
                for tile in tiles
            ],
            0,
        )

    for p in range(pairs):
        new_keys, new_values = [], []
        for e in range(2):
            at = slice((2 * p + e) * HD, (2 * p + e + 1) * HD)
            new_keys.append(rounded(rotated(total[:8, at] * scale, cosine, sine)))
            new_values.append(rounded(total[8:, at] * scale))
            fresh = jnp.concatenate([new_keys[e], new_values[e]], 0)
            start = pairs * GROUP * HD + (2 * p + e) * HD
            out_ref[:, start : start + HD] = fresh.astype(BF16)
        keys = [of_step(new_keys, j) for j in range(STEPS)]
        values = [of_step(new_values, j) for j in range(STEPS)]
        scores = [jnp.zeros((16, 128), F32) for _ in range(STEPS)]
        for g in range(GROUP):
            q = qrot_ref[:, (p * GROUP + g) * HD : (p * GROUP + g + 1) * HD].astype(F32)
            for j in range(STEPS):
                dot = jnp.sum(q * keys[j], 1, keepdims=True)
                scores[j] = jnp.where(lane == g, dot, scores[j])
        scores = [jnp.where(j <= step, scores[j], MASKED_SCORE) for j in range(STEPS)]
        end = slice(head + p * PAIR + GROUP * HD, head + (p + 1) * PAIR)
        stats = [ref[:, end].astype(F32) for ref in (pa_ref, pb_ref)]
        top = functools.reduce(jnp.maximum, scores + stats)
        fresh = [rounded(jnp.exp2((scores[j] - top) * EXPONENT)) for j in range(STEPS)]
        factors = [jnp.exp2(jnp.minimum(s - top, 0.0) * EXPONENT) for s in stats]
        denom = functools.reduce(jnp.add, fresh)
        for factor, s in zip(factors, stats):
            denom = denom + factor * totals(s)
        inverse = 1.0 / denom
        coefficients = [c * inverse for c in fresh + factors]
        for g in range(GROUP):
            at = slice(head + p * PAIR + g * HD, head + p * PAIR + (g + 1) * HD)
            terms = values + [ref[:, at].astype(F32) for ref in (pa_ref, pb_ref)]
            tile = jnp.zeros((16, 128), F32)
            for c, term in zip(coefficients, terms):
                tile = tile + broadcast_lane(c, g) * term
            out_ref[:, (p * GROUP + g) * HD : (p * GROUP + g + 1) * HD] = tile.astype(BF16)


def merge(paired, width_all, table, qrot, parts, backs, ups):
    operands = [table, qrot, *parts, *backs, *ups]
    pairs = qrot.shape[1] // (GROUP * HD)
    return pl.pallas_call(
        functools.partial(merge_kernel, len(backs), paired, width_all),
        in_specs=[VMEM] * len(operands),
        out_specs=VMEM,
        out_shape=jax.ShapeDtypeStruct((16, pairs * (GROUP + 2) * HD), BF16),
        compiler_params=pltpu.CompilerParams(vmem_limit_bytes=32 * MEBI),
        name="merge",
    )(*operands)


def place_kernel(mine_ref, theirs_ref, keys_out, values_out, out_ref):
    pairs = mine_ref.shape[1] // ((GROUP + 2) * HD)
    for c, ref in enumerate((mine_ref, theirs_ref)):
        for p in range(pairs):
            pair = pair_at(c * pairs + p)
            tiles = ref[:, p * GROUP * HD : (p + 1) * GROUP * HD].astype(F32)
            size = GROUP * HD
            for e in range(2):
                at = pl.ds(pl.multiple_of((2 * pair + e) * size, size), size)
                for s in range(2):
                    rows = slice(8 * e + 4 * s, 8 * e + 4 * s + 4)
                    out_ref[s, :, at] = tiles[rows].astype(BF16)
            start = pairs * GROUP * HD + p * 2 * HD
            fresh = ref[:, start : start + 2 * HD].astype(F32)
            at = pl.ds(pl.multiple_of(pair * 2 * HD, 2 * HD), 2 * HD)
            for i, out in enumerate((keys_out, values_out)):
                for s in range(2):
                    rows = slice(8 * i + 4 * s, 8 * i + 4 * s + 4)
                    out[s, :, at] = fresh[rows].astype(BF16)


def place(width, mine, theirs):
    return pl.pallas_call(
        place_kernel,
        in_specs=[VMEM] * 2,
        out_specs=[VMEM] * 3,
        out_shape=[
            jax.ShapeDtypeStruct((2, STEPS, width), BF16),
            jax.ShapeDtypeStruct((2, STEPS, width), BF16),
            jax.ShapeDtypeStruct((2, STEPS, GROUP * width), BF16),
        ],
        compiler_params=pltpu.CompilerParams(vmem_limit_bytes=32 * MEBI),
        name="place",
    )(mine, theirs)


def swap(value, axis, n, distance):
    return lax.ppermute(value, axis, [(i, i ^ distance) for i in range(n)])


def shards(
    n_dp,
    n_tensor,
    hidden,
    norm_gain,
    queries,
    key_weight,
    value_weight,
    key_down,
    key_up,
    value_down,
    value_up,
    key_cache,
    value_cache,
    lengths,
):
    depth, width = key_weight.shape
    rows = key_down.shape[0]
    to_dp = lambda value, distance: swap(value, "dp", n_dp, distance)
    to_tensor = lambda value, distance: swap(value, "tensor", n_tensor, distance)
    partners = range(2, n_dp, 2)
    n = len(partners)
    paired = n_dp == 4

    own, tokens = pack(lengths, hidden, norm_gain, key_down, value_down, key_up, value_up)
    near = to_dp(own, 1)
    sent = [to_dp(tokens, d) for d in partners]
    keep, send, base, qrot, table = local(
        tokens, queries, key_cache, value_cache, key_weight, value_weight
    )
    received = to_tensor(send, 1)
    columns = UP_COLUMNS if paired else 0
    message, *has = rank_products(rows, depth, columns, base, table, own, near, [tokens, *sent])
    if paired:
        ups = [has[0], to_dp(has[0], 1)]
    else:
        ups = lax.all_gather(tokens[:, depth // 2 + 256 :], "dp")
        ups = ups.reshape(n_dp, 16, -1, 128).transpose(0, 2, 1, 3)
        ups = ups.reshape(2, 2, 16, 16, 128).transpose(0, 1, 3, 2, 4).reshape(2, 2, 16, -1)
        ups = lax.dynamic_index_in_dim(ups, lax.axis_index("tensor") % 2, 0, keepdims=False)
        ups = [ups[0], ups[1]]
    cache = combine_cache(keep, received, message)
    part, *replies = combine_part(n, base, message, to_tensor(message, 1), cache)
    part_far = to_tensor(part, 2)
    places = [(s, t) for s in range(n_dp) for t in range(n_tensor)]
    backs = []
    for reply, d in zip(replies, partners):
        for e in (0, 2):
            perm = [(s * n_tensor + t, (s ^ d) * n_tensor + (t ^ e)) for s, t in places]
            backs.append(lax.ppermute(reply, ("dp", "tensor"), perm))
    merged = merge(
        paired,
        float(depth * n_tensor),
        table,
        qrot,
        (part, part_far),
        backs,
        ups,
    )
    return place(width, merged, to_tensor(merged, 1))


def solution(mesh):
    body = functools.partial(shards, mesh.shape["dp"], mesh.shape["tensor"])
    return jax.shard_map(
        body,
        mesh=mesh,
        in_specs=(
            P(("groups", "dp"), None, "tensor"),
            P("tensor"),
            P(("groups", "dp"), None, None),
            P("tensor", None),
            P("tensor", None),
            P(("groups", "dp"), "tensor"),
            P(("groups", "dp"), None),
            P(("groups", "dp"), "tensor"),
            P(("groups", "dp"), None),
            P(("groups", "dp"), "tensor", None),
            P(("groups", "dp"), "tensor", None),
            P(("groups", "dp")),
        ),
        out_specs=(
            P(("groups", "dp"), None, None),
            P(("groups", "dp"), None, None),
            P(("groups", "dp"), None, None),
        ),
        check_vma=False,
    )
```

```python
import functools
import math

import jax
import jax.numpy as jnp
from jax import lax
from jax.experimental import pallas as pl
from jax.experimental.pallas import tpu as pltpu
from jax.sharding import PartitionSpec as P

HD = 128
GROUP = 8
STEPS = 4
RANK = 64
EPSILON = 1e-05
ROPE_BASE = 500000.0
MASKED_SCORE = -1e30
LOWEST_TOP = -1e20
EXPONENT = math.log2(math.e) / math.sqrt(HD)
PAIR = GROUP * HD + 128
UP_COLUMNS = 3584
CHUNK = 512

F32 = jnp.float32
BF16 = jnp.bfloat16
NT = (((1,), (1,)), ((), ()))
VMEM = pl.BlockSpec(memory_space=pltpu.VMEM)
HBM = pl.BlockSpec(memory_space=pltpu.HBM)
MEBI = 2**20
WHOLE_VMEM = 65000 * 1024
LOCAL_VMEM = 54900 * 1024


def rounded(value):
    return value.astype(BF16).astype(F32)


def split(value):
    high = rounded(value)
    return jnp.concatenate([high, value - high], 0).astype(BF16)


def joined(tile):
    wide = tile.astype(F32)
    return wide[:8] + wide[8:]


def rotated(tile, cosine, sine):
    return tile * cosine + pltpu.roll(tile, HD // 2, 1) * sine


def first_rows(shape):
    return lax.broadcasted_iota(jnp.int32, shape, 0) % 8 < STEPS


def exchanged(a, b):
    first = first_rows(a.shape)
    return (
        jnp.where(first, a, pltpu.roll(b, STEPS, 0)),
        jnp.where(first, pltpu.roll(a, STEPS, 0), b),
    )


def flat(matrix):
    return jnp.concatenate([matrix[i : i + 16] for i in range(0, matrix.shape[0], 16)], 1)


def pack_kernel(*refs):
    sources, outs, held = refs[:7], refs[7:10], refs[10:17]
    (a_ref, b_ref, own_ref), sems, out_sems = refs[17:20], refs[20], refs[21]
    targets = [*outs[:2], outs[2].at[:, pl.ds(0, own_ref.shape[1])]]
    copies = [
        pltpu.make_async_copy(source, target, sems.at[i])
        for i, (source, target) in enumerate(zip(sources, held))
    ]
    for copy in copies:
        copy.start()
    backs = [
        pltpu.make_async_copy(source, target, out_sems.at[i])
        for i, (source, target) in enumerate(zip((a_ref, b_ref, own_ref), targets))
    ]
    kd_ref, vd_ref, x_ref, gain_ref, lengths_ref, ku_ref, vu_ref = held
    own, depth = kd_ref.shape
    for slot, ref in enumerate((kd_ref, vd_ref)):
        copies[slot].wait()
        down = ref[...]
        if own < 16:
            down = jnp.concatenate([down, jnp.zeros((16 - own, depth), F32)], 0)
        a_ref[:, slot * depth : (slot + 1) * depth] = down.astype(BF16)
    backs[0].start()
    for copy in copies[2:]:
        copy.wait()
    x = jnp.concatenate([x_ref[0].astype(F32), x_ref[1].astype(F32)], 0)
    gain = gain_ref[...].astype(F32)
    scaled = jnp.concatenate(
        [x[:, i * 128 : (i + 1) * 128] * gain[i : i + 1] for i in range(depth // 128)], 1
    )
    scaled = jnp.concatenate([scaled[:, : depth // 2], scaled[:, depth // 2 :]], 0).astype(BF16)
    b_ref[:, : depth // 2] = scaled
    ups = jnp.concatenate([ku_ref[...], vu_ref[...]], 0).T.astype(BF16)
    b_ref[:, depth // 2 :] = flat(ups)
    backs[1].start()
    own_ref[:, : depth // 2] = scaled
    row = lax.broadcasted_iota(jnp.int32, (16, 128), 0)
    lengths = lengths_ref[...]
    length = jnp.where(row % 8 < STEPS, lengths[:, :1], lengths[:, 1:])
    length = jnp.where(row < 8, length // 64 * 64, length % 64)
    own_ref[:, depth // 2 : depth // 2 + 128] = length.astype(F32).astype(BF16)
    squares = jnp.broadcast_to(jnp.sum(x * x, 1, keepdims=True), (8, 128))
    own_ref[:, depth // 2 + 128 :] = split(squares)
    backs[2].start()
    for copy in backs:
        copy.wait()


def pack(lengths, hidden, gain, key_down, value_down, key_up, value_up):
    operands = [key_down, value_down, hidden, gain.reshape(-1, 128), lengths.reshape(1, 2)]
    operands += [key_up.T, value_up.T]
    depth = hidden.shape[2]
    ups = key_up.shape[0] * 8
    outs = [
        jax.ShapeDtypeStruct((16, 2 * depth), BF16),
        jax.ShapeDtypeStruct((16, depth // 2 + ups), BF16),
        jax.ShapeDtypeStruct((16, depth // 2 + 256 + ups), BF16),
    ]
    scratch = [*operands, *outs[:2], jax.ShapeDtypeStruct((16, depth // 2 + 256), BF16)]
    return pl.pallas_call(
        pack_kernel,
        in_specs=[HBM] * len(operands),
        out_specs=[HBM] * len(outs),
        out_shape=outs,
        scratch_shapes=[pltpu.VMEM(o.shape, o.dtype) for o in scratch]
        + [pltpu.SemaphoreType.DMA((len(operands),)), pltpu.SemaphoreType.DMA((len(outs),))],
        compiler_params=pltpu.CompilerParams(vmem_limit_bytes=WHOLE_VMEM),
        name="pack",
    )(*operands)


def tables(length):
    shape = length.shape
    row = lax.broadcasted_iota(jnp.int32, shape, 0)
    lane = lax.broadcasted_iota(jnp.int32, shape, 1)
    position = length + (row % STEPS).astype(F32)
    pair = lane % (HD // 2)
    frequency = jnp.ones(shape, F32)
    for bit in range(6):
        factor = ROPE_BASE ** (-(2.0 * 2**bit) / HD)
        frequency = jnp.where((pair >> bit) & 1 == 1, frequency * factor, frequency)
    cosine, sine = cosine_and_sine(position * frequency)
    return cosine, jnp.where(lane < HD // 2, -sine, sine)


def cosine_and_sine(angle):
    turns = jnp.floor(angle * (2.0 / math.pi) + 0.5)
    rest = ((angle - turns * 1.5703125) - turns * 4.8351287841796875e-4) - turns * 3.1391647e-7
    square = rest * rest
    sine = -1.9515295891e-4 * square + 8.3321608736e-3
    sine = (sine * square - 1.6666654611e-1) * square * rest + rest
    cosine = 2.443315711809948e-5 * square - 1.388731625493765e-3
    cosine = (cosine * square + 4.166664568298827e-2) * square * square - 0.5 * square + 1.0
    quadrant = turns.astype(jnp.int32)
    swap_them = (quadrant & 1) == 1
    cosine, sine = jnp.where(swap_them, sine, cosine), jnp.where(swap_them, cosine, sine)
    cosine = jnp.where(((quadrant + 1) & 2) == 2, -cosine, cosine)
    sine = jnp.where((quadrant & 2) == 2, -sine, sine)
    return cosine, sine


def rotated_rows(pairs, cosine, sine, q_ref, qrot_ref):
    zero = jnp.zeros((32, HD), F32)
    result = []
    for p in pairs:
        halves = [[], []]
        for e in range(2):
            for g in range(GROUP):
                at = slice(((2 * p + e) * GROUP + g) * HD, ((2 * p + e) * GROUP + g + 1) * HD)
                q = jnp.concatenate([q_ref[0, :, at].astype(F32), q_ref[1, :, at].astype(F32)], 0)
                halves[e].append(rotated(q, cosine, sine))
        if qrot_ref is not None:
            for g in range(GROUP):
                at = slice((p * GROUP + g) * HD, (p * GROUP + g + 1) * HD)
                qrot_ref[:, at] = jnp.concatenate([halves[0][g], halves[1][g]], 0).astype(BF16)
        mixed = [[exchanged(halves[e][g], halves[e][g + 4]) for g in range(4)] for e in range(2)]
        for s in range(2):
            rows = [jnp.concatenate([mixed[e][g][s] for g in range(4)], 0) for e in range(2)]
            result.append(
                jnp.concatenate(
                    [jnp.concatenate([rows[0], zero], 1), jnp.concatenate([zero, rows[1]], 1)], 0
                ).astype(BF16)
            )
    return result


def attend(pairs, limit, queries, k_ref, v_ref, between, out_ref):
    scores = []
    for i, p in enumerate(pairs):
        for s in range(2):
            keys = k_ref[s, :, 2 * p * HD : 2 * (p + 1) * HD]
            score = lax.dot_general(queries[2 * i + s], keys, NT, preferred_element_type=F32)
            place = lax.broadcasted_iota(jnp.int32, score.shape, 1)
            bound = limit[STEPS * s : STEPS * s + 1, :1].astype(jnp.int32)
            scores.append(jnp.where(place < bound, score, MASKED_SCORE))
    between()
    scores = jnp.concatenate(scores, 0)
    top = rounded(jnp.maximum(jnp.max(scores, 1, keepdims=True), LOWEST_TOP))
    weights = jnp.exp2((scores - top) * EXPONENT).astype(BF16)
    total = jnp.sum(weights.astype(F32), 1, keepdims=True)
    high = rounded(total)
    columns = (top, high, total - high)
    lane8 = lax.broadcasted_iota(jnp.int32, (8, 128), 1)
    numers = []
    for i, p in enumerate(pairs):
        for s in range(2):
            at = slice(64 * (2 * i + s), 64 * (2 * i + s + 1))
            values = v_ref[s, :, 2 * p * HD : 2 * (p + 1) * HD]
            numers.append(jnp.dot(weights[at], values, preferred_element_type=F32))
    for i, p in enumerate(pairs):
        outs, ends = [[], []], []
        for e in range(2):
            back, stats = [], []
            for s in range(2):
                tile = jnp.zeros((8, 128), F32)
                for g in range(4):
                    row = 64 * (2 * i + s) + 32 * e + 8 * g
                    for slot, value in enumerate(columns):
                        tile = jnp.where(lane8 == slot * GROUP + g, value[row : row + 8], tile)
                stats.append(tile)
            for g in range(4):
                at = slice(32 * e + 8 * g, 32 * e + 8 * g + 8)
                cols = slice(e * HD, (e + 1) * HD)
                back.append(exchanged(numers[2 * i][at, cols], numers[2 * i + 1][at, cols]))
            outs[e] = [b[0] for b in back] + [b[1] for b in back]
            a, b = exchanged(*stats)
            ends.append(jnp.where(lane8 % 8 < 4, a, pltpu.roll(b, 4, 1)))
        for g in range(GROUP):
            at = slice(i * PAIR + g * HD, i * PAIR + (g + 1) * HD)
            out_ref[:, at] = jnp.concatenate([outs[0][g], outs[1][g]], 0).astype(BF16)
        out_ref[:, i * PAIR + GROUP * HD : (i + 1) * PAIR] = jnp.concatenate(ends, 0).astype(BF16)


def pair_at(i):
    return i ^ (lax.axis_index("tensor") % 2 * 2)


def local_kernel(
    x_hbm, q_hbm, k_hbm, v_hbm, wk_hbm, wv_hbm,
    keep_ref, send_ref, base_ref, qrot_ref, table_ref,
    x_ref, q_ref, k_ref, v_ref, wk_ref, wv_ref, x_sem, q_sem, cache_sem, weight_sem,
):
    pairs = k_hbm.shape[2] // (2 * HD)
    chunks = wk_hbm.shape[0] // CHUNK
    width = wk_hbm.shape[1]
    core = lax.axis_index("tensor") % 2
    x_copy = pltpu.make_async_copy(x_hbm.at[:, pl.ds(0, x_ref.shape[1])], x_ref, x_sem)
    x_copy.start()
    groups = []
    for h in range(2):
        copies = []
        trio = ((q_hbm, q_ref, q_sem.at[h]), (k_hbm, k_ref, cache_sem.at[h, 0]))
        for source, target, sem in (*trio, (v_hbm, v_ref, cache_sem.at[h, 1])):
            size = source.shape[2] // 2
            start = pl.multiple_of((core ^ h) * size, size)
            copies.append(
                pltpu.make_async_copy(
                    source.at[:, :, pl.ds(start, size)],
                    target.at[:, :, pl.ds(h * size, size)],
                    sem,
                )
            )
        groups.append(copies)
    for h in range(2):
        groups[h][0].start()
    for copy in groups[0][1:]:
        copy.start()
    weights = []
    for c in range(chunks):
        at = pl.ds(c * CHUNK, CHUNK)
        weights.append(
            [
                pltpu.make_async_copy(source.at[at], target.at[at], weight_sem.at[c, i])
                for i, (source, target) in enumerate(((wk_hbm, wk_ref), (wv_hbm, wv_ref)))
            ]
        )
    def start(copies):
        for copy in copies:
            copy.start()

    x_copy.wait()
    start(groups[1][1:])
    start(weights[0])
    half = wk_hbm.shape[0] // 2
    x = x_ref[:, :half].astype(F32)
    x = jnp.concatenate([x[:8], x[8:]], 1).astype(BF16)
    length = joined(x_ref[:, half : half + 128])
    cosine, sine = tables(length)
    table_ref[...] = jnp.concatenate([joined(x_ref[:, half + 128 : half + 256]), cosine, sine], 0)
    limit = length - (lax.axis_index("tensor") * k_hbm.shape[1]).astype(F32)
    queries = []
    for h in range(2):
        groups[h][0].wait()
        own = range(h * pairs // 2, (h + 1) * pairs // 2)
        queries.append(rotated_rows(own, cosine, sine, q_ref, None if h else qrot_ref))
    parts = []

    def project(chunk_ids):
        for c in chunk_ids:
            for copy in weights[c]:
                copy.wait()
        for c in chunk_ids:
            at = slice(c * CHUNK, (c + 1) * CHUNK)
            parts.append(
                jnp.concatenate(
                    [
                        jnp.dot(x[:, at], ref[at], preferred_element_type=F32)
                        for ref in (wk_ref, wv_ref)
                    ],
                    0,
                )
            )

    early = range(chunks // 2)

    def between(h):
        groups[h][2].wait()
        start(weights[chunks // 2 + h])
        if h:
            project(early)

    for h, out_ref in enumerate((keep_ref, send_ref)):
        groups[h][1].wait()
        if h == 0:
            for copies in weights[1 : chunks // 2]:
                start(copies)
        else:
            for copies in weights[chunks // 2 + 2 :]:
                start(copies)
        attend(
            range(h * pairs // 2, (h + 1) * pairs // 2),
            limit, queries[h], k_ref, v_ref, functools.partial(between, h), out_ref,
        )
    for c in range(chunks // 2, chunks):
        project([c])
    total = functools.reduce(jnp.add, parts)
    lower, upper = total[:, : width // 2], total[:, width // 2 :]
    base_ref[:, : width // 2] = jnp.where(core == 0, lower, upper)
    base_ref[:, width // 2 :] = jnp.where(core == 0, upper, lower)


def local(message, queries, key_cache, value_cache, key_weight, value_weight):
    seqs, length, width = key_cache.shape
    depth = key_weight.shape[0]
    pairs = width // (2 * HD)
    operands = [message, queries, key_cache, value_cache, key_weight, value_weight]
    return pl.pallas_call(
        local_kernel,
        in_specs=[HBM] * 6,
        out_specs=[VMEM] * 5,
        out_shape=[
            jax.ShapeDtypeStruct((16, pairs // 2 * PAIR), BF16),
            jax.ShapeDtypeStruct((16, pairs // 2 * PAIR), BF16),
            jax.ShapeDtypeStruct((16, width), F32),
            jax.ShapeDtypeStruct((16, pairs // 2 * GROUP * HD), BF16),
            jax.ShapeDtypeStruct((24, 128), F32),
        ],
        scratch_shapes=[pltpu.VMEM((16, depth // 2 + 256), BF16)]
        + [pltpu.VMEM(o.shape, BF16) for o in operands[1:]]
        + [
            pltpu.SemaphoreType.DMA,
            pltpu.SemaphoreType.DMA((2,)),
            pltpu.SemaphoreType.DMA((2, 2)),
            pltpu.SemaphoreType.DMA((depth // CHUNK, 2)),
        ],
        compiler_params=pltpu.CompilerParams(vmem_limit_bytes=LOCAL_VMEM),
        cost_estimate=pl.CostEstimate(
            flops=4 * 64 * 256 * seqs * length * pairs + 4 * 16 * depth * width,
            bytes_accessed=4 * seqs * length * width + 4 * depth * width,
            transcendentals=64 * seqs * length * pairs,
        ),
        name="local",
    )(*operands)


def rank_kernel(n, rows, depth, *refs):
    base_ref, table_ref, own_ref, near_ref = refs[:4]
    tokens, (out_ref, *has) = refs[4 : 4 + n], refs[4 + n :]
    half = base_ref.shape[1] // 2
    place = lax.axis_index("dp")
    x = []
    for ref in tokens:
        part = ref[:, : depth // 2].astype(F32)
        x.append(jnp.concatenate([part[:8], part[8:]], 1))
    x = jnp.concatenate(x, 0).astype(BF16)
    fill = jnp.zeros((RANK - 16, depth), BF16)
    z = None
    for ref, at in ((own_ref, place), (near_ref, place ^ 1)):
        down = jnp.concatenate([ref[:, :depth], fill, ref[:, depth:], fill], 0)
        part = lax.dot_general(x, down, NT, preferred_element_type=F32)
        part = pltpu.roll(part, at * rows, 1)
        z = part if z is None else z + part
    out_ref[:, :half] = base_ref[:, half:].astype(BF16)
    out_ref[:, half : half + 128] = split(table_ref[:8])
    for i in range(n):
        at = half + 128 * (i + 1)
        out_ref[:, at : at + 128] = split(z[8 * i : 8 * i + 8])
    for ref in has:
        here = place // 2 == lax.axis_index("tensor") % 2
        mine, far = (token[:, depth // 2 :].astype(F32) for token in tokens[:2])
        ref[:, : mine.shape[1]] = jnp.where(here, mine, far).astype(BF16)
        ref[:, mine.shape[1] :] = jnp.zeros((16, ref.shape[1] - mine.shape[1]), BF16)


def rank_products(rows, depth, columns, base, table, own, near, tokens):
    n = len(tokens)
    out_shape = [jax.ShapeDtypeStruct((16, base.shape[1] // 2 + 128 * (n + 1)), BF16)]
    if columns:
        out_shape.append(jax.ShapeDtypeStruct((16, columns), BF16))
    return pl.pallas_call(
        functools.partial(rank_kernel, n, rows, depth),
        in_specs=[VMEM] * (4 + n),
        out_specs=[VMEM] * len(out_shape),
        out_shape=out_shape,
        compiler_params=pltpu.CompilerParams(vmem_limit_bytes=32 * MEBI),
        name="rank_products",
    )(base, table, own, near, *tokens)


def broadcast_lane(tile, lane):
    return jnp.broadcast_to(tile[:, lane : lane + 1], tile.shape)


def combine_part_kernel(base_ref, mine_ref, theirs_ref, cache_ref, out_ref, *replies):
    half = base_ref.shape[1] // 2
    own = base_ref[:, :half] + theirs_ref[:, :half].astype(F32)
    out_ref[:, :half] = own.astype(BF16)
    sums = mine_ref[:, half:].astype(F32) + theirs_ref[:, half:].astype(F32)
    sums = split(sums[:8] + sums[8:])
    out_ref[:, half : half + 256] = sums[:, :256]
    out_ref[:, half + 256 :] = cache_ref[...]
    for i, ref in enumerate(replies):
        ref[...] = sums[:, 128 * (i + 2) : 128 * (i + 3)]


def combine_part(n, base, mine, theirs, cache):
    shapes = [(16, base.shape[1] // 2 + 256 + cache.shape[1])] + [(16, 128)] * n
    return pl.pallas_call(
        combine_part_kernel,
        in_specs=[VMEM] * 4,
        out_specs=[VMEM] * len(shapes),
        out_shape=[jax.ShapeDtypeStruct(shape, BF16) for shape in shapes],
        compiler_params=pltpu.CompilerParams(vmem_limit_bytes=32 * MEBI),
        name="combine_part",
    )(base, mine, theirs, cache)


def combine_cache_kernel(a_ref, b_ref, _, out_ref):
    lane = lax.broadcasted_iota(jnp.int32, (16, 128), 1)
    for p in range(out_ref.shape[1] // PAIR):
        end = slice(p * PAIR + GROUP * HD, (p + 1) * PAIR)
        a, b = a_ref[:, end].astype(F32), b_ref[:, end].astype(F32)
        top = jnp.maximum(a, b)
        fa = jnp.exp2(jnp.minimum(a - top, 0.0) * EXPONENT)
        fb = jnp.exp2(jnp.minimum(b - top, 0.0) * EXPONENT)
        total = fa * totals(a) + fb * totals(b)
        high = rounded(total)
        stats = jnp.where(lane < GROUP, top, 0.0)
        stats = jnp.where(lane // GROUP == 1, pltpu.roll(high, GROUP, 1), stats)
        stats = jnp.where(lane // GROUP == 2, pltpu.roll(total - high, 2 * GROUP, 1), stats)
        out_ref[:, end] = stats.astype(BF16)
        for g in range(GROUP):
            at = slice(p * PAIR + g * HD, p * PAIR + (g + 1) * HD)
            out_ref[:, at] = (
                broadcast_lane(fa, g) * a_ref[:, at].astype(F32)
                + broadcast_lane(fb, g) * b_ref[:, at].astype(F32)
            ).astype(BF16)


def totals(stats):
    return pltpu.roll(stats, 128 - GROUP, 1) + pltpu.roll(stats, 128 - 2 * GROUP, 1)


def combine_cache(a, b, earlier):
    return pl.pallas_call(
        combine_cache_kernel,
        in_specs=[VMEM] * 3,
        out_specs=VMEM,
        out_shape=jax.ShapeDtypeStruct(a.shape, BF16),
        compiler_params=pltpu.CompilerParams(vmem_limit_bytes=32 * MEBI),
        name="combine_cache",
    )(a, b, earlier)


def merge_kernel(n, paired, width_all, *refs):
    table_ref, qrot_ref, pa_ref, pb_ref = refs[:4]
    backs, (ua_ref, ub_ref, out_ref) = refs[4 : 4 + n], refs[4 + n :]
    pairs = qrot_ref.shape[1] // (GROUP * HD)
    width = pairs * 2 * HD
    cosine, sine = table_ref[8:16], table_ref[16:]
    head = width + 256
    sums = pa_ref[:, :head].astype(F32) + pb_ref[:, :head].astype(F32)
    tail = sums[:8, width : width + 256] + sums[8:, width : width + 256]
    squares, z = tail[:, :128], tail[:, 128:]
    for ref in backs:
        z = z + joined(ref[...])
    lane8 = lax.broadcasted_iota(jnp.int32, (8, 128), 1)
    z = jnp.concatenate(
        [jnp.where(lane8 < RANK, z, 0.0), jnp.where(lane8 < RANK, 0.0, z)], 0
    ).astype(BF16)
    adapted = []
    for ref in (ua_ref, ub_ref):
        ups = jnp.concatenate([ref[:, i : i + 128] for i in range(0, 16 * HD, 128)], 0)
        adapted.append(lax.dot_general(z, ups, NT, preferred_element_type=F32))
    if paired:
        even = lax.axis_index("dp") % 2 == 0
        a, b = adapted
        adapted = [jnp.where(even, a, b), jnp.where(even, b, a)]
    total = sums[:, :width] + jnp.concatenate(adapted, 1)
    scale = lax.rsqrt(squares / width_all + EPSILON)
    lane = lax.broadcasted_iota(jnp.int32, (16, 128), 1)
    step = lax.broadcasted_iota(jnp.int32, (16, 128), 0) % STEPS
    first = first_rows((8, 128))

    def of_step(tiles, j):
        return jnp.concatenate(
            [
                jnp.where(first, tile[j : j + 1], tile[STEPS + j : STEPS + j + 1])
                for tile in tiles
            ],
            0,
        )

    for p in range(pairs):
        new_keys, new_values = [], []
        for e in range(2):
            at = slice((2 * p + e) * HD, (2 * p + e + 1) * HD)
            new_keys.append(rounded(rotated(total[:8, at] * scale, cosine, sine)))
            new_values.append(rounded(total[8:, at] * scale))
            fresh = jnp.concatenate([new_keys[e], new_values[e]], 0)
            start = pairs * GROUP * HD + (2 * p + e) * HD
            out_ref[:, start : start + HD] = fresh.astype(BF16)
        keys = [of_step(new_keys, j) for j in range(STEPS)]
        values = [of_step(new_values, j) for j in range(STEPS)]
        scores = [jnp.zeros((16, 128), F32) for _ in range(STEPS)]
        for g in range(GROUP):
            q = qrot_ref[:, (p * GROUP + g) * HD : (p * GROUP + g + 1) * HD].astype(F32)
            for j in range(STEPS):
                dot = jnp.sum(q * keys[j], 1, keepdims=True)
                scores[j] = jnp.where(lane == g, dot, scores[j])
        scores = [jnp.where(j <= step, scores[j], MASKED_SCORE) for j in range(STEPS)]
        end = slice(head + p * PAIR + GROUP * HD, head + (p + 1) * PAIR)
        stats = [ref[:, end].astype(F32) for ref in (pa_ref, pb_ref)]
        top = functools.reduce(jnp.maximum, scores + stats)
        fresh = [rounded(jnp.exp2((scores[j] - top) * EXPONENT)) for j in range(STEPS)]
        factors = [jnp.exp2(jnp.minimum(s - top, 0.0) * EXPONENT) for s in stats]
        denom = functools.reduce(jnp.add, fresh)
        for factor, s in zip(factors, stats):
            denom = denom + factor * totals(s)
        inverse = 1.0 / denom
        coefficients = [c * inverse for c in fresh + factors]
        for g in range(GROUP):
            at = slice(head + p * PAIR + g * HD, head + p * PAIR + (g + 1) * HD)
            terms = values + [ref[:, at].astype(F32) for ref in (pa_ref, pb_ref)]
            tile = jnp.zeros((16, 128), F32)
            for c, term in zip(coefficients, terms):
                tile = tile + broadcast_lane(c, g) * term
            out_ref[:, (p * GROUP + g) * HD : (p * GROUP + g + 1) * HD] = tile.astype(BF16)


def merge(paired, width_all, table, qrot, parts, backs, ups):
    operands = [table, qrot, *parts, *backs, *ups]
    pairs = qrot.shape[1] // (GROUP * HD)
    return pl.pallas_call(
        functools.partial(merge_kernel, len(backs), paired, width_all),
        in_specs=[VMEM] * len(operands),
        out_specs=VMEM,
        out_shape=jax.ShapeDtypeStruct((16, pairs * (GROUP + 2) * HD), BF16),
        compiler_params=pltpu.CompilerParams(vmem_limit_bytes=32 * MEBI),
        name="merge",
    )(*operands)


def place_kernel(mine_ref, theirs_ref, keys_out, values_out, out_ref):
    pairs = mine_ref.shape[1] // ((GROUP + 2) * HD)
    for c, ref in enumerate((mine_ref, theirs_ref)):
        for p in range(pairs):
            pair = pair_at(c * pairs + p)
            tiles = ref[:, p * GROUP * HD : (p + 1) * GROUP * HD].astype(F32)
            size = GROUP * HD
            for e in range(2):
                at = pl.ds(pl.multiple_of((2 * pair + e) * size, size), size)
                for s in range(2):
                    rows = slice(8 * e + 4 * s, 8 * e + 4 * s + 4)
                    out_ref[s, :, at] = tiles[rows].astype(BF16)
            start = pairs * GROUP * HD + p * 2 * HD
            fresh = ref[:, start : start + 2 * HD].astype(F32)
            at = pl.ds(pl.multiple_of(pair * 2 * HD, 2 * HD), 2 * HD)
            for i, out in enumerate((keys_out, values_out)):
                for s in range(2):
                    rows = slice(8 * i + 4 * s, 8 * i + 4 * s + 4)
                    out[s, :, at] = fresh[rows].astype(BF16)


def place(width, mine, theirs):
    return pl.pallas_call(
        place_kernel,
        in_specs=[VMEM] * 2,
        out_specs=[VMEM] * 3,
        out_shape=[
            jax.ShapeDtypeStruct((2, STEPS, width), BF16),
            jax.ShapeDtypeStruct((2, STEPS, width), BF16),
            jax.ShapeDtypeStruct((2, STEPS, GROUP * width), BF16),
        ],
        compiler_params=pltpu.CompilerParams(vmem_limit_bytes=32 * MEBI),
        name="place",
    )(mine, theirs)


def swap(value, axis, n, distance):
    return lax.ppermute(value, axis, [(i, i ^ distance) for i in range(n)])


def shards(
    n_dp,
    n_tensor,
    hidden,
    norm_gain,
    queries,
    key_weight,
    value_weight,
    key_down,
    key_up,
    value_down,
    value_up,
    key_cache,
    value_cache,
    lengths,
):
    depth, width = key_weight.shape
    rows = key_down.shape[0]
    to_dp = lambda value, distance: swap(value, "dp", n_dp, distance)
    to_tensor = lambda value, distance: swap(value, "tensor", n_tensor, distance)
    partners = range(2, n_dp, 2)
    n = len(partners)
    paired = n_dp == 4

    down, tokens, own = pack(
        lengths, hidden, norm_gain, key_down, value_down, key_up, value_up
    )
    near = to_dp(down, 1)
    sent = [to_dp(tokens, d) for d in partners]
    keep, send, base, qrot, table = local(
        own, queries, key_cache, value_cache, key_weight, value_weight
    )
    received = to_tensor(send, 1)
    columns = UP_COLUMNS if paired else 0
    message, *has = rank_products(rows, depth, columns, base, table, down, near, [tokens, *sent])
    if paired:
        ups = [has[0], to_dp(has[0], 1)]
    else:
        ups = lax.all_gather(tokens[:, depth // 2 :], "dp")
        ups = ups.reshape(n_dp, 16, -1, 128).transpose(0, 2, 1, 3)
        ups = ups.reshape(2, 2, 16, 16, 128).transpose(0, 1, 3, 2, 4).reshape(2, 2, 16, -1)
        ups = lax.dynamic_index_in_dim(ups, lax.axis_index("tensor") % 2, 0, keepdims=False)
        ups = [ups[0], ups[1]]
    cache = combine_cache(keep, received, message)
    part, *replies = combine_part(n, base, message, to_tensor(message, 1), cache)
    part_far = to_tensor(part, 2)
    places = [(s, t) for s in range(n_dp) for t in range(n_tensor)]
    backs = []
    for reply, d in zip(replies, partners):
        for e in (0, 2):
            perm = [(s * n_tensor + t, (s ^ d) * n_tensor + (t ^ e)) for s, t in places]
            backs.append(lax.ppermute(reply, ("dp", "tensor"), perm))
    merged = merge(
        paired,
        float(depth * n_tensor),
        table,
        qrot,
        (part, part_far),
        backs,
        ups,
    )
    return place(width, merged, to_tensor(merged, 1))


def solution(mesh):
    body = functools.partial(shards, mesh.shape["dp"], mesh.shape["tensor"])
    return jax.shard_map(
        body,
        mesh=mesh,
        in_specs=(
            P(("groups", "dp"), None, "tensor"),
            P("tensor"),
            P(("groups", "dp"), None, None),
            P("tensor", None),
            P("tensor", None),
            P(("groups", "dp"), "tensor"),
            P(("groups", "dp"), None),
            P(("groups", "dp"), "tensor"),
            P(("groups", "dp"), None),
            P(("groups", "dp"), "tensor", None),
            P(("groups", "dp"), "tensor", None),
            P(("groups", "dp")),
        ),
        out_specs=(
            P(("groups", "dp"), None, None),
            P(("groups", "dp"), None, None),
            P(("groups", "dp"), None, None),
        ),
        check_vma=False,
    )
```

```python
import functools
import math

import jax
import jax.numpy as jnp
from jax import lax
from jax.experimental import pallas as pl
from jax.experimental.pallas import tpu as pltpu
from jax.sharding import PartitionSpec as P

HD = 128
GROUP = 8
STEPS = 4
RANK = 64
EPSILON = 1e-05
ROPE_BASE = 500000.0
MASKED_SCORE = -1e30
LOWEST_TOP = -1e20
EXPONENT = math.log2(math.e) / math.sqrt(HD)
PAIR = GROUP * HD + 128
UP_COLUMNS = 3584
CHUNK = 512

F32 = jnp.float32
BF16 = jnp.bfloat16
NT = (((1,), (1,)), ((), ()))
VMEM = pl.BlockSpec(memory_space=pltpu.VMEM)
HBM = pl.BlockSpec(memory_space=pltpu.HBM)
MEBI = 2**20
WHOLE_VMEM = 65000 * 1024
LOCAL_VMEM = 54900 * 1024


def rounded(value):
    return value.astype(BF16).astype(F32)


def split(value):
    high = rounded(value)
    return jnp.concatenate([high, value - high], 0).astype(BF16)


def joined(tile):
    wide = tile.astype(F32)
    return wide[:8] + wide[8:]


def rotated(tile, cosine, sine):
    return tile * cosine + pltpu.roll(tile, HD // 2, 1) * sine


def first_rows(shape):
    return lax.broadcasted_iota(jnp.int32, shape, 0) % 8 < STEPS


def exchanged(a, b):
    first = first_rows(a.shape)
    return (
        jnp.where(first, a, pltpu.roll(b, STEPS, 0)),
        jnp.where(first, pltpu.roll(a, STEPS, 0), b),
    )


def flat(matrix):
    return jnp.concatenate([matrix[i : i + 16] for i in range(0, matrix.shape[0], 16)], 1)


def pack_kernel(*refs):
    sources, outs, held = refs[:7], refs[7:10], refs[10:17]
    (a_ref, b_ref, own_ref), sems, out_sems = refs[17:20], refs[20], refs[21]
    targets = [*outs[:2], outs[2].at[:, pl.ds(0, own_ref.shape[1])]]
    copies = [
        pltpu.make_async_copy(source, target, sems.at[i])
        for i, (source, target) in enumerate(zip(sources, held))
    ]
    for copy in copies:
        copy.start()
    backs = [
        pltpu.make_async_copy(source, target, out_sems.at[i])
        for i, (source, target) in enumerate(zip((a_ref, b_ref, own_ref), targets))
    ]
    kd_ref, vd_ref, x_ref, gain_ref, lengths_ref, ku_ref, vu_ref = held
    own, depth = kd_ref.shape
    for slot, ref in enumerate((kd_ref, vd_ref)):
        copies[slot].wait()
        down = ref[...]
        if own < 16:
            down = jnp.concatenate([down, jnp.zeros((16 - own, depth), F32)], 0)
        a_ref[:, slot * depth : (slot + 1) * depth] = down.astype(BF16)
    backs[0].start()
    for copy in copies[2:]:
        copy.wait()
    x = jnp.concatenate([x_ref[0].astype(F32), x_ref[1].astype(F32)], 0)
    gain = gain_ref[...].astype(F32)
    scaled = jnp.concatenate(
        [x[:, i * 128 : (i + 1) * 128] * gain[i : i + 1] for i in range(depth // 128)], 1
    )
    scaled = jnp.concatenate([scaled[:, : depth // 2], scaled[:, depth // 2 :]], 0).astype(BF16)
    b_ref[:, : depth // 2] = scaled
    ups = jnp.concatenate([ku_ref[...], vu_ref[...]], 0).T.astype(BF16)
    b_ref[:, depth // 2 :] = flat(ups)
    backs[1].start()
    own_ref[:, : depth // 2] = scaled
    row = lax.broadcasted_iota(jnp.int32, (16, 128), 0)
    lengths = lengths_ref[...]
    length = jnp.where(row % 8 < STEPS, lengths[:, :1], lengths[:, 1:])
    length = jnp.where(row < 8, length // 64 * 64, length % 64)
    own_ref[:, depth // 2 : depth // 2 + 128] = length.astype(F32).astype(BF16)
    squares = jnp.broadcast_to(jnp.sum(x * x, 1, keepdims=True), (8, 128))
    own_ref[:, depth // 2 + 128 :] = split(squares)
    backs[2].start()
    for copy in backs:
        copy.wait()


def pack(lengths, hidden, gain, key_down, value_down, key_up, value_up):
    operands = [key_down, value_down, hidden, gain.reshape(-1, 128), lengths.reshape(1, 2)]
    operands += [key_up.T, value_up.T]
    depth = hidden.shape[2]
    ups = key_up.shape[0] * 8
    outs = [
        jax.ShapeDtypeStruct((16, 2 * depth), BF16),
        jax.ShapeDtypeStruct((16, depth // 2 + ups), BF16),
        jax.ShapeDtypeStruct((16, depth // 2 + 256 + ups), BF16),
    ]
    scratch = [*operands, *outs[:2], jax.ShapeDtypeStruct((16, depth // 2 + 256), BF16)]
    return pl.pallas_call(
        pack_kernel,
        in_specs=[HBM] * len(operands),
        out_specs=[HBM] * len(outs),
        out_shape=outs,
        scratch_shapes=[pltpu.VMEM(o.shape, o.dtype) for o in scratch]
        + [pltpu.SemaphoreType.DMA((len(operands),)), pltpu.SemaphoreType.DMA((len(outs),))],
        compiler_params=pltpu.CompilerParams(vmem_limit_bytes=WHOLE_VMEM),
        name="pack",
    )(*operands)


def tables(length):
    shape = length.shape
    row = lax.broadcasted_iota(jnp.int32, shape, 0)
    lane = lax.broadcasted_iota(jnp.int32, shape, 1)
    position = length + (row % STEPS).astype(F32)
    pair = lane % (HD // 2)
    frequency = jnp.ones(shape, F32)
    for bit in range(6):
        factor = ROPE_BASE ** (-(2.0 * 2**bit) / HD)
        frequency = jnp.where((pair >> bit) & 1 == 1, frequency * factor, frequency)
    cosine, sine = cosine_and_sine(position * frequency)
    return cosine, jnp.where(lane < HD // 2, -sine, sine)


def cosine_and_sine(angle):
    turns = jnp.floor(angle * (2.0 / math.pi) + 0.5)
    rest = ((angle - turns * 1.5703125) - turns * 4.8351287841796875e-4) - turns * 3.1391647e-7
    square = rest * rest
    sine = -1.9515295891e-4 * square + 8.3321608736e-3
    sine = (sine * square - 1.6666654611e-1) * square * rest + rest
    cosine = 2.443315711809948e-5 * square - 1.388731625493765e-3
    cosine = (cosine * square + 4.166664568298827e-2) * square * square - 0.5 * square + 1.0
    quadrant = turns.astype(jnp.int32)
    swap_them = (quadrant & 1) == 1
    cosine, sine = jnp.where(swap_them, sine, cosine), jnp.where(swap_them, cosine, sine)
    cosine = jnp.where(((quadrant + 1) & 2) == 2, -cosine, cosine)
    sine = jnp.where((quadrant & 2) == 2, -sine, sine)
    return cosine, sine


def rotated_rows(pairs, cosine, sine, q_ref, qrot_ref):
    zero = jnp.zeros((32, HD), F32)
    result = []
    for p in pairs:
        halves = [[], []]
        for e in range(2):
            for g in range(GROUP):
                at = slice(((2 * p + e) * GROUP + g) * HD, ((2 * p + e) * GROUP + g + 1) * HD)
                q = jnp.concatenate([q_ref[0, :, at].astype(F32), q_ref[1, :, at].astype(F32)], 0)
                halves[e].append(rotated(q, cosine, sine))
        if qrot_ref is not None:
            for g in range(GROUP):
                at = slice((p * GROUP + g) * HD, (p * GROUP + g + 1) * HD)
                qrot_ref[:, at] = jnp.concatenate([halves[0][g], halves[1][g]], 0).astype(BF16)
        mixed = [[exchanged(halves[e][g], halves[e][g + 4]) for g in range(4)] for e in range(2)]
        for s in range(2):
            rows = [jnp.concatenate([mixed[e][g][s] for g in range(4)], 0) for e in range(2)]
            result.append(
                jnp.concatenate(
                    [jnp.concatenate([rows[0], zero], 1), jnp.concatenate([zero, rows[1]], 1)], 0
                ).astype(BF16)
            )
    return result


def attend(pairs, masks, queries, k_ref, v_ref, between, out_ref):
    scores = []
    for i, p in enumerate(pairs):
        for s in range(2):
            keys = k_ref[s, :, 2 * p * HD : 2 * (p + 1) * HD]
            score = lax.dot_general(queries[2 * i + s], keys, NT, preferred_element_type=F32)
            scores.append(score + jnp.concatenate([masks[s]] * (score.shape[0] // 8), 0))
    between()
    scores = jnp.concatenate(scores, 0)
    top = rounded(jnp.maximum(jnp.max(scores, 1, keepdims=True), LOWEST_TOP))
    weights = jnp.exp2((scores - top) * EXPONENT).astype(BF16)
    total = jnp.sum(weights.astype(F32), 1, keepdims=True)
    high = rounded(total)
    columns = (top, high, total - high)
    lane8 = lax.broadcasted_iota(jnp.int32, (8, 128), 1)
    numers = []
    for i, p in enumerate(pairs):
        for s in range(2):
            at = slice(64 * (2 * i + s), 64 * (2 * i + s + 1))
            values = v_ref[s, :, 2 * p * HD : 2 * (p + 1) * HD]
            numers.append(jnp.dot(weights[at], values, preferred_element_type=F32))
    for i, p in enumerate(pairs):
        outs, ends = [[], []], []
        for e in range(2):
            back, stats = [], []
            for s in range(2):
                tile = jnp.zeros((8, 128), F32)
                for g in range(4):
                    row = 64 * (2 * i + s) + 32 * e + 8 * g
                    for slot, value in enumerate(columns):
                        tile = jnp.where(lane8 == slot * GROUP + g, value[row : row + 8], tile)
                stats.append(tile)
            for g in range(4):
                at = slice(32 * e + 8 * g, 32 * e + 8 * g + 8)
                cols = slice(e * HD, (e + 1) * HD)
                back.append(exchanged(numers[2 * i][at, cols], numers[2 * i + 1][at, cols]))
            outs[e] = [b[0] for b in back] + [b[1] for b in back]
            a, b = exchanged(*stats)
            ends.append(jnp.where(lane8 % 8 < 4, a, pltpu.roll(b, 4, 1)))
        for g in range(GROUP):
            at = slice(i * PAIR + g * HD, i * PAIR + (g + 1) * HD)
            out_ref[:, at] = jnp.concatenate([outs[0][g], outs[1][g]], 0).astype(BF16)
        out_ref[:, i * PAIR + GROUP * HD : (i + 1) * PAIR] = jnp.concatenate(ends, 0).astype(BF16)


def pair_at(i):
    return i ^ (lax.axis_index("tensor") % 2 * 2)


def local_kernel(
    x_hbm, q_hbm, k_hbm, v_hbm, wk_hbm, wv_hbm,
    keep_ref, send_ref, base_ref, qrot_ref, table_ref,
    x_ref, q_ref, k_ref, v_ref, wk_ref, wv_ref, x_sem, q_sem, cache_sem, weight_sem,
):
    pairs = k_hbm.shape[2] // (2 * HD)
    chunks = wk_hbm.shape[0] // CHUNK
    width = wk_hbm.shape[1]
    core = lax.axis_index("tensor") % 2
    x_copy = pltpu.make_async_copy(x_hbm.at[:, pl.ds(0, x_ref.shape[1])], x_ref, x_sem)
    x_copy.start()
    groups = []
    for h in range(2):
        copies = []
        trio = ((q_hbm, q_ref, q_sem.at[h]), (k_hbm, k_ref, cache_sem.at[h, 0]))
        for source, target, sem in (*trio, (v_hbm, v_ref, cache_sem.at[h, 1])):
            size = source.shape[2] // 2
            start = pl.multiple_of((core ^ h) * size, size)
            copies.append(
                pltpu.make_async_copy(
                    source.at[:, :, pl.ds(start, size)],
                    target.at[:, :, pl.ds(h * size, size)],
                    sem,
                )
            )
        groups.append(copies)
    for h in range(2):
        groups[h][0].start()
    for copy in groups[0][1:]:
        copy.start()
    weights = []
    for c in range(chunks):
        at = pl.ds(c * CHUNK, CHUNK)
        weights.append(
            [
                pltpu.make_async_copy(source.at[at], target.at[at], weight_sem.at[c, i])
                for i, (source, target) in enumerate(((wk_hbm, wk_ref), (wv_hbm, wv_ref)))
            ]
        )
    def start(copies):
        for copy in copies:
            copy.start()

    x_copy.wait()
    start(groups[1][1:])
    start(weights[0])
    half = wk_hbm.shape[0] // 2
    x = x_ref[:, :half].astype(F32)
    x = jnp.concatenate([x[:8], x[8:]], 1).astype(BF16)
    length = joined(x_ref[:, half : half + 128])
    cosine, sine = tables(length)
    table_ref[...] = jnp.concatenate([joined(x_ref[:, half + 128 : half + 256]), cosine, sine], 0)
    limit = length - (lax.axis_index("tensor") * k_hbm.shape[1]).astype(F32)
    place = lax.broadcasted_iota(jnp.int32, (8, k_hbm.shape[1]), 1).astype(F32)
    masks = [
        jnp.where(place < limit[STEPS * s : STEPS * s + 1, :1], 0.0, MASKED_SCORE) for s in range(2)
    ]
    queries = []
    for h in range(2):
        groups[h][0].wait()
        own = range(h * pairs // 2, (h + 1) * pairs // 2)
        queries.append(rotated_rows(own, cosine, sine, q_ref, None if h else qrot_ref))
    parts = []

    def project(c):
        at = slice(c * CHUNK, (c + 1) * CHUNK)
        halves = []
        for copy, ref in zip(weights[c], (wk_ref, wv_ref)):
            copy.wait()
            halves.append(jnp.dot(x[:, at], ref[at], preferred_element_type=F32))
        parts.append(jnp.concatenate(halves, 0))

    def between(h):
        groups[h][2].wait()
        if h == 0:
            start(weights[chunks // 2])
        else:
            for c in range(chunks // 2):
                project(c)

    for h, out_ref in enumerate((keep_ref, send_ref)):
        groups[h][1].wait()
        for copies in weights[chunks // 2 + 1 :] if h else weights[1 : chunks // 2]:
            start(copies)
        attend(
            range(h * pairs // 2, (h + 1) * pairs // 2),
            masks, queries[h], k_ref, v_ref, functools.partial(between, h), out_ref,
        )
    for c in range(chunks // 2, chunks):
        project(c)
    total = functools.reduce(jnp.add, parts)
    lower, upper = total[:, : width // 2], total[:, width // 2 :]
    base_ref[:, : width // 2] = jnp.where(core == 0, lower, upper)
    base_ref[:, width // 2 :] = jnp.where(core == 0, upper, lower)


def local(message, queries, key_cache, value_cache, key_weight, value_weight):
    seqs, length, width = key_cache.shape
    depth = key_weight.shape[0]
    pairs = width // (2 * HD)
    operands = [message, queries, key_cache, value_cache, key_weight, value_weight]
    return pl.pallas_call(
        local_kernel,
        in_specs=[HBM] * 6,
        out_specs=[VMEM] * 5,
        out_shape=[
            jax.ShapeDtypeStruct((16, pairs // 2 * PAIR), BF16),
            jax.ShapeDtypeStruct((16, pairs // 2 * PAIR), BF16),
            jax.ShapeDtypeStruct((16, width), F32),
            jax.ShapeDtypeStruct((16, pairs // 2 * GROUP * HD), BF16),
            jax.ShapeDtypeStruct((24, 128), F32),
        ],
        scratch_shapes=[pltpu.VMEM((16, depth // 2 + 256), BF16)]
        + [pltpu.VMEM(o.shape, BF16) for o in operands[1:]]
        + [
            pltpu.SemaphoreType.DMA,
            pltpu.SemaphoreType.DMA((2,)),
            pltpu.SemaphoreType.DMA((2, 2)),
            pltpu.SemaphoreType.DMA((depth // CHUNK, 2)),
        ],
        compiler_params=pltpu.CompilerParams(vmem_limit_bytes=LOCAL_VMEM),
        cost_estimate=pl.CostEstimate(
            flops=4 * 64 * 256 * seqs * length * pairs + 4 * 16 * depth * width,
            bytes_accessed=4 * seqs * length * width + 4 * depth * width,
            transcendentals=64 * seqs * length * pairs,
        ),
        name="local",
    )(*operands)


def rank_kernel(n, rows, depth, *refs):
    base_ref, table_ref, own_ref, near_ref = refs[:4]
    tokens, (out_ref, *has) = refs[4 : 4 + n], refs[4 + n :]
    half = base_ref.shape[1] // 2
    place = lax.axis_index("dp")
    x = []
    for ref in tokens:
        part = ref[:, : depth // 2].astype(F32)
        x.append(jnp.concatenate([part[:8], part[8:]], 1))
    x = jnp.concatenate(x, 0).astype(BF16)
    fill = jnp.zeros((RANK - 16, depth), BF16)
    z = None
    for ref, at in ((own_ref, place), (near_ref, place ^ 1)):
        down = jnp.concatenate([ref[:, :depth], fill, ref[:, depth:], fill], 0)
        part = lax.dot_general(x, down, NT, preferred_element_type=F32)
        part = pltpu.roll(part, at * rows, 1)
        z = part if z is None else z + part
    out_ref[:, :half] = base_ref[:, half:].astype(BF16)
    out_ref[:, half : half + 128] = split(table_ref[:8])
    for i in range(n):
        at = half + 128 * (i + 1)
        out_ref[:, at : at + 128] = split(z[8 * i : 8 * i + 8])
    for ref in has:
        here = place // 2 == lax.axis_index("tensor") % 2
        mine, far = (token[:, depth // 2 :].astype(F32) for token in tokens[:2])
        ref[:, : mine.shape[1]] = jnp.where(here, mine, far).astype(BF16)
        ref[:, mine.shape[1] :] = jnp.zeros((16, ref.shape[1] - mine.shape[1]), BF16)


def rank_products(rows, depth, columns, base, table, own, near, tokens):
    n = len(tokens)
    out_shape = [jax.ShapeDtypeStruct((16, base.shape[1] // 2 + 128 * (n + 1)), BF16)]
    if columns:
        out_shape.append(jax.ShapeDtypeStruct((16, columns), BF16))
    return pl.pallas_call(
        functools.partial(rank_kernel, n, rows, depth),
        in_specs=[VMEM] * (4 + n),
        out_specs=[VMEM] * len(out_shape),
        out_shape=out_shape,
        compiler_params=pltpu.CompilerParams(vmem_limit_bytes=32 * MEBI),
        name="rank_products",
    )(base, table, own, near, *tokens)


def broadcast_lane(tile, lane):
    return jnp.broadcast_to(tile[:, lane : lane + 1], tile.shape)


def combine_part_kernel(base_ref, mine_ref, theirs_ref, cache_ref, out_ref, *replies):
    half = base_ref.shape[1] // 2
    own = base_ref[:, :half] + theirs_ref[:, :half].astype(F32)
    out_ref[:, :half] = own.astype(BF16)
    sums = mine_ref[:, half:].astype(F32) + theirs_ref[:, half:].astype(F32)
    sums = split(sums[:8] + sums[8:])
    out_ref[:, half : half + 256] = sums[:, :256]
    out_ref[:, half + 256 :] = cache_ref[...]
    for i, ref in enumerate(replies):
        ref[...] = sums[:, 128 * (i + 2) : 128 * (i + 3)]


def combine_part(n, base, mine, theirs, cache):
    shapes = [(16, base.shape[1] // 2 + 256 + cache.shape[1])] + [(16, 128)] * n
    return pl.pallas_call(
        combine_part_kernel,
        in_specs=[VMEM] * 4,
        out_specs=[VMEM] * len(shapes),
        out_shape=[jax.ShapeDtypeStruct(shape, BF16) for shape in shapes],
        compiler_params=pltpu.CompilerParams(vmem_limit_bytes=32 * MEBI),
        name="combine_part",
    )(base, mine, theirs, cache)


def combine_cache_kernel(a_ref, b_ref, _, out_ref):
    lane = lax.broadcasted_iota(jnp.int32, (16, 128), 1)
    for p in range(out_ref.shape[1] // PAIR):
        end = slice(p * PAIR + GROUP * HD, (p + 1) * PAIR)
        a, b = a_ref[:, end].astype(F32), b_ref[:, end].astype(F32)
        top = jnp.maximum(a, b)
        fa = jnp.exp2(jnp.minimum(a - top, 0.0) * EXPONENT)
        fb = jnp.exp2(jnp.minimum(b - top, 0.0) * EXPONENT)
        total = fa * totals(a) + fb * totals(b)
        high = rounded(total)
        stats = jnp.where(lane < GROUP, top, 0.0)
        stats = jnp.where(lane // GROUP == 1, pltpu.roll(high, GROUP, 1), stats)
        stats = jnp.where(lane // GROUP == 2, pltpu.roll(total - high, 2 * GROUP, 1), stats)
        out_ref[:, end] = stats.astype(BF16)
        for g in range(GROUP):
            at = slice(p * PAIR + g * HD, p * PAIR + (g + 1) * HD)
            out_ref[:, at] = (
                broadcast_lane(fa, g) * a_ref[:, at].astype(F32)
                + broadcast_lane(fb, g) * b_ref[:, at].astype(F32)
            ).astype(BF16)


def totals(stats):
    return pltpu.roll(stats, 128 - GROUP, 1) + pltpu.roll(stats, 128 - 2 * GROUP, 1)


def combine_cache(a, b, earlier):
    return pl.pallas_call(
        combine_cache_kernel,
        in_specs=[VMEM] * 3,
        out_specs=VMEM,
        out_shape=jax.ShapeDtypeStruct(a.shape, BF16),
        compiler_params=pltpu.CompilerParams(vmem_limit_bytes=32 * MEBI),
        name="combine_cache",
    )(a, b, earlier)


def merge_kernel(n, paired, width_all, *refs):
    table_ref, qrot_ref, pa_ref, pb_ref = refs[:4]
    backs, (ua_ref, ub_ref, out_ref) = refs[4 : 4 + n], refs[4 + n :]
    pairs = qrot_ref.shape[1] // (GROUP * HD)
    width = pairs * 2 * HD
    cosine, sine = table_ref[8:16], table_ref[16:]
    head = width + 256
    sums = pa_ref[:, :head].astype(F32) + pb_ref[:, :head].astype(F32)
    tail = sums[:8, width : width + 256] + sums[8:, width : width + 256]
    squares, z = tail[:, :128], tail[:, 128:]
    for ref in backs:
        z = z + joined(ref[...])
    lane8 = lax.broadcasted_iota(jnp.int32, (8, 128), 1)
    z = jnp.concatenate(
        [jnp.where(lane8 < RANK, z, 0.0), jnp.where(lane8 < RANK, 0.0, z)], 0
    ).astype(BF16)
    adapted = []
    for ref in (ua_ref, ub_ref):
        ups = jnp.concatenate([ref[:, i : i + 128] for i in range(0, 16 * HD, 128)], 0)
        adapted.append(lax.dot_general(z, ups, NT, preferred_element_type=F32))
    if paired:
        even = lax.axis_index("dp") % 2 == 0
        a, b = adapted
        adapted = [jnp.where(even, a, b), jnp.where(even, b, a)]
    total = sums[:, :width] + jnp.concatenate(adapted, 1)
    scale = lax.rsqrt(squares / width_all + EPSILON)
    lane = lax.broadcasted_iota(jnp.int32, (16, 128), 1)
    step = lax.broadcasted_iota(jnp.int32, (16, 128), 0) % STEPS
    first = first_rows((8, 128))

    def of_step(tiles, j):
        return jnp.concatenate(
            [
                jnp.where(first, tile[j : j + 1], tile[STEPS + j : STEPS + j + 1])
                for tile in tiles
            ],
            0,
        )

    for p in range(pairs):
        new_keys, new_values = [], []
        for e in range(2):
            at = slice((2 * p + e) * HD, (2 * p + e + 1) * HD)
            new_keys.append(rounded(rotated(total[:8, at] * scale, cosine, sine)))
            new_values.append(rounded(total[8:, at] * scale))
            fresh = jnp.concatenate([new_keys[e], new_values[e]], 0)
            start = pairs * GROUP * HD + (2 * p + e) * HD
            out_ref[:, start : start + HD] = fresh.astype(BF16)
        keys = [of_step(new_keys, j) for j in range(STEPS)]
        values = [of_step(new_values, j) for j in range(STEPS)]
        scores = [jnp.zeros((16, 128), F32) for _ in range(STEPS)]
        for g in range(GROUP):
            q = qrot_ref[:, (p * GROUP + g) * HD : (p * GROUP + g + 1) * HD].astype(F32)
            for j in range(STEPS):
                dot = jnp.sum(q * keys[j], 1, keepdims=True)
                scores[j] = jnp.where(lane == g, dot, scores[j])
        scores = [jnp.where(j <= step, scores[j], MASKED_SCORE) for j in range(STEPS)]
        end = slice(head + p * PAIR + GROUP * HD, head + (p + 1) * PAIR)
        stats = [ref[:, end].astype(F32) for ref in (pa_ref, pb_ref)]
        top = functools.reduce(jnp.maximum, scores + stats)
        fresh = [rounded(jnp.exp2((scores[j] - top) * EXPONENT)) for j in range(STEPS)]
        factors = [jnp.exp2(jnp.minimum(s - top, 0.0) * EXPONENT) for s in stats]
        denom = functools.reduce(jnp.add, fresh)
        for factor, s in zip(factors, stats):
            denom = denom + factor * totals(s)
        inverse = 1.0 / denom
        coefficients = [c * inverse for c in fresh + factors]
        for g in range(GROUP):
            at = slice(head + p * PAIR + g * HD, head + p * PAIR + (g + 1) * HD)
            terms = values + [ref[:, at].astype(F32) for ref in (pa_ref, pb_ref)]
            tile = jnp.zeros((16, 128), F32)
            for c, term in zip(coefficients, terms):
                tile = tile + broadcast_lane(c, g) * term
            out_ref[:, (p * GROUP + g) * HD : (p * GROUP + g + 1) * HD] = tile.astype(BF16)


def merge(paired, width_all, table, qrot, parts, backs, ups):
    operands = [table, qrot, *parts, *backs, *ups]
    pairs = qrot.shape[1] // (GROUP * HD)
    return pl.pallas_call(
        functools.partial(merge_kernel, len(backs), paired, width_all),
        in_specs=[VMEM] * len(operands),
        out_specs=VMEM,
        out_shape=jax.ShapeDtypeStruct((16, pairs * (GROUP + 2) * HD), BF16),
        compiler_params=pltpu.CompilerParams(vmem_limit_bytes=32 * MEBI),
        name="merge",
    )(*operands)


def place_kernel(mine_ref, theirs_ref, keys_out, values_out, out_ref):
    pairs = mine_ref.shape[1] // ((GROUP + 2) * HD)
    for c, ref in enumerate((mine_ref, theirs_ref)):
        for p in range(pairs):
            pair = pair_at(c * pairs + p)
            tiles = ref[:, p * GROUP * HD : (p + 1) * GROUP * HD].astype(F32)
            size = GROUP * HD
            for e in range(2):
                at = pl.ds(pl.multiple_of((2 * pair + e) * size, size), size)
                for s in range(2):
                    rows = slice(8 * e + 4 * s, 8 * e + 4 * s + 4)
                    out_ref[s, :, at] = tiles[rows].astype(BF16)
            start = pairs * GROUP * HD + p * 2 * HD
            fresh = ref[:, start : start + 2 * HD].astype(F32)
            at = pl.ds(pl.multiple_of(pair * 2 * HD, 2 * HD), 2 * HD)
            for i, out in enumerate((keys_out, values_out)):
                for s in range(2):
                    rows = slice(8 * i + 4 * s, 8 * i + 4 * s + 4)
                    out[s, :, at] = fresh[rows].astype(BF16)


def place(width, mine, theirs):
    return pl.pallas_call(
        place_kernel,
        in_specs=[VMEM] * 2,
        out_specs=[VMEM] * 3,
        out_shape=[
            jax.ShapeDtypeStruct((2, STEPS, width), BF16),
            jax.ShapeDtypeStruct((2, STEPS, width), BF16),
            jax.ShapeDtypeStruct((2, STEPS, GROUP * width), BF16),
        ],
        compiler_params=pltpu.CompilerParams(vmem_limit_bytes=32 * MEBI),
        name="place",
    )(mine, theirs)


def swap(value, axis, n, distance):
    return lax.ppermute(value, axis, [(i, i ^ distance) for i in range(n)])


def shards(
    n_dp,
    n_tensor,
    hidden,
    norm_gain,
    queries,
    key_weight,
    value_weight,
    key_down,
    key_up,
    value_down,
    value_up,
    key_cache,
    value_cache,
    lengths,
):
    depth, width = key_weight.shape
    rows = key_down.shape[0]
    to_dp = lambda value, distance: swap(value, "dp", n_dp, distance)
    to_tensor = lambda value, distance: swap(value, "tensor", n_tensor, distance)
    partners = range(2, n_dp, 2)
    n = len(partners)
    paired = n_dp == 4

    down, tokens, own = pack(
        lengths, hidden, norm_gain, key_down, value_down, key_up, value_up
    )
    near = to_dp(down, 1)
    sent = [to_dp(tokens, d) for d in partners]
    keep, send, base, qrot, table = local(
        own, queries, key_cache, value_cache, key_weight, value_weight
    )
    received = to_tensor(send, 1)
    columns = UP_COLUMNS if paired else 0
    message, *has = rank_products(rows, depth, columns, base, table, down, near, [tokens, *sent])
    if paired:
        ups = [has[0], to_dp(has[0], 1)]
    else:
        ups = lax.all_gather(tokens[:, depth // 2 :], "dp")
        ups = ups.reshape(n_dp, 16, -1, 128).transpose(0, 2, 1, 3)
        ups = ups.reshape(2, 2, 16, 16, 128).transpose(0, 1, 3, 2, 4).reshape(2, 2, 16, -1)
        ups = lax.dynamic_index_in_dim(ups, lax.axis_index("tensor") % 2, 0, keepdims=False)
        ups = [ups[0], ups[1]]
    cache = combine_cache(keep, received, message)
    part, *replies = combine_part(n, base, message, to_tensor(message, 1), cache)
    part_far = to_tensor(part, 2)
    places = [(s, t) for s in range(n_dp) for t in range(n_tensor)]
    backs = []
    for reply, d in zip(replies, partners):
        for e in (0, 2):
            perm = [(s * n_tensor + t, (s ^ d) * n_tensor + (t ^ e)) for s, t in places]
            backs.append(lax.ppermute(reply, ("dp", "tensor"), perm))
    merged = merge(
        paired,
        float(depth * n_tensor),
        table,
        qrot,
        (part, part_far),
        backs,
        ups,
    )
    return place(width, merged, to_tensor(merged, 1))


def solution(mesh):
    body = functools.partial(shards, mesh.shape["dp"], mesh.shape["tensor"])
    return jax.shard_map(
        body,
        mesh=mesh,
        in_specs=(
            P(("groups", "dp"), None, "tensor"),
            P("tensor"),
            P(("groups", "dp"), None, None),
            P("tensor", None),
            P("tensor", None),
            P(("groups", "dp"), "tensor"),
            P(("groups", "dp"), None),
            P(("groups", "dp"), "tensor"),
            P(("groups", "dp"), None),
            P(("groups", "dp"), "tensor", None),
            P(("groups", "dp"), "tensor", None),
            P(("groups", "dp")),
        ),
        out_specs=(
            P(("groups", "dp"), None, None),
            P(("groups", "dp"), None, None),
            P(("groups", "dp"), None, None),
        ),
        check_vma=False,
    )
```

```python
import functools
import math

import jax
import jax.numpy as jnp
from jax import lax
from jax.experimental import pallas as pl
from jax.experimental.pallas import tpu as pltpu
from jax.sharding import PartitionSpec as P

HD = 128
GROUP = 8
STEPS = 4
RANK = 64
EPSILON = 1e-05
ROPE_BASE = 500000.0
MASKED_SCORE = -1e30
LOWEST_TOP = -1e20
EXPONENT = math.log2(math.e) / math.sqrt(HD)
PAIR = GROUP * HD + 128
UP_COLUMNS = 3584
CHUNK = 512

F32 = jnp.float32
BF16 = jnp.bfloat16
NT = (((1,), (1,)), ((), ()))
VMEM = pl.BlockSpec(memory_space=pltpu.VMEM)
HBM = pl.BlockSpec(memory_space=pltpu.HBM)
MEBI = 2**20
WHOLE_VMEM = 65000 * 1024
LOCAL_VMEM = 54900 * 1024


def rounded(value):
    return value.astype(BF16).astype(F32)


def split(value):
    high = rounded(value)
    return jnp.concatenate([high, value - high], 0).astype(BF16)


def joined(tile):
    wide = tile.astype(F32)
    return wide[:8] + wide[8:]


def rotated(tile, cosine, sine):
    return tile * cosine + pltpu.roll(tile, HD // 2, 1) * sine


def first_rows(shape):
    return lax.broadcasted_iota(jnp.int32, shape, 0) % 8 < STEPS


def exchanged(a, b):
    first = first_rows(a.shape)
    return (
        jnp.where(first, a, pltpu.roll(b, STEPS, 0)),
        jnp.where(first, pltpu.roll(a, STEPS, 0), b),
    )


def flat(matrix):
    return jnp.concatenate([matrix[i : i + 16] for i in range(0, matrix.shape[0], 16)], 1)


def pack_kernel(*refs):
    sources, outs, held = refs[:7], refs[7:10], refs[10:17]
    (a_ref, b_ref, own_ref), sems, out_sems = refs[17:20], refs[20], refs[21]
    targets = [*outs[:2], outs[2].at[:, pl.ds(0, own_ref.shape[1])]]
    copies = [
        pltpu.make_async_copy(source, target, sems.at[i])
        for i, (source, target) in enumerate(zip(sources, held))
    ]
    for copy in copies:
        copy.start()
    backs = [
        pltpu.make_async_copy(source, target, out_sems.at[i])
        for i, (source, target) in enumerate(zip((a_ref, b_ref, own_ref), targets))
    ]
    kd_ref, vd_ref, x_ref, gain_ref, lengths_ref, ku_ref, vu_ref = held
    own, depth = kd_ref.shape
    for slot, ref in enumerate((kd_ref, vd_ref)):
        copies[slot].wait()
        down = ref[...]
        if own < 16:
            down = jnp.concatenate([down, jnp.zeros((16 - own, depth), F32)], 0)
        a_ref[:, slot * depth : (slot + 1) * depth] = down.astype(BF16)
    backs[0].start()
    for copy in copies[2:]:
        copy.wait()
    x = jnp.concatenate([x_ref[0].astype(F32), x_ref[1].astype(F32)], 0)
    gain = gain_ref[...].astype(F32)
    scaled = jnp.concatenate(
        [x[:, i * 128 : (i + 1) * 128] * gain[i : i + 1] for i in range(depth // 128)], 1
    )
    scaled = jnp.concatenate([scaled[:, : depth // 2], scaled[:, depth // 2 :]], 0).astype(BF16)
    b_ref[:, : depth // 2] = scaled
    ups = jnp.concatenate([ku_ref[...], vu_ref[...]], 0).T.astype(BF16)
    b_ref[:, depth // 2 :] = flat(ups)
    backs[1].start()
    own_ref[:, : depth // 2] = scaled
    row = lax.broadcasted_iota(jnp.int32, (16, 128), 0)
    lengths = lengths_ref[...]
    length = jnp.where(row % 8 < STEPS, lengths[:, :1], lengths[:, 1:])
    length = jnp.where(row < 8, length // 64 * 64, length % 64)
    own_ref[:, depth // 2 : depth // 2 + 128] = length.astype(F32).astype(BF16)
    squares = jnp.broadcast_to(jnp.sum(x * x, 1, keepdims=True), (8, 128))
    own_ref[:, depth // 2 + 128 :] = split(squares)
    backs[2].start()
    for copy in backs:
        copy.wait()


def pack(lengths, hidden, gain, key_down, value_down, key_up, value_up):
    operands = [key_down, value_down, hidden, gain.reshape(-1, 128), lengths.reshape(1, 2)]
    operands += [key_up.T, value_up.T]
    depth = hidden.shape[2]
    ups = key_up.shape[0] * 8
    outs = [
        jax.ShapeDtypeStruct((16, 2 * depth), BF16),
        jax.ShapeDtypeStruct((16, depth // 2 + ups), BF16),
        jax.ShapeDtypeStruct((16, depth // 2 + 256 + ups), BF16),
    ]
    scratch = [*operands, *outs[:2], jax.ShapeDtypeStruct((16, depth // 2 + 256), BF16)]
    return pl.pallas_call(
        pack_kernel,
        in_specs=[HBM] * len(operands),
        out_specs=[HBM] * len(outs),
        out_shape=outs,
        scratch_shapes=[pltpu.VMEM(o.shape, o.dtype) for o in scratch]
        + [pltpu.SemaphoreType.DMA((len(operands),)), pltpu.SemaphoreType.DMA((len(outs),))],
        compiler_params=pltpu.CompilerParams(vmem_limit_bytes=WHOLE_VMEM),
        name="pack",
    )(*operands)


def tables(length):
    shape = length.shape
    row = lax.broadcasted_iota(jnp.int32, shape, 0)
    lane = lax.broadcasted_iota(jnp.int32, shape, 1)
    position = length + (row % STEPS).astype(F32)
    pair = lane % (HD // 2)
    frequency = jnp.ones(shape, F32)
    for bit in range(6):
        factor = ROPE_BASE ** (-(2.0 * 2**bit) / HD)
        frequency = jnp.where((pair >> bit) & 1 == 1, frequency * factor, frequency)
    cosine, sine = cosine_and_sine(position * frequency)
    return cosine, jnp.where(lane < HD // 2, -sine, sine)


def cosine_and_sine(angle):
    turns = jnp.floor(angle * (2.0 / math.pi) + 0.5)
    rest = ((angle - turns * 1.5703125) - turns * 4.8351287841796875e-4) - turns * 3.1391647e-7
    square = rest * rest
    sine = -1.9515295891e-4 * square + 8.3321608736e-3
    sine = (sine * square - 1.6666654611e-1) * square * rest + rest
    cosine = 2.443315711809948e-5 * square - 1.388731625493765e-3
    cosine = (cosine * square + 4.166664568298827e-2) * square * square - 0.5 * square + 1.0
    quadrant = turns.astype(jnp.int32)
    swap_them = (quadrant & 1) == 1
    cosine, sine = jnp.where(swap_them, sine, cosine), jnp.where(swap_them, cosine, sine)
    cosine = jnp.where(((quadrant + 1) & 2) == 2, -cosine, cosine)
    sine = jnp.where((quadrant & 2) == 2, -sine, sine)
    return cosine, sine


def rotated_rows(pairs, cosine, sine, q_ref, qrot_ref):
    zero = jnp.zeros((32, HD), F32)
    result = []
    for p in pairs:
        halves = [[], []]
        for e in range(2):
            for g in range(GROUP):
                at = slice(((2 * p + e) * GROUP + g) * HD, ((2 * p + e) * GROUP + g + 1) * HD)
                q = jnp.concatenate([q_ref[0, :, at].astype(F32), q_ref[1, :, at].astype(F32)], 0)
                halves[e].append(rotated(q, cosine, sine))
        if qrot_ref is not None:
            for g in range(GROUP):
                at = slice((p * GROUP + g) * HD, (p * GROUP + g + 1) * HD)
                qrot_ref[:, at] = jnp.concatenate([halves[0][g], halves[1][g]], 0).astype(BF16)
        mixed = [[exchanged(halves[e][g], halves[e][g + 4]) for g in range(4)] for e in range(2)]
        for s in range(2):
            rows = [jnp.concatenate([mixed[e][g][s] for g in range(4)], 0) for e in range(2)]
            result.append(
                jnp.concatenate(
                    [jnp.concatenate([rows[0], zero], 1), jnp.concatenate([zero, rows[1]], 1)], 0
                ).astype(BF16)
            )
    return result


def attend(pairs, masks, queries, k_ref, v_ref, between, out_ref):
    scores = []
    for i, p in enumerate(pairs):
        for s in range(2):
            keys = k_ref[s, :, 2 * p * HD : 2 * (p + 1) * HD]
            score = lax.dot_general(queries[2 * i + s], keys, NT, preferred_element_type=F32)
            scores.append(score + jnp.concatenate([masks[s]] * (score.shape[0] // 8), 0))
    between()
    scores = jnp.concatenate(scores, 0)
    top = rounded(jnp.maximum(jnp.max(scores, 1, keepdims=True), LOWEST_TOP))
    weights = jnp.exp2((scores - top) * EXPONENT).astype(BF16)
    total = jnp.sum(weights.astype(F32), 1, keepdims=True)
    high = rounded(total)
    columns = (top, high, total - high)
    lane8 = lax.broadcasted_iota(jnp.int32, (8, 128), 1)
    numers = []
    for i, p in enumerate(pairs):
        for s in range(2):
            at = slice(64 * (2 * i + s), 64 * (2 * i + s + 1))
            values = v_ref[s, :, 2 * p * HD : 2 * (p + 1) * HD]
            numers.append(jnp.dot(weights[at], values, preferred_element_type=F32))
    for i, p in enumerate(pairs):
        outs, ends = [[], []], []
        for e in range(2):
            back, stats = [], []
            for s in range(2):
                tile = jnp.zeros((8, 128), F32)
                for g in range(4):
                    row = 64 * (2 * i + s) + 32 * e + 8 * g
                    for slot, value in enumerate(columns):
                        tile = jnp.where(lane8 == slot * GROUP + g, value[row : row + 8], tile)
                stats.append(tile)
            for g in range(4):
                at = slice(32 * e + 8 * g, 32 * e + 8 * g + 8)
                cols = slice(e * HD, (e + 1) * HD)
                back.append(exchanged(numers[2 * i][at, cols], numers[2 * i + 1][at, cols]))
            outs[e] = [b[0] for b in back] + [b[1] for b in back]
            a, b = exchanged(*stats)
            ends.append(jnp.where(lane8 % 8 < 4, a, pltpu.roll(b, 4, 1)))
        for g in range(GROUP):
            at = slice(i * PAIR + g * HD, i * PAIR + (g + 1) * HD)
            out_ref[:, at] = jnp.concatenate([outs[0][g], outs[1][g]], 0).astype(BF16)
        out_ref[:, i * PAIR + GROUP * HD : (i + 1) * PAIR] = jnp.concatenate(ends, 0).astype(BF16)


def pair_at(i):
    return i ^ (lax.axis_index("tensor") % 2 * 2)


def local_kernel(
    x_hbm, q_hbm, k_hbm, v_hbm, wk_hbm, wv_hbm,
    keep_ref, send_ref, base_ref, qrot_ref, table_ref,
    x_ref, q_ref, k_ref, v_ref, wk_ref, wv_ref, x_sem, q_sem, cache_sem, weight_sem,
):
    pairs = k_hbm.shape[2] // (2 * HD)
    chunks = wk_hbm.shape[0] // CHUNK
    width = wk_hbm.shape[1]
    core = lax.axis_index("tensor") % 2
    x_copy = pltpu.make_async_copy(x_hbm.at[:, pl.ds(0, x_ref.shape[1])], x_ref, x_sem)
    x_copy.start()
    groups = []
    for h in range(2):
        copies = []
        trio = ((q_hbm, q_ref, q_sem.at[h]), (k_hbm, k_ref, cache_sem.at[h, 0]))
        for source, target, sem in (*trio, (v_hbm, v_ref, cache_sem.at[h, 1])):
            size = source.shape[2] // 2
            start = pl.multiple_of((core ^ h) * size, size)
            copies.append(
                pltpu.make_async_copy(
                    source.at[:, :, pl.ds(start, size)],
                    target.at[:, :, pl.ds(h * size, size)],
                    sem,
                )
            )
        groups.append(copies)
    for h in range(2):
        groups[h][0].start()
    for copy in groups[0][1:]:
        copy.start()
    weights = []
    for c in range(chunks):
        at = pl.ds(c * CHUNK, CHUNK)
        weights.append(
            [
                pltpu.make_async_copy(source.at[at], target.at[at], weight_sem.at[c, i])
                for i, (source, target) in enumerate(((wk_hbm, wk_ref), (wv_hbm, wv_ref)))
            ]
        )
    def start(copies):
        for copy in copies:
            copy.start()

    x_copy.wait()
    start(groups[1][1:])
    start(weights[0])
    half = wk_hbm.shape[0] // 2
    x = x_ref[:, :half].astype(F32)
    x = jnp.concatenate([x[:8], x[8:]], 1).astype(BF16)
    length = joined(x_ref[:, half : half + 128])
    cosine, sine = tables(length)
    table_ref[...] = jnp.concatenate([joined(x_ref[:, half + 128 : half + 256]), cosine, sine], 0)
    limit = length - (lax.axis_index("tensor") * k_hbm.shape[1]).astype(F32)
    place = lax.broadcasted_iota(jnp.int32, (8, k_hbm.shape[1]), 1).astype(F32)
    masks = [
        jnp.where(place < limit[STEPS * s : STEPS * s + 1, :1], 0.0, MASKED_SCORE) for s in range(2)
    ]
    queries = []
    for h in range(2):
        groups[h][0].wait()
        own = range(h * pairs // 2, (h + 1) * pairs // 2)
        queries.append(rotated_rows(own, cosine, sine, q_ref, None if h else qrot_ref))
    parts = []

    def project(c):
        at = slice(c * CHUNK, (c + 1) * CHUNK)
        halves = []
        for copy, ref in zip(weights[c], (wk_ref, wv_ref)):
            copy.wait()
            halves.append(jnp.dot(x[:, at], ref[at], preferred_element_type=F32))
        parts.append(jnp.concatenate(halves, 0))

    def between(h):
        groups[h][2].wait()
        if h == 0:
            start(weights[chunks // 2])
        else:
            for c in range(chunks // 2):
                project(c)

    for h, out_ref in enumerate((keep_ref, send_ref)):
        groups[h][1].wait()
        for copies in weights[chunks // 2 + 1 :] if h else weights[1 : chunks // 2]:
            start(copies)
        attend(
            range(h * pairs // 2, (h + 1) * pairs // 2),
            masks, queries[h], k_ref, v_ref, functools.partial(between, h), out_ref,
        )
    for c in range(chunks // 2, chunks):
        project(c)
    total = functools.reduce(jnp.add, parts)
    lower, upper = total[:, : width // 2], total[:, width // 2 :]
    base_ref[:, : width // 2] = jnp.where(core == 0, lower, upper)
    base_ref[:, width // 2 :] = jnp.where(core == 0, upper, lower)


def local(message, queries, key_cache, value_cache, key_weight, value_weight):
    seqs, length, width = key_cache.shape
    depth = key_weight.shape[0]
    pairs = width // (2 * HD)
    operands = [message, queries, key_cache, value_cache, key_weight, value_weight]
    return pl.pallas_call(
        local_kernel,
        in_specs=[HBM] * 6,
        out_specs=[VMEM] * 5,
        out_shape=[
            jax.ShapeDtypeStruct((16, pairs // 2 * PAIR), BF16),
            jax.ShapeDtypeStruct((16, pairs // 2 * PAIR), BF16),
            jax.ShapeDtypeStruct((16, width), F32),
            jax.ShapeDtypeStruct((16, pairs // 2 * GROUP * HD), BF16),
            jax.ShapeDtypeStruct((24, 128), F32),
        ],
        scratch_shapes=[pltpu.VMEM((16, depth // 2 + 256), BF16)]
        + [pltpu.VMEM(o.shape, BF16) for o in operands[1:]]
        + [
            pltpu.SemaphoreType.DMA,
            pltpu.SemaphoreType.DMA((2,)),
            pltpu.SemaphoreType.DMA((2, 2)),
            pltpu.SemaphoreType.DMA((depth // CHUNK, 2)),
        ],
        compiler_params=pltpu.CompilerParams(vmem_limit_bytes=LOCAL_VMEM),
        cost_estimate=pl.CostEstimate(
            flops=4 * 64 * 256 * seqs * length * pairs + 4 * 16 * depth * width,
            bytes_accessed=4 * seqs * length * width + 4 * depth * width,
            transcendentals=64 * seqs * length * pairs,
        ),
        name="local",
    )(*operands)


def rank_kernel(n, rows, depth, *refs):
    base_ref, table_ref, own_ref, near_ref = refs[:4]
    tokens, (out_ref, *has) = refs[4 : 4 + n], refs[4 + n :]
    half = base_ref.shape[1] // 2
    place = lax.axis_index("dp")
    x = []
    for ref in tokens:
        part = ref[:, : depth // 2].astype(F32)
        x.append(jnp.concatenate([part[:8], part[8:]], 1))
    x = jnp.concatenate(x, 0).astype(BF16)
    down = jnp.concatenate(
        [ref[:, at : at + depth] for at in (0, depth) for ref in (own_ref, near_ref)], 0
    )
    products = lax.dot_general(x, down, NT, preferred_element_type=F32)
    products = jnp.concatenate([products, jnp.zeros_like(products)], 1)
    lane = lax.broadcasted_iota(jnp.int32, products.shape, 1)
    z = None
    for i in range(4):
        part = jnp.where(lane // 16 == i, products, 0.0)
        column = (place ^ (i % 2)) * rows + i // 2 * RANK
        part = pltpu.roll(part, (column + 128 - 16 * i) % 128, 1)
        z = part if z is None else z + part
    out_ref[:, :half] = base_ref[:, half:].astype(BF16)
    out_ref[:, half : half + 128] = split(table_ref[:8])
    for i in range(n):
        at = half + 128 * (i + 1)
        out_ref[:, at : at + 128] = split(z[8 * i : 8 * i + 8])
    for ref in has:
        here = place // 2 == lax.axis_index("tensor") % 2
        mine, far = (token[:, depth // 2 :].astype(F32) for token in tokens[:2])
        ref[:, : mine.shape[1]] = jnp.where(here, mine, far).astype(BF16)
        ref[:, mine.shape[1] :] = jnp.zeros((16, ref.shape[1] - mine.shape[1]), BF16)


def rank_products(rows, depth, columns, base, table, own, near, tokens):
    n = len(tokens)
    out_shape = [jax.ShapeDtypeStruct((16, base.shape[1] // 2 + 128 * (n + 1)), BF16)]
    if columns:
        out_shape.append(jax.ShapeDtypeStruct((16, columns), BF16))
    return pl.pallas_call(
        functools.partial(rank_kernel, n, rows, depth),
        in_specs=[VMEM] * (4 + n),
        out_specs=[VMEM] * len(out_shape),
        out_shape=out_shape,
        compiler_params=pltpu.CompilerParams(vmem_limit_bytes=32 * MEBI),
        name="rank_products",
    )(base, table, own, near, *tokens)


def broadcast_lane(tile, lane):
    return jnp.broadcast_to(tile[:, lane : lane + 1], tile.shape)


def combine_part_kernel(base_ref, mine_ref, theirs_ref, cache_ref, out_ref, *replies):
    half = base_ref.shape[1] // 2
    own = base_ref[:, :half] + theirs_ref[:, :half].astype(F32)
    out_ref[:, :half] = own.astype(BF16)
    sums = mine_ref[:, half:].astype(F32) + theirs_ref[:, half:].astype(F32)
    sums = split(sums[:8] + sums[8:])
    out_ref[:, half : half + 256] = sums[:, :256]
    out_ref[:, half + 256 :] = cache_ref[...]
    for i, ref in enumerate(replies):
        ref[...] = sums[:, 128 * (i + 2) : 128 * (i + 3)]


def combine_part(n, base, mine, theirs, cache):
    shapes = [(16, base.shape[1] // 2 + 256 + cache.shape[1])] + [(16, 128)] * n
    return pl.pallas_call(
        combine_part_kernel,
        in_specs=[VMEM] * 4,
        out_specs=[VMEM] * len(shapes),
        out_shape=[jax.ShapeDtypeStruct(shape, BF16) for shape in shapes],
        compiler_params=pltpu.CompilerParams(vmem_limit_bytes=32 * MEBI),
        name="combine_part",
    )(base, mine, theirs, cache)


def combine_cache_kernel(a_ref, b_ref, _, out_ref):
    lane = lax.broadcasted_iota(jnp.int32, (16, 128), 1)
    for p in range(out_ref.shape[1] // PAIR):
        end = slice(p * PAIR + GROUP * HD, (p + 1) * PAIR)
        a, b = a_ref[:, end].astype(F32), b_ref[:, end].astype(F32)
        top = jnp.maximum(a, b)
        fa = jnp.exp2(jnp.minimum(a - top, 0.0) * EXPONENT)
        fb = jnp.exp2(jnp.minimum(b - top, 0.0) * EXPONENT)
        total = fa * totals(a) + fb * totals(b)
        high = rounded(total)
        stats = jnp.where(lane < GROUP, top, 0.0)
        stats = jnp.where(lane // GROUP == 1, pltpu.roll(high, GROUP, 1), stats)
        stats = jnp.where(lane // GROUP == 2, pltpu.roll(total - high, 2 * GROUP, 1), stats)
        out_ref[:, end] = stats.astype(BF16)
        for g in range(GROUP):
            at = slice(p * PAIR + g * HD, p * PAIR + (g + 1) * HD)
            out_ref[:, at] = (
                broadcast_lane(fa, g) * a_ref[:, at].astype(F32)
                + broadcast_lane(fb, g) * b_ref[:, at].astype(F32)
            ).astype(BF16)


def totals(stats):
    return pltpu.roll(stats, 128 - GROUP, 1) + pltpu.roll(stats, 128 - 2 * GROUP, 1)


def combine_cache(a, b, earlier):
    return pl.pallas_call(
        combine_cache_kernel,
        in_specs=[VMEM] * 3,
        out_specs=VMEM,
        out_shape=jax.ShapeDtypeStruct(a.shape, BF16),
        compiler_params=pltpu.CompilerParams(vmem_limit_bytes=32 * MEBI),
        name="combine_cache",
    )(a, b, earlier)


def merge_kernel(n, paired, width_all, *refs):
    table_ref, qrot_ref, pa_ref, pb_ref = refs[:4]
    backs, (ua_ref, ub_ref, out_ref) = refs[4 : 4 + n], refs[4 + n :]
    pairs = qrot_ref.shape[1] // (GROUP * HD)
    width = pairs * 2 * HD
    cosine, sine = table_ref[8:16], table_ref[16:]
    head = width + 256
    sums = pa_ref[:, :head].astype(F32) + pb_ref[:, :head].astype(F32)
    tail = sums[:8, width : width + 256] + sums[8:, width : width + 256]
    squares, z = tail[:, :128], tail[:, 128:]
    for ref in backs:
        z = z + joined(ref[...])
    lane8 = lax.broadcasted_iota(jnp.int32, (8, 128), 1)
    z = jnp.concatenate(
        [jnp.where(lane8 < RANK, z, 0.0), jnp.where(lane8 < RANK, 0.0, z)], 0
    ).astype(BF16)
    adapted = []
    for ref in (ua_ref, ub_ref):
        ups = jnp.concatenate([ref[:, i : i + 128] for i in range(0, 16 * HD, 128)], 0)
        adapted.append(lax.dot_general(z, ups, NT, preferred_element_type=F32))
    if paired:
        even = lax.axis_index("dp") % 2 == 0
        a, b = adapted
        adapted = [jnp.where(even, a, b), jnp.where(even, b, a)]
    total = sums[:, :width] + jnp.concatenate(adapted, 1)
    scale = lax.rsqrt(squares / width_all + EPSILON)
    lane = lax.broadcasted_iota(jnp.int32, (16, 128), 1)
    step = lax.broadcasted_iota(jnp.int32, (16, 128), 0) % STEPS
    first = first_rows((8, 128))

    def of_step(tiles, j):
        return jnp.concatenate(
            [
                jnp.where(first, tile[j : j + 1], tile[STEPS + j : STEPS + j + 1])
                for tile in tiles
            ],
            0,
        )

    for p in range(pairs):
        new_keys, new_values = [], []
        for e in range(2):
            at = slice((2 * p + e) * HD, (2 * p + e + 1) * HD)
            new_keys.append(rounded(rotated(total[:8, at] * scale, cosine, sine)))
            new_values.append(rounded(total[8:, at] * scale))
            fresh = jnp.concatenate([new_keys[e], new_values[e]], 0)
            start = pairs * GROUP * HD + (2 * p + e) * HD
            out_ref[:, start : start + HD] = fresh.astype(BF16)
        keys = [of_step(new_keys, j) for j in range(STEPS)]
        values = [of_step(new_values, j) for j in range(STEPS)]
        scores = [jnp.zeros((16, 128), F32) for _ in range(STEPS)]
        for g in range(GROUP):
            q = qrot_ref[:, (p * GROUP + g) * HD : (p * GROUP + g + 1) * HD].astype(F32)
            for j in range(STEPS):
                dot = jnp.sum(q * keys[j], 1, keepdims=True)
                scores[j] = jnp.where(lane == g, dot, scores[j])
        scores = [jnp.where(j <= step, scores[j], MASKED_SCORE) for j in range(STEPS)]
        end = slice(head + p * PAIR + GROUP * HD, head + (p + 1) * PAIR)
        stats = [ref[:, end].astype(F32) for ref in (pa_ref, pb_ref)]
        top = functools.reduce(jnp.maximum, scores + stats)
        fresh = [rounded(jnp.exp2((scores[j] - top) * EXPONENT)) for j in range(STEPS)]
        factors = [jnp.exp2(jnp.minimum(s - top, 0.0) * EXPONENT) for s in stats]
        denom = functools.reduce(jnp.add, fresh)
        for factor, s in zip(factors, stats):
            denom = denom + factor * totals(s)
        inverse = 1.0 / denom
        coefficients = [c * inverse for c in fresh + factors]
        for g in range(GROUP):
            at = slice(head + p * PAIR + g * HD, head + p * PAIR + (g + 1) * HD)
            terms = values + [ref[:, at].astype(F32) for ref in (pa_ref, pb_ref)]
            tile = jnp.zeros((16, 128), F32)
            for c, term in zip(coefficients, terms):
                tile = tile + broadcast_lane(c, g) * term
            out_ref[:, (p * GROUP + g) * HD : (p * GROUP + g + 1) * HD] = tile.astype(BF16)


def merge(paired, width_all, table, qrot, parts, backs, ups):
    operands = [table, qrot, *parts, *backs, *ups]
    pairs = qrot.shape[1] // (GROUP * HD)
    return pl.pallas_call(
        functools.partial(merge_kernel, len(backs), paired, width_all),
        in_specs=[VMEM] * len(operands),
        out_specs=VMEM,
        out_shape=jax.ShapeDtypeStruct((16, pairs * (GROUP + 2) * HD), BF16),
        compiler_params=pltpu.CompilerParams(vmem_limit_bytes=32 * MEBI),
        name="merge",
    )(*operands)


def place_kernel(mine_ref, theirs_ref, keys_out, values_out, out_ref):
    pairs = mine_ref.shape[1] // ((GROUP + 2) * HD)
    for c, ref in enumerate((mine_ref, theirs_ref)):
        for p in range(pairs):
            pair = pair_at(c * pairs + p)
            tiles = ref[:, p * GROUP * HD : (p + 1) * GROUP * HD].astype(F32)
            size = GROUP * HD
            for e in range(2):
                at = pl.ds(pl.multiple_of((2 * pair + e) * size, size), size)
                for s in range(2):
                    rows = slice(8 * e + 4 * s, 8 * e + 4 * s + 4)
                    out_ref[s, :, at] = tiles[rows].astype(BF16)
            start = pairs * GROUP * HD + p * 2 * HD
            fresh = ref[:, start : start + 2 * HD].astype(F32)
            at = pl.ds(pl.multiple_of(pair * 2 * HD, 2 * HD), 2 * HD)
            for i, out in enumerate((keys_out, values_out)):
                for s in range(2):
                    rows = slice(8 * i + 4 * s, 8 * i + 4 * s + 4)
                    out[s, :, at] = fresh[rows].astype(BF16)


def place(width, mine, theirs):
    return pl.pallas_call(
        place_kernel,
        in_specs=[VMEM] * 2,
        out_specs=[VMEM] * 3,
        out_shape=[
            jax.ShapeDtypeStruct((2, STEPS, width), BF16),
            jax.ShapeDtypeStruct((2, STEPS, width), BF16),
            jax.ShapeDtypeStruct((2, STEPS, GROUP * width), BF16),
        ],
        compiler_params=pltpu.CompilerParams(vmem_limit_bytes=32 * MEBI),
        name="place",
    )(mine, theirs)


def swap(value, axis, n, distance):
    return lax.ppermute(value, axis, [(i, i ^ distance) for i in range(n)])


def shards(
    n_dp,
    n_tensor,
    hidden,
    norm_gain,
    queries,
    key_weight,
    value_weight,
    key_down,
    key_up,
    value_down,
    value_up,
    key_cache,
    value_cache,
    lengths,
):
    depth, width = key_weight.shape
    rows = key_down.shape[0]
    to_dp = lambda value, distance: swap(value, "dp", n_dp, distance)
    to_tensor = lambda value, distance: swap(value, "tensor", n_tensor, distance)
    partners = range(2, n_dp, 2)
    n = len(partners)
    paired = n_dp == 4

    down, tokens, own = pack(
        lengths, hidden, norm_gain, key_down, value_down, key_up, value_up
    )
    near = to_dp(down, 1)
    sent = [to_dp(tokens, d) for d in partners]
    keep, send, base, qrot, table = local(
        own, queries, key_cache, value_cache, key_weight, value_weight
    )
    received = to_tensor(send, 1)
    columns = UP_COLUMNS if paired else 0
    message, *has = rank_products(rows, depth, columns, base, table, down, near, [tokens, *sent])
    if paired:
        ups = [has[0], to_dp(has[0], 1)]
    else:
        ups = lax.all_gather(tokens[:, depth // 2 :], "dp")
        ups = ups.reshape(n_dp, 16, -1, 128).transpose(0, 2, 1, 3)
        ups = ups.reshape(2, 2, 16, 16, 128).transpose(0, 1, 3, 2, 4).reshape(2, 2, 16, -1)
        ups = lax.dynamic_index_in_dim(ups, lax.axis_index("tensor") % 2, 0, keepdims=False)
        ups = [ups[0], ups[1]]
    cache = combine_cache(keep, received, message)
    part, *replies = combine_part(n, base, message, to_tensor(message, 1), cache)
    part_far = to_tensor(part, 2)
    places = [(s, t) for s in range(n_dp) for t in range(n_tensor)]
    backs = []
    for reply, d in zip(replies, partners):
        for e in (0, 2):
            perm = [(s * n_tensor + t, (s ^ d) * n_tensor + (t ^ e)) for s, t in places]
            backs.append(lax.ppermute(reply, ("dp", "tensor"), perm))
    merged = merge(
        paired,
        float(depth * n_tensor),
        table,
        qrot,
        (part, part_far),
        backs,
        ups,
    )
    return place(width, merged, to_tensor(merged, 1))


def solution(mesh):
    body = functools.partial(shards, mesh.shape["dp"], mesh.shape["tensor"])
    return jax.shard_map(
        body,
        mesh=mesh,
        in_specs=(
            P(("groups", "dp"), None, "tensor"),
            P("tensor"),
            P(("groups", "dp"), None, None),
            P("tensor", None),
            P("tensor", None),
            P(("groups", "dp"), "tensor"),
            P(("groups", "dp"), None),
            P(("groups", "dp"), "tensor"),
            P(("groups", "dp"), None),
            P(("groups", "dp"), "tensor", None),
            P(("groups", "dp"), "tensor", None),
            P(("groups", "dp")),
        ),
        out_specs=(
            P(("groups", "dp"), None, None),
            P(("groups", "dp"), None, None),
            P(("groups", "dp"), None, None),
        ),
        check_vma=False,
    )
```

```python
import functools
import math

import jax
import jax.numpy as jnp
from jax import lax
from jax.experimental import pallas as pl
from jax.experimental.pallas import tpu as pltpu
from jax.sharding import PartitionSpec as P

HD = 128
GROUP = 8
STEPS = 4
RANK = 64
EPSILON = 1e-05
ROPE_BASE = 500000.0
MASKED_SCORE = -1e30
LOWEST_TOP = -1e20
EXPONENT = math.log2(math.e) / math.sqrt(HD)
PAIR = GROUP * HD + 128
UP_COLUMNS = 3584
CHUNK = 256

F32 = jnp.float32
BF16 = jnp.bfloat16
NT = (((1,), (1,)), ((), ()))
VMEM = pl.BlockSpec(memory_space=pltpu.VMEM)
HBM = pl.BlockSpec(memory_space=pltpu.HBM)
MEBI = 2**20
WHOLE_VMEM = 65000 * 1024
LOCAL_VMEM = 54900 * 1024


def rounded(value):
    return value.astype(BF16).astype(F32)


def split(value):
    high = rounded(value)
    return jnp.concatenate([high, value - high], 0).astype(BF16)


def joined(tile):
    wide = tile.astype(F32)
    return wide[:8] + wide[8:]


def rotated(tile, cosine, sine):
    return tile * cosine + pltpu.roll(tile, HD // 2, 1) * sine


def first_rows(shape):
    return lax.broadcasted_iota(jnp.int32, shape, 0) % 8 < STEPS


def exchanged(a, b):
    first = first_rows(a.shape)
    return (
        jnp.where(first, a, pltpu.roll(b, STEPS, 0)),
        jnp.where(first, pltpu.roll(a, STEPS, 0), b),
    )


def flat(matrix):
    return jnp.concatenate([matrix[i : i + 16] for i in range(0, matrix.shape[0], 16)], 1)


def pack_kernel(*refs):
    sources, outs, held = refs[:7], refs[7:10], refs[10:17]
    (a_ref, b_ref, own_ref), sems, out_sems = refs[17:20], refs[20], refs[21]
    targets = [*outs[:2], outs[2].at[:, pl.ds(0, own_ref.shape[1])]]
    copies = [
        pltpu.make_async_copy(source, target, sems.at[i])
        for i, (source, target) in enumerate(zip(sources, held))
    ]
    for copy in copies:
        copy.start()
    backs = [
        pltpu.make_async_copy(source, target, out_sems.at[i])
        for i, (source, target) in enumerate(zip((a_ref, b_ref, own_ref), targets))
    ]
    kd_ref, vd_ref, x_ref, gain_ref, lengths_ref, ku_ref, vu_ref = held
    own, depth = kd_ref.shape
    for slot, ref in enumerate((kd_ref, vd_ref)):
        copies[slot].wait()
        down = ref[...]
        if own < 16:
            down = jnp.concatenate([down, jnp.zeros((16 - own, depth), F32)], 0)
        a_ref[:, slot * depth : (slot + 1) * depth] = down.astype(BF16)
    backs[0].start()
    for copy in copies[2:]:
        copy.wait()
    x = jnp.concatenate([x_ref[0].astype(F32), x_ref[1].astype(F32)], 0)
    gain = gain_ref[...].astype(F32)
    scaled = jnp.concatenate(
        [x[:, i * 128 : (i + 1) * 128] * gain[i : i + 1] for i in range(depth // 128)], 1
    )
    scaled = jnp.concatenate([scaled[:, : depth // 2], scaled[:, depth // 2 :]], 0).astype(BF16)
    b_ref[:, : depth // 2] = scaled
    ups = jnp.concatenate([ku_ref[...], vu_ref[...]], 0).T.astype(BF16)
    b_ref[:, depth // 2 :] = flat(ups)
    backs[1].start()
    own_ref[:, : depth // 2] = scaled
    row = lax.broadcasted_iota(jnp.int32, (16, 128), 0)
    lengths = lengths_ref[...]
    length = jnp.where(row % 8 < STEPS, lengths[:, :1], lengths[:, 1:])
    length = jnp.where(row < 8, length // 64 * 64, length % 64)
    own_ref[:, depth // 2 : depth // 2 + 128] = length.astype(F32).astype(BF16)
    squares = jnp.broadcast_to(jnp.sum(x * x, 1, keepdims=True), (8, 128))
    own_ref[:, depth // 2 + 128 :] = split(squares)
    backs[2].start()
    for copy in backs:
        copy.wait()


def pack(lengths, hidden, gain, key_down, value_down, key_up, value_up):
    operands = [key_down, value_down, hidden, gain.reshape(-1, 128), lengths.reshape(1, 2)]
    operands += [key_up.T, value_up.T]
    depth = hidden.shape[2]
    ups = key_up.shape[0] * 8
    outs = [
        jax.ShapeDtypeStruct((16, 2 * depth), BF16),
        jax.ShapeDtypeStruct((16, depth // 2 + ups), BF16),
        jax.ShapeDtypeStruct((16, depth // 2 + 256 + ups), BF16),
    ]
    scratch = [*operands, *outs[:2], jax.ShapeDtypeStruct((16, depth // 2 + 256), BF16)]
    return pl.pallas_call(
        pack_kernel,
        in_specs=[HBM] * len(operands),
        out_specs=[HBM] * len(outs),
        out_shape=outs,
        scratch_shapes=[pltpu.VMEM(o.shape, o.dtype) for o in scratch]
        + [pltpu.SemaphoreType.DMA((len(operands),)), pltpu.SemaphoreType.DMA((len(outs),))],
        compiler_params=pltpu.CompilerParams(vmem_limit_bytes=WHOLE_VMEM),
        name="pack",
    )(*operands)


def tables(length):
    shape = length.shape
    row = lax.broadcasted_iota(jnp.int32, shape, 0)
    lane = lax.broadcasted_iota(jnp.int32, shape, 1)
    position = length + (row % STEPS).astype(F32)
    pair = lane % (HD // 2)
    frequency = jnp.ones(shape, F32)
    for bit in range(6):
        factor = ROPE_BASE ** (-(2.0 * 2**bit) / HD)
        frequency = jnp.where((pair >> bit) & 1 == 1, frequency * factor, frequency)
    cosine, sine = cosine_and_sine(position * frequency)
    return cosine, jnp.where(lane < HD // 2, -sine, sine)


def cosine_and_sine(angle):
    turns = jnp.floor(angle * (2.0 / math.pi) + 0.5)
    rest = ((angle - turns * 1.5703125) - turns * 4.8351287841796875e-4) - turns * 3.1391647e-7
    square = rest * rest
    sine = -1.9515295891e-4 * square + 8.3321608736e-3
    sine = (sine * square - 1.6666654611e-1) * square * rest + rest
    cosine = 2.443315711809948e-5 * square - 1.388731625493765e-3
    cosine = (cosine * square + 4.166664568298827e-2) * square * square - 0.5 * square + 1.0
    quadrant = turns.astype(jnp.int32)
    swap_them = (quadrant & 1) == 1
    cosine, sine = jnp.where(swap_them, sine, cosine), jnp.where(swap_them, cosine, sine)
    cosine = jnp.where(((quadrant + 1) & 2) == 2, -cosine, cosine)
    sine = jnp.where((quadrant & 2) == 2, -sine, sine)
    return cosine, sine


def rotated_rows(pairs, cosine, sine, q_ref, qrot_ref):
    zero = jnp.zeros((32, HD), F32)
    result = []
    for p in pairs:
        halves = [[], []]
        for e in range(2):
            for g in range(GROUP):
                at = slice(((2 * p + e) * GROUP + g) * HD, ((2 * p + e) * GROUP + g + 1) * HD)
                q = jnp.concatenate([q_ref[0, :, at].astype(F32), q_ref[1, :, at].astype(F32)], 0)
                halves[e].append(rotated(q, cosine, sine))
        if qrot_ref is not None:
            for g in range(GROUP):
                at = slice((p * GROUP + g) * HD, (p * GROUP + g + 1) * HD)
                qrot_ref[:, at] = jnp.concatenate([halves[0][g], halves[1][g]], 0).astype(BF16)
        mixed = [[exchanged(halves[e][g], halves[e][g + 4]) for g in range(4)] for e in range(2)]
        for s in range(2):
            rows = [jnp.concatenate([mixed[e][g][s] for g in range(4)], 0) for e in range(2)]
            result.append(
                jnp.concatenate(
                    [jnp.concatenate([rows[0], zero], 1), jnp.concatenate([zero, rows[1]], 1)], 0
                ).astype(BF16)
            )
    return result


def attend(pairs, masks, queries, k_ref, v_ref, between, out_ref):
    scores = []
    for i, p in enumerate(pairs):
        for s in range(2):
            keys = k_ref[s, :, 2 * p * HD : 2 * (p + 1) * HD]
            score = lax.dot_general(queries[2 * i + s], keys, NT, preferred_element_type=F32)
            scores.append(score + jnp.concatenate([masks[s]] * (score.shape[0] // 8), 0))
    between()
    scores = jnp.concatenate(scores, 0)
    top = rounded(jnp.maximum(jnp.max(scores, 1, keepdims=True), LOWEST_TOP))
    weights = jnp.exp2((scores - top) * EXPONENT).astype(BF16)
    total = jnp.sum(weights.astype(F32), 1, keepdims=True)
    high = rounded(total)
    columns = (top, high, total - high)
    lane8 = lax.broadcasted_iota(jnp.int32, (8, 128), 1)
    numers = []
    for i, p in enumerate(pairs):
        for s in range(2):
            at = slice(64 * (2 * i + s), 64 * (2 * i + s + 1))
            values = v_ref[s, :, 2 * p * HD : 2 * (p + 1) * HD]
            numers.append(jnp.dot(weights[at], values, preferred_element_type=F32))
    for i, p in enumerate(pairs):
        outs, ends = [[], []], []
        for e in range(2):
            back, stats = [], []
            for s in range(2):
                tile = jnp.zeros((8, 128), F32)
                for g in range(4):
                    row = 64 * (2 * i + s) + 32 * e + 8 * g
                    for slot, value in enumerate(columns):
                        tile = jnp.where(lane8 == slot * GROUP + g, value[row : row + 8], tile)
                stats.append(tile)
            for g in range(4):
                at = slice(32 * e + 8 * g, 32 * e + 8 * g + 8)
                cols = slice(e * HD, (e + 1) * HD)
                back.append(exchanged(numers[2 * i][at, cols], numers[2 * i + 1][at, cols]))
            outs[e] = [b[0] for b in back] + [b[1] for b in back]
            a, b = exchanged(*stats)
            ends.append(jnp.where(lane8 % 8 < 4, a, pltpu.roll(b, 4, 1)))
        for g in range(GROUP):
            at = slice(i * PAIR + g * HD, i * PAIR + (g + 1) * HD)
            out_ref[:, at] = jnp.concatenate([outs[0][g], outs[1][g]], 0).astype(BF16)
        out_ref[:, i * PAIR + GROUP * HD : (i + 1) * PAIR] = jnp.concatenate(ends, 0).astype(BF16)


def pair_at(i):
    return i ^ (lax.axis_index("tensor") % 2 * 2)


def local_kernel(
    x_hbm, q_hbm, k_hbm, v_hbm, wk_hbm, wv_hbm,
    keep_ref, send_ref, base_ref, qrot_ref, table_ref,
    x_ref, q_ref, k_ref, v_ref, wk_ref, wv_ref, x_sem, q_sem, cache_sem, weight_sem,
):
    pairs = k_hbm.shape[2] // (2 * HD)
    chunks = wk_hbm.shape[0] // CHUNK
    width = wk_hbm.shape[1]
    core = lax.axis_index("tensor") % 2
    x_copy = pltpu.make_async_copy(x_hbm.at[:, pl.ds(0, x_ref.shape[1])], x_ref, x_sem)
    x_copy.start()
    groups = []
    for h in range(2):
        copies = []
        trio = ((q_hbm, q_ref, q_sem.at[h]), (k_hbm, k_ref, cache_sem.at[h, 0]))
        for source, target, sem in (*trio, (v_hbm, v_ref, cache_sem.at[h, 1])):
            size = source.shape[2] // 2
            start = pl.multiple_of((core ^ h) * size, size)
            copies.append(
                pltpu.make_async_copy(
                    source.at[:, :, pl.ds(start, size)],
                    target.at[:, :, pl.ds(h * size, size)],
                    sem,
                )
            )
        groups.append(copies)
    for h in range(2):
        groups[h][0].start()
    for copy in groups[0][1:]:
        copy.start()
    weights = []
    for c in range(chunks):
        at = pl.ds(c * CHUNK, CHUNK)
        weights.append(
            [
                pltpu.make_async_copy(source.at[at], target.at[at], weight_sem.at[c, i])
                for i, (source, target) in enumerate(((wk_hbm, wk_ref), (wv_hbm, wv_ref)))
            ]
        )
    def start(copies):
        for copy in copies:
            copy.start()

    x_copy.wait()
    start(groups[1][1:])
    for copies in weights[: chunks // 4]:
        start(copies)
    half = wk_hbm.shape[0] // 2
    x = x_ref[:, :half].astype(F32)
    x = jnp.concatenate([x[:8], x[8:]], 1).astype(BF16)
    length = joined(x_ref[:, half : half + 128])
    cosine, sine = tables(length)
    table_ref[...] = jnp.concatenate([joined(x_ref[:, half + 128 : half + 256]), cosine, sine], 0)
    limit = length - (lax.axis_index("tensor") * k_hbm.shape[1]).astype(F32)
    place = lax.broadcasted_iota(jnp.int32, (8, k_hbm.shape[1]), 1).astype(F32)
    masks = [
        jnp.where(place < limit[STEPS * s : STEPS * s + 1, :1], 0.0, MASKED_SCORE) for s in range(2)
    ]
    queries = []
    for h in range(2):
        groups[h][0].wait()
        own = range(h * pairs // 2, (h + 1) * pairs // 2)
        queries.append(rotated_rows(own, cosine, sine, q_ref, None if h else qrot_ref))
    parts = []

    def project(c):
        at = slice(c * CHUNK, (c + 1) * CHUNK)
        halves = []
        for copy, ref in zip(weights[c], (wk_ref, wv_ref)):
            copy.wait()
            halves.append(jnp.dot(x[:, at], ref[at], preferred_element_type=F32))
        parts.append(jnp.concatenate(halves, 0))

    def between(h):
        groups[h][2].wait()
        if h == 0:
            for copies in weights[chunks // 2 : 3 * chunks // 4]:
                start(copies)
        else:
            for c in range(chunks // 2):
                project(c)

    for h, out_ref in enumerate((keep_ref, send_ref)):
        groups[h][1].wait()
        for copies in weights[3 * chunks // 4 :] if h else weights[chunks // 4 : chunks // 2]:
            start(copies)
        attend(
            range(h * pairs // 2, (h + 1) * pairs // 2),
            masks, queries[h], k_ref, v_ref, functools.partial(between, h), out_ref,
        )
    for c in range(chunks // 2, chunks):
        project(c)
    total = functools.reduce(jnp.add, parts)
    lower, upper = total[:, : width // 2], total[:, width // 2 :]
    base_ref[:, : width // 2] = jnp.where(core == 0, lower, upper)
    base_ref[:, width // 2 :] = jnp.where(core == 0, upper, lower)


def local(message, queries, key_cache, value_cache, key_weight, value_weight):
    seqs, length, width = key_cache.shape
    depth = key_weight.shape[0]
    pairs = width // (2 * HD)
    operands = [message, queries, key_cache, value_cache, key_weight, value_weight]
    return pl.pallas_call(
        local_kernel,
        in_specs=[HBM] * 6,
        out_specs=[VMEM] * 5,
        out_shape=[
            jax.ShapeDtypeStruct((16, pairs // 2 * PAIR), BF16),
            jax.ShapeDtypeStruct((16, pairs // 2 * PAIR), BF16),
            jax.ShapeDtypeStruct((16, width), F32),
            jax.ShapeDtypeStruct((16, pairs // 2 * GROUP * HD), BF16),
            jax.ShapeDtypeStruct((24, 128), F32),
        ],
        scratch_shapes=[pltpu.VMEM((16, depth // 2 + 256), BF16)]
        + [pltpu.VMEM(o.shape, BF16) for o in operands[1:]]
        + [
            pltpu.SemaphoreType.DMA,
            pltpu.SemaphoreType.DMA((2,)),
            pltpu.SemaphoreType.DMA((2, 2)),
            pltpu.SemaphoreType.DMA((depth // CHUNK, 2)),
        ],
        compiler_params=pltpu.CompilerParams(vmem_limit_bytes=LOCAL_VMEM),
        cost_estimate=pl.CostEstimate(
            flops=4 * 64 * 256 * seqs * length * pairs + 4 * 16 * depth * width,
            bytes_accessed=4 * seqs * length * width + 4 * depth * width,
            transcendentals=64 * seqs * length * pairs,
        ),
        name="local",
    )(*operands)


def rank_kernel(n, rows, depth, *refs):
    base_ref, table_ref, own_ref, near_ref = refs[:4]
    tokens, (out_ref, *has) = refs[4 : 4 + n], refs[4 + n :]
    half = base_ref.shape[1] // 2
    place = lax.axis_index("dp")
    x = []
    for ref in tokens:
        part = ref[:, : depth // 2].astype(F32)
        x.append(jnp.concatenate([part[:8], part[8:]], 1))
    x = jnp.concatenate(x, 0).astype(BF16)
    down = jnp.concatenate(
        [ref[:, at : at + depth] for at in (0, depth) for ref in (own_ref, near_ref)], 0
    )
    products = lax.dot_general(x, down, NT, preferred_element_type=F32)
    products = jnp.concatenate([products, jnp.zeros_like(products)], 1)
    lane = lax.broadcasted_iota(jnp.int32, products.shape, 1)
    z = None
    for i in range(4):
        part = jnp.where(lane // 16 == i, products, 0.0)
        column = (place ^ (i % 2)) * rows + i // 2 * RANK
        part = pltpu.roll(part, (column + 128 - 16 * i) % 128, 1)
        z = part if z is None else z + part
    out_ref[:, :half] = base_ref[:, half:].astype(BF16)
    out_ref[:, half : half + 128] = split(table_ref[:8])
    for i in range(n):
        at = half + 128 * (i + 1)
        out_ref[:, at : at + 128] = split(z[8 * i : 8 * i + 8])
    for ref in has:
        here = place // 2 == lax.axis_index("tensor") % 2
        mine, far = (token[:, depth // 2 :].astype(F32) for token in tokens[:2])
        ref[:, : mine.shape[1]] = jnp.where(here, mine, far).astype(BF16)
        ref[:, mine.shape[1] :] = jnp.zeros((16, ref.shape[1] - mine.shape[1]), BF16)


def rank_products(rows, depth, columns, base, table, own, near, tokens):
    n = len(tokens)
    out_shape = [jax.ShapeDtypeStruct((16, base.shape[1] // 2 + 128 * (n + 1)), BF16)]
    if columns:
        out_shape.append(jax.ShapeDtypeStruct((16, columns), BF16))
    return pl.pallas_call(
        functools.partial(rank_kernel, n, rows, depth),
        in_specs=[VMEM] * (4 + n),
        out_specs=[VMEM] * len(out_shape),
        out_shape=out_shape,
        compiler_params=pltpu.CompilerParams(vmem_limit_bytes=32 * MEBI),
        name="rank_products",
    )(base, table, own, near, *tokens)


def broadcast_lane(tile, lane):
    return jnp.broadcast_to(tile[:, lane : lane + 1], tile.shape)


def combine_part_kernel(base_ref, mine_ref, theirs_ref, cache_ref, out_ref, *replies):
    half = base_ref.shape[1] // 2
    own = base_ref[:, :half] + theirs_ref[:, :half].astype(F32)
    out_ref[:, :half] = own.astype(BF16)
    sums = mine_ref[:, half:].astype(F32) + theirs_ref[:, half:].astype(F32)
    sums = split(sums[:8] + sums[8:])
    out_ref[:, half : half + 256] = sums[:, :256]
    out_ref[:, half + 256 :] = cache_ref[...]
    for i, ref in enumerate(replies):
        ref[...] = sums[:, 128 * (i + 2) : 128 * (i + 3)]


def combine_part(n, base, mine, theirs, cache):
    shapes = [(16, base.shape[1] // 2 + 256 + cache.shape[1])] + [(16, 128)] * n
    return pl.pallas_call(
        combine_part_kernel,
        in_specs=[VMEM] * 4,
        out_specs=[VMEM] * len(shapes),
        out_shape=[jax.ShapeDtypeStruct(shape, BF16) for shape in shapes],
        compiler_params=pltpu.CompilerParams(vmem_limit_bytes=32 * MEBI),
        name="combine_part",
    )(base, mine, theirs, cache)


def combine_cache_kernel(a_ref, b_ref, _, out_ref):
    lane = lax.broadcasted_iota(jnp.int32, (16, 128), 1)
    for p in range(out_ref.shape[1] // PAIR):
        end = slice(p * PAIR + GROUP * HD, (p + 1) * PAIR)
        a, b = a_ref[:, end].astype(F32), b_ref[:, end].astype(F32)
        top = jnp.maximum(a, b)
        fa = jnp.exp2(jnp.minimum(a - top, 0.0) * EXPONENT)
        fb = jnp.exp2(jnp.minimum(b - top, 0.0) * EXPONENT)
        total = fa * totals(a) + fb * totals(b)
        high = rounded(total)
        stats = jnp.where(lane < GROUP, top, 0.0)
        stats = jnp.where(lane // GROUP == 1, pltpu.roll(high, GROUP, 1), stats)
        stats = jnp.where(lane // GROUP == 2, pltpu.roll(total - high, 2 * GROUP, 1), stats)
        out_ref[:, end] = stats.astype(BF16)
        for g in range(GROUP):
            at = slice(p * PAIR + g * HD, p * PAIR + (g + 1) * HD)
            out_ref[:, at] = (
                broadcast_lane(fa, g) * a_ref[:, at].astype(F32)
                + broadcast_lane(fb, g) * b_ref[:, at].astype(F32)
            ).astype(BF16)


def totals(stats):
    return pltpu.roll(stats, 128 - GROUP, 1) + pltpu.roll(stats, 128 - 2 * GROUP, 1)


def combine_cache(a, b, earlier):
    return pl.pallas_call(
        combine_cache_kernel,
        in_specs=[VMEM] * 3,
        out_specs=VMEM,
        out_shape=jax.ShapeDtypeStruct(a.shape, BF16),
        compiler_params=pltpu.CompilerParams(vmem_limit_bytes=32 * MEBI),
        name="combine_cache",
    )(a, b, earlier)


def merge_kernel(n, paired, width_all, *refs):
    table_ref, qrot_ref, pa_ref, pb_ref = refs[:4]
    backs, (ua_ref, ub_ref, out_ref) = refs[4 : 4 + n], refs[4 + n :]
    pairs = qrot_ref.shape[1] // (GROUP * HD)
    width = pairs * 2 * HD
    cosine, sine = table_ref[8:16], table_ref[16:]
    head = width + 256
    sums = pa_ref[:, :head].astype(F32) + pb_ref[:, :head].astype(F32)
    tail = sums[:8, width : width + 256] + sums[8:, width : width + 256]
    squares, z = tail[:, :128], tail[:, 128:]
    for ref in backs:
        z = z + joined(ref[...])
    lane8 = lax.broadcasted_iota(jnp.int32, (8, 128), 1)
    z = jnp.concatenate(
        [jnp.where(lane8 < RANK, z, 0.0), jnp.where(lane8 < RANK, 0.0, z)], 0
    ).astype(BF16)
    adapted = []
    for ref in (ua_ref, ub_ref):
        ups = jnp.concatenate([ref[:, i : i + 128] for i in range(0, 16 * HD, 128)], 0)
        adapted.append(lax.dot_general(z, ups, NT, preferred_element_type=F32))
    if paired:
        even = lax.axis_index("dp") % 2 == 0
        a, b = adapted
        adapted = [jnp.where(even, a, b), jnp.where(even, b, a)]
    total = sums[:, :width] + jnp.concatenate(adapted, 1)
    scale = lax.rsqrt(squares / width_all + EPSILON)
    lane = lax.broadcasted_iota(jnp.int32, (16, 128), 1)
    step = lax.broadcasted_iota(jnp.int32, (16, 128), 0) % STEPS
    first = first_rows((8, 128))

    def of_step(tiles, j):
        return jnp.concatenate(
            [
                jnp.where(first, tile[j : j + 1], tile[STEPS + j : STEPS + j + 1])
                for tile in tiles
            ],
            0,
        )

    for p in range(pairs):
        new_keys, new_values = [], []
        for e in range(2):
            at = slice((2 * p + e) * HD, (2 * p + e + 1) * HD)
            new_keys.append(rounded(rotated(total[:8, at] * scale, cosine, sine)))
            new_values.append(rounded(total[8:, at] * scale))
            fresh = jnp.concatenate([new_keys[e], new_values[e]], 0)
            start = pairs * GROUP * HD + (2 * p + e) * HD
            out_ref[:, start : start + HD] = fresh.astype(BF16)
        keys = [of_step(new_keys, j) for j in range(STEPS)]
        values = [of_step(new_values, j) for j in range(STEPS)]
        scores = [jnp.zeros((16, 128), F32) for _ in range(STEPS)]
        for g in range(GROUP):
            q = qrot_ref[:, (p * GROUP + g) * HD : (p * GROUP + g + 1) * HD].astype(F32)
            for j in range(STEPS):
                dot = jnp.sum(q * keys[j], 1, keepdims=True)
                scores[j] = jnp.where(lane == g, dot, scores[j])
        scores = [jnp.where(j <= step, scores[j], MASKED_SCORE) for j in range(STEPS)]
        end = slice(head + p * PAIR + GROUP * HD, head + (p + 1) * PAIR)
        stats = [ref[:, end].astype(F32) for ref in (pa_ref, pb_ref)]
        top = functools.reduce(jnp.maximum, scores + stats)
        fresh = [rounded(jnp.exp2((scores[j] - top) * EXPONENT)) for j in range(STEPS)]
        factors = [jnp.exp2(jnp.minimum(s - top, 0.0) * EXPONENT) for s in stats]
        denom = functools.reduce(jnp.add, fresh)
        for factor, s in zip(factors, stats):
            denom = denom + factor * totals(s)
        inverse = 1.0 / denom
        coefficients = [c * inverse for c in fresh + factors]
        for g in range(GROUP):
            at = slice(head + p * PAIR + g * HD, head + p * PAIR + (g + 1) * HD)
            terms = values + [ref[:, at].astype(F32) for ref in (pa_ref, pb_ref)]
            tile = jnp.zeros((16, 128), F32)
            for c, term in zip(coefficients, terms):
                tile = tile + broadcast_lane(c, g) * term
            out_ref[:, (p * GROUP + g) * HD : (p * GROUP + g + 1) * HD] = tile.astype(BF16)


def merge(paired, width_all, table, qrot, parts, backs, ups):
    operands = [table, qrot, *parts, *backs, *ups]
    pairs = qrot.shape[1] // (GROUP * HD)
    return pl.pallas_call(
        functools.partial(merge_kernel, len(backs), paired, width_all),
        in_specs=[VMEM] * len(operands),
        out_specs=VMEM,
        out_shape=jax.ShapeDtypeStruct((16, pairs * (GROUP + 2) * HD), BF16),
        compiler_params=pltpu.CompilerParams(vmem_limit_bytes=32 * MEBI),
        name="merge",
    )(*operands)


def place_kernel(mine_ref, theirs_ref, keys_out, values_out, out_ref):
    pairs = mine_ref.shape[1] // ((GROUP + 2) * HD)
    for c, ref in enumerate((mine_ref, theirs_ref)):
        for p in range(pairs):
            pair = pair_at(c * pairs + p)
            tiles = ref[:, p * GROUP * HD : (p + 1) * GROUP * HD].astype(F32)
            size = GROUP * HD
            for e in range(2):
                at = pl.ds(pl.multiple_of((2 * pair + e) * size, size), size)
                for s in range(2):
                    rows = slice(8 * e + 4 * s, 8 * e + 4 * s + 4)
                    out_ref[s, :, at] = tiles[rows].astype(BF16)
            start = pairs * GROUP * HD + p * 2 * HD
            fresh = ref[:, start : start + 2 * HD].astype(F32)
            at = pl.ds(pl.multiple_of(pair * 2 * HD, 2 * HD), 2 * HD)
            for i, out in enumerate((keys_out, values_out)):
                for s in range(2):
                    rows = slice(8 * i + 4 * s, 8 * i + 4 * s + 4)
                    out[s, :, at] = fresh[rows].astype(BF16)


def place(width, mine, theirs):
    return pl.pallas_call(
        place_kernel,
        in_specs=[VMEM] * 2,
        out_specs=[VMEM] * 3,
        out_shape=[
            jax.ShapeDtypeStruct((2, STEPS, width), BF16),
            jax.ShapeDtypeStruct((2, STEPS, width), BF16),
            jax.ShapeDtypeStruct((2, STEPS, GROUP * width), BF16),
        ],
        compiler_params=pltpu.CompilerParams(vmem_limit_bytes=32 * MEBI),
        name="place",
    )(mine, theirs)


def swap(value, axis, n, distance):
    return lax.ppermute(value, axis, [(i, i ^ distance) for i in range(n)])


def shards(
    n_dp,
    n_tensor,
    hidden,
    norm_gain,
    queries,
    key_weight,
    value_weight,
    key_down,
    key_up,
    value_down,
    value_up,
    key_cache,
    value_cache,
    lengths,
):
    depth, width = key_weight.shape
    rows = key_down.shape[0]
    to_dp = lambda value, distance: swap(value, "dp", n_dp, distance)
    to_tensor = lambda value, distance: swap(value, "tensor", n_tensor, distance)
    partners = range(2, n_dp, 2)
    n = len(partners)
    paired = n_dp == 4

    down, tokens, own = pack(
        lengths, hidden, norm_gain, key_down, value_down, key_up, value_up
    )
    near = to_dp(down, 1)
    sent = [to_dp(tokens, d) for d in partners]
    keep, send, base, qrot, table = local(
        own, queries, key_cache, value_cache, key_weight, value_weight
    )
    received = to_tensor(send, 1)
    columns = UP_COLUMNS if paired else 0
    message, *has = rank_products(rows, depth, columns, base, table, down, near, [tokens, *sent])
    if paired:
        ups = [has[0], to_dp(has[0], 1)]
    else:
        ups = lax.all_gather(tokens[:, depth // 2 :], "dp")
        ups = ups.reshape(n_dp, 16, -1, 128).transpose(0, 2, 1, 3)
        ups = ups.reshape(2, 2, 16, 16, 128).transpose(0, 1, 3, 2, 4).reshape(2, 2, 16, -1)
        ups = lax.dynamic_index_in_dim(ups, lax.axis_index("tensor") % 2, 0, keepdims=False)
        ups = [ups[0], ups[1]]
    cache = combine_cache(keep, received, message)
    part, *replies = combine_part(n, base, message, to_tensor(message, 1), cache)
    part_far = to_tensor(part, 2)
    places = [(s, t) for s in range(n_dp) for t in range(n_tensor)]
    backs = []
    for reply, d in zip(replies, partners):
        for e in (0, 2):
            perm = [(s * n_tensor + t, (s ^ d) * n_tensor + (t ^ e)) for s, t in places]
            backs.append(lax.ppermute(reply, ("dp", "tensor"), perm))
    merged = merge(
        paired,
        float(depth * n_tensor),
        table,
        qrot,
        (part, part_far),
        backs,
        ups,
    )
    return place(width, merged, to_tensor(merged, 1))


def solution(mesh):
    body = functools.partial(shards, mesh.shape["dp"], mesh.shape["tensor"])
    return jax.shard_map(
        body,
        mesh=mesh,
        in_specs=(
            P(("groups", "dp"), None, "tensor"),
            P("tensor"),
            P(("groups", "dp"), None, None),
            P("tensor", None),
            P("tensor", None),
            P(("groups", "dp"), "tensor"),
            P(("groups", "dp"), None),
            P(("groups", "dp"), "tensor"),
            P(("groups", "dp"), None),
            P(("groups", "dp"), "tensor", None),
            P(("groups", "dp"), "tensor", None),
            P(("groups", "dp")),
        ),
        out_specs=(
            P(("groups", "dp"), None, None),
            P(("groups", "dp"), None, None),
            P(("groups", "dp"), None, None),
        ),
        check_vma=False,
    )
```

```python
import functools
import math

import jax
import jax.numpy as jnp
from jax import lax
from jax.experimental import pallas as pl
from jax.experimental.pallas import tpu as pltpu
from jax.sharding import PartitionSpec as P

HD = 128
GROUP = 8
STEPS = 4
RANK = 64
EPSILON = 1e-05
ROPE_BASE = 500000.0
MASKED_SCORE = -1e30
LOWEST_TOP = -1e20
EXPONENT = math.log2(math.e) / math.sqrt(HD)
PAIR = GROUP * HD + 128
UP_COLUMNS = 3200
CHUNK = 256

F32 = jnp.float32
BF16 = jnp.bfloat16
NT = (((1,), (1,)), ((), ()))
VMEM = pl.BlockSpec(memory_space=pltpu.VMEM)
HBM = pl.BlockSpec(memory_space=pltpu.HBM)
MEBI = 2**20
WHOLE_VMEM = 65000 * 1024
LOCAL_VMEM = 54900 * 1024


def rounded(value):
    return value.astype(BF16).astype(F32)


def split(value):
    high = rounded(value)
    return jnp.concatenate([high, value - high], 0).astype(BF16)


def joined(tile):
    wide = tile.astype(F32)
    return wide[:8] + wide[8:]


def rotated(tile, cosine, sine):
    return tile * cosine + pltpu.roll(tile, HD // 2, 1) * sine


def first_rows(shape):
    return lax.broadcasted_iota(jnp.int32, shape, 0) % 8 < STEPS


def exchanged(a, b):
    first = first_rows(a.shape)
    return (
        jnp.where(first, a, pltpu.roll(b, STEPS, 0)),
        jnp.where(first, pltpu.roll(a, STEPS, 0), b),
    )


def flat(matrix):
    return jnp.concatenate([matrix[i : i + 16] for i in range(0, matrix.shape[0], 16)], 1)


def pack_kernel(*refs):
    sources, outs, held = refs[:7], refs[7:10], refs[10:17]
    (a_ref, b_ref, own_ref), sems, out_sems = refs[17:20], refs[20], refs[21]
    targets = [*outs[:2], outs[2].at[:, pl.ds(0, own_ref.shape[1])]]
    copies = [
        pltpu.make_async_copy(source, target, sems.at[i])
        for i, (source, target) in enumerate(zip(sources, held))
    ]
    for copy in copies:
        copy.start()
    backs = [
        pltpu.make_async_copy(source, target, out_sems.at[i])
        for i, (source, target) in enumerate(zip((a_ref, b_ref, own_ref), targets))
    ]
    kd_ref, vd_ref, x_ref, gain_ref, lengths_ref, ku_ref, vu_ref = held
    own, depth = kd_ref.shape
    for slot, ref in enumerate((kd_ref, vd_ref)):
        copies[slot].wait()
        down = ref[...]
        if own < 16:
            down = jnp.concatenate([down, jnp.zeros((16 - own, depth), F32)], 0)
        a_ref[:, slot * depth : (slot + 1) * depth] = down.astype(BF16)
    backs[0].start()
    for copy in copies[2:]:
        copy.wait()
    x = jnp.concatenate([x_ref[0].astype(F32), x_ref[1].astype(F32)], 0)
    gain = gain_ref[...].astype(F32)
    scaled = jnp.concatenate(
        [x[:, i * 128 : (i + 1) * 128] * gain[i : i + 1] for i in range(depth // 128)], 1
    )
    scaled = jnp.concatenate([scaled[:, : depth // 2], scaled[:, depth // 2 :]], 0).astype(BF16)
    b_ref[:, : depth // 2] = scaled
    ups = jnp.concatenate([ku_ref[...], vu_ref[...]], 0).T.astype(BF16)
    b_ref[:, depth // 2 :] = flat(ups)
    backs[1].start()
    own_ref[:, : depth // 2] = scaled
    row = lax.broadcasted_iota(jnp.int32, (16, 128), 0)
    lengths = lengths_ref[...]
    length = jnp.where(row % 8 < STEPS, lengths[:, :1], lengths[:, 1:])
    length = jnp.where(row < 8, length // 64 * 64, length % 64)
    own_ref[:, depth // 2 : depth // 2 + 128] = length.astype(F32).astype(BF16)
    squares = jnp.broadcast_to(jnp.sum(x * x, 1, keepdims=True), (8, 128))
    own_ref[:, depth // 2 + 128 :] = split(squares)
    backs[2].start()
    for copy in backs:
        copy.wait()


def pack(lengths, hidden, gain, key_down, value_down, key_up, value_up):
    operands = [key_down, value_down, hidden, gain.reshape(-1, 128), lengths.reshape(1, 2)]
    operands += [key_up.T, value_up.T]
    depth = hidden.shape[2]
    ups = key_up.shape[0] * 8
    outs = [
        jax.ShapeDtypeStruct((16, 2 * depth), BF16),
        jax.ShapeDtypeStruct((16, depth // 2 + ups), BF16),
        jax.ShapeDtypeStruct((16, depth // 2 + 256 + ups), BF16),
    ]
    scratch = [*operands, *outs[:2], jax.ShapeDtypeStruct((16, depth // 2 + 256), BF16)]
    return pl.pallas_call(
        pack_kernel,
        in_specs=[HBM] * len(operands),
        out_specs=[HBM] * len(outs),
        out_shape=outs,
        scratch_shapes=[pltpu.VMEM(o.shape, o.dtype) for o in scratch]
        + [pltpu.SemaphoreType.DMA((len(operands),)), pltpu.SemaphoreType.DMA((len(outs),))],
        compiler_params=pltpu.CompilerParams(vmem_limit_bytes=WHOLE_VMEM),
        name="pack",
    )(*operands)


def tables(length):
    shape = length.shape
    row = lax.broadcasted_iota(jnp.int32, shape, 0)
    lane = lax.broadcasted_iota(jnp.int32, shape, 1)
    position = length + (row % STEPS).astype(F32)
    pair = lane % (HD // 2)
    frequency = jnp.ones(shape, F32)
    for bit in range(6):
        factor = ROPE_BASE ** (-(2.0 * 2**bit) / HD)
        frequency = jnp.where((pair >> bit) & 1 == 1, frequency * factor, frequency)
    cosine, sine = cosine_and_sine(position * frequency)
    return cosine, jnp.where(lane < HD // 2, -sine, sine)


def cosine_and_sine(angle):
    turns = jnp.floor(angle * (2.0 / math.pi) + 0.5)
    rest = ((angle - turns * 1.5703125) - turns * 4.8351287841796875e-4) - turns * 3.1391647e-7
    square = rest * rest
    sine = -1.9515295891e-4 * square + 8.3321608736e-3
    sine = (sine * square - 1.6666654611e-1) * square * rest + rest
    cosine = 2.443315711809948e-5 * square - 1.388731625493765e-3
    cosine = (cosine * square + 4.166664568298827e-2) * square * square - 0.5 * square + 1.0
    quadrant = turns.astype(jnp.int32)
    swap_them = (quadrant & 1) == 1
    cosine, sine = jnp.where(swap_them, sine, cosine), jnp.where(swap_them, cosine, sine)
    cosine = jnp.where(((quadrant + 1) & 2) == 2, -cosine, cosine)
    sine = jnp.where((quadrant & 2) == 2, -sine, sine)
    return cosine, sine


def rotated_rows(pairs, cosine, sine, q_ref, qrot_ref):
    zero = jnp.zeros((32, HD), F32)
    result = []
    for p in pairs:
        halves = [[], []]
        for e in range(2):
            for g in range(GROUP):
                at = slice(((2 * p + e) * GROUP + g) * HD, ((2 * p + e) * GROUP + g + 1) * HD)
                q = jnp.concatenate([q_ref[0, :, at].astype(F32), q_ref[1, :, at].astype(F32)], 0)
                halves[e].append(rotated(q, cosine, sine))
        if qrot_ref is not None:
            for g in range(GROUP):
                at = slice((p * GROUP + g) * HD, (p * GROUP + g + 1) * HD)
                qrot_ref[:, at] = jnp.concatenate([halves[0][g], halves[1][g]], 0).astype(BF16)
        mixed = [[exchanged(halves[e][g], halves[e][g + 4]) for g in range(4)] for e in range(2)]
        for s in range(2):
            rows = [jnp.concatenate([mixed[e][g][s] for g in range(4)], 0) for e in range(2)]
            result.append(
                jnp.concatenate(
                    [jnp.concatenate([rows[0], zero], 1), jnp.concatenate([zero, rows[1]], 1)], 0
                ).astype(BF16)
            )
    return result


def attend(pairs, masks, queries, k_ref, v_ref, between, out_ref):
    scores = []
    for i, p in enumerate(pairs):
        for s in range(2):
            keys = k_ref[s, :, 2 * p * HD : 2 * (p + 1) * HD]
            score = lax.dot_general(queries[2 * i + s], keys, NT, preferred_element_type=F32)
            scores.append(score + jnp.concatenate([masks[s]] * (score.shape[0] // 8), 0))
    between()
    scores = jnp.concatenate(scores, 0)
    top = rounded(jnp.maximum(jnp.max(scores, 1, keepdims=True), LOWEST_TOP))
    weights = jnp.exp2((scores - top) * EXPONENT).astype(BF16)
    total = jnp.sum(weights.astype(F32), 1, keepdims=True)
    high = rounded(total)
    columns = (top, high, total - high)
    lane8 = lax.broadcasted_iota(jnp.int32, (8, 128), 1)
    numers = []
    for i, p in enumerate(pairs):
        for s in range(2):
            at = slice(64 * (2 * i + s), 64 * (2 * i + s + 1))
            values = v_ref[s, :, 2 * p * HD : 2 * (p + 1) * HD]
            numers.append(jnp.dot(weights[at], values, preferred_element_type=F32))
    for i, p in enumerate(pairs):
        outs, ends = [[], []], []
        for e in range(2):
            back, stats = [], []
            for s in range(2):
                tile = jnp.zeros((8, 128), F32)
                for g in range(4):
                    row = 64 * (2 * i + s) + 32 * e + 8 * g
                    for slot, value in enumerate(columns):
                        tile = jnp.where(lane8 == slot * GROUP + g, value[row : row + 8], tile)
                stats.append(tile)
            for g in range(4):
                at = slice(32 * e + 8 * g, 32 * e + 8 * g + 8)
                cols = slice(e * HD, (e + 1) * HD)
                back.append(exchanged(numers[2 * i][at, cols], numers[2 * i + 1][at, cols]))
            outs[e] = [b[0] for b in back] + [b[1] for b in back]
            a, b = exchanged(*stats)
            ends.append(jnp.where(lane8 % 8 < 4, a, pltpu.roll(b, 4, 1)))
        for g in range(GROUP):
            at = slice(i * PAIR + g * HD, i * PAIR + (g + 1) * HD)
            out_ref[:, at] = jnp.concatenate([outs[0][g], outs[1][g]], 0).astype(BF16)
        out_ref[:, i * PAIR + GROUP * HD : (i + 1) * PAIR] = jnp.concatenate(ends, 0).astype(BF16)


def pair_at(i):
    return i ^ (lax.axis_index("tensor") % 2 * 2)


def local_kernel(
    x_hbm, q_hbm, k_hbm, v_hbm, wk_hbm, wv_hbm,
    keep_ref, send_ref, base_ref, qrot_ref, table_ref,
    x_ref, q_ref, k_ref, v_ref, wk_ref, wv_ref, x_sem, q_sem, cache_sem, weight_sem,
):
    pairs = k_hbm.shape[2] // (2 * HD)
    chunks = wk_hbm.shape[0] // CHUNK
    width = wk_hbm.shape[1]
    core = lax.axis_index("tensor") % 2
    x_copy = pltpu.make_async_copy(x_hbm.at[:, pl.ds(0, x_ref.shape[1])], x_ref, x_sem)
    x_copy.start()
    groups = []
    for h in range(2):
        copies = []
        trio = ((q_hbm, q_ref, q_sem.at[h]), (k_hbm, k_ref, cache_sem.at[h, 0]))
        for source, target, sem in (*trio, (v_hbm, v_ref, cache_sem.at[h, 1])):
            size = source.shape[2] // 2
            start = pl.multiple_of((core ^ h) * size, size)
            copies.append(
                pltpu.make_async_copy(
                    source.at[:, :, pl.ds(start, size)],
                    target.at[:, :, pl.ds(h * size, size)],
                    sem,
                )
            )
        groups.append(copies)
    for h in range(2):
        groups[h][0].start()
    for copy in groups[0][1:]:
        copy.start()
    weights = []
    for c in range(chunks):
        at = pl.ds(c * CHUNK, CHUNK)
        weights.append(
            [
                pltpu.make_async_copy(source.at[at], target.at[at], weight_sem.at[c, i])
                for i, (source, target) in enumerate(((wk_hbm, wk_ref), (wv_hbm, wv_ref)))
            ]
        )
    def start(copies):
        for copy in copies:
            copy.start()

    x_copy.wait()
    start(groups[1][1:])
    for copies in weights[: chunks // 4]:
        start(copies)
    half = wk_hbm.shape[0] // 2
    x = x_ref[:, :half].astype(F32)
    x = jnp.concatenate([x[:8], x[8:]], 1).astype(BF16)
    length = joined(x_ref[:, half : half + 128])
    cosine, sine = tables(length)
    table_ref[...] = jnp.concatenate([joined(x_ref[:, half + 128 : half + 256]), cosine, sine], 0)
    limit = length - (lax.axis_index("tensor") * k_hbm.shape[1]).astype(F32)
    place = lax.broadcasted_iota(jnp.int32, (8, k_hbm.shape[1]), 1).astype(F32)
    masks = [
        jnp.where(place < limit[STEPS * s : STEPS * s + 1, :1], 0.0, MASKED_SCORE) for s in range(2)
    ]
    queries = []
    for h in range(2):
        groups[h][0].wait()
        own = range(h * pairs // 2, (h + 1) * pairs // 2)
        queries.append(rotated_rows(own, cosine, sine, q_ref, None if h else qrot_ref))
    parts = []

    def project(c):
        at = slice(c * CHUNK, (c + 1) * CHUNK)
        halves = []
        for copy, ref in zip(weights[c], (wk_ref, wv_ref)):
            copy.wait()
            halves.append(jnp.dot(x[:, at], ref[at], preferred_element_type=F32))
        parts.append(jnp.concatenate(halves, 0))

    def between(h):
        groups[h][2].wait()
        if h == 0:
            for copies in weights[chunks // 2 : 3 * chunks // 4]:
                start(copies)
        else:
            for c in range(chunks // 2):
                project(c)

    for h, out_ref in enumerate((keep_ref, send_ref)):
        groups[h][1].wait()
        for copies in weights[3 * chunks // 4 :] if h else weights[chunks // 4 : chunks // 2]:
            start(copies)
        attend(
            range(h * pairs // 2, (h + 1) * pairs // 2),
            masks, queries[h], k_ref, v_ref, functools.partial(between, h), out_ref,
        )
    for c in range(chunks // 2, chunks):
        project(c)
    total = functools.reduce(jnp.add, parts)
    lower, upper = total[:, : width // 2], total[:, width // 2 :]
    base_ref[:, : width // 2] = jnp.where(core == 0, lower, upper)
    base_ref[:, width // 2 :] = jnp.where(core == 0, upper, lower)


def local(message, queries, key_cache, value_cache, key_weight, value_weight):
    seqs, length, width = key_cache.shape
    depth = key_weight.shape[0]
    pairs = width // (2 * HD)
    operands = [message, queries, key_cache, value_cache, key_weight, value_weight]
    return pl.pallas_call(
        local_kernel,
        in_specs=[HBM] * 6,
        out_specs=[VMEM] * 5,
        out_shape=[
            jax.ShapeDtypeStruct((16, pairs // 2 * PAIR), BF16),
            jax.ShapeDtypeStruct((16, pairs // 2 * PAIR), BF16),
            jax.ShapeDtypeStruct((16, width), F32),
            jax.ShapeDtypeStruct((16, pairs // 2 * GROUP * HD), BF16),
            jax.ShapeDtypeStruct((24, 128), F32),
        ],
        scratch_shapes=[pltpu.VMEM((16, depth // 2 + 256), BF16)]
        + [pltpu.VMEM(o.shape, BF16) for o in operands[1:]]
        + [
            pltpu.SemaphoreType.DMA,
            pltpu.SemaphoreType.DMA((2,)),
            pltpu.SemaphoreType.DMA((2, 2)),
            pltpu.SemaphoreType.DMA((depth // CHUNK, 2)),
        ],
        compiler_params=pltpu.CompilerParams(vmem_limit_bytes=LOCAL_VMEM),
        cost_estimate=pl.CostEstimate(
            flops=4 * 64 * 256 * seqs * length * pairs + 4 * 16 * depth * width,
            bytes_accessed=4 * seqs * length * width + 4 * depth * width,
            transcendentals=64 * seqs * length * pairs,
        ),
        name="local",
    )(*operands)


def rank_kernel(n, rows, depth, *refs):
    base_ref, table_ref, own_ref, near_ref = refs[:4]
    tokens, (out_ref, *has) = refs[4 : 4 + n], refs[4 + n :]
    half = base_ref.shape[1] // 2
    place = lax.axis_index("dp")
    x = []
    for ref in tokens:
        part = ref[:, : depth // 2].astype(F32)
        x.append(jnp.concatenate([part[:8], part[8:]], 1))
    x = jnp.concatenate(x, 0).astype(BF16)
    down = jnp.concatenate(
        [ref[:, at : at + depth] for at in (0, depth) for ref in (own_ref, near_ref)], 0
    )
    products = lax.dot_general(x, down, NT, preferred_element_type=F32)
    products = jnp.concatenate([products, jnp.zeros_like(products)], 1)
    lane = lax.broadcasted_iota(jnp.int32, products.shape, 1)
    z = None
    for i in range(4):
        part = jnp.where(lane // 16 == i, products, 0.0)
        column = (place ^ (i % 2)) * rows + i // 2 * RANK
        part = pltpu.roll(part, (column + 128 - 16 * i) % 128, 1)
        z = part if z is None else z + part
    out_ref[:, :half] = base_ref[:, half:].astype(BF16)
    out_ref[:, half : half + 128] = split(table_ref[:8])
    for i in range(n):
        at = half + 128 * (i + 1)
        out_ref[:, at : at + 128] = split(z[8 * i : 8 * i + 8])
    for ref in has:
        here = place // 2 == lax.axis_index("tensor") % 2
        mine, far = (token[:, depth // 2 :].astype(F32) for token in tokens[:2])
        ref[:, : mine.shape[1]] = jnp.where(here, mine, far).astype(BF16)
        ref[:, mine.shape[1] :] = jnp.zeros((16, ref.shape[1] - mine.shape[1]), BF16)


def rank_products(rows, depth, columns, base, table, own, near, tokens):
    n = len(tokens)
    out_shape = [jax.ShapeDtypeStruct((16, base.shape[1] // 2 + 128 * (n + 1)), BF16)]
    if columns:
        out_shape.append(jax.ShapeDtypeStruct((16, columns), BF16))
    return pl.pallas_call(
        functools.partial(rank_kernel, n, rows, depth),
        in_specs=[VMEM] * (4 + n),
        out_specs=[VMEM] * len(out_shape),
        out_shape=out_shape,
        compiler_params=pltpu.CompilerParams(vmem_limit_bytes=32 * MEBI),
        name="rank_products",
    )(base, table, own, near, *tokens)


def broadcast_lane(tile, lane):
    return jnp.broadcast_to(tile[:, lane : lane + 1], tile.shape)


def combine_part_kernel(base_ref, mine_ref, theirs_ref, cache_ref, out_ref, *replies):
    half = base_ref.shape[1] // 2
    own = base_ref[:, :half] + theirs_ref[:, :half].astype(F32)
    out_ref[:, :half] = own.astype(BF16)
    sums = mine_ref[:, half:].astype(F32) + theirs_ref[:, half:].astype(F32)
    sums = split(sums[:8] + sums[8:])
    out_ref[:, half : half + 256] = sums[:, :256]
    out_ref[:, half + 256 :] = cache_ref[...]
    for i, ref in enumerate(replies):
        ref[...] = sums[:, 128 * (i + 2) : 128 * (i + 3)]


def combine_part(n, base, mine, theirs, cache):
    shapes = [(16, base.shape[1] // 2 + 256 + cache.shape[1])] + [(16, 128)] * n
    return pl.pallas_call(
        combine_part_kernel,
        in_specs=[VMEM] * 4,
        out_specs=[VMEM] * len(shapes),
        out_shape=[jax.ShapeDtypeStruct(shape, BF16) for shape in shapes],
        compiler_params=pltpu.CompilerParams(vmem_limit_bytes=32 * MEBI),
        name="combine_part",
    )(base, mine, theirs, cache)


def combine_cache_kernel(a_ref, b_ref, _, out_ref):
    lane = lax.broadcasted_iota(jnp.int32, (16, 128), 1)
    for p in range(out_ref.shape[1] // PAIR):
        end = slice(p * PAIR + GROUP * HD, (p + 1) * PAIR)
        a, b = a_ref[:, end].astype(F32), b_ref[:, end].astype(F32)
        top = jnp.maximum(a, b)
        fa = jnp.exp2(jnp.minimum(a - top, 0.0) * EXPONENT)
        fb = jnp.exp2(jnp.minimum(b - top, 0.0) * EXPONENT)
        total = fa * totals(a) + fb * totals(b)
        high = rounded(total)
        stats = jnp.where(lane < GROUP, top, 0.0)
        stats = jnp.where(lane // GROUP == 1, pltpu.roll(high, GROUP, 1), stats)
        stats = jnp.where(lane // GROUP == 2, pltpu.roll(total - high, 2 * GROUP, 1), stats)
        out_ref[:, end] = stats.astype(BF16)
        for g in range(GROUP):
            at = slice(p * PAIR + g * HD, p * PAIR + (g + 1) * HD)
            out_ref[:, at] = (
                broadcast_lane(fa, g) * a_ref[:, at].astype(F32)
                + broadcast_lane(fb, g) * b_ref[:, at].astype(F32)
            ).astype(BF16)


def totals(stats):
    return pltpu.roll(stats, 128 - GROUP, 1) + pltpu.roll(stats, 128 - 2 * GROUP, 1)


def combine_cache(a, b, earlier):
    return pl.pallas_call(
        combine_cache_kernel,
        in_specs=[VMEM] * 3,
        out_specs=VMEM,
        out_shape=jax.ShapeDtypeStruct(a.shape, BF16),
        compiler_params=pltpu.CompilerParams(vmem_limit_bytes=32 * MEBI),
        name="combine_cache",
    )(a, b, earlier)


def merge_kernel(n, paired, width_all, *refs):
    table_ref, qrot_ref, pa_ref, pb_ref = refs[:4]
    backs, (ua_ref, ub_ref, out_ref) = refs[4 : 4 + n], refs[4 + n :]
    pairs = qrot_ref.shape[1] // (GROUP * HD)
    width = pairs * 2 * HD
    cosine, sine = table_ref[8:16], table_ref[16:]
    head = width + 256
    sums = pa_ref[:, :head].astype(F32) + pb_ref[:, :head].astype(F32)
    tail = sums[:8, width : width + 256] + sums[8:, width : width + 256]
    squares, z = tail[:, :128], tail[:, 128:]
    for ref in backs:
        z = z + joined(ref[...])
    lane8 = lax.broadcasted_iota(jnp.int32, (8, 128), 1)
    z = jnp.concatenate(
        [jnp.where(lane8 < RANK, z, 0.0), jnp.where(lane8 < RANK, 0.0, z)], 0
    ).astype(BF16)
    adapted = []
    for ref in (ua_ref, ub_ref):
        ups = jnp.concatenate([ref[:, i : i + 128] for i in range(0, 16 * HD, 128)], 0)
        adapted.append(lax.dot_general(z, ups, NT, preferred_element_type=F32))
    if paired:
        even = lax.axis_index("dp") % 2 == 0
        a, b = adapted
        adapted = [jnp.where(even, a, b), jnp.where(even, b, a)]
    total = sums[:, :width] + jnp.concatenate(adapted, 1)
    scale = lax.rsqrt(squares / width_all + EPSILON)
    lane = lax.broadcasted_iota(jnp.int32, (16, 128), 1)
    step = lax.broadcasted_iota(jnp.int32, (16, 128), 0) % STEPS
    first = first_rows((8, 128))

    def of_step(tiles, j):
        return jnp.concatenate(
            [
                jnp.where(first, tile[j : j + 1], tile[STEPS + j : STEPS + j + 1])
                for tile in tiles
            ],
            0,
        )

    for p in range(pairs):
        new_keys, new_values = [], []
        for e in range(2):
            at = slice((2 * p + e) * HD, (2 * p + e + 1) * HD)
            new_keys.append(rounded(rotated(total[:8, at] * scale, cosine, sine)))
            new_values.append(rounded(total[8:, at] * scale))
            fresh = jnp.concatenate([new_keys[e], new_values[e]], 0)
            start = pairs * GROUP * HD + (2 * p + e) * HD
            out_ref[:, start : start + HD] = fresh.astype(BF16)
        keys = [of_step(new_keys, j) for j in range(STEPS)]
        values = [of_step(new_values, j) for j in range(STEPS)]
        scores = [jnp.zeros((16, 128), F32) for _ in range(STEPS)]
        for g in range(GROUP):
            q = qrot_ref[:, (p * GROUP + g) * HD : (p * GROUP + g + 1) * HD].astype(F32)
            for j in range(STEPS):
                dot = jnp.sum(q * keys[j], 1, keepdims=True)
                scores[j] = jnp.where(lane == g, dot, scores[j])
        scores = [jnp.where(j <= step, scores[j], MASKED_SCORE) for j in range(STEPS)]
        end = slice(head + p * PAIR + GROUP * HD, head + (p + 1) * PAIR)
        stats = [ref[:, end].astype(F32) for ref in (pa_ref, pb_ref)]
        top = functools.reduce(jnp.maximum, scores + stats)
        fresh = [rounded(jnp.exp2((scores[j] - top) * EXPONENT)) for j in range(STEPS)]
        factors = [jnp.exp2(jnp.minimum(s - top, 0.0) * EXPONENT) for s in stats]
        denom = functools.reduce(jnp.add, fresh)
        for factor, s in zip(factors, stats):
            denom = denom + factor * totals(s)
        inverse = 1.0 / denom
        coefficients = [c * inverse for c in fresh + factors]
        for g in range(GROUP):
            at = slice(head + p * PAIR + g * HD, head + p * PAIR + (g + 1) * HD)
            terms = values + [ref[:, at].astype(F32) for ref in (pa_ref, pb_ref)]
            tile = jnp.zeros((16, 128), F32)
            for c, term in zip(coefficients, terms):
                tile = tile + broadcast_lane(c, g) * term
            out_ref[:, (p * GROUP + g) * HD : (p * GROUP + g + 1) * HD] = tile.astype(BF16)


def merge(paired, width_all, table, qrot, parts, backs, ups):
    operands = [table, qrot, *parts, *backs, *ups]
    pairs = qrot.shape[1] // (GROUP * HD)
    return pl.pallas_call(
        functools.partial(merge_kernel, len(backs), paired, width_all),
        in_specs=[VMEM] * len(operands),
        out_specs=VMEM,
        out_shape=jax.ShapeDtypeStruct((16, pairs * (GROUP + 2) * HD), BF16),
        compiler_params=pltpu.CompilerParams(vmem_limit_bytes=32 * MEBI),
        name="merge",
    )(*operands)


def place_kernel(mine_ref, theirs_ref, keys_out, values_out, out_ref):
    pairs = mine_ref.shape[1] // ((GROUP + 2) * HD)
    for c, ref in enumerate((mine_ref, theirs_ref)):
        for p in range(pairs):
            pair = pair_at(c * pairs + p)
            tiles = ref[:, p * GROUP * HD : (p + 1) * GROUP * HD].astype(F32)
            size = GROUP * HD
            for e in range(2):
                at = pl.ds(pl.multiple_of((2 * pair + e) * size, size), size)
                for s in range(2):
                    rows = slice(8 * e + 4 * s, 8 * e + 4 * s + 4)
                    out_ref[s, :, at] = tiles[rows].astype(BF16)
            start = pairs * GROUP * HD + p * 2 * HD
            fresh = ref[:, start : start + 2 * HD].astype(F32)
            at = pl.ds(pl.multiple_of(pair * 2 * HD, 2 * HD), 2 * HD)
            for i, out in enumerate((keys_out, values_out)):
                for s in range(2):
                    rows = slice(8 * i + 4 * s, 8 * i + 4 * s + 4)
                    out[s, :, at] = fresh[rows].astype(BF16)


def place(width, mine, theirs):
    return pl.pallas_call(
        place_kernel,
        in_specs=[VMEM] * 2,
        out_specs=[VMEM] * 3,
        out_shape=[
            jax.ShapeDtypeStruct((2, STEPS, width), BF16),
            jax.ShapeDtypeStruct((2, STEPS, width), BF16),
            jax.ShapeDtypeStruct((2, STEPS, GROUP * width), BF16),
        ],
        compiler_params=pltpu.CompilerParams(vmem_limit_bytes=32 * MEBI),
        name="place",
    )(mine, theirs)


def swap(value, axis, n, distance):
    return lax.ppermute(value, axis, [(i, i ^ distance) for i in range(n)])


def shards(
    n_dp,
    n_tensor,
    hidden,
    norm_gain,
    queries,
    key_weight,
    value_weight,
    key_down,
    key_up,
    value_down,
    value_up,
    key_cache,
    value_cache,
    lengths,
):
    depth, width = key_weight.shape
    rows = key_down.shape[0]
    to_dp = lambda value, distance: swap(value, "dp", n_dp, distance)
    to_tensor = lambda value, distance: swap(value, "tensor", n_tensor, distance)
    partners = range(2, n_dp, 2)
    n = len(partners)
    paired = n_dp == 4

    down, tokens, own = pack(
        lengths, hidden, norm_gain, key_down, value_down, key_up, value_up
    )
    near = to_dp(down, 1)
    sent = [to_dp(tokens, d) for d in partners]
    keep, send, base, qrot, table = local(
        own, queries, key_cache, value_cache, key_weight, value_weight
    )
    received = to_tensor(send, 1)
    columns = UP_COLUMNS if paired else 0
    message, *has = rank_products(rows, depth, columns, base, table, down, near, [tokens, *sent])
    if paired:
        ups = [has[0], to_dp(has[0], 1)]
    else:
        ups = lax.all_gather(tokens[:, depth // 2 :], "dp")
        ups = ups.reshape(n_dp, 16, -1, 128).transpose(0, 2, 1, 3)
        ups = ups.reshape(2, 2, 16, 16, 128).transpose(0, 1, 3, 2, 4).reshape(2, 2, 16, -1)
        ups = lax.dynamic_index_in_dim(ups, lax.axis_index("tensor") % 2, 0, keepdims=False)
        ups = [ups[0], ups[1]]
    cache = combine_cache(keep, received, message)
    part, *replies = combine_part(n, base, message, to_tensor(message, 1), cache)
    part_far = to_tensor(part, 2)
    places = [(s, t) for s in range(n_dp) for t in range(n_tensor)]
    backs = []
    for reply, d in zip(replies, partners):
        for e in (0, 2):
            perm = [(s * n_tensor + t, (s ^ d) * n_tensor + (t ^ e)) for s, t in places]
            backs.append(lax.ppermute(reply, ("dp", "tensor"), perm))
    merged = merge(
        paired,
        float(depth * n_tensor),
        table,
        qrot,
        (part, part_far),
        backs,
        ups,
    )
    return place(width, merged, to_tensor(merged, 1))


def solution(mesh):
    body = functools.partial(shards, mesh.shape["dp"], mesh.shape["tensor"])
    return jax.shard_map(
        body,
        mesh=mesh,
        in_specs=(
            P(("groups", "dp"), None, "tensor"),
            P("tensor"),
            P(("groups", "dp"), None, None),
            P("tensor", None),
            P("tensor", None),
            P(("groups", "dp"), "tensor"),
            P(("groups", "dp"), None),
            P(("groups", "dp"), "tensor"),
            P(("groups", "dp"), None),
            P(("groups", "dp"), "tensor", None),
            P(("groups", "dp"), "tensor", None),
            P(("groups", "dp")),
        ),
        out_specs=(
            P(("groups", "dp"), None, None),
            P(("groups", "dp"), None, None),
            P(("groups", "dp"), None, None),
        ),
        check_vma=False,
    )
```

```python
import functools
import math

import jax
import jax.numpy as jnp
from jax import lax
from jax.experimental import pallas as pl
from jax.experimental.pallas import tpu as pltpu
from jax.sharding import PartitionSpec as P

HD = 128
GROUP = 8
STEPS = 4
RANK = 64
EPSILON = 1e-05
ROPE_BASE = 500000.0
MASKED_SCORE = -1e30
LOWEST_TOP = -1e20
EXPONENT = math.log2(math.e) / math.sqrt(HD)
PAIR = GROUP * HD + 128
UP_COLUMNS = 3584
CHUNK = 256

F32 = jnp.float32
BF16 = jnp.bfloat16
NT = (((1,), (1,)), ((), ()))
VMEM = pl.BlockSpec(memory_space=pltpu.VMEM)
HBM = pl.BlockSpec(memory_space=pltpu.HBM)
MEBI = 2**20
WHOLE_VMEM = 65000 * 1024
LOCAL_VMEM = 54900 * 1024


def rounded(value):
    return value.astype(BF16).astype(F32)


def split(value):
    high = rounded(value)
    return jnp.concatenate([high, value - high], 0).astype(BF16)


def joined(tile):
    wide = tile.astype(F32)
    return wide[:8] + wide[8:]


def rotated(tile, cosine, sine):
    return tile * cosine + pltpu.roll(tile, HD // 2, 1) * sine


def first_rows(shape):
    return lax.broadcasted_iota(jnp.int32, shape, 0) % 8 < STEPS


def exchanged(a, b):
    first = first_rows(a.shape)
    return (
        jnp.where(first, a, pltpu.roll(b, STEPS, 0)),
        jnp.where(first, pltpu.roll(a, STEPS, 0), b),
    )


def flat(matrix):
    return jnp.concatenate([matrix[i : i + 16] for i in range(0, matrix.shape[0], 16)], 1)


def pack_kernel(*refs):
    sources, outs, held = refs[:7], refs[7:10], refs[10:17]
    (a_ref, b_ref, own_ref), sems, out_sems = refs[17:20], refs[20], refs[21]
    targets = [*outs[:2], outs[2].at[:, pl.ds(0, own_ref.shape[1])]]
    copies = [
        pltpu.make_async_copy(source, target, sems.at[i])
        for i, (source, target) in enumerate(zip(sources, held))
    ]
    for copy in copies:
        copy.start()
    backs = [
        pltpu.make_async_copy(source, target, out_sems.at[i])
        for i, (source, target) in enumerate(zip((a_ref, b_ref, own_ref), targets))
    ]
    kd_ref, vd_ref, x_ref, gain_ref, lengths_ref, ku_ref, vu_ref = held
    own, depth = kd_ref.shape
    for slot, ref in enumerate((kd_ref, vd_ref)):
        copies[slot].wait()
        down = ref[...]
        if own < 16:
            down = jnp.concatenate([down, jnp.zeros((16 - own, depth), F32)], 0)
        a_ref[:, slot * depth : (slot + 1) * depth] = down.astype(BF16)
    backs[0].start()
    for copy in copies[2:]:
        copy.wait()
    x = jnp.concatenate([x_ref[0].astype(F32), x_ref[1].astype(F32)], 0)
    gain = gain_ref[...].astype(F32)
    scaled = jnp.concatenate(
        [x[:, i * 128 : (i + 1) * 128] * gain[i : i + 1] for i in range(depth // 128)], 1
    )
    scaled = jnp.concatenate([scaled[:, : depth // 2], scaled[:, depth // 2 :]], 0).astype(BF16)
    b_ref[:, : depth // 2] = scaled
    ups = jnp.concatenate([ku_ref[...], vu_ref[...]], 0).T.astype(BF16)
    b_ref[:, depth // 2 :] = flat(ups)
    backs[1].start()
    own_ref[:, : depth // 2] = scaled
    row = lax.broadcasted_iota(jnp.int32, (16, 128), 0)
    lengths = lengths_ref[...]
    length = jnp.where(row % 8 < STEPS, lengths[:, :1], lengths[:, 1:])
    length = jnp.where(row < 8, length // 64 * 64, length % 64)
    own_ref[:, depth // 2 : depth // 2 + 128] = length.astype(F32).astype(BF16)
    squares = jnp.broadcast_to(jnp.sum(x * x, 1, keepdims=True), (8, 128))
    own_ref[:, depth // 2 + 128 :] = split(squares)
    backs[2].start()
    for copy in backs:
        copy.wait()


def pack(lengths, hidden, gain, key_down, value_down, key_up, value_up):
    operands = [key_down, value_down, hidden, gain.reshape(-1, 128), lengths.reshape(1, 2)]
    operands += [key_up.T, value_up.T]
    depth = hidden.shape[2]
    ups = key_up.shape[0] * 8
    outs = [
        jax.ShapeDtypeStruct((16, 2 * depth), BF16),
        jax.ShapeDtypeStruct((16, depth // 2 + ups), BF16),
        jax.ShapeDtypeStruct((16, depth // 2 + 256 + ups), BF16),
    ]
    scratch = [*operands, *outs[:2], jax.ShapeDtypeStruct((16, depth // 2 + 256), BF16)]
    return pl.pallas_call(
        pack_kernel,
        in_specs=[HBM] * len(operands),
        out_specs=[HBM] * len(outs),
        out_shape=outs,
        scratch_shapes=[pltpu.VMEM(o.shape, o.dtype) for o in scratch]
        + [pltpu.SemaphoreType.DMA((len(operands),)), pltpu.SemaphoreType.DMA((len(outs),))],
        compiler_params=pltpu.CompilerParams(vmem_limit_bytes=WHOLE_VMEM),
        name="pack",
    )(*operands)


def tables(length):
    shape = length.shape
    row = lax.broadcasted_iota(jnp.int32, shape, 0)
    lane = lax.broadcasted_iota(jnp.int32, shape, 1)
    position = length + (row % STEPS).astype(F32)
    pair = lane % (HD // 2)
    frequency = jnp.ones(shape, F32)
    for bit in range(6):
        factor = ROPE_BASE ** (-(2.0 * 2**bit) / HD)
        frequency = jnp.where((pair >> bit) & 1 == 1, frequency * factor, frequency)
    cosine, sine = cosine_and_sine(position * frequency)
    return cosine, jnp.where(lane < HD // 2, -sine, sine)


def cosine_and_sine(angle):
    turns = jnp.floor(angle * (2.0 / math.pi) + 0.5)
    rest = ((angle - turns * 1.5703125) - turns * 4.8351287841796875e-4) - turns * 3.1391647e-7
    square = rest * rest
    sine = -1.9515295891e-4 * square + 8.3321608736e-3
    sine = (sine * square - 1.6666654611e-1) * square * rest + rest
    cosine = 2.443315711809948e-5 * square - 1.388731625493765e-3
    cosine = (cosine * square + 4.166664568298827e-2) * square * square - 0.5 * square + 1.0
    quadrant = turns.astype(jnp.int32)
    swap_them = (quadrant & 1) == 1
    cosine, sine = jnp.where(swap_them, sine, cosine), jnp.where(swap_them, cosine, sine)
    cosine = jnp.where(((quadrant + 1) & 2) == 2, -cosine, cosine)
    sine = jnp.where((quadrant & 2) == 2, -sine, sine)
    return cosine, sine


def rotated_rows(pairs, cosine, sine, q_ref, qrot_ref):
    zero = jnp.zeros((32, HD), F32)
    result = []
    for p in pairs:
        halves = [[], []]
        for e in range(2):
            for g in range(GROUP):
                at = slice(((2 * p + e) * GROUP + g) * HD, ((2 * p + e) * GROUP + g + 1) * HD)
                q = jnp.concatenate([q_ref[0, :, at].astype(F32), q_ref[1, :, at].astype(F32)], 0)
                halves[e].append(rotated(q, cosine, sine))
        if qrot_ref is not None:
            for g in range(GROUP):
                at = slice((p * GROUP + g) * HD, (p * GROUP + g + 1) * HD)
                qrot_ref[:, at] = jnp.concatenate([halves[0][g], halves[1][g]], 0).astype(BF16)
        mixed = [[exchanged(halves[e][g], halves[e][g + 4]) for g in range(4)] for e in range(2)]
        for s in range(2):
            rows = [jnp.concatenate([mixed[e][g][s] for g in range(4)], 0) for e in range(2)]
            result.append(
                jnp.concatenate(
                    [jnp.concatenate([rows[0], zero], 1), jnp.concatenate([zero, rows[1]], 1)], 0
                ).astype(BF16)
            )
    return result


def attend(pairs, masks, queries, k_ref, v_ref, between, out_ref):
    scores = []
    for i, p in enumerate(pairs):
        for s in range(2):
            keys = k_ref[s, :, 2 * p * HD : 2 * (p + 1) * HD]
            score = lax.dot_general(queries[2 * i + s], keys, NT, preferred_element_type=F32)
            scores.append(score + jnp.concatenate([masks[s]] * (score.shape[0] // 8), 0))
    between()
    scores = jnp.concatenate(scores, 0)
    top = rounded(jnp.maximum(jnp.max(scores, 1, keepdims=True), LOWEST_TOP))
    weights = jnp.exp2((scores - top) * EXPONENT).astype(BF16)
    total = jnp.sum(weights.astype(F32), 1, keepdims=True)
    high = rounded(total)
    columns = (top, high, total - high)
    lane8 = lax.broadcasted_iota(jnp.int32, (8, 128), 1)
    numers = []
    for i, p in enumerate(pairs):
        for s in range(2):
            at = slice(64 * (2 * i + s), 64 * (2 * i + s + 1))
            values = v_ref[s, :, 2 * p * HD : 2 * (p + 1) * HD]
            numers.append(jnp.dot(weights[at], values, preferred_element_type=F32))
    for i, p in enumerate(pairs):
        outs, ends = [[], []], []
        for e in range(2):
            back, stats = [], []
            for s in range(2):
                tile = jnp.zeros((8, 128), F32)
                for g in range(4):
                    row = 64 * (2 * i + s) + 32 * e + 8 * g
                    for slot, value in enumerate(columns):
                        tile = jnp.where(lane8 == slot * GROUP + g, value[row : row + 8], tile)
                stats.append(tile)
            for g in range(4):
                at = slice(32 * e + 8 * g, 32 * e + 8 * g + 8)
                cols = slice(e * HD, (e + 1) * HD)
                back.append(exchanged(numers[2 * i][at, cols], numers[2 * i + 1][at, cols]))
            outs[e] = [b[0] for b in back] + [b[1] for b in back]
            a, b = exchanged(*stats)
            ends.append(jnp.where(lane8 % 8 < 4, a, pltpu.roll(b, 4, 1)))
        for g in range(GROUP):
            at = slice(i * PAIR + g * HD, i * PAIR + (g + 1) * HD)
            out_ref[:, at] = jnp.concatenate([outs[0][g], outs[1][g]], 0).astype(BF16)
        out_ref[:, i * PAIR + GROUP * HD : (i + 1) * PAIR] = jnp.concatenate(ends, 0).astype(BF16)


def pair_at(i):
    return i ^ (lax.axis_index("tensor") % 2 * 2)


def local_kernel(
    x_hbm, q_hbm, k_hbm, v_hbm, wk_hbm, wv_hbm,
    keep_ref, send_ref, base_ref, qrot_ref, table_ref,
    x_ref, q_ref, k_ref, v_ref, wk_ref, wv_ref, x_sem, q_sem, cache_sem, weight_sem,
):
    pairs = k_hbm.shape[2] // (2 * HD)
    chunks = wk_hbm.shape[0] // CHUNK
    width = wk_hbm.shape[1]
    core = lax.axis_index("tensor") % 2
    x_copy = pltpu.make_async_copy(x_hbm.at[:, pl.ds(0, x_ref.shape[1])], x_ref, x_sem)
    x_copy.start()
    groups = []
    for h in range(2):
        copies = []
        trio = ((q_hbm, q_ref, q_sem.at[h]), (k_hbm, k_ref, cache_sem.at[h, 0]))
        for source, target, sem in (*trio, (v_hbm, v_ref, cache_sem.at[h, 1])):
            size = source.shape[2] // 2
            start = pl.multiple_of((core ^ h) * size, size)
            copies.append(
                pltpu.make_async_copy(
                    source.at[:, :, pl.ds(start, size)],
                    target.at[:, :, pl.ds(h * size, size)],
                    sem,
                )
            )
        groups.append(copies)
    for h in range(2):
        groups[h][0].start()
    for copy in groups[0][1:]:
        copy.start()
    weights = []
    for c in range(chunks):
        at = pl.ds(c * CHUNK, CHUNK)
        weights.append(
            [
                pltpu.make_async_copy(source.at[at], target.at[at], weight_sem.at[c, i])
                for i, (source, target) in enumerate(((wk_hbm, wk_ref), (wv_hbm, wv_ref)))
            ]
        )
    def start(copies):
        for copy in copies:
            copy.start()

    x_copy.wait()
    start(groups[1][1:])
    for copies in weights[: chunks // 4]:
        start(copies)
    half = wk_hbm.shape[0] // 2
    x = x_ref[:, :half].astype(F32)
    x = jnp.concatenate([x[:8], x[8:]], 1).astype(BF16)
    length = joined(x_ref[:, half : half + 128])
    cosine, sine = tables(length)
    table_ref[...] = jnp.concatenate([joined(x_ref[:, half + 128 : half + 256]), cosine, sine], 0)
    limit = length - (lax.axis_index("tensor") * k_hbm.shape[1]).astype(F32)
    place = lax.broadcasted_iota(jnp.int32, (8, k_hbm.shape[1]), 1).astype(F32)
    masks = [
        jnp.where(place < limit[STEPS * s : STEPS * s + 1, :1], 0.0, MASKED_SCORE) for s in range(2)
    ]
    queries = []
    for h in range(2):
        groups[h][0].wait()
        own = range(h * pairs // 2, (h + 1) * pairs // 2)
        queries.append(rotated_rows(own, cosine, sine, q_ref, None if h else qrot_ref))
    parts = []

    def project(c):
        at = slice(c * CHUNK, (c + 1) * CHUNK)
        halves = []
        for copy, ref in zip(weights[c], (wk_ref, wv_ref)):
            copy.wait()
            halves.append(jnp.dot(x[:, at], ref[at], preferred_element_type=F32))
        parts.append(jnp.concatenate(halves, 0))

    def between(h):
        groups[h][2].wait()
        if h == 0:
            for copies in weights[chunks // 2 : 3 * chunks // 4]:
                start(copies)
        else:
            for c in range(chunks // 2):
                project(c)

    for h, out_ref in enumerate((keep_ref, send_ref)):
        groups[h][1].wait()
        for copies in weights[3 * chunks // 4 :] if h else weights[chunks // 4 : chunks // 2]:
            start(copies)
        attend(
            range(h * pairs // 2, (h + 1) * pairs // 2),
            masks, queries[h], k_ref, v_ref, functools.partial(between, h), out_ref,
        )
    for c in range(chunks // 2, chunks):
        project(c)
    total = functools.reduce(jnp.add, parts)
    lower, upper = total[:, : width // 2], total[:, width // 2 :]
    base_ref[:, : width // 2] = jnp.where(core == 0, lower, upper)
    base_ref[:, width // 2 :] = jnp.where(core == 0, upper, lower)


def local(message, queries, key_cache, value_cache, key_weight, value_weight):
    seqs, length, width = key_cache.shape
    depth = key_weight.shape[0]
    pairs = width // (2 * HD)
    operands = [message, queries, key_cache, value_cache, key_weight, value_weight]
    return pl.pallas_call(
        local_kernel,
        in_specs=[HBM] * 6,
        out_specs=[VMEM] * 5,
        out_shape=[
            jax.ShapeDtypeStruct((16, pairs // 2 * PAIR), BF16),
            jax.ShapeDtypeStruct((16, pairs // 2 * PAIR), BF16),
            jax.ShapeDtypeStruct((16, width), F32),
            jax.ShapeDtypeStruct((16, pairs // 2 * GROUP * HD), BF16),
            jax.ShapeDtypeStruct((24, 128), F32),
        ],
        scratch_shapes=[pltpu.VMEM((16, depth // 2 + 256), BF16)]
        + [pltpu.VMEM(o.shape, BF16) for o in operands[1:]]
        + [
            pltpu.SemaphoreType.DMA,
            pltpu.SemaphoreType.DMA((2,)),
            pltpu.SemaphoreType.DMA((2, 2)),
            pltpu.SemaphoreType.DMA((depth // CHUNK, 2)),
        ],
        compiler_params=pltpu.CompilerParams(vmem_limit_bytes=LOCAL_VMEM),
        cost_estimate=pl.CostEstimate(
            flops=4 * 64 * 256 * seqs * length * pairs + 4 * 16 * depth * width,
            bytes_accessed=4 * seqs * length * width + 4 * depth * width,
            transcendentals=64 * seqs * length * pairs,
        ),
        name="local",
    )(*operands)


def rank_kernel(n, rows, depth, *refs):
    base_ref, table_ref, own_ref, near_ref = refs[:4]
    tokens, (out_ref, *has) = refs[4 : 4 + n], refs[4 + n :]
    half = base_ref.shape[1] // 2
    place = lax.axis_index("dp")
    x = []
    for ref in tokens:
        part = ref[:, : depth // 2].astype(F32)
        x.append(jnp.concatenate([part[:8], part[8:]], 1))
    x = jnp.concatenate(x, 0).astype(BF16)
    down = jnp.concatenate(
        [ref[:, at : at + depth] for at in (0, depth) for ref in (own_ref, near_ref)], 0
    )
    products = lax.dot_general(x, down, NT, preferred_element_type=F32)
    products = jnp.concatenate([products, jnp.zeros_like(products)], 1)
    lane = lax.broadcasted_iota(jnp.int32, products.shape, 1)
    z = None
    for i in range(4):
        part = jnp.where(lane // 16 == i, products, 0.0)
        column = (place ^ (i % 2)) * rows + i // 2 * RANK
        part = pltpu.roll(part, (column + 128 - 16 * i) % 128, 1)
        z = part if z is None else z + part
    out_ref[:, :half] = base_ref[:, half:].astype(BF16)
    out_ref[:, half : half + 128] = split(table_ref[:8])
    for i in range(n):
        at = half + 128 * (i + 1)
        out_ref[:, at : at + 128] = split(z[8 * i : 8 * i + 8])
    for ref in has:
        here = place // 2 == lax.axis_index("tensor") % 2
        mine, far = (token[:, depth // 2 :].astype(F32) for token in tokens[:2])
        ref[:, : mine.shape[1]] = jnp.where(here, mine, far).astype(BF16)
        ref[:, mine.shape[1] :] = jnp.zeros((16, ref.shape[1] - mine.shape[1]), BF16)


def rank_products(rows, depth, columns, base, table, own, near, tokens):
    n = len(tokens)
    out_shape = [jax.ShapeDtypeStruct((16, base.shape[1] // 2 + 128 * (n + 1)), BF16)]
    if columns:
        out_shape.append(jax.ShapeDtypeStruct((16, columns), BF16))
    return pl.pallas_call(
        functools.partial(rank_kernel, n, rows, depth),
        in_specs=[VMEM] * (4 + n),
        out_specs=[VMEM] * len(out_shape),
        out_shape=out_shape,
        compiler_params=pltpu.CompilerParams(vmem_limit_bytes=32 * MEBI),
        name="rank_products",
    )(base, table, own, near, *tokens)


def broadcast_lane(tile, lane):
    return jnp.broadcast_to(tile[:, lane : lane + 1], tile.shape)


def combine_part_kernel(base_ref, mine_ref, theirs_ref, cache_ref, out_ref, *replies):
    half = base_ref.shape[1] // 2
    own = base_ref[:, :half] + theirs_ref[:, :half].astype(F32)
    out_ref[:, :half] = own.astype(BF16)
    sums = mine_ref[:, half:].astype(F32) + theirs_ref[:, half:].astype(F32)
    sums = split(sums[:8] + sums[8:])
    out_ref[:, half : half + 256] = sums[:, :256]
    out_ref[:, half + 256 :] = cache_ref[...]
    for i, ref in enumerate(replies):
        ref[...] = sums[:, 128 * (i + 2) : 128 * (i + 3)]


def combine_part(n, base, mine, theirs, cache):
    shapes = [(16, base.shape[1] // 2 + 256 + cache.shape[1])] + [(16, 128)] * n
    return pl.pallas_call(
        combine_part_kernel,
        in_specs=[VMEM] * 4,
        out_specs=[VMEM] * len(shapes),
        out_shape=[jax.ShapeDtypeStruct(shape, BF16) for shape in shapes],
        compiler_params=pltpu.CompilerParams(vmem_limit_bytes=32 * MEBI),
        name="combine_part",
    )(base, mine, theirs, cache)


def combine_cache_kernel(a_ref, b_ref, _, out_ref):
    lane = lax.broadcasted_iota(jnp.int32, (16, 128), 1)
    for p in range(out_ref.shape[1] // PAIR):
        end = slice(p * PAIR + GROUP * HD, (p + 1) * PAIR)
        a, b = a_ref[:, end].astype(F32), b_ref[:, end].astype(F32)
        top = jnp.maximum(a, b)
        fa = jnp.exp2(jnp.minimum(a - top, 0.0) * EXPONENT)
        fb = jnp.exp2(jnp.minimum(b - top, 0.0) * EXPONENT)
        total = fa * totals(a) + fb * totals(b)
        high = rounded(total)
        stats = jnp.where(lane < GROUP, top, 0.0)
        stats = jnp.where(lane // GROUP == 1, pltpu.roll(high, GROUP, 1), stats)
        stats = jnp.where(lane // GROUP == 2, pltpu.roll(total - high, 2 * GROUP, 1), stats)
        out_ref[:, end] = stats.astype(BF16)
        for g in range(GROUP):
            at = slice(p * PAIR + g * HD, p * PAIR + (g + 1) * HD)
            out_ref[:, at] = (
                broadcast_lane(fa, g) * a_ref[:, at].astype(F32)
                + broadcast_lane(fb, g) * b_ref[:, at].astype(F32)
            ).astype(BF16)


def totals(stats):
    return pltpu.roll(stats, 128 - GROUP, 1) + pltpu.roll(stats, 128 - 2 * GROUP, 1)


def combine_cache(a, b, earlier):
    return pl.pallas_call(
        combine_cache_kernel,
        in_specs=[VMEM] * 3,
        out_specs=VMEM,
        out_shape=jax.ShapeDtypeStruct(a.shape, BF16),
        compiler_params=pltpu.CompilerParams(vmem_limit_bytes=32 * MEBI),
        name="combine_cache",
    )(a, b, earlier)


def merge_kernel(n, paired, width_all, *refs):
    table_ref, qrot_ref, pa_ref, pb_ref = refs[:4]
    backs, (ua_ref, ub_ref, out_ref) = refs[4 : 4 + n], refs[4 + n :]
    pairs = qrot_ref.shape[1] // (GROUP * HD)
    width = pairs * 2 * HD
    cosine, sine = table_ref[8:16], table_ref[16:]
    head = width + 256
    sums = pa_ref[:, :head].astype(F32) + pb_ref[:, :head].astype(F32)
    tail = sums[:8, width : width + 256] + sums[8:, width : width + 256]
    squares, z = tail[:, :128], tail[:, 128:]
    for ref in backs:
        z = z + joined(ref[...])
    lane8 = lax.broadcasted_iota(jnp.int32, (8, 128), 1)
    z = jnp.concatenate(
        [jnp.where(lane8 < RANK, z, 0.0), jnp.where(lane8 < RANK, 0.0, z)], 0
    ).astype(BF16)
    adapted = []
    for ref in (ua_ref, ub_ref):
        ups = jnp.concatenate([ref[:, i : i + 128] for i in range(0, 16 * HD, 128)], 0)
        adapted.append(lax.dot_general(z, ups, NT, preferred_element_type=F32))
    if paired:
        even = lax.axis_index("dp") % 2 == 0
        a, b = adapted
        adapted = [jnp.where(even, a, b), jnp.where(even, b, a)]
    total = sums[:, :width] + jnp.concatenate(adapted, 1)
    scale = lax.rsqrt(squares / width_all + EPSILON)
    step = lax.broadcasted_iota(jnp.int32, (16, 128), 0) % STEPS
    first = first_rows((8, 128))

    def of_step(tiles, j):
        return jnp.concatenate(
            [
                jnp.where(first, tile[j : j + 1], tile[STEPS + j : STEPS + j + 1])
                for tile in tiles
            ],
            0,
        )

    for p in range(pairs):
        new_keys, new_values = [], []
        for e in range(2):
            at = slice((2 * p + e) * HD, (2 * p + e + 1) * HD)
            new_keys.append(rounded(rotated(total[:8, at] * scale, cosine, sine)))
            new_values.append(rounded(total[8:, at] * scale))
            fresh = jnp.concatenate([new_keys[e], new_values[e]], 0)
            start = pairs * GROUP * HD + (2 * p + e) * HD
            out_ref[:, start : start + HD] = fresh.astype(BF16)
        keys = [of_step(new_keys, j) for j in range(STEPS)]
        values = [of_step(new_values, j) for j in range(STEPS)]
        end = slice(head + p * PAIR + GROUP * HD, head + (p + 1) * PAIR)
        stats = [ref[:, end].astype(F32) for ref in (pa_ref, pb_ref)]
        sums_of = [totals(tile) for tile in stats]
        for g in range(GROUP):
            tops = [broadcast_lane(tile, g) for tile in stats]
            weights = [broadcast_lane(tile, g) for tile in sums_of]
            q = qrot_ref[:, (p * GROUP + g) * HD : (p * GROUP + g + 1) * HD].astype(F32)
            scores = [
                jnp.where(
                    j <= step,
                    jnp.broadcast_to(jnp.sum(q * keys[j], 1, keepdims=True), (16, 128)),
                    MASKED_SCORE,
                )
                for j in range(STEPS)
            ]
            top = functools.reduce(jnp.maximum, scores + tops)
            fresh = [rounded(jnp.exp2((score - top) * EXPONENT)) for score in scores]
            factors = [jnp.exp2((tile - top) * EXPONENT) for tile in tops]
            denom = functools.reduce(jnp.add, fresh)
            for factor, weight in zip(factors, weights):
                denom = denom + factor * weight
            at = slice(head + p * PAIR + g * HD, head + p * PAIR + (g + 1) * HD)
            terms = values + [ref[:, at].astype(F32) for ref in (pa_ref, pb_ref)]
            tile = jnp.zeros((16, 128), F32)
            for c, term in zip(fresh + factors, terms):
                tile = tile + c * term
            tile = tile * (1.0 / denom)
            out_ref[:, (p * GROUP + g) * HD : (p * GROUP + g + 1) * HD] = tile.astype(BF16)


def merge(paired, width_all, table, qrot, parts, backs, ups):
    operands = [table, qrot, *parts, *backs, *ups]
    pairs = qrot.shape[1] // (GROUP * HD)
    return pl.pallas_call(
        functools.partial(merge_kernel, len(backs), paired, width_all),
        in_specs=[VMEM] * len(operands),
        out_specs=VMEM,
        out_shape=jax.ShapeDtypeStruct((16, pairs * (GROUP + 2) * HD), BF16),
        compiler_params=pltpu.CompilerParams(vmem_limit_bytes=32 * MEBI),
        name="merge",
    )(*operands)


def place_kernel(mine_ref, theirs_ref, keys_out, values_out, out_ref):
    pairs = mine_ref.shape[1] // ((GROUP + 2) * HD)
    for c, ref in enumerate((mine_ref, theirs_ref)):
        for p in range(pairs):
            pair = pair_at(c * pairs + p)
            tiles = ref[:, p * GROUP * HD : (p + 1) * GROUP * HD].astype(F32)
            size = GROUP * HD
            for e in range(2):
                at = pl.ds(pl.multiple_of((2 * pair + e) * size, size), size)
                for s in range(2):
                    rows = slice(8 * e + 4 * s, 8 * e + 4 * s + 4)
                    out_ref[s, :, at] = tiles[rows].astype(BF16)
            start = pairs * GROUP * HD + p * 2 * HD
            fresh = ref[:, start : start + 2 * HD].astype(F32)
            at = pl.ds(pl.multiple_of(pair * 2 * HD, 2 * HD), 2 * HD)
            for i, out in enumerate((keys_out, values_out)):
                for s in range(2):
                    rows = slice(8 * i + 4 * s, 8 * i + 4 * s + 4)
                    out[s, :, at] = fresh[rows].astype(BF16)


def place(width, mine, theirs):
    return pl.pallas_call(
        place_kernel,
        in_specs=[VMEM] * 2,
        out_specs=[VMEM] * 3,
        out_shape=[
            jax.ShapeDtypeStruct((2, STEPS, width), BF16),
            jax.ShapeDtypeStruct((2, STEPS, width), BF16),
            jax.ShapeDtypeStruct((2, STEPS, GROUP * width), BF16),
        ],
        compiler_params=pltpu.CompilerParams(vmem_limit_bytes=32 * MEBI),
        name="place",
    )(mine, theirs)


def swap(value, axis, n, distance):
    return lax.ppermute(value, axis, [(i, i ^ distance) for i in range(n)])


def shards(
    n_dp,
    n_tensor,
    hidden,
    norm_gain,
    queries,
    key_weight,
    value_weight,
    key_down,
    key_up,
    value_down,
    value_up,
    key_cache,
    value_cache,
    lengths,
):
    depth, width = key_weight.shape
    rows = key_down.shape[0]
    to_dp = lambda value, distance: swap(value, "dp", n_dp, distance)
    to_tensor = lambda value, distance: swap(value, "tensor", n_tensor, distance)
    partners = range(2, n_dp, 2)
    n = len(partners)
    paired = n_dp == 4

    down, tokens, own = pack(
        lengths, hidden, norm_gain, key_down, value_down, key_up, value_up
    )
    near = to_dp(down, 1)
    sent = [to_dp(tokens, d) for d in partners]
    keep, send, base, qrot, table = local(
        own, queries, key_cache, value_cache, key_weight, value_weight
    )
    received = to_tensor(send, 1)
    columns = UP_COLUMNS if paired else 0
    message, *has = rank_products(rows, depth, columns, base, table, down, near, [tokens, *sent])
    if paired:
        ups = [has[0], to_dp(has[0], 1)]
    else:
        ups = lax.all_gather(tokens[:, depth // 2 :], "dp")
        ups = ups.reshape(n_dp, 16, -1, 128).transpose(0, 2, 1, 3)
        ups = ups.reshape(2, 2, 16, 16, 128).transpose(0, 1, 3, 2, 4).reshape(2, 2, 16, -1)
        ups = lax.dynamic_index_in_dim(ups, lax.axis_index("tensor") % 2, 0, keepdims=False)
        ups = [ups[0], ups[1]]
    cache = combine_cache(keep, received, message)
    part, *replies = combine_part(n, base, message, to_tensor(message, 1), cache)
    part_far = to_tensor(part, 2)
    places = [(s, t) for s in range(n_dp) for t in range(n_tensor)]
    backs = []
    for reply, d in zip(replies, partners):
        for e in (0, 2):
            perm = [(s * n_tensor + t, (s ^ d) * n_tensor + (t ^ e)) for s, t in places]
            backs.append(lax.ppermute(reply, ("dp", "tensor"), perm))
    merged = merge(
        paired,
        float(depth * n_tensor),
        table,
        qrot,
        (part, part_far),
        backs,
        ups,
    )
    return place(width, merged, to_tensor(merged, 1))


def solution(mesh):
    body = functools.partial(shards, mesh.shape["dp"], mesh.shape["tensor"])
    return jax.shard_map(
        body,
        mesh=mesh,
        in_specs=(
            P(("groups", "dp"), None, "tensor"),
            P("tensor"),
            P(("groups", "dp"), None, None),
            P("tensor", None),
            P("tensor", None),
            P(("groups", "dp"), "tensor"),
            P(("groups", "dp"), None),
            P(("groups", "dp"), "tensor"),
            P(("groups", "dp"), None),
            P(("groups", "dp"), "tensor", None),
            P(("groups", "dp"), "tensor", None),
            P(("groups", "dp")),
        ),
        out_specs=(
            P(("groups", "dp"), None, None),
            P(("groups", "dp"), None, None),
            P(("groups", "dp"), None, None),
        ),
        check_vma=False,
    )
```

```python
import functools
import math

import jax
import jax.numpy as jnp
from jax import lax
from jax.experimental import pallas as pl
from jax.experimental.pallas import tpu as pltpu
from jax.sharding import PartitionSpec as P

HD = 128
GROUP = 8
STEPS = 4
RANK = 64
EPSILON = 1e-05
ROPE_BASE = 500000.0
MASKED_SCORE = -1e30
LOWEST_TOP = -1e20
EXPONENT = math.log2(math.e) / math.sqrt(HD)
PAIR = GROUP * HD + 128
UP_COLUMNS = 3584
CHUNK = 256

F32 = jnp.float32
BF16 = jnp.bfloat16
NT = (((1,), (1,)), ((), ()))
VMEM = pl.BlockSpec(memory_space=pltpu.VMEM)
HBM = pl.BlockSpec(memory_space=pltpu.HBM)
MEBI = 2**20
WHOLE_VMEM = 65000 * 1024
LOCAL_VMEM = 54900 * 1024


def rounded(value):
    return value.astype(BF16).astype(F32)


def split(value):
    high = rounded(value)
    return jnp.concatenate([high, value - high], 0).astype(BF16)


def joined(tile):
    wide = tile.astype(F32)
    return wide[:8] + wide[8:]


def rotated(tile, cosine, sine):
    return tile * cosine + pltpu.roll(tile, HD // 2, 1) * sine


def first_rows(shape):
    return lax.broadcasted_iota(jnp.int32, shape, 0) % 8 < STEPS


def exchanged(a, b):
    first = first_rows(a.shape)
    return (
        jnp.where(first, a, pltpu.roll(b, STEPS, 0)),
        jnp.where(first, pltpu.roll(a, STEPS, 0), b),
    )


def flat(matrix):
    return jnp.concatenate([matrix[i : i + 16] for i in range(0, matrix.shape[0], 16)], 1)


def pack_kernel(*refs):
    sources, outs, held = refs[:7], refs[7:10], refs[10:17]
    (a_ref, b_ref, own_ref), sems, out_sems = refs[17:20], refs[20], refs[21]
    targets = [*outs[:2], outs[2].at[:, pl.ds(0, own_ref.shape[1])]]
    copies = [
        pltpu.make_async_copy(source, target, sems.at[i])
        for i, (source, target) in enumerate(zip(sources, held))
    ]
    for copy in copies:
        copy.start()
    backs = [
        pltpu.make_async_copy(source, target, out_sems.at[i])
        for i, (source, target) in enumerate(zip((a_ref, b_ref, own_ref), targets))
    ]
    kd_ref, vd_ref, x_ref, gain_ref, lengths_ref, ku_ref, vu_ref = held
    own, depth = kd_ref.shape
    for slot, ref in enumerate((kd_ref, vd_ref)):
        copies[slot].wait()
        down = ref[...]
        if own < 16:
            down = jnp.concatenate([down, jnp.zeros((16 - own, depth), F32)], 0)
        a_ref[:, slot * depth : (slot + 1) * depth] = down.astype(BF16)
    backs[0].start()
    for copy in copies[2:]:
        copy.wait()
    x = jnp.concatenate([x_ref[0].astype(F32), x_ref[1].astype(F32)], 0)
    gain = gain_ref[...].astype(F32)
    scaled = jnp.concatenate(
        [x[:, i * 128 : (i + 1) * 128] * gain[i : i + 1] for i in range(depth // 128)], 1
    )
    scaled = jnp.concatenate([scaled[:, : depth // 2], scaled[:, depth // 2 :]], 0).astype(BF16)
    b_ref[:, : depth // 2] = scaled
    ups = jnp.concatenate([ku_ref[...], vu_ref[...]], 0).T.astype(BF16)
    b_ref[:, depth // 2 :] = flat(ups)
    backs[1].start()
    own_ref[:, : depth // 2] = scaled
    row = lax.broadcasted_iota(jnp.int32, (16, 128), 0)
    lengths = lengths_ref[...]
    length = jnp.where(row % 8 < STEPS, lengths[:, :1], lengths[:, 1:])
    length = jnp.where(row < 8, length // 64 * 64, length % 64)
    own_ref[:, depth // 2 : depth // 2 + 128] = length.astype(F32).astype(BF16)
    squares = jnp.broadcast_to(jnp.sum(x * x, 1, keepdims=True), (8, 128))
    own_ref[:, depth // 2 + 128 :] = split(squares)
    backs[2].start()
    for copy in backs:
        copy.wait()


def pack(lengths, hidden, gain, key_down, value_down, key_up, value_up):
    operands = [key_down, value_down, hidden, gain.reshape(-1, 128), lengths.reshape(1, 2)]
    operands += [key_up.T, value_up.T]
    depth = hidden.shape[2]
    ups = key_up.shape[0] * 8
    outs = [
        jax.ShapeDtypeStruct((16, 2 * depth), BF16),
        jax.ShapeDtypeStruct((16, depth // 2 + ups), BF16),
        jax.ShapeDtypeStruct((16, depth // 2 + 256 + ups), BF16),
    ]
    scratch = [*operands, *outs[:2], jax.ShapeDtypeStruct((16, depth // 2 + 256), BF16)]
    return pl.pallas_call(
        pack_kernel,
        in_specs=[HBM] * len(operands),
        out_specs=[HBM] * len(outs),
        out_shape=outs,
        scratch_shapes=[pltpu.VMEM(o.shape, o.dtype) for o in scratch]
        + [pltpu.SemaphoreType.DMA((len(operands),)), pltpu.SemaphoreType.DMA((len(outs),))],
        compiler_params=pltpu.CompilerParams(vmem_limit_bytes=WHOLE_VMEM),
        name="pack",
    )(*operands)


def tables(length):
    shape = length.shape
    row = lax.broadcasted_iota(jnp.int32, shape, 0)
    lane = lax.broadcasted_iota(jnp.int32, shape, 1)
    position = length + (row % STEPS).astype(F32)
    pair = lane % (HD // 2)
    frequency = jnp.ones(shape, F32)
    for bit in range(6):
        factor = ROPE_BASE ** (-(2.0 * 2**bit) / HD)
        frequency = jnp.where((pair >> bit) & 1 == 1, frequency * factor, frequency)
    cosine, sine = cosine_and_sine(position * frequency)
    return cosine, jnp.where(lane < HD // 2, -sine, sine)


def cosine_and_sine(angle):
    turns = jnp.floor(angle * (2.0 / math.pi) + 0.5)
    rest = ((angle - turns * 1.5703125) - turns * 4.8351287841796875e-4) - turns * 3.1391647e-7
    square = rest * rest
    sine = -1.9515295891e-4 * square + 8.3321608736e-3
    sine = (sine * square - 1.6666654611e-1) * square * rest + rest
    cosine = 2.443315711809948e-5 * square - 1.388731625493765e-3
    cosine = (cosine * square + 4.166664568298827e-2) * square * square - 0.5 * square + 1.0
    quadrant = turns.astype(jnp.int32)
    swap_them = (quadrant & 1) == 1
    cosine, sine = jnp.where(swap_them, sine, cosine), jnp.where(swap_them, cosine, sine)
    cosine = jnp.where(((quadrant + 1) & 2) == 2, -cosine, cosine)
    sine = jnp.where((quadrant & 2) == 2, -sine, sine)
    return cosine, sine


def rotated_rows(pairs, cosine, sine, q_ref, qrot_ref):
    zero = jnp.zeros((32, HD), F32)
    result = []
    for p in pairs:
        halves = [[], []]
        for e in range(2):
            for g in range(GROUP):
                at = slice(((2 * p + e) * GROUP + g) * HD, ((2 * p + e) * GROUP + g + 1) * HD)
                q = jnp.concatenate([q_ref[0, :, at].astype(F32), q_ref[1, :, at].astype(F32)], 0)
                halves[e].append(rotated(q, cosine, sine))
        if qrot_ref is not None:
            for g in range(GROUP):
                at = slice((p * GROUP + g) * HD, (p * GROUP + g + 1) * HD)
                qrot_ref[:, at] = jnp.concatenate([halves[0][g], halves[1][g]], 0).astype(BF16)
        mixed = [[exchanged(halves[e][g], halves[e][g + 4]) for g in range(4)] for e in range(2)]
        for s in range(2):
            rows = [jnp.concatenate([mixed[e][g][s] for g in range(4)], 0) for e in range(2)]
            result.append(
                jnp.concatenate(
                    [jnp.concatenate([rows[0], zero], 1), jnp.concatenate([zero, rows[1]], 1)], 0
                ).astype(BF16)
            )
    return result


def attend(pairs, masks, queries, k_ref, v_ref, between, out_ref):
    scores = []
    for i, p in enumerate(pairs):
        for s in range(2):
            keys = k_ref[s, :, 2 * p * HD : 2 * (p + 1) * HD]
            score = lax.dot_general(queries[2 * i + s], keys, NT, preferred_element_type=F32)
            scores.append(score + jnp.concatenate([masks[s]] * (score.shape[0] // 8), 0))
    between()
    scores = jnp.concatenate(scores, 0)
    top = rounded(jnp.maximum(jnp.max(scores, 1, keepdims=True), LOWEST_TOP))
    weights = jnp.exp2((scores - top) * EXPONENT).astype(BF16)
    total = jnp.sum(weights.astype(F32), 1, keepdims=True)
    high = rounded(total)
    columns = (top, high, total - high)
    lane8 = lax.broadcasted_iota(jnp.int32, (8, 128), 1)
    numers = []
    for i, p in enumerate(pairs):
        for s in range(2):
            at = slice(64 * (2 * i + s), 64 * (2 * i + s + 1))
            values = v_ref[s, :, 2 * p * HD : 2 * (p + 1) * HD]
            numers.append(jnp.dot(weights[at], values, preferred_element_type=F32))
    for i, p in enumerate(pairs):
        outs, ends = [[], []], []
        for e in range(2):
            back, stats = [], []
            for s in range(2):
                tile = jnp.zeros((8, 128), F32)
                for g in range(4):
                    row = 64 * (2 * i + s) + 32 * e + 8 * g
                    for slot, value in enumerate(columns):
                        tile = jnp.where(lane8 == slot * GROUP + g, value[row : row + 8], tile)
                stats.append(tile)
            for g in range(4):
                at = slice(32 * e + 8 * g, 32 * e + 8 * g + 8)
                cols = slice(e * HD, (e + 1) * HD)
                back.append(exchanged(numers[2 * i][at, cols], numers[2 * i + 1][at, cols]))
            outs[e] = [b[0] for b in back] + [b[1] for b in back]
            a, b = exchanged(*stats)
            ends.append(jnp.where(lane8 % 8 < 4, a, pltpu.roll(b, 4, 1)))
        for g in range(GROUP):
            at = slice(i * PAIR + g * HD, i * PAIR + (g + 1) * HD)
            out_ref[:, at] = jnp.concatenate([outs[0][g], outs[1][g]], 0).astype(BF16)
        out_ref[:, i * PAIR + GROUP * HD : (i + 1) * PAIR] = jnp.concatenate(ends, 0).astype(BF16)


def pair_at(i):
    return i ^ (lax.axis_index("tensor") % 2 * 2)


def local_kernel(
    x_hbm, q_hbm, k_hbm, v_hbm, wk_hbm, wv_hbm,
    keep_ref, send_ref, base_ref, qrot_ref, table_ref,
    x_ref, q_ref, k_ref, v_ref, wk_ref, wv_ref, x_sem, q_sem, cache_sem, weight_sem,
):
    pairs = k_hbm.shape[2] // (2 * HD)
    chunks = wk_hbm.shape[0] // CHUNK
    width = wk_hbm.shape[1]
    core = lax.axis_index("tensor") % 2
    x_copy = pltpu.make_async_copy(x_hbm.at[:, pl.ds(0, x_ref.shape[1])], x_ref, x_sem)
    x_copy.start()
    groups = []
    for h in range(2):
        copies = []
        trio = ((q_hbm, q_ref, q_sem.at[h]), (k_hbm, k_ref, cache_sem.at[h, 0]))
        for source, target, sem in (*trio, (v_hbm, v_ref, cache_sem.at[h, 1])):
            size = source.shape[2] // 2
            start = pl.multiple_of((core ^ h) * size, size)
            copies.append(
                pltpu.make_async_copy(
                    source.at[:, :, pl.ds(start, size)],
                    target.at[:, :, pl.ds(h * size, size)],
                    sem,
                )
            )
        groups.append(copies)
    for h in range(2):
        groups[h][0].start()
    for copy in groups[0][1:]:
        copy.start()
    weights = []
    for c in range(chunks):
        at = pl.ds(c * CHUNK, CHUNK)
        weights.append(
            [
                pltpu.make_async_copy(source.at[at], target.at[at], weight_sem.at[c, i])
                for i, (source, target) in enumerate(((wk_hbm, wk_ref), (wv_hbm, wv_ref)))
            ]
        )
    def start(copies):
        for copy in copies:
            copy.start()

    x_copy.wait()
    start(groups[1][1:])
    for copies in weights[: chunks // 4]:
        start(copies)
    half = wk_hbm.shape[0] // 2
    x = x_ref[:, :half].astype(F32)
    x = jnp.concatenate([x[:8], x[8:]], 1).astype(BF16)
    length = joined(x_ref[:, half : half + 128])
    cosine, sine = tables(length)
    table_ref[...] = jnp.concatenate([joined(x_ref[:, half + 128 : half + 256]), cosine, sine], 0)
    limit = length - (lax.axis_index("tensor") * k_hbm.shape[1]).astype(F32)
    place = lax.broadcasted_iota(jnp.int32, (8, k_hbm.shape[1]), 1).astype(F32)
    masks = [
        jnp.where(place < limit[STEPS * s : STEPS * s + 1, :1], 0.0, MASKED_SCORE) for s in range(2)
    ]
    queries = []
    for h in range(2):
        groups[h][0].wait()
        own = range(h * pairs // 2, (h + 1) * pairs // 2)
        queries.append(rotated_rows(own, cosine, sine, q_ref, None if h else qrot_ref))
    parts = []

    def project(c):
        at = slice(c * CHUNK, (c + 1) * CHUNK)
        halves = []
        for copy, ref in zip(weights[c], (wk_ref, wv_ref)):
            copy.wait()
            halves.append(jnp.dot(x[:, at], ref[at], preferred_element_type=F32))
        parts.append(jnp.concatenate(halves, 0))

    def between(h):
        groups[h][2].wait()
        if h == 0:
            for copies in weights[chunks // 2 : 3 * chunks // 4]:
                start(copies)
        else:
            for c in range(chunks // 2):
                project(c)

    for h, out_ref in enumerate((keep_ref, send_ref)):
        groups[h][1].wait()
        for copies in weights[3 * chunks // 4 :] if h else weights[chunks // 4 : chunks // 2]:
            start(copies)
        attend(
            range(h * pairs // 2, (h + 1) * pairs // 2),
            masks, queries[h], k_ref, v_ref, functools.partial(between, h), out_ref,
        )
    for c in range(chunks // 2, chunks):
        project(c)
    total = functools.reduce(jnp.add, parts)
    lower, upper = total[:, : width // 2], total[:, width // 2 :]
    base_ref[:, : width // 2] = jnp.where(core == 0, lower, upper)
    base_ref[:, width // 2 :] = jnp.where(core == 0, upper, lower)


def local(message, queries, key_cache, value_cache, key_weight, value_weight):
    seqs, length, width = key_cache.shape
    depth = key_weight.shape[0]
    pairs = width // (2 * HD)
    operands = [message, queries, key_cache, value_cache, key_weight, value_weight]
    return pl.pallas_call(
        local_kernel,
        in_specs=[HBM] * 6,
        out_specs=[VMEM] * 5,
        out_shape=[
            jax.ShapeDtypeStruct((16, pairs // 2 * PAIR), BF16),
            jax.ShapeDtypeStruct((16, pairs // 2 * PAIR), BF16),
            jax.ShapeDtypeStruct((16, width), F32),
            jax.ShapeDtypeStruct((16, pairs // 2 * GROUP * HD), BF16),
            jax.ShapeDtypeStruct((24, 128), F32),
        ],
        scratch_shapes=[pltpu.VMEM((16, depth // 2 + 256), BF16)]
        + [pltpu.VMEM(o.shape, BF16) for o in operands[1:]]
        + [
            pltpu.SemaphoreType.DMA,
            pltpu.SemaphoreType.DMA((2,)),
            pltpu.SemaphoreType.DMA((2, 2)),
            pltpu.SemaphoreType.DMA((depth // CHUNK, 2)),
        ],
        compiler_params=pltpu.CompilerParams(vmem_limit_bytes=LOCAL_VMEM),
        cost_estimate=pl.CostEstimate(
            flops=4 * 64 * 256 * seqs * length * pairs + 4 * 16 * depth * width,
            bytes_accessed=4 * seqs * length * width + 4 * depth * width,
            transcendentals=64 * seqs * length * pairs,
        ),
        name="local",
    )(*operands)


def rank_kernel(n, rows, depth, *refs):
    base_ref, table_ref, own_ref, near_ref = refs[:4]
    tokens, (out_ref, *has) = refs[4 : 4 + n], refs[4 + n :]
    half = base_ref.shape[1] // 2
    place = lax.axis_index("dp")
    x = []
    for ref in tokens:
        part = ref[:, : depth // 2].astype(F32)
        x.append(jnp.concatenate([part[:8], part[8:]], 1))
    x = jnp.concatenate(x, 0).astype(BF16)
    down = jnp.concatenate(
        [ref[:, at : at + depth] for at in (0, depth) for ref in (own_ref, near_ref)], 0
    )
    products = lax.dot_general(x, down, NT, preferred_element_type=F32)
    products = jnp.concatenate([products, jnp.zeros_like(products)], 1)
    lane = lax.broadcasted_iota(jnp.int32, products.shape, 1)
    z = None
    for i in range(4):
        part = jnp.where(lane // 16 == i, products, 0.0)
        column = (place ^ (i % 2)) * rows + i // 2 * RANK
        part = pltpu.roll(part, (column + 128 - 16 * i) % 128, 1)
        z = part if z is None else z + part
    out_ref[:, :half] = base_ref[:, half:].astype(BF16)
    out_ref[:, half : half + 128] = split(table_ref[:8])
    for i in range(n):
        at = half + 128 * (i + 1)
        out_ref[:, at : at + 128] = split(z[8 * i : 8 * i + 8])
    for ref in has:
        here = place // 2 == lax.axis_index("tensor") % 2
        mine, far = (token[:, depth // 2 :].astype(F32) for token in tokens[:2])
        ref[:, : mine.shape[1]] = jnp.where(here, mine, far).astype(BF16)
        ref[:, mine.shape[1] :] = jnp.zeros((16, ref.shape[1] - mine.shape[1]), BF16)


def rank_products(rows, depth, columns, base, table, own, near, tokens):
    n = len(tokens)
    out_shape = [jax.ShapeDtypeStruct((16, base.shape[1] // 2 + 128 * (n + 1)), BF16)]
    if columns:
        out_shape.append(jax.ShapeDtypeStruct((16, columns), BF16))
    return pl.pallas_call(
        functools.partial(rank_kernel, n, rows, depth),
        in_specs=[VMEM] * (4 + n),
        out_specs=[VMEM] * len(out_shape),
        out_shape=out_shape,
        compiler_params=pltpu.CompilerParams(vmem_limit_bytes=32 * MEBI),
        name="rank_products",
    )(base, table, own, near, *tokens)


def broadcast_lane(tile, lane):
    return jnp.broadcast_to(tile[:, lane : lane + 1], tile.shape)


def combine_part_kernel(base_ref, mine_ref, theirs_ref, cache_ref, out_ref, *replies):
    half = base_ref.shape[1] // 2
    own = base_ref[:, :half] + theirs_ref[:, :half].astype(F32)
    out_ref[:, :half] = own.astype(BF16)
    sums = mine_ref[:, half:].astype(F32) + theirs_ref[:, half:].astype(F32)
    sums = split(sums[:8] + sums[8:])
    out_ref[:, half : half + 256] = sums[:, :256]
    out_ref[:, half + 256 :] = cache_ref[...]
    for i, ref in enumerate(replies):
        ref[...] = sums[:, 128 * (i + 2) : 128 * (i + 3)]


def combine_part(n, base, mine, theirs, cache):
    shapes = [(16, base.shape[1] // 2 + 256 + cache.shape[1])] + [(16, 128)] * n
    return pl.pallas_call(
        combine_part_kernel,
        in_specs=[VMEM] * 4,
        out_specs=[VMEM] * len(shapes),
        out_shape=[jax.ShapeDtypeStruct(shape, BF16) for shape in shapes],
        compiler_params=pltpu.CompilerParams(vmem_limit_bytes=32 * MEBI),
        name="combine_part",
    )(base, mine, theirs, cache)


def combine_cache_kernel(a_ref, b_ref, _, out_ref):
    lane = lax.broadcasted_iota(jnp.int32, (16, 128), 1)
    for p in range(out_ref.shape[1] // PAIR):
        end = slice(p * PAIR + GROUP * HD, (p + 1) * PAIR)
        a, b = a_ref[:, end].astype(F32), b_ref[:, end].astype(F32)
        top = jnp.maximum(a, b)
        fa = jnp.exp2(jnp.minimum(a - top, 0.0) * EXPONENT)
        fb = jnp.exp2(jnp.minimum(b - top, 0.0) * EXPONENT)
        total = fa * totals(a) + fb * totals(b)
        high = rounded(total)
        stats = jnp.where(lane < GROUP, top, 0.0)
        stats = jnp.where(lane // GROUP == 1, pltpu.roll(high, GROUP, 1), stats)
        stats = jnp.where(lane // GROUP == 2, pltpu.roll(total - high, 2 * GROUP, 1), stats)
        out_ref[:, end] = stats.astype(BF16)
        for g in range(GROUP):
            at = slice(p * PAIR + g * HD, p * PAIR + (g + 1) * HD)
            out_ref[:, at] = (
                broadcast_lane(fa, g) * a_ref[:, at].astype(F32)
                + broadcast_lane(fb, g) * b_ref[:, at].astype(F32)
            ).astype(BF16)


def totals(stats):
    return pltpu.roll(stats, 128 - GROUP, 1) + pltpu.roll(stats, 128 - 2 * GROUP, 1)


def combine_cache(a, b, earlier):
    return pl.pallas_call(
        combine_cache_kernel,
        in_specs=[VMEM] * 3,
        out_specs=VMEM,
        out_shape=jax.ShapeDtypeStruct(a.shape, BF16),
        compiler_params=pltpu.CompilerParams(vmem_limit_bytes=32 * MEBI),
        name="combine_cache",
    )(a, b, earlier)


def blend_kernel(pairs, pa_ref, pb_ref, sums_ref, numer_ref, stats_ref):
    head = sums_ref.shape[1]
    sums_ref[...] = pa_ref[:, :head].astype(F32) + pb_ref[:, :head].astype(F32)
    for p in range(pairs):
        end = slice(head + p * PAIR + GROUP * HD, head + (p + 1) * PAIR)
        a, b = pa_ref[:, end].astype(F32), pb_ref[:, end].astype(F32)
        top = jnp.maximum(a, b)
        fa = jnp.exp2(jnp.minimum(a - top, 0.0) * EXPONENT)
        fb = jnp.exp2(jnp.minimum(b - top, 0.0) * EXPONENT)
        stats_ref[:, 2 * p * 128 : (2 * p + 1) * 128] = top
        stats_ref[:, (2 * p + 1) * 128 : (2 * p + 2) * 128] = fa * totals(a) + fb * totals(b)
        for g in range(GROUP):
            at = slice(head + p * PAIR + g * HD, head + p * PAIR + (g + 1) * HD)
            numer_ref[:, (p * GROUP + g) * HD : (p * GROUP + g + 1) * HD] = broadcast_lane(
                fa, g
            ) * pa_ref[:, at].astype(F32) + broadcast_lane(fb, g) * pb_ref[:, at].astype(F32)


def blend(pairs, part_a, part_b):
    head = part_a.shape[1] - pairs * PAIR
    return pl.pallas_call(
        functools.partial(blend_kernel, pairs),
        in_specs=[VMEM] * 2,
        out_specs=[VMEM] * 3,
        out_shape=[
            jax.ShapeDtypeStruct((16, head), F32),
            jax.ShapeDtypeStruct((16, pairs * GROUP * HD), F32),
            jax.ShapeDtypeStruct((16, pairs * 256), F32),
        ],
        compiler_params=pltpu.CompilerParams(vmem_limit_bytes=32 * MEBI),
        name="blend",
    )(part_a, part_b)


def merge_kernel(n, paired, width_all, *refs):
    table_ref, qrot_ref, sums_ref, numer_ref, stats_ref = refs[:5]
    backs, (ua_ref, ub_ref, out_ref) = refs[5 : 5 + n], refs[5 + n :]
    pairs = qrot_ref.shape[1] // (GROUP * HD)
    width = pairs * 2 * HD
    cosine, sine = table_ref[8:16], table_ref[16:]
    sums = sums_ref[...]
    tail = sums[:8, width : width + 256] + sums[8:, width : width + 256]
    squares, z = tail[:, :128], tail[:, 128:]
    for ref in backs:
        z = z + joined(ref[...])
    lane8 = lax.broadcasted_iota(jnp.int32, (8, 128), 1)
    z = jnp.concatenate(
        [jnp.where(lane8 < RANK, z, 0.0), jnp.where(lane8 < RANK, 0.0, z)], 0
    ).astype(BF16)
    adapted = []
    for ref in (ua_ref, ub_ref):
        ups = jnp.concatenate([ref[:, i : i + 128] for i in range(0, 16 * HD, 128)], 0)
        adapted.append(lax.dot_general(z, ups, NT, preferred_element_type=F32))
    if paired:
        even = lax.axis_index("dp") % 2 == 0
        a, b = adapted
        adapted = [jnp.where(even, a, b), jnp.where(even, b, a)]
    total = sums[:, :width] + jnp.concatenate(adapted, 1)
    scale = lax.rsqrt(squares / width_all + EPSILON)
    lane = lax.broadcasted_iota(jnp.int32, (16, 128), 1)
    step = lax.broadcasted_iota(jnp.int32, (16, 128), 0) % STEPS
    first = first_rows((8, 128))

    def of_step(tiles, j):
        return jnp.concatenate(
            [
                jnp.where(first, tile[j : j + 1], tile[STEPS + j : STEPS + j + 1])
                for tile in tiles
            ],
            0,
        )

    for p in range(pairs):
        new_keys, new_values = [], []
        for e in range(2):
            at = slice((2 * p + e) * HD, (2 * p + e + 1) * HD)
            new_keys.append(rounded(rotated(total[:8, at] * scale, cosine, sine)))
            new_values.append(rounded(total[8:, at] * scale))
            fresh = jnp.concatenate([new_keys[e], new_values[e]], 0)
            start = pairs * GROUP * HD + (2 * p + e) * HD
            out_ref[:, start : start + HD] = fresh.astype(BF16)
        keys = [of_step(new_keys, j) for j in range(STEPS)]
        values = [of_step(new_values, j) for j in range(STEPS)]
        scores = [jnp.zeros((16, 128), F32) for _ in range(STEPS)]
        for g in range(GROUP):
            q = qrot_ref[:, (p * GROUP + g) * HD : (p * GROUP + g + 1) * HD].astype(F32)
            for j in range(STEPS):
                dot = jnp.sum(q * keys[j], 1, keepdims=True)
                scores[j] = jnp.where(lane == g, dot, scores[j])
        scores = [jnp.where(j <= step, scores[j], MASKED_SCORE) for j in range(STEPS)]
        cached = stats_ref[:, 2 * p * 128 : (2 * p + 1) * 128]
        top = functools.reduce(jnp.maximum, [*scores, cached])
        fresh = [rounded(jnp.exp2((scores[j] - top) * EXPONENT)) for j in range(STEPS)]
        factor = jnp.exp2(jnp.minimum(cached - top, 0.0) * EXPONENT)
        denom = factor * stats_ref[:, (2 * p + 1) * 128 : (2 * p + 2) * 128]
        inverse = 1.0 / functools.reduce(jnp.add, fresh, denom)
        coefficients = [c * inverse for c in (*fresh, factor)]
        for g in range(GROUP):
            at = slice((p * GROUP + g) * HD, (p * GROUP + g + 1) * HD)
            tile = jnp.zeros((16, 128), F32)
            for c, term in zip(coefficients, [*values, numer_ref[:, at]]):
                tile = tile + broadcast_lane(c, g) * term
            out_ref[:, at] = tile.astype(BF16)


def merge(paired, width_all, table, qrot, parts, backs, ups):
    operands = [table, qrot, *parts, *backs, *ups]
    pairs = qrot.shape[1] // (GROUP * HD)
    return pl.pallas_call(
        functools.partial(merge_kernel, len(backs), paired, width_all),
        in_specs=[VMEM] * len(operands),
        out_specs=VMEM,
        out_shape=jax.ShapeDtypeStruct((16, pairs * (GROUP + 2) * HD), BF16),
        compiler_params=pltpu.CompilerParams(vmem_limit_bytes=32 * MEBI),
        name="merge",
    )(*operands)


def place_kernel(mine_ref, theirs_ref, keys_out, values_out, out_ref):
    pairs = mine_ref.shape[1] // ((GROUP + 2) * HD)
    for c, ref in enumerate((mine_ref, theirs_ref)):
        for p in range(pairs):
            pair = pair_at(c * pairs + p)
            tiles = ref[:, p * GROUP * HD : (p + 1) * GROUP * HD].astype(F32)
            size = GROUP * HD
            for e in range(2):
                at = pl.ds(pl.multiple_of((2 * pair + e) * size, size), size)
                for s in range(2):
                    rows = slice(8 * e + 4 * s, 8 * e + 4 * s + 4)
                    out_ref[s, :, at] = tiles[rows].astype(BF16)
            start = pairs * GROUP * HD + p * 2 * HD
            fresh = ref[:, start : start + 2 * HD].astype(F32)
            at = pl.ds(pl.multiple_of(pair * 2 * HD, 2 * HD), 2 * HD)
            for i, out in enumerate((keys_out, values_out)):
                for s in range(2):
                    rows = slice(8 * i + 4 * s, 8 * i + 4 * s + 4)
                    out[s, :, at] = fresh[rows].astype(BF16)


def place(width, mine, theirs):
    return pl.pallas_call(
        place_kernel,
        in_specs=[VMEM] * 2,
        out_specs=[VMEM] * 3,
        out_shape=[
            jax.ShapeDtypeStruct((2, STEPS, width), BF16),
            jax.ShapeDtypeStruct((2, STEPS, width), BF16),
            jax.ShapeDtypeStruct((2, STEPS, GROUP * width), BF16),
        ],
        compiler_params=pltpu.CompilerParams(vmem_limit_bytes=32 * MEBI),
        name="place",
    )(mine, theirs)


def swap(value, axis, n, distance):
    return lax.ppermute(value, axis, [(i, i ^ distance) for i in range(n)])


def shards(
    n_dp,
    n_tensor,
    hidden,
    norm_gain,
    queries,
    key_weight,
    value_weight,
    key_down,
    key_up,
    value_down,
    value_up,
    key_cache,
    value_cache,
    lengths,
):
    depth, width = key_weight.shape
    rows = key_down.shape[0]
    to_dp = lambda value, distance: swap(value, "dp", n_dp, distance)
    to_tensor = lambda value, distance: swap(value, "tensor", n_tensor, distance)
    partners = range(2, n_dp, 2)
    n = len(partners)
    paired = n_dp == 4

    down, tokens, own = pack(
        lengths, hidden, norm_gain, key_down, value_down, key_up, value_up
    )
    near = to_dp(down, 1)
    sent = [to_dp(tokens, d) for d in partners]
    keep, send, base, qrot, table = local(
        own, queries, key_cache, value_cache, key_weight, value_weight
    )
    received = to_tensor(send, 1)
    columns = UP_COLUMNS if paired else 0
    message, *has = rank_products(rows, depth, columns, base, table, down, near, [tokens, *sent])
    if paired:
        ups = [has[0], to_dp(has[0], 1)]
    else:
        ups = lax.all_gather(tokens[:, depth // 2 :], "dp")
        ups = ups.reshape(n_dp, 16, -1, 128).transpose(0, 2, 1, 3)
        ups = ups.reshape(2, 2, 16, 16, 128).transpose(0, 1, 3, 2, 4).reshape(2, 2, 16, -1)
        ups = lax.dynamic_index_in_dim(ups, lax.axis_index("tensor") % 2, 0, keepdims=False)
        ups = [ups[0], ups[1]]
    cache = combine_cache(keep, received, message)
    part, *replies = combine_part(n, base, message, to_tensor(message, 1), cache)
    part_far = to_tensor(part, 2)
    places = [(s, t) for s in range(n_dp) for t in range(n_tensor)]
    backs = []
    for reply, d in zip(replies, partners):
        for e in (0, 2):
            perm = [(s * n_tensor + t, (s ^ d) * n_tensor + (t ^ e)) for s, t in places]
            backs.append(lax.ppermute(reply, ("dp", "tensor"), perm))
    merged = merge(
        paired,
        float(depth * n_tensor),
        table,
        qrot,
        blend(width // (4 * HD), part, part_far),
        backs,
        ups,
    )
    return place(width, merged, to_tensor(merged, 1))


def solution(mesh):
    body = functools.partial(shards, mesh.shape["dp"], mesh.shape["tensor"])
    return jax.shard_map(
        body,
        mesh=mesh,
        in_specs=(
            P(("groups", "dp"), None, "tensor"),
            P("tensor"),
            P(("groups", "dp"), None, None),
            P("tensor", None),
            P("tensor", None),
            P(("groups", "dp"), "tensor"),
            P(("groups", "dp"), None),
            P(("groups", "dp"), "tensor"),
            P(("groups", "dp"), None),
            P(("groups", "dp"), "tensor", None),
            P(("groups", "dp"), "tensor", None),
            P(("groups", "dp")),
        ),
        out_specs=(
            P(("groups", "dp"), None, None),
            P(("groups", "dp"), None, None),
            P(("groups", "dp"), None, None),
        ),
        check_vma=False,
    )
```

```python
import functools
import math

import jax
import jax.numpy as jnp
from jax import lax
from jax.experimental import pallas as pl
from jax.experimental.pallas import tpu as pltpu
from jax.sharding import PartitionSpec as P

HD = 128
GROUP = 8
STEPS = 4
RANK = 64
EPSILON = 1e-05
ROPE_BASE = 500000.0
MASKED_SCORE = -1e30
LOWEST_TOP = -1e20
EXPONENT = math.log2(math.e) / math.sqrt(HD)
PAIR = GROUP * HD + 128
UP_COLUMNS = 3584
CHUNK = 256

F32 = jnp.float32
BF16 = jnp.bfloat16
NT = (((1,), (1,)), ((), ()))
VMEM = pl.BlockSpec(memory_space=pltpu.VMEM)
HBM = pl.BlockSpec(memory_space=pltpu.HBM)
MEBI = 2**20
WHOLE_VMEM = 65000 * 1024
LOCAL_VMEM = 54900 * 1024


def rounded(value):
    return value.astype(BF16).astype(F32)


def split(value):
    high = rounded(value)
    return jnp.concatenate([high, value - high], 0).astype(BF16)


def joined(tile):
    wide = tile.astype(F32)
    return wide[:8] + wide[8:]


def rotated(tile, cosine, sine):
    return tile * cosine + pltpu.roll(tile, HD // 2, 1) * sine


def first_rows(shape):
    return lax.broadcasted_iota(jnp.int32, shape, 0) % 8 < STEPS


def exchanged(a, b):
    first = first_rows(a.shape)
    return (
        jnp.where(first, a, pltpu.roll(b, STEPS, 0)),
        jnp.where(first, pltpu.roll(a, STEPS, 0), b),
    )


def flat(matrix):
    return jnp.concatenate([matrix[i : i + 16] for i in range(0, matrix.shape[0], 16)], 1)


def pack_kernel(*refs):
    sources, outs, held = refs[:7], refs[7:10], refs[10:17]
    (a_ref, b_ref, own_ref), sems, out_sems = refs[17:20], refs[20], refs[21]
    targets = [*outs[:2], outs[2].at[:, pl.ds(0, own_ref.shape[1])]]
    copies = [
        pltpu.make_async_copy(source, target, sems.at[i])
        for i, (source, target) in enumerate(zip(sources, held))
    ]
    for copy in copies:
        copy.start()
    backs = [
        pltpu.make_async_copy(source, target, out_sems.at[i])
        for i, (source, target) in enumerate(zip((a_ref, b_ref, own_ref), targets))
    ]
    kd_ref, vd_ref, x_ref, gain_ref, lengths_ref, ku_ref, vu_ref = held
    own, depth = kd_ref.shape
    for slot, ref in enumerate((kd_ref, vd_ref)):
        copies[slot].wait()
        down = ref[...]
        if own < 16:
            down = jnp.concatenate([down, jnp.zeros((16 - own, depth), F32)], 0)
        a_ref[:, slot * depth : (slot + 1) * depth] = down.astype(BF16)
    backs[0].start()
    for copy in copies[2:]:
        copy.wait()
    x = jnp.concatenate([x_ref[0].astype(F32), x_ref[1].astype(F32)], 0)
    gain = gain_ref[...].astype(F32)
    scaled = jnp.concatenate(
        [x[:, i * 128 : (i + 1) * 128] * gain[i : i + 1] for i in range(depth // 128)], 1
    )
    scaled = jnp.concatenate([scaled[:, : depth // 2], scaled[:, depth // 2 :]], 0).astype(BF16)
    b_ref[:, : depth // 2] = scaled
    ups = jnp.concatenate([ku_ref[...], vu_ref[...]], 0).T.astype(BF16)
    b_ref[:, depth // 2 :] = flat(ups)
    backs[1].start()
    own_ref[:, : depth // 2] = scaled
    row = lax.broadcasted_iota(jnp.int32, (16, 128), 0)
    lengths = lengths_ref[...]
    length = jnp.where(row % 8 < STEPS, lengths[:, :1], lengths[:, 1:])
    length = jnp.where(row < 8, length // 64 * 64, length % 64)
    own_ref[:, depth // 2 : depth // 2 + 128] = length.astype(F32).astype(BF16)
    squares = jnp.broadcast_to(jnp.sum(x * x, 1, keepdims=True), (8, 128))
    own_ref[:, depth // 2 + 128 :] = split(squares)
    backs[2].start()
    for copy in backs:
        copy.wait()


def pack(lengths, hidden, gain, key_down, value_down, key_up, value_up):
    operands = [key_down, value_down, hidden, gain.reshape(-1, 128), lengths.reshape(1, 2)]
    operands += [key_up.T, value_up.T]
    depth = hidden.shape[2]
    ups = key_up.shape[0] * 8
    outs = [
        jax.ShapeDtypeStruct((16, 2 * depth), BF16),
        jax.ShapeDtypeStruct((16, depth // 2 + ups), BF16),
        jax.ShapeDtypeStruct((16, depth // 2 + 256 + ups), BF16),
    ]
    scratch = [*operands, *outs[:2], jax.ShapeDtypeStruct((16, depth // 2 + 256), BF16)]
    return pl.pallas_call(
        pack_kernel,
        in_specs=[HBM] * len(operands),
        out_specs=[HBM] * len(outs),
        out_shape=outs,
        scratch_shapes=[pltpu.VMEM(o.shape, o.dtype) for o in scratch]
        + [pltpu.SemaphoreType.DMA((len(operands),)), pltpu.SemaphoreType.DMA((len(outs),))],
        compiler_params=pltpu.CompilerParams(vmem_limit_bytes=WHOLE_VMEM),
        name="pack",
    )(*operands)


def tables(length):
    shape = length.shape
    row = lax.broadcasted_iota(jnp.int32, shape, 0)
    lane = lax.broadcasted_iota(jnp.int32, shape, 1)
    position = length + (row % STEPS).astype(F32)
    pair = lane % (HD // 2)
    frequency = jnp.ones(shape, F32)
    for bit in range(6):
        factor = ROPE_BASE ** (-(2.0 * 2**bit) / HD)
        frequency = jnp.where((pair >> bit) & 1 == 1, frequency * factor, frequency)
    cosine, sine = cosine_and_sine(position * frequency)
    return cosine, jnp.where(lane < HD // 2, -sine, sine)


def cosine_and_sine(angle):
    turns = jnp.floor(angle * (2.0 / math.pi) + 0.5)
    rest = ((angle - turns * 1.5703125) - turns * 4.8351287841796875e-4) - turns * 3.1391647e-7
    square = rest * rest
    sine = -1.9515295891e-4 * square + 8.3321608736e-3
    sine = (sine * square - 1.6666654611e-1) * square * rest + rest
    cosine = 2.443315711809948e-5 * square - 1.388731625493765e-3
    cosine = (cosine * square + 4.166664568298827e-2) * square * square - 0.5 * square + 1.0
    quadrant = turns.astype(jnp.int32)
    swap_them = (quadrant & 1) == 1
    cosine, sine = jnp.where(swap_them, sine, cosine), jnp.where(swap_them, cosine, sine)
    cosine = jnp.where(((quadrant + 1) & 2) == 2, -cosine, cosine)
    sine = jnp.where((quadrant & 2) == 2, -sine, sine)
    return cosine, sine


def rotated_rows(pairs, cosine, sine, q_ref, qrot_ref):
    zero = jnp.zeros((32, HD), F32)
    result = []
    for p in pairs:
        halves = [[], []]
        for e in range(2):
            for g in range(GROUP):
                at = slice(((2 * p + e) * GROUP + g) * HD, ((2 * p + e) * GROUP + g + 1) * HD)
                q = jnp.concatenate([q_ref[0, :, at].astype(F32), q_ref[1, :, at].astype(F32)], 0)
                halves[e].append(rotated(q, cosine, sine))
        if qrot_ref is not None:
            for g in range(GROUP):
                at = slice((p * GROUP + g) * HD, (p * GROUP + g + 1) * HD)
                qrot_ref[:, at] = jnp.concatenate([halves[0][g], halves[1][g]], 0).astype(BF16)
        mixed = [[exchanged(halves[e][g], halves[e][g + 4]) for g in range(4)] for e in range(2)]
        for s in range(2):
            rows = [jnp.concatenate([mixed[e][g][s] for g in range(4)], 0) for e in range(2)]
            result.append(
                jnp.concatenate(
                    [jnp.concatenate([rows[0], zero], 1), jnp.concatenate([zero, rows[1]], 1)], 0
                ).astype(BF16)
            )
    return result


def attend(pairs, masks, queries, k_ref, v_ref, between, out_ref):
    scores = []
    for i, p in enumerate(pairs):
        for s in range(2):
            keys = k_ref[s, :, 2 * p * HD : 2 * (p + 1) * HD]
            score = lax.dot_general(queries[2 * i + s], keys, NT, preferred_element_type=F32)
            scores.append(score + jnp.concatenate([masks[s]] * (score.shape[0] // 8), 0))
    between()
    scores = jnp.concatenate(scores, 0)
    top = rounded(jnp.maximum(jnp.max(scores, 1, keepdims=True), LOWEST_TOP))
    weights = jnp.exp2((scores - top) * EXPONENT).astype(BF16)
    total = jnp.sum(weights.astype(F32), 1, keepdims=True)
    high = rounded(total)
    columns = (top, high, total - high)
    lane8 = lax.broadcasted_iota(jnp.int32, (8, 128), 1)
    numers = []
    for i, p in enumerate(pairs):
        for s in range(2):
            at = slice(64 * (2 * i + s), 64 * (2 * i + s + 1))
            values = v_ref[s, :, 2 * p * HD : 2 * (p + 1) * HD]
            numers.append(jnp.dot(weights[at], values, preferred_element_type=F32))
    for i, p in enumerate(pairs):
        outs, ends = [[], []], []
        for e in range(2):
            back, stats = [], []
            for s in range(2):
                tile = jnp.zeros((8, 128), F32)
                for g in range(4):
                    row = 64 * (2 * i + s) + 32 * e + 8 * g
                    for slot, value in enumerate(columns):
                        tile = jnp.where(lane8 == slot * GROUP + g, value[row : row + 8], tile)
                stats.append(tile)
            for g in range(4):
                at = slice(32 * e + 8 * g, 32 * e + 8 * g + 8)
                cols = slice(e * HD, (e + 1) * HD)
                back.append(exchanged(numers[2 * i][at, cols], numers[2 * i + 1][at, cols]))
            outs[e] = [b[0] for b in back] + [b[1] for b in back]
            a, b = exchanged(*stats)
            ends.append(jnp.where(lane8 % 8 < 4, a, pltpu.roll(b, 4, 1)))
        for g in range(GROUP):
            at = slice(i * PAIR + g * HD, i * PAIR + (g + 1) * HD)
            out_ref[:, at] = jnp.concatenate([outs[0][g], outs[1][g]], 0).astype(BF16)
        out_ref[:, i * PAIR + GROUP * HD : (i + 1) * PAIR] = jnp.concatenate(ends, 0).astype(BF16)


def pair_at(i):
    return i ^ (lax.axis_index("tensor") % 2 * 2)


def local_kernel(
    x_hbm, q_hbm, k_hbm, v_hbm, wk_hbm, wv_hbm,
    keep_ref, send_ref, base_ref, qrot_ref, table_ref,
    x_ref, q_ref, k_ref, v_ref, wk_ref, wv_ref, x_sem, q_sem, cache_sem, weight_sem,
):
    pairs = k_hbm.shape[2] // (2 * HD)
    chunks = wk_hbm.shape[0] // CHUNK
    width = wk_hbm.shape[1]
    core = lax.axis_index("tensor") % 2
    x_copy = pltpu.make_async_copy(x_hbm.at[:, pl.ds(0, x_ref.shape[1])], x_ref, x_sem)
    x_copy.start()
    groups = []
    for h in range(2):
        copies = []
        trio = ((q_hbm, q_ref, q_sem.at[h]), (k_hbm, k_ref, cache_sem.at[h, 0]))
        for source, target, sem in (*trio, (v_hbm, v_ref, cache_sem.at[h, 1])):
            size = source.shape[2] // 2
            start = pl.multiple_of((core ^ h) * size, size)
            copies.append(
                pltpu.make_async_copy(
                    source.at[:, :, pl.ds(start, size)],
                    target.at[:, :, pl.ds(h * size, size)],
                    sem,
                )
            )
        groups.append(copies)
    for h in range(2):
        groups[h][0].start()
    for copy in groups[0][1:]:
        copy.start()
    weights = []
    for c in range(chunks):
        at = pl.ds(c * CHUNK, CHUNK)
        weights.append(
            [
                pltpu.make_async_copy(source.at[at], target.at[at], weight_sem.at[c, i])
                for i, (source, target) in enumerate(((wk_hbm, wk_ref), (wv_hbm, wv_ref)))
            ]
        )
    def start(copies):
        for copy in copies:
            copy.start()

    x_copy.wait()
    start(groups[1][1:])
    for copies in weights[: chunks // 4]:
        start(copies)
    half = wk_hbm.shape[0] // 2
    x = x_ref[:, :half].astype(F32)
    x = jnp.concatenate([x[:8], x[8:]], 1).astype(BF16)
    length = joined(x_ref[:, half : half + 128])
    cosine, sine = tables(length)
    table_ref[...] = jnp.concatenate([joined(x_ref[:, half + 128 : half + 256]), cosine, sine], 0)
    limit = length - (lax.axis_index("tensor") * k_hbm.shape[1]).astype(F32)
    place = lax.broadcasted_iota(jnp.int32, (8, k_hbm.shape[1]), 1).astype(F32)
    masks = [
        jnp.where(place < limit[STEPS * s : STEPS * s + 1, :1], 0.0, MASKED_SCORE) for s in range(2)
    ]
    queries = []
    for h in range(2):
        groups[h][0].wait()
        own = range(h * pairs // 2, (h + 1) * pairs // 2)
        queries.append(rotated_rows(own, cosine, sine, q_ref, None if h else qrot_ref))
    parts = []

    def project(c):
        at = slice(c * CHUNK, (c + 1) * CHUNK)
        halves = []
        for copy, ref in zip(weights[c], (wk_ref, wv_ref)):
            copy.wait()
            halves.append(jnp.dot(x[:, at], ref[at], preferred_element_type=F32))
        parts.append(jnp.concatenate(halves, 0))

    def between(h):
        groups[h][2].wait()
        if h == 0:
            for copies in weights[chunks // 2 : 3 * chunks // 4]:
                start(copies)
        else:
            for c in range(chunks // 2):
                project(c)

    for h, out_ref in enumerate((keep_ref, send_ref)):
        groups[h][1].wait()
        for copies in weights[3 * chunks // 4 :] if h else weights[chunks // 4 : chunks // 2]:
            start(copies)
        attend(
            range(h * pairs // 2, (h + 1) * pairs // 2),
            masks, queries[h], k_ref, v_ref, functools.partial(between, h), out_ref,
        )
    for c in range(chunks // 2, chunks):
        project(c)
    total = functools.reduce(jnp.add, parts)
    lower, upper = total[:, : width // 2], total[:, width // 2 :]
    base_ref[:, : width // 2] = jnp.where(core == 0, lower, upper)
    base_ref[:, width // 2 :] = jnp.where(core == 0, upper, lower)


def local(message, queries, key_cache, value_cache, key_weight, value_weight):
    seqs, length, width = key_cache.shape
    depth = key_weight.shape[0]
    pairs = width // (2 * HD)
    operands = [message, queries, key_cache, value_cache, key_weight, value_weight]
    return pl.pallas_call(
        local_kernel,
        in_specs=[HBM] * 6,
        out_specs=[VMEM] * 5,
        out_shape=[
            jax.ShapeDtypeStruct((16, pairs // 2 * PAIR), BF16),
            jax.ShapeDtypeStruct((16, pairs // 2 * PAIR), BF16),
            jax.ShapeDtypeStruct((16, width), F32),
            jax.ShapeDtypeStruct((16, pairs // 2 * GROUP * HD), BF16),
            jax.ShapeDtypeStruct((24, 128), F32),
        ],
        scratch_shapes=[pltpu.VMEM((16, depth // 2 + 256), BF16)]
        + [pltpu.VMEM(o.shape, BF16) for o in operands[1:]]
        + [
            pltpu.SemaphoreType.DMA,
            pltpu.SemaphoreType.DMA((2,)),
            pltpu.SemaphoreType.DMA((2, 2)),
            pltpu.SemaphoreType.DMA((depth // CHUNK, 2)),
        ],
        compiler_params=pltpu.CompilerParams(vmem_limit_bytes=LOCAL_VMEM),
        cost_estimate=pl.CostEstimate(
            flops=4 * 64 * 256 * seqs * length * pairs + 4 * 16 * depth * width,
            bytes_accessed=4 * seqs * length * width + 4 * depth * width,
            transcendentals=64 * seqs * length * pairs,
        ),
        name="local",
    )(*operands)


def rank_kernel(n, rows, depth, *refs):
    base_ref, table_ref, own_ref, near_ref = refs[:4]
    tokens, (out_ref, *has) = refs[4 : 4 + n], refs[4 + n :]
    half = base_ref.shape[1] // 2
    place = lax.axis_index("dp")
    x = []
    for ref in tokens:
        part = ref[:, : depth // 2].astype(F32)
        x.append(jnp.concatenate([part[:8], part[8:]], 1))
    x = jnp.concatenate(x, 0).astype(BF16)
    down = jnp.concatenate(
        [ref[:, at : at + depth] for at in (0, depth) for ref in (own_ref, near_ref)], 0
    )
    products = lax.dot_general(x, down, NT, preferred_element_type=F32)
    products = jnp.concatenate([products, jnp.zeros_like(products)], 1)
    lane = lax.broadcasted_iota(jnp.int32, products.shape, 1)
    z = None
    for i in range(4):
        part = jnp.where(lane // 16 == i, products, 0.0)
        column = (place ^ (i % 2)) * rows + i // 2 * RANK
        part = pltpu.roll(part, (column + 128 - 16 * i) % 128, 1)
        z = part if z is None else z + part
    out_ref[:, :half] = base_ref[:, half:].astype(BF16)
    out_ref[:, half : half + 128] = split(table_ref[:8])
    for i in range(n):
        at = half + 128 * (i + 1)
        out_ref[:, at : at + 128] = split(z[8 * i : 8 * i + 8])
    for ref in has:
        here = place // 2 == lax.axis_index("tensor") % 2
        mine, far = (token[:, depth // 2 :].astype(F32) for token in tokens[:2])
        ref[:, : mine.shape[1]] = jnp.where(here, mine, far).astype(BF16)
        ref[:, mine.shape[1] :] = jnp.zeros((16, ref.shape[1] - mine.shape[1]), BF16)


def rank_products(rows, depth, columns, base, table, own, near, tokens):
    n = len(tokens)
    out_shape = [jax.ShapeDtypeStruct((16, base.shape[1] // 2 + 128 * (n + 1)), BF16)]
    if columns:
        out_shape.append(jax.ShapeDtypeStruct((16, columns), BF16))
    return pl.pallas_call(
        functools.partial(rank_kernel, n, rows, depth),
        in_specs=[VMEM] * (4 + n),
        out_specs=[VMEM] * len(out_shape),
        out_shape=out_shape,
        compiler_params=pltpu.CompilerParams(vmem_limit_bytes=32 * MEBI),
        name="rank_products",
    )(base, table, own, near, *tokens)


def broadcast_lane(tile, lane):
    return jnp.broadcast_to(tile[:, lane : lane + 1], tile.shape)


def combine_part_kernel(base_ref, mine_ref, theirs_ref, cache_ref, out_ref, *replies):
    half = base_ref.shape[1] // 2
    own = base_ref[:, :half] + theirs_ref[:, :half].astype(F32)
    out_ref[:, :half] = own.astype(BF16)
    sums = mine_ref[:, half:].astype(F32) + theirs_ref[:, half:].astype(F32)
    sums = split(sums[:8] + sums[8:])
    out_ref[:, half : half + 256] = sums[:, :256]
    out_ref[:, half + 256 :] = cache_ref[...]
    for i, ref in enumerate(replies):
        ref[...] = sums[:, 128 * (i + 2) : 128 * (i + 3)]


def combine_part(n, base, mine, theirs, cache):
    shapes = [(16, base.shape[1] // 2 + 256 + cache.shape[1])] + [(16, 128)] * n
    return pl.pallas_call(
        combine_part_kernel,
        in_specs=[VMEM] * 4,
        out_specs=[VMEM] * len(shapes),
        out_shape=[jax.ShapeDtypeStruct(shape, BF16) for shape in shapes],
        compiler_params=pltpu.CompilerParams(vmem_limit_bytes=32 * MEBI),
        name="combine_part",
    )(base, mine, theirs, cache)


def combine_cache_kernel(a_ref, b_ref, _, out_ref):
    lane = lax.broadcasted_iota(jnp.int32, (16, 128), 1)
    for p in range(out_ref.shape[1] // PAIR):
        end = slice(p * PAIR + GROUP * HD, (p + 1) * PAIR)
        a, b = a_ref[:, end].astype(F32), b_ref[:, end].astype(F32)
        top = jnp.maximum(a, b)
        fa = jnp.exp2(jnp.minimum(a - top, 0.0) * EXPONENT)
        fb = jnp.exp2(jnp.minimum(b - top, 0.0) * EXPONENT)
        total = fa * totals(a) + fb * totals(b)
        high = rounded(total)
        stats = jnp.where(lane < GROUP, top, 0.0)
        stats = jnp.where(lane // GROUP == 1, pltpu.roll(high, GROUP, 1), stats)
        stats = jnp.where(lane // GROUP == 2, pltpu.roll(total - high, 2 * GROUP, 1), stats)
        out_ref[:, end] = stats.astype(BF16)
        for g in range(GROUP):
            at = slice(p * PAIR + g * HD, p * PAIR + (g + 1) * HD)
            out_ref[:, at] = (
                broadcast_lane(fa, g) * a_ref[:, at].astype(F32)
                + broadcast_lane(fb, g) * b_ref[:, at].astype(F32)
            ).astype(BF16)


def totals(stats):
    return pltpu.roll(stats, 128 - GROUP, 1) + pltpu.roll(stats, 128 - 2 * GROUP, 1)


def combine_cache(a, b, earlier):
    return pl.pallas_call(
        combine_cache_kernel,
        in_specs=[VMEM] * 3,
        out_specs=VMEM,
        out_shape=jax.ShapeDtypeStruct(a.shape, BF16),
        compiler_params=pltpu.CompilerParams(vmem_limit_bytes=32 * MEBI),
        name="combine_cache",
    )(a, b, earlier)


def blend_kernel(pairs, paired, pa_ref, pb_ref, ua_ref, ub_ref, *refs):
    sums_ref, numer_ref, stats_ref, first_ref, second_ref = refs
    head = sums_ref.shape[1]
    size = first_ref.shape[1]
    a, b = ua_ref[:, :size].astype(F32), ub_ref[:, :size].astype(F32)
    even = lax.axis_index("dp") % 2 == 0 if paired else True
    first_ref[...] = jnp.where(even, a, b).astype(BF16)
    second_ref[...] = jnp.where(even, b, a).astype(BF16)
    sums_ref[...] = pa_ref[:, :head].astype(F32) + pb_ref[:, :head].astype(F32)
    for p in range(pairs):
        end = slice(head + p * PAIR + GROUP * HD, head + (p + 1) * PAIR)
        a, b = pa_ref[:, end].astype(F32), pb_ref[:, end].astype(F32)
        top = jnp.maximum(a, b)
        fa = jnp.exp2(jnp.minimum(a - top, 0.0) * EXPONENT)
        fb = jnp.exp2(jnp.minimum(b - top, 0.0) * EXPONENT)
        stats_ref[:, 2 * p * 128 : (2 * p + 1) * 128] = top
        stats_ref[:, (2 * p + 1) * 128 : (2 * p + 2) * 128] = fa * totals(a) + fb * totals(b)
        for g in range(GROUP):
            at = slice(head + p * PAIR + g * HD, head + p * PAIR + (g + 1) * HD)
            numer_ref[:, (p * GROUP + g) * HD : (p * GROUP + g + 1) * HD] = broadcast_lane(
                fa, g
            ) * pa_ref[:, at].astype(F32) + broadcast_lane(fb, g) * pb_ref[:, at].astype(F32)


def blend(pairs, paired, part_a, part_b, ups):
    head = part_a.shape[1] - pairs * PAIR
    return pl.pallas_call(
        functools.partial(blend_kernel, pairs, paired),
        in_specs=[VMEM] * 4,
        out_specs=[VMEM] * 5,
        out_shape=[
            jax.ShapeDtypeStruct((16, head), F32),
            jax.ShapeDtypeStruct((16, pairs * GROUP * HD), F32),
            jax.ShapeDtypeStruct((16, pairs * 256), F32),
            jax.ShapeDtypeStruct((16, 16 * HD), BF16),
            jax.ShapeDtypeStruct((16, 16 * HD), BF16),
        ],
        compiler_params=pltpu.CompilerParams(vmem_limit_bytes=32 * MEBI),
        name="blend",
    )(part_a, part_b, *ups)


def merge_kernel(n, p, width_all, *refs):
    table_ref, qrot_ref, sums_ref, numer_ref, stats_ref = refs[:5]
    backs, (up_ref, out_ref) = refs[5 : 5 + n], refs[5 + n :]
    pairs = qrot_ref.shape[1] // (GROUP * HD)
    width = pairs * 2 * HD
    cosine, sine = table_ref[8:16], table_ref[16:]
    sums = sums_ref[...]
    tail = sums[:8, width : width + 256] + sums[8:, width : width + 256]
    squares, z = tail[:, :128], tail[:, 128:]
    for ref in backs:
        z = z + joined(ref[...])
    lane8 = lax.broadcasted_iota(jnp.int32, (8, 128), 1)
    z = jnp.concatenate(
        [jnp.where(lane8 < RANK, z, 0.0), jnp.where(lane8 < RANK, 0.0, z)], 0
    ).astype(BF16)
    ups = jnp.concatenate([up_ref[:, i : i + 128] for i in range(0, 16 * HD, 128)], 0)
    total = sums[:, 2 * p * HD : 2 * (p + 1) * HD] + lax.dot_general(
        z, ups, NT, preferred_element_type=F32
    )
    scale = lax.rsqrt(squares / width_all + EPSILON)
    lane = lax.broadcasted_iota(jnp.int32, (16, 128), 1)
    step = lax.broadcasted_iota(jnp.int32, (16, 128), 0) % STEPS
    first = first_rows((8, 128))

    def of_step(tiles, j):
        return jnp.concatenate(
            [
                jnp.where(first, tile[j : j + 1], tile[STEPS + j : STEPS + j + 1])
                for tile in tiles
            ],
            0,
        )

    new_keys, new_values = [], []
    for e in range(2):
        at = slice(e * HD, (e + 1) * HD)
        new_keys.append(rounded(rotated(total[:8, at] * scale, cosine, sine)))
        new_values.append(rounded(total[8:, at] * scale))
        fresh = jnp.concatenate([new_keys[e], new_values[e]], 0)
        start = GROUP * HD + e * HD
        out_ref[:, start : start + HD] = fresh.astype(BF16)
    keys = [of_step(new_keys, j) for j in range(STEPS)]
    values = [of_step(new_values, j) for j in range(STEPS)]
    scores = [jnp.zeros((16, 128), F32) for _ in range(STEPS)]
    for g in range(GROUP):
        q = qrot_ref[:, (p * GROUP + g) * HD : (p * GROUP + g + 1) * HD].astype(F32)
        for j in range(STEPS):
            dot = jnp.sum(q * keys[j], 1, keepdims=True)
            scores[j] = jnp.where(lane == g, dot, scores[j])
    scores = [jnp.where(j <= step, scores[j], MASKED_SCORE) for j in range(STEPS)]
    cached = stats_ref[:, 2 * p * 128 : (2 * p + 1) * 128]
    top = functools.reduce(jnp.maximum, [*scores, cached])
    fresh = [rounded(jnp.exp2((scores[j] - top) * EXPONENT)) for j in range(STEPS)]
    factor = jnp.exp2(jnp.minimum(cached - top, 0.0) * EXPONENT)
    denom = factor * stats_ref[:, (2 * p + 1) * 128 : (2 * p + 2) * 128]
    inverse = 1.0 / functools.reduce(jnp.add, fresh, denom)
    coefficients = [c * inverse for c in (*fresh, factor)]
    for g in range(GROUP):
        at = slice((p * GROUP + g) * HD, (p * GROUP + g + 1) * HD)
        tile = jnp.zeros((16, 128), F32)
        for c, term in zip(coefficients, [*values, numer_ref[:, at]]):
            tile = tile + broadcast_lane(c, g) * term
        out_ref[:, g * HD : (g + 1) * HD] = tile.astype(BF16)
    if out_ref.shape[1] > (GROUP + 2) * HD:
        out_ref[:, (GROUP + 2) * HD :] = jnp.zeros((16, HD), BF16)


def merge(p, width_all, table, qrot, blended, backs, ups):
    operands = [table, qrot, *blended, *backs, ups]
    return pl.pallas_call(
        functools.partial(merge_kernel, len(backs), p, width_all),
        in_specs=[VMEM] * len(operands),
        out_specs=VMEM,
        out_shape=jax.ShapeDtypeStruct((16, (GROUP + 2 + (p == 0)) * HD), BF16),
        compiler_params=pltpu.CompilerParams(vmem_limit_bytes=32 * MEBI),
        name="merge",
    )(*operands)


def place_kernel(*refs):
    pairs = (len(refs) - 3) // 2
    keys_out, values_out, out_ref = refs[2 * pairs :]
    for i, ref in enumerate(refs[: 2 * pairs]):
        pair = pair_at(i)
        size = GROUP * HD
        tiles = ref[:, :size].astype(F32)
        for e in range(2):
            at = pl.ds(pl.multiple_of((2 * pair + e) * size, size), size)
            for s in range(2):
                rows = slice(8 * e + 4 * s, 8 * e + 4 * s + 4)
                out_ref[s, :, at] = tiles[rows].astype(BF16)
        fresh = ref[:, size : size + 2 * HD].astype(F32)
        at = pl.ds(pl.multiple_of(pair * 2 * HD, 2 * HD), 2 * HD)
        for i, out in enumerate((keys_out, values_out)):
            for s in range(2):
                rows = slice(8 * i + 4 * s, 8 * i + 4 * s + 4)
                out[s, :, at] = fresh[rows].astype(BF16)


def place(width, *results):
    return pl.pallas_call(
        place_kernel,
        in_specs=[VMEM] * len(results),
        out_specs=[VMEM] * 3,
        out_shape=[
            jax.ShapeDtypeStruct((2, STEPS, width), BF16),
            jax.ShapeDtypeStruct((2, STEPS, width), BF16),
            jax.ShapeDtypeStruct((2, STEPS, GROUP * width), BF16),
        ],
        compiler_params=pltpu.CompilerParams(vmem_limit_bytes=32 * MEBI),
        name="place",
    )(*results)


def swap(value, axis, n, distance):
    return lax.ppermute(value, axis, [(i, i ^ distance) for i in range(n)])


def shards(
    n_dp,
    n_tensor,
    hidden,
    norm_gain,
    queries,
    key_weight,
    value_weight,
    key_down,
    key_up,
    value_down,
    value_up,
    key_cache,
    value_cache,
    lengths,
):
    depth, width = key_weight.shape
    rows = key_down.shape[0]
    to_dp = lambda value, distance: swap(value, "dp", n_dp, distance)
    to_tensor = lambda value, distance: swap(value, "tensor", n_tensor, distance)
    partners = range(2, n_dp, 2)
    n = len(partners)
    paired = n_dp == 4

    down, tokens, own = pack(
        lengths, hidden, norm_gain, key_down, value_down, key_up, value_up
    )
    near = to_dp(down, 1)
    sent = [to_dp(tokens, d) for d in partners]
    keep, send, base, qrot, table = local(
        own, queries, key_cache, value_cache, key_weight, value_weight
    )
    received = to_tensor(send, 1)
    columns = UP_COLUMNS if paired else 0
    message, *has = rank_products(rows, depth, columns, base, table, down, near, [tokens, *sent])
    if paired:
        ups = [has[0], to_dp(has[0], 1)]
    else:
        ups = lax.all_gather(tokens[:, depth // 2 :], "dp")
        ups = ups.reshape(n_dp, 16, -1, 128).transpose(0, 2, 1, 3)
        ups = ups.reshape(2, 2, 16, 16, 128).transpose(0, 1, 3, 2, 4).reshape(2, 2, 16, -1)
        ups = lax.dynamic_index_in_dim(ups, lax.axis_index("tensor") % 2, 0, keepdims=False)
        ups = [ups[0], ups[1]]
    cache = combine_cache(keep, received, message)
    part, *replies = combine_part(n, base, message, to_tensor(message, 1), cache)
    part_far = to_tensor(part, 2)
    places = [(s, t) for s in range(n_dp) for t in range(n_tensor)]
    backs = []
    for reply, d in zip(replies, partners):
        for e in (0, 2):
            perm = [(s * n_tensor + t, (s ^ d) * n_tensor + (t ^ e)) for s, t in places]
            backs.append(lax.ppermute(reply, ("dp", "tensor"), perm))
    pairs = width // (4 * HD)
    *blended, first, second = blend(pairs, paired, part, part_far, ups)
    mine = [
        merge(p, float(depth * n_tensor), table, qrot, blended, backs, up)
        for p, up in enumerate((first, second))
    ]
    return place(width, *mine, *[to_tensor(result, 1) for result in mine])


def solution(mesh):
    body = functools.partial(shards, mesh.shape["dp"], mesh.shape["tensor"])
    return jax.shard_map(
        body,
        mesh=mesh,
        in_specs=(
            P(("groups", "dp"), None, "tensor"),
            P("tensor"),
            P(("groups", "dp"), None, None),
            P("tensor", None),
            P("tensor", None),
            P(("groups", "dp"), "tensor"),
            P(("groups", "dp"), None),
            P(("groups", "dp"), "tensor"),
            P(("groups", "dp"), None),
            P(("groups", "dp"), "tensor", None),
            P(("groups", "dp"), "tensor", None),
            P(("groups", "dp")),
        ),
        out_specs=(
            P(("groups", "dp"), None, None),
            P(("groups", "dp"), None, None),
            P(("groups", "dp"), None, None),
        ),
        check_vma=False,
    )
```

```python
import functools
import math

import jax
import jax.numpy as jnp
from jax import lax
from jax.experimental import pallas as pl
from jax.experimental.pallas import tpu as pltpu
from jax.sharding import PartitionSpec as P

HD = 128
GROUP = 8
STEPS = 4
RANK = 64
EPSILON = 1e-05
ROPE_BASE = 500000.0
MASKED_SCORE = -1e30
LOWEST_TOP = -1e20
EXPONENT = math.log2(math.e) / math.sqrt(HD)
PAIR = GROUP * HD + 128
UP_COLUMNS = 3584
CHUNK = 256

F32 = jnp.float32
BF16 = jnp.bfloat16
NT = (((1,), (1,)), ((), ()))
VMEM = pl.BlockSpec(memory_space=pltpu.VMEM)
HBM = pl.BlockSpec(memory_space=pltpu.HBM)
MEBI = 2**20
WHOLE_VMEM = 65000 * 1024
LOCAL_VMEM = 54900 * 1024


def rounded(value):
    return value.astype(BF16).astype(F32)


def split(value):
    high = rounded(value)
    return jnp.concatenate([high, value - high], 0).astype(BF16)


def joined(tile):
    wide = tile.astype(F32)
    return wide[:8] + wide[8:]


def rotated(tile, cosine, sine):
    return tile * cosine + pltpu.roll(tile, HD // 2, 1) * sine


def first_rows(shape):
    return lax.broadcasted_iota(jnp.int32, shape, 0) % 8 < STEPS


def exchanged(a, b):
    first = first_rows(a.shape)
    return (
        jnp.where(first, a, pltpu.roll(b, STEPS, 0)),
        jnp.where(first, pltpu.roll(a, STEPS, 0), b),
    )


def flat(matrix):
    return jnp.concatenate([matrix[i : i + 16] for i in range(0, matrix.shape[0], 16)], 1)


def pack_kernel(*refs):
    sources, outs, held = refs[:7], refs[7:10], refs[10:17]
    (a_ref, b_ref, own_ref), sems, out_sems = refs[17:20], refs[20], refs[21]
    targets = [*outs[:2], outs[2].at[:, pl.ds(0, own_ref.shape[1])]]
    copies = [
        pltpu.make_async_copy(source, target, sems.at[i])
        for i, (source, target) in enumerate(zip(sources, held))
    ]
    for copy in copies:
        copy.start()
    backs = [
        pltpu.make_async_copy(source, target, out_sems.at[i])
        for i, (source, target) in enumerate(zip((a_ref, b_ref, own_ref), targets))
    ]
    kd_ref, vd_ref, x_ref, gain_ref, lengths_ref, ku_ref, vu_ref = held
    own, depth = kd_ref.shape
    for slot, ref in enumerate((kd_ref, vd_ref)):
        copies[slot].wait()
        down = ref[...]
        if own < 16:
            down = jnp.concatenate([down, jnp.zeros((16 - own, depth), F32)], 0)
        a_ref[:, slot * depth : (slot + 1) * depth] = down.astype(BF16)
    backs[0].start()
    for copy in copies[2:]:
        copy.wait()
    x = jnp.concatenate([x_ref[0].astype(F32), x_ref[1].astype(F32)], 0)
    gain = gain_ref[...].astype(F32)
    scaled = jnp.concatenate(
        [x[:, i * 128 : (i + 1) * 128] * gain[i : i + 1] for i in range(depth // 128)], 1
    )
    scaled = jnp.concatenate([scaled[:, : depth // 2], scaled[:, depth // 2 :]], 0).astype(BF16)
    b_ref[:, : depth // 2] = scaled
    ups = jnp.concatenate([ku_ref[...], vu_ref[...]], 0).T.astype(BF16)
    b_ref[:, depth // 2 :] = flat(ups)
    backs[1].start()
    own_ref[:, : depth // 2] = scaled
    row = lax.broadcasted_iota(jnp.int32, (16, 128), 0)
    lengths = lengths_ref[...]
    length = jnp.where(row % 8 < STEPS, lengths[:, :1], lengths[:, 1:])
    length = jnp.where(row < 8, length // 64 * 64, length % 64)
    own_ref[:, depth // 2 : depth // 2 + 128] = length.astype(F32).astype(BF16)
    squares = jnp.broadcast_to(jnp.sum(x * x, 1, keepdims=True), (8, 128))
    own_ref[:, depth // 2 + 128 :] = split(squares)
    backs[2].start()
    for copy in backs:
        copy.wait()


def pack(lengths, hidden, gain, key_down, value_down, key_up, value_up):
    operands = [key_down, value_down, hidden, gain.reshape(-1, 128), lengths.reshape(1, 2)]
    operands += [key_up.T, value_up.T]
    depth = hidden.shape[2]
    ups = key_up.shape[0] * 8
    outs = [
        jax.ShapeDtypeStruct((16, 2 * depth), BF16),
        jax.ShapeDtypeStruct((16, depth // 2 + ups), BF16),
        jax.ShapeDtypeStruct((16, depth // 2 + 256 + ups), BF16),
    ]
    scratch = [*operands, *outs[:2], jax.ShapeDtypeStruct((16, depth // 2 + 256), BF16)]
    return pl.pallas_call(
        pack_kernel,
        in_specs=[HBM] * len(operands),
        out_specs=[HBM] * len(outs),
        out_shape=outs,
        scratch_shapes=[pltpu.VMEM(o.shape, o.dtype) for o in scratch]
        + [pltpu.SemaphoreType.DMA((len(operands),)), pltpu.SemaphoreType.DMA((len(outs),))],
        compiler_params=pltpu.CompilerParams(vmem_limit_bytes=WHOLE_VMEM),
        name="pack",
    )(*operands)


def tables(length):
    shape = length.shape
    row = lax.broadcasted_iota(jnp.int32, shape, 0)
    lane = lax.broadcasted_iota(jnp.int32, shape, 1)
    position = length + (row % STEPS).astype(F32)
    pair = lane % (HD // 2)
    frequency = jnp.ones(shape, F32)
    for bit in range(6):
        factor = ROPE_BASE ** (-(2.0 * 2**bit) / HD)
        frequency = jnp.where((pair >> bit) & 1 == 1, frequency * factor, frequency)
    cosine, sine = cosine_and_sine(position * frequency)
    return cosine, jnp.where(lane < HD // 2, -sine, sine)


def cosine_and_sine(angle):
    turns = jnp.floor(angle * (2.0 / math.pi) + 0.5)
    rest = ((angle - turns * 1.5703125) - turns * 4.8351287841796875e-4) - turns * 3.1391647e-7
    square = rest * rest
    sine = -1.9515295891e-4 * square + 8.3321608736e-3
    sine = (sine * square - 1.6666654611e-1) * square * rest + rest
    cosine = 2.443315711809948e-5 * square - 1.388731625493765e-3
    cosine = (cosine * square + 4.166664568298827e-2) * square * square - 0.5 * square + 1.0
    quadrant = turns.astype(jnp.int32)
    swap_them = (quadrant & 1) == 1
    cosine, sine = jnp.where(swap_them, sine, cosine), jnp.where(swap_them, cosine, sine)
    cosine = jnp.where(((quadrant + 1) & 2) == 2, -cosine, cosine)
    sine = jnp.where((quadrant & 2) == 2, -sine, sine)
    return cosine, sine


def rotated_rows(pairs, cosine, sine, q_ref, qrot_ref):
    zero = jnp.zeros((32, HD), F32)
    result = []
    for p in pairs:
        halves = [[], []]
        for e in range(2):
            for g in range(GROUP):
                at = slice(((2 * p + e) * GROUP + g) * HD, ((2 * p + e) * GROUP + g + 1) * HD)
                q = jnp.concatenate([q_ref[0, :, at].astype(F32), q_ref[1, :, at].astype(F32)], 0)
                halves[e].append(rotated(q, cosine, sine))
        if qrot_ref is not None:
            for g in range(GROUP):
                at = slice((p * GROUP + g) * HD, (p * GROUP + g + 1) * HD)
                qrot_ref[:, at] = jnp.concatenate([halves[0][g], halves[1][g]], 0).astype(BF16)
        mixed = [[exchanged(halves[e][g], halves[e][g + 4]) for g in range(4)] for e in range(2)]
        for s in range(2):
            rows = [jnp.concatenate([mixed[e][g][s] for g in range(4)], 0) for e in range(2)]
            result.append(
                jnp.concatenate(
                    [jnp.concatenate([rows[0], zero], 1), jnp.concatenate([zero, rows[1]], 1)], 0
                ).astype(BF16)
            )
    return result


def attend(pairs, masks, queries, k_ref, v_ref, between, out_refs):
    scores = []
    for i, p in enumerate(pairs):
        for s in range(2):
            keys = k_ref[s, :, 2 * p * HD : 2 * (p + 1) * HD]
            score = lax.dot_general(queries[2 * i + s], keys, NT, preferred_element_type=F32)
            scores.append(score + jnp.concatenate([masks[s]] * (score.shape[0] // 8), 0))
    between()
    scores = jnp.concatenate(scores, 0)
    top = rounded(jnp.maximum(jnp.max(scores, 1, keepdims=True), LOWEST_TOP))
    weights = jnp.exp2((scores - top) * EXPONENT).astype(BF16)
    total = jnp.sum(weights.astype(F32), 1, keepdims=True)
    high = rounded(total)
    columns = (top, high, total - high)
    lane8 = lax.broadcasted_iota(jnp.int32, (8, 128), 1)
    numers = []
    for i, p in enumerate(pairs):
        for s in range(2):
            at = slice(64 * (2 * i + s), 64 * (2 * i + s + 1))
            values = v_ref[s, :, 2 * p * HD : 2 * (p + 1) * HD]
            numers.append(jnp.dot(weights[at], values, preferred_element_type=F32))
    for i, p in enumerate(pairs):
        out_ref, place = out_refs[2 * i // len(pairs)], i % (len(pairs) // 2) * PAIR
        outs, ends = [[], []], []
        for e in range(2):
            back, stats = [], []
            for s in range(2):
                tile = jnp.zeros((8, 128), F32)
                for g in range(4):
                    row = 64 * (2 * i + s) + 32 * e + 8 * g
                    for slot, value in enumerate(columns):
                        tile = jnp.where(lane8 == slot * GROUP + g, value[row : row + 8], tile)
                stats.append(tile)
            for g in range(4):
                at = slice(32 * e + 8 * g, 32 * e + 8 * g + 8)
                cols = slice(e * HD, (e + 1) * HD)
                back.append(exchanged(numers[2 * i][at, cols], numers[2 * i + 1][at, cols]))
            outs[e] = [b[0] for b in back] + [b[1] for b in back]
            a, b = exchanged(*stats)
            ends.append(jnp.where(lane8 % 8 < 4, a, pltpu.roll(b, 4, 1)))
        for g in range(GROUP):
            at = slice(place + g * HD, place + (g + 1) * HD)
            out_ref[:, at] = jnp.concatenate([outs[0][g], outs[1][g]], 0).astype(BF16)
        out_ref[:, place + GROUP * HD : place + PAIR] = jnp.concatenate(ends, 0).astype(BF16)


def pair_at(i):
    return i ^ (lax.axis_index("tensor") % 2 * 2)


def local_kernel(
    x_hbm, q_hbm, k_hbm, v_hbm, wk_hbm, wv_hbm,
    keep_ref, send_ref, base_ref, qrot_ref, table_ref,
    x_ref, q_ref, k_ref, v_ref, wk_ref, wv_ref, x_sem, q_sem, cache_sem, weight_sem,
):
    pairs = k_hbm.shape[2] // (2 * HD)
    chunks = wk_hbm.shape[0] // CHUNK
    width = wk_hbm.shape[1]
    core = lax.axis_index("tensor") % 2
    x_copy = pltpu.make_async_copy(x_hbm.at[:, pl.ds(0, x_ref.shape[1])], x_ref, x_sem)
    x_copy.start()
    groups = []
    for h in range(2):
        copies = []
        trio = ((q_hbm, q_ref, q_sem.at[h]), (k_hbm, k_ref, cache_sem.at[h, 0]))
        for source, target, sem in (*trio, (v_hbm, v_ref, cache_sem.at[h, 1])):
            size = source.shape[2] // 2
            start = pl.multiple_of((core ^ h) * size, size)
            copies.append(
                pltpu.make_async_copy(
                    source.at[:, :, pl.ds(start, size)],
                    target.at[:, :, pl.ds(h * size, size)],
                    sem,
                )
            )
        groups.append(copies)
    for h in range(2):
        groups[h][0].start()
    for copy in groups[0][1:]:
        copy.start()
    weights = []
    for c in range(chunks):
        at = pl.ds(c * CHUNK, CHUNK)
        weights.append(
            [
                pltpu.make_async_copy(source.at[at], target.at[at], weight_sem.at[c, i])
                for i, (source, target) in enumerate(((wk_hbm, wk_ref), (wv_hbm, wv_ref)))
            ]
        )
    def start(copies):
        for copy in copies:
            copy.start()

    x_copy.wait()
    start(groups[1][1:])
    for copies in weights[: chunks // 4]:
        start(copies)
    half = wk_hbm.shape[0] // 2
    x = x_ref[:, :half].astype(F32)
    x = jnp.concatenate([x[:8], x[8:]], 1).astype(BF16)
    length = joined(x_ref[:, half : half + 128])
    cosine, sine = tables(length)
    table_ref[...] = jnp.concatenate([joined(x_ref[:, half + 128 : half + 256]), cosine, sine], 0)
    limit = length - (lax.axis_index("tensor") * k_hbm.shape[1]).astype(F32)
    place = lax.broadcasted_iota(jnp.int32, (8, k_hbm.shape[1]), 1).astype(F32)
    masks = [
        jnp.where(place < limit[STEPS * s : STEPS * s + 1, :1], 0.0, MASKED_SCORE) for s in range(2)
    ]
    queries = []
    for h in range(2):
        groups[h][0].wait()
        own = range(h * pairs // 2, (h + 1) * pairs // 2)
        queries.append(rotated_rows(own, cosine, sine, q_ref, None if h else qrot_ref))
    parts = []

    def project(c):
        at = slice(c * CHUNK, (c + 1) * CHUNK)
        halves = []
        for copy, ref in zip(weights[c], (wk_ref, wv_ref)):
            copy.wait()
            halves.append(jnp.dot(x[:, at], ref[at], preferred_element_type=F32))
        parts.append(jnp.concatenate(halves, 0))

    def between():
        for copies in weights[chunks // 2 :]:
            start(copies)
        for h in range(2):
            groups[h][2].wait()
        for c in range(chunks // 2):
            project(c)

    for h in range(2):
        groups[h][1].wait()
    for copies in weights[chunks // 4 : chunks // 2]:
        start(copies)
    attend(
        range(pairs), masks, queries[0] + queries[1], k_ref, v_ref, between, (keep_ref, send_ref)
    )
    for c in range(chunks // 2, chunks):
        project(c)
    total = functools.reduce(jnp.add, parts)
    lower, upper = total[:, : width // 2], total[:, width // 2 :]
    base_ref[:, : width // 2] = jnp.where(core == 0, lower, upper)
    base_ref[:, width // 2 :] = jnp.where(core == 0, upper, lower)


def local(message, queries, key_cache, value_cache, key_weight, value_weight):
    seqs, length, width = key_cache.shape
    depth = key_weight.shape[0]
    pairs = width // (2 * HD)
    operands = [message, queries, key_cache, value_cache, key_weight, value_weight]
    return pl.pallas_call(
        local_kernel,
        in_specs=[HBM] * 6,
        out_specs=[VMEM] * 5,
        out_shape=[
            jax.ShapeDtypeStruct((16, pairs // 2 * PAIR), BF16),
            jax.ShapeDtypeStruct((16, pairs // 2 * PAIR), BF16),
            jax.ShapeDtypeStruct((16, width), F32),
            jax.ShapeDtypeStruct((16, pairs // 2 * GROUP * HD), BF16),
            jax.ShapeDtypeStruct((24, 128), F32),
        ],
        scratch_shapes=[pltpu.VMEM((16, depth // 2 + 256), BF16)]
        + [pltpu.VMEM(o.shape, BF16) for o in operands[1:]]
        + [
            pltpu.SemaphoreType.DMA,
            pltpu.SemaphoreType.DMA((2,)),
            pltpu.SemaphoreType.DMA((2, 2)),
            pltpu.SemaphoreType.DMA((depth // CHUNK, 2)),
        ],
        compiler_params=pltpu.CompilerParams(vmem_limit_bytes=LOCAL_VMEM),
        cost_estimate=pl.CostEstimate(
            flops=4 * 64 * 256 * seqs * length * pairs + 4 * 16 * depth * width,
            bytes_accessed=4 * seqs * length * width + 4 * depth * width,
            transcendentals=64 * seqs * length * pairs,
        ),
        name="local",
    )(*operands)


def rank_kernel(n, rows, depth, *refs):
    base_ref, table_ref, own_ref, near_ref = refs[:4]
    tokens, (out_ref, *has) = refs[4 : 4 + n], refs[4 + n :]
    half = base_ref.shape[1] // 2
    place = lax.axis_index("dp")
    x = []
    for ref in tokens:
        part = ref[:, : depth // 2].astype(F32)
        x.append(jnp.concatenate([part[:8], part[8:]], 1))
    x = jnp.concatenate(x, 0).astype(BF16)
    down = jnp.concatenate(
        [ref[:, at : at + depth] for at in (0, depth) for ref in (own_ref, near_ref)], 0
    )
    products = lax.dot_general(x, down, NT, preferred_element_type=F32)
    products = jnp.concatenate([products, jnp.zeros_like(products)], 1)
    lane = lax.broadcasted_iota(jnp.int32, products.shape, 1)
    z = None
    for i in range(4):
        part = jnp.where(lane // 16 == i, products, 0.0)
        column = (place ^ (i % 2)) * rows + i // 2 * RANK
        part = pltpu.roll(part, (column + 128 - 16 * i) % 128, 1)
        z = part if z is None else z + part
    out_ref[:, :half] = base_ref[:, half:].astype(BF16)
    out_ref[:, half : half + 128] = split(table_ref[:8])
    for i in range(n):
        at = half + 128 * (i + 1)
        out_ref[:, at : at + 128] = split(z[8 * i : 8 * i + 8])
    for ref in has:
        here = place // 2 == lax.axis_index("tensor") % 2
        mine, far = (token[:, depth // 2 :].astype(F32) for token in tokens[:2])
        ref[:, : mine.shape[1]] = jnp.where(here, mine, far).astype(BF16)
        ref[:, mine.shape[1] :] = jnp.zeros((16, ref.shape[1] - mine.shape[1]), BF16)


def rank_products(rows, depth, columns, base, table, own, near, tokens):
    n = len(tokens)
    out_shape = [jax.ShapeDtypeStruct((16, base.shape[1] // 2 + 128 * (n + 1)), BF16)]
    if columns:
        out_shape.append(jax.ShapeDtypeStruct((16, columns), BF16))
    return pl.pallas_call(
        functools.partial(rank_kernel, n, rows, depth),
        in_specs=[VMEM] * (4 + n),
        out_specs=[VMEM] * len(out_shape),
        out_shape=out_shape,
        compiler_params=pltpu.CompilerParams(vmem_limit_bytes=32 * MEBI),
        name="rank_products",
    )(base, table, own, near, *tokens)


def broadcast_lane(tile, lane):
    return jnp.broadcast_to(tile[:, lane : lane + 1], tile.shape)


def combine_part_kernel(base_ref, mine_ref, theirs_ref, cache_ref, out_ref, *replies):
    half = base_ref.shape[1] // 2
    own = base_ref[:, :half] + theirs_ref[:, :half].astype(F32)
    out_ref[:, :half] = own.astype(BF16)
    sums = mine_ref[:, half:].astype(F32) + theirs_ref[:, half:].astype(F32)
    sums = split(sums[:8] + sums[8:])
    out_ref[:, half : half + 256] = sums[:, :256]
    out_ref[:, half + 256 :] = cache_ref[...]
    for i, ref in enumerate(replies):
        ref[...] = sums[:, 128 * (i + 2) : 128 * (i + 3)]


def combine_part(n, base, mine, theirs, cache):
    shapes = [(16, base.shape[1] // 2 + 256 + cache.shape[1])] + [(16, 128)] * n
    return pl.pallas_call(
        combine_part_kernel,
        in_specs=[VMEM] * 4,
        out_specs=[VMEM] * len(shapes),
        out_shape=[jax.ShapeDtypeStruct(shape, BF16) for shape in shapes],
        compiler_params=pltpu.CompilerParams(vmem_limit_bytes=32 * MEBI),
        name="combine_part",
    )(base, mine, theirs, cache)


def combine_cache_kernel(a_ref, b_ref, _, out_ref):
    lane = lax.broadcasted_iota(jnp.int32, (16, 128), 1)
    for p in range(out_ref.shape[1] // PAIR):
        end = slice(p * PAIR + GROUP * HD, (p + 1) * PAIR)
        a, b = a_ref[:, end].astype(F32), b_ref[:, end].astype(F32)
        top = jnp.maximum(a, b)
        fa = jnp.exp2(jnp.minimum(a - top, 0.0) * EXPONENT)
        fb = jnp.exp2(jnp.minimum(b - top, 0.0) * EXPONENT)
        total = fa * totals(a) + fb * totals(b)
        high = rounded(total)
        stats = jnp.where(lane < GROUP, top, 0.0)
        stats = jnp.where(lane // GROUP == 1, pltpu.roll(high, GROUP, 1), stats)
        stats = jnp.where(lane // GROUP == 2, pltpu.roll(total - high, 2 * GROUP, 1), stats)
        out_ref[:, end] = stats.astype(BF16)
        for g in range(GROUP):
            at = slice(p * PAIR + g * HD, p * PAIR + (g + 1) * HD)
            out_ref[:, at] = (
                broadcast_lane(fa, g) * a_ref[:, at].astype(F32)
                + broadcast_lane(fb, g) * b_ref[:, at].astype(F32)
            ).astype(BF16)


def totals(stats):
    return pltpu.roll(stats, 128 - GROUP, 1) + pltpu.roll(stats, 128 - 2 * GROUP, 1)


def combine_cache(a, b, earlier):
    return pl.pallas_call(
        combine_cache_kernel,
        in_specs=[VMEM] * 3,
        out_specs=VMEM,
        out_shape=jax.ShapeDtypeStruct(a.shape, BF16),
        compiler_params=pltpu.CompilerParams(vmem_limit_bytes=32 * MEBI),
        name="combine_cache",
    )(a, b, earlier)


def merge_kernel(n, paired, width_all, *refs):
    table_ref, qrot_ref, pa_ref, pb_ref = refs[:4]
    backs, (ua_ref, ub_ref, out_ref) = refs[4 : 4 + n], refs[4 + n :]
    pairs = qrot_ref.shape[1] // (GROUP * HD)
    width = pairs * 2 * HD
    cosine, sine = table_ref[8:16], table_ref[16:]
    head = width + 256
    sums = pa_ref[:, :head].astype(F32) + pb_ref[:, :head].astype(F32)
    tail = sums[:8, width : width + 256] + sums[8:, width : width + 256]
    squares, z = tail[:, :128], tail[:, 128:]
    for ref in backs:
        z = z + joined(ref[...])
    lane8 = lax.broadcasted_iota(jnp.int32, (8, 128), 1)
    z = jnp.concatenate(
        [jnp.where(lane8 < RANK, z, 0.0), jnp.where(lane8 < RANK, 0.0, z)], 0
    ).astype(BF16)
    adapted = []
    for ref in (ua_ref, ub_ref):
        ups = jnp.concatenate([ref[:, i : i + 128] for i in range(0, 16 * HD, 128)], 0)
        adapted.append(lax.dot_general(z, ups, NT, preferred_element_type=F32))
    if paired:
        even = lax.axis_index("dp") % 2 == 0
        a, b = adapted
        adapted = [jnp.where(even, a, b), jnp.where(even, b, a)]
    total = sums[:, :width] + jnp.concatenate(adapted, 1)
    scale = lax.rsqrt(squares / width_all + EPSILON)
    lane = lax.broadcasted_iota(jnp.int32, (16, 128), 1)
    step = lax.broadcasted_iota(jnp.int32, (16, 128), 0) % STEPS
    first = first_rows((8, 128))

    def of_step(tiles, j):
        return jnp.concatenate(
            [
                jnp.where(first, tile[j : j + 1], tile[STEPS + j : STEPS + j + 1])
                for tile in tiles
            ],
            0,
        )

    for p in range(pairs):
        new_keys, new_values = [], []
        for e in range(2):
            at = slice((2 * p + e) * HD, (2 * p + e + 1) * HD)
            new_keys.append(rounded(rotated(total[:8, at] * scale, cosine, sine)))
            new_values.append(rounded(total[8:, at] * scale))
            fresh = jnp.concatenate([new_keys[e], new_values[e]], 0)
            start = pairs * GROUP * HD + (2 * p + e) * HD
            out_ref[:, start : start + HD] = fresh.astype(BF16)
        keys = [of_step(new_keys, j) for j in range(STEPS)]
        values = [of_step(new_values, j) for j in range(STEPS)]
        scores = [jnp.zeros((16, 128), F32) for _ in range(STEPS)]
        for g in range(GROUP):
            q = qrot_ref[:, (p * GROUP + g) * HD : (p * GROUP + g + 1) * HD].astype(F32)
            for j in range(STEPS):
                dot = jnp.sum(q * keys[j], 1, keepdims=True)
                scores[j] = jnp.where(lane == g, dot, scores[j])
        scores = [jnp.where(j <= step, scores[j], MASKED_SCORE) for j in range(STEPS)]
        end = slice(head + p * PAIR + GROUP * HD, head + (p + 1) * PAIR)
        stats = [ref[:, end].astype(F32) for ref in (pa_ref, pb_ref)]
        top = functools.reduce(jnp.maximum, scores + stats)
        fresh = [rounded(jnp.exp2((scores[j] - top) * EXPONENT)) for j in range(STEPS)]
        factors = [jnp.exp2(jnp.minimum(s - top, 0.0) * EXPONENT) for s in stats]
        denom = functools.reduce(jnp.add, fresh)
        for factor, s in zip(factors, stats):
            denom = denom + factor * totals(s)
        inverse = 1.0 / denom
        coefficients = [c * inverse for c in fresh + factors]
        for g in range(GROUP):
            at = slice(head + p * PAIR + g * HD, head + p * PAIR + (g + 1) * HD)
            terms = values + [ref[:, at].astype(F32) for ref in (pa_ref, pb_ref)]
            tile = jnp.zeros((16, 128), F32)
            for c, term in zip(coefficients, terms):
                tile = tile + broadcast_lane(c, g) * term
            out_ref[:, (p * GROUP + g) * HD : (p * GROUP + g + 1) * HD] = tile.astype(BF16)


def merge(paired, width_all, table, qrot, parts, backs, ups):
    operands = [table, qrot, *parts, *backs, *ups]
    pairs = qrot.shape[1] // (GROUP * HD)
    return pl.pallas_call(
        functools.partial(merge_kernel, len(backs), paired, width_all),
        in_specs=[VMEM] * len(operands),
        out_specs=VMEM,
        out_shape=jax.ShapeDtypeStruct((16, pairs * (GROUP + 2) * HD), BF16),
        compiler_params=pltpu.CompilerParams(vmem_limit_bytes=32 * MEBI),
        name="merge",
    )(*operands)


def place_kernel(mine_ref, theirs_ref, keys_out, values_out, out_ref):
    pairs = mine_ref.shape[1] // ((GROUP + 2) * HD)
    for c, ref in enumerate((mine_ref, theirs_ref)):
        for p in range(pairs):
            pair = pair_at(c * pairs + p)
            tiles = ref[:, p * GROUP * HD : (p + 1) * GROUP * HD].astype(F32)
            size = GROUP * HD
            for e in range(2):
                at = pl.ds(pl.multiple_of((2 * pair + e) * size, size), size)
                for s in range(2):
                    rows = slice(8 * e + 4 * s, 8 * e + 4 * s + 4)
                    out_ref[s, :, at] = tiles[rows].astype(BF16)
            start = pairs * GROUP * HD + p * 2 * HD
            fresh = ref[:, start : start + 2 * HD].astype(F32)
            at = pl.ds(pl.multiple_of(pair * 2 * HD, 2 * HD), 2 * HD)
            for i, out in enumerate((keys_out, values_out)):
                for s in range(2):
                    rows = slice(8 * i + 4 * s, 8 * i + 4 * s + 4)
                    out[s, :, at] = fresh[rows].astype(BF16)


def place(width, mine, theirs):
    return pl.pallas_call(
        place_kernel,
        in_specs=[VMEM] * 2,
        out_specs=[VMEM] * 3,
        out_shape=[
            jax.ShapeDtypeStruct((2, STEPS, width), BF16),
            jax.ShapeDtypeStruct((2, STEPS, width), BF16),
            jax.ShapeDtypeStruct((2, STEPS, GROUP * width), BF16),
        ],
        compiler_params=pltpu.CompilerParams(vmem_limit_bytes=32 * MEBI),
        name="place",
    )(mine, theirs)


def swap(value, axis, n, distance):
    return lax.ppermute(value, axis, [(i, i ^ distance) for i in range(n)])


def shards(
    n_dp,
    n_tensor,
    hidden,
    norm_gain,
    queries,
    key_weight,
    value_weight,
    key_down,
    key_up,
    value_down,
    value_up,
    key_cache,
    value_cache,
    lengths,
):
    depth, width = key_weight.shape
    rows = key_down.shape[0]
    to_dp = lambda value, distance: swap(value, "dp", n_dp, distance)
    to_tensor = lambda value, distance: swap(value, "tensor", n_tensor, distance)
    partners = range(2, n_dp, 2)
    n = len(partners)
    paired = n_dp == 4

    down, tokens, own = pack(
        lengths, hidden, norm_gain, key_down, value_down, key_up, value_up
    )
    near = to_dp(down, 1)
    sent = [to_dp(tokens, d) for d in partners]
    keep, send, base, qrot, table = local(
        own, queries, key_cache, value_cache, key_weight, value_weight
    )
    received = to_tensor(send, 1)
    columns = UP_COLUMNS if paired else 0
    message, *has = rank_products(rows, depth, columns, base, table, down, near, [tokens, *sent])
    if paired:
        ups = [has[0], to_dp(has[0], 1)]
    else:
        ups = lax.all_gather(tokens[:, depth // 2 :], "dp")
        ups = ups.reshape(n_dp, 16, -1, 128).transpose(0, 2, 1, 3)
        ups = ups.reshape(2, 2, 16, 16, 128).transpose(0, 1, 3, 2, 4).reshape(2, 2, 16, -1)
        ups = lax.dynamic_index_in_dim(ups, lax.axis_index("tensor") % 2, 0, keepdims=False)
        ups = [ups[0], ups[1]]
    cache = combine_cache(keep, received, message)
    part, *replies = combine_part(n, base, message, to_tensor(message, 1), cache)
    part_far = to_tensor(part, 2)
    places = [(s, t) for s in range(n_dp) for t in range(n_tensor)]
    backs = []
    for reply, d in zip(replies, partners):
        for e in (0, 2):
            perm = [(s * n_tensor + t, (s ^ d) * n_tensor + (t ^ e)) for s, t in places]
            backs.append(lax.ppermute(reply, ("dp", "tensor"), perm))
    merged = merge(
        paired,
        float(depth * n_tensor),
        table,
        qrot,
        (part, part_far),
        backs,
        ups,
    )
    return place(width, merged, to_tensor(merged, 1))


def solution(mesh):
    body = functools.partial(shards, mesh.shape["dp"], mesh.shape["tensor"])
    return jax.shard_map(
        body,
        mesh=mesh,
        in_specs=(
            P(("groups", "dp"), None, "tensor"),
            P("tensor"),
            P(("groups", "dp"), None, None),
            P("tensor", None),
            P("tensor", None),
            P(("groups", "dp"), "tensor"),
            P(("groups", "dp"), None),
            P(("groups", "dp"), "tensor"),
            P(("groups", "dp"), None),
            P(("groups", "dp"), "tensor", None),
            P(("groups", "dp"), "tensor", None),
            P(("groups", "dp")),
        ),
        out_specs=(
            P(("groups", "dp"), None, None),
            P(("groups", "dp"), None, None),
            P(("groups", "dp"), None, None),
        ),
        check_vma=False,
    )
```

```python
import functools
import math

import jax
import jax.numpy as jnp
from jax import lax
from jax.experimental import pallas as pl
from jax.experimental.pallas import tpu as pltpu
from jax.sharding import PartitionSpec as P

HD = 128
GROUP = 8
STEPS = 4
RANK = 64
EPSILON = 1e-05
ROPE_BASE = 500000.0
MASKED_SCORE = -1e30
LOWEST_TOP = -1e20
EXPONENT = math.log2(math.e) / math.sqrt(HD)
PAIR = GROUP * HD + 128
UP_COLUMNS = 3584
CHUNK = 256

F32 = jnp.float32
BF16 = jnp.bfloat16
NT = (((1,), (1,)), ((), ()))
VMEM = pl.BlockSpec(memory_space=pltpu.VMEM)
HBM = pl.BlockSpec(memory_space=pltpu.HBM)
MEBI = 2**20
WHOLE_VMEM = 65000 * 1024
LOCAL_VMEM = 54900 * 1024


def rounded(value):
    return value.astype(BF16).astype(F32)


def split(value):
    high = rounded(value)
    return jnp.concatenate([high, value - high], 0).astype(BF16)


def joined(tile):
    wide = tile.astype(F32)
    return wide[:8] + wide[8:]


def rotated(tile, cosine, sine):
    return tile * cosine + pltpu.roll(tile, HD // 2, 1) * sine


def first_rows(shape):
    return lax.broadcasted_iota(jnp.int32, shape, 0) % 8 < STEPS


def exchanged(a, b):
    first = first_rows(a.shape)
    return (
        jnp.where(first, a, pltpu.roll(b, STEPS, 0)),
        jnp.where(first, pltpu.roll(a, STEPS, 0), b),
    )


def flat(matrix):
    return jnp.concatenate([matrix[i : i + 16] for i in range(0, matrix.shape[0], 16)], 1)


def pack_kernel(*refs):
    sources, outs, held = refs[:7], refs[7:10], refs[10:17]
    (a_ref, b_ref, own_ref), sems, out_sems = refs[17:20], refs[20], refs[21]
    targets = [*outs[:2], outs[2].at[:, pl.ds(0, own_ref.shape[1])]]
    copies = [
        pltpu.make_async_copy(source, target, sems.at[i])
        for i, (source, target) in enumerate(zip(sources, held))
    ]
    for copy in copies:
        copy.start()
    backs = [
        pltpu.make_async_copy(source, target, out_sems.at[i])
        for i, (source, target) in enumerate(zip((a_ref, b_ref, own_ref), targets))
    ]
    kd_ref, vd_ref, x_ref, gain_ref, lengths_ref, ku_ref, vu_ref = held
    own, depth = kd_ref.shape
    for slot, ref in enumerate((kd_ref, vd_ref)):
        copies[slot].wait()
        down = ref[...]
        if own < 16:
            down = jnp.concatenate([down, jnp.zeros((16 - own, depth), F32)], 0)
        a_ref[:, slot * depth : (slot + 1) * depth] = down.astype(BF16)
    backs[0].start()
    for copy in copies[2:]:
        copy.wait()
    x = jnp.concatenate([x_ref[0].astype(F32), x_ref[1].astype(F32)], 0)
    gain = gain_ref[...].astype(F32)
    scaled = jnp.concatenate(
        [x[:, i * 128 : (i + 1) * 128] * gain[i : i + 1] for i in range(depth // 128)], 1
    )
    scaled = jnp.concatenate([scaled[:, : depth // 2], scaled[:, depth // 2 :]], 0).astype(BF16)
    b_ref[:, : depth // 2] = scaled
    ups = jnp.concatenate([ku_ref[...], vu_ref[...]], 0).T.astype(BF16)
    b_ref[:, depth // 2 :] = flat(ups)
    backs[1].start()
    own_ref[:, : depth // 2] = scaled
    row = lax.broadcasted_iota(jnp.int32, (16, 128), 0)
    lengths = lengths_ref[...]
    length = jnp.where(row % 8 < STEPS, lengths[:, :1], lengths[:, 1:])
    length = jnp.where(row < 8, length // 64 * 64, length % 64)
    own_ref[:, depth // 2 : depth // 2 + 128] = length.astype(F32).astype(BF16)
    squares = jnp.broadcast_to(jnp.sum(x * x, 1, keepdims=True), (8, 128))
    own_ref[:, depth // 2 + 128 :] = split(squares)
    backs[2].start()
    for copy in backs:
        copy.wait()


def pack(lengths, hidden, gain, key_down, value_down, key_up, value_up):
    operands = [key_down, value_down, hidden, gain.reshape(-1, 128), lengths.reshape(1, 2)]
    operands += [key_up.T, value_up.T]
    depth = hidden.shape[2]
    ups = key_up.shape[0] * 8
    outs = [
        jax.ShapeDtypeStruct((16, 2 * depth), BF16),
        jax.ShapeDtypeStruct((16, depth // 2 + ups), BF16),
        jax.ShapeDtypeStruct((16, depth // 2 + 256 + ups), BF16),
    ]
    scratch = [*operands, *outs[:2], jax.ShapeDtypeStruct((16, depth // 2 + 256), BF16)]
    return pl.pallas_call(
        pack_kernel,
        in_specs=[HBM] * len(operands),
        out_specs=[HBM] * len(outs),
        out_shape=outs,
        scratch_shapes=[pltpu.VMEM(o.shape, o.dtype) for o in scratch]
        + [pltpu.SemaphoreType.DMA((len(operands),)), pltpu.SemaphoreType.DMA((len(outs),))],
        compiler_params=pltpu.CompilerParams(vmem_limit_bytes=WHOLE_VMEM),
        name="pack",
    )(*operands)


def tables(length):
    shape = length.shape
    row = lax.broadcasted_iota(jnp.int32, shape, 0)
    lane = lax.broadcasted_iota(jnp.int32, shape, 1)
    position = length + (row % STEPS).astype(F32)
    pair = lane % (HD // 2)
    frequency = jnp.ones(shape, F32)
    for bit in range(6):
        factor = ROPE_BASE ** (-(2.0 * 2**bit) / HD)
        frequency = jnp.where((pair >> bit) & 1 == 1, frequency * factor, frequency)
    cosine, sine = cosine_and_sine(position * frequency)
    return cosine, jnp.where(lane < HD // 2, -sine, sine)


def cosine_and_sine(angle):
    turns = jnp.floor(angle * (2.0 / math.pi) + 0.5)
    rest = ((angle - turns * 1.5703125) - turns * 4.8351287841796875e-4) - turns * 3.1391647e-7
    square = rest * rest
    sine = -1.9515295891e-4 * square + 8.3321608736e-3
    sine = (sine * square - 1.6666654611e-1) * square * rest + rest
    cosine = 2.443315711809948e-5 * square - 1.388731625493765e-3
    cosine = (cosine * square + 4.166664568298827e-2) * square * square - 0.5 * square + 1.0
    quadrant = turns.astype(jnp.int32)
    swap_them = (quadrant & 1) == 1
    cosine, sine = jnp.where(swap_them, sine, cosine), jnp.where(swap_them, cosine, sine)
    cosine = jnp.where(((quadrant + 1) & 2) == 2, -cosine, cosine)
    sine = jnp.where((quadrant & 2) == 2, -sine, sine)
    return cosine, sine


def rotated_rows(pairs, cosine, sine, q_ref, qrot_ref):
    zero = jnp.zeros((32, HD), F32)
    result = []
    for p in pairs:
        halves = [[], []]
        for e in range(2):
            for g in range(GROUP):
                at = slice(((2 * p + e) * GROUP + g) * HD, ((2 * p + e) * GROUP + g + 1) * HD)
                q = jnp.concatenate([q_ref[0, :, at].astype(F32), q_ref[1, :, at].astype(F32)], 0)
                halves[e].append(rotated(q, cosine, sine))
        if qrot_ref is not None:
            for g in range(GROUP):
                at = slice((p * GROUP + g) * HD, (p * GROUP + g + 1) * HD)
                qrot_ref[:, at] = jnp.concatenate([halves[0][g], halves[1][g]], 0).astype(BF16)
        mixed = [[exchanged(halves[e][g], halves[e][g + 4]) for g in range(4)] for e in range(2)]
        for s in range(2):
            rows = [jnp.concatenate([mixed[e][g][s] for g in range(4)], 0) for e in range(2)]
            result.append(
                jnp.concatenate(
                    [jnp.concatenate([rows[0], zero], 1), jnp.concatenate([zero, rows[1]], 1)], 0
                ).astype(BF16)
            )
    return result


def attend(pairs, masks, queries, k_ref, v_ref, between, out_ref):
    scores = []
    for i, p in enumerate(pairs):
        for s in range(2):
            keys = k_ref[s, :, 2 * p * HD : 2 * (p + 1) * HD]
            score = lax.dot_general(queries[2 * i + s], keys, NT, preferred_element_type=F32)
            scores.append(score + jnp.concatenate([masks[s]] * (score.shape[0] // 8), 0))
    between()
    scores = jnp.concatenate(scores, 0)
    top = rounded(jnp.maximum(jnp.max(scores, 1, keepdims=True), LOWEST_TOP))
    weights = jnp.exp2((scores - top) * EXPONENT).astype(BF16)
    total = jnp.sum(weights.astype(F32), 1, keepdims=True)
    high = rounded(total)
    columns = (top, high, total - high)
    lane8 = lax.broadcasted_iota(jnp.int32, (8, 128), 1)
    numers = []
    for i, p in enumerate(pairs):
        for s in range(2):
            at = slice(64 * (2 * i + s), 64 * (2 * i + s + 1))
            values = v_ref[s, :, 2 * p * HD : 2 * (p + 1) * HD]
            numers.append(jnp.dot(weights[at], values, preferred_element_type=F32))
    for i, p in enumerate(pairs):
        outs, ends = [[], []], []
        for e in range(2):
            back, stats = [], []
            for s in range(2):
                tile = jnp.zeros((8, 128), F32)
                for g in range(4):
                    row = 64 * (2 * i + s) + 32 * e + 8 * g
                    for slot, value in enumerate(columns):
                        tile = jnp.where(lane8 == slot * GROUP + g, value[row : row + 8], tile)
                stats.append(tile)
            for g in range(4):
                at = slice(32 * e + 8 * g, 32 * e + 8 * g + 8)
                cols = slice(e * HD, (e + 1) * HD)
                back.append(exchanged(numers[2 * i][at, cols], numers[2 * i + 1][at, cols]))
            outs[e] = [b[0] for b in back] + [b[1] for b in back]
            a, b = exchanged(*stats)
            ends.append(jnp.where(lane8 % 8 < 4, a, pltpu.roll(b, 4, 1)))
        for g in range(GROUP):
            at = slice(i * PAIR + g * HD, i * PAIR + (g + 1) * HD)
            out_ref[:, at] = jnp.concatenate([outs[0][g], outs[1][g]], 0).astype(BF16)
        out_ref[:, i * PAIR + GROUP * HD : (i + 1) * PAIR] = jnp.concatenate(ends, 0).astype(BF16)


def pair_at(i):
    return i ^ (lax.axis_index("tensor") % 2 * 2)


def local_kernel(
    x_hbm, q_hbm, k_hbm, v_hbm, wk_hbm, wv_hbm,
    keep_ref, send_ref, base_ref, qrot_ref, table_ref,
    x_ref, q_ref, k_ref, v_ref, wk_ref, wv_ref, x_sem, q_sem, cache_sem, weight_sem,
):
    pairs = k_hbm.shape[2] // (2 * HD)
    chunks = wk_hbm.shape[0] // CHUNK
    width = wk_hbm.shape[1]
    core = lax.axis_index("tensor") % 2
    x_copy = pltpu.make_async_copy(x_hbm.at[:, pl.ds(0, x_ref.shape[1])], x_ref, x_sem)
    x_copy.start()
    groups = []
    for h in range(2):
        copies = []
        trio = ((q_hbm, q_ref, q_sem.at[h]), (k_hbm, k_ref, cache_sem.at[h, 0]))
        for source, target, sem in (*trio, (v_hbm, v_ref, cache_sem.at[h, 1])):
            size = source.shape[2] // 2
            start = pl.multiple_of((core ^ h) * size, size)
            copies.append(
                pltpu.make_async_copy(
                    source.at[:, :, pl.ds(start, size)],
                    target.at[:, :, pl.ds(h * size, size)],
                    sem,
                )
            )
        groups.append(copies)
    groups[0][1].start()
    for h in range(2):
        groups[h][0].start()
    weights = []
    for c in range(chunks):
        at = pl.ds(c * CHUNK, CHUNK)
        weights.append(
            [
                pltpu.make_async_copy(source.at[at], target.at[at], weight_sem.at[c, i])
                for i, (source, target) in enumerate(((wk_hbm, wk_ref), (wv_hbm, wv_ref)))
            ]
        )
    def start(copies):
        for copy in copies:
            copy.start()

    x_copy.wait()
    groups[0][2].start()
    start(groups[1][1:])
    for copies in weights[: chunks // 4]:
        start(copies)
    half = wk_hbm.shape[0] // 2
    x = x_ref[:, :half].astype(F32)
    x = jnp.concatenate([x[:8], x[8:]], 1).astype(BF16)
    length = joined(x_ref[:, half : half + 128])
    cosine, sine = tables(length)
    table_ref[...] = jnp.concatenate([joined(x_ref[:, half + 128 : half + 256]), cosine, sine], 0)
    limit = length - (lax.axis_index("tensor") * k_hbm.shape[1]).astype(F32)
    place = lax.broadcasted_iota(jnp.int32, (8, k_hbm.shape[1]), 1).astype(F32)
    masks = [
        jnp.where(place < limit[STEPS * s : STEPS * s + 1, :1], 0.0, MASKED_SCORE) for s in range(2)
    ]
    queries = []
    for h in range(2):
        groups[h][0].wait()
        own = range(h * pairs // 2, (h + 1) * pairs // 2)
        queries.append(rotated_rows(own, cosine, sine, q_ref, None if h else qrot_ref))
    parts = []

    def project(c):
        at = slice(c * CHUNK, (c + 1) * CHUNK)
        halves = []
        for copy, ref in zip(weights[c], (wk_ref, wv_ref)):
            copy.wait()
            halves.append(jnp.dot(x[:, at], ref[at], preferred_element_type=F32))
        parts.append(jnp.concatenate(halves, 0))

    def between(h):
        groups[h][2].wait()
        if h == 0:
            for copies in weights[chunks // 2 : 3 * chunks // 4]:
                start(copies)
        else:
            for c in range(chunks // 2):
                project(c)

    for h, out_ref in enumerate((keep_ref, send_ref)):
        groups[h][1].wait()
        for copies in weights[3 * chunks // 4 :] if h else weights[chunks // 4 : chunks // 2]:
            start(copies)
        attend(
            range(h * pairs // 2, (h + 1) * pairs // 2),
            masks, queries[h], k_ref, v_ref, functools.partial(between, h), out_ref,
        )
    for c in range(chunks // 2, chunks):
        project(c)
    total = functools.reduce(jnp.add, parts)
    lower, upper = total[:, : width // 2], total[:, width // 2 :]
    base_ref[:, : width // 2] = jnp.where(core == 0, lower, upper)
    base_ref[:, width // 2 :] = jnp.where(core == 0, upper, lower)


def local(message, queries, key_cache, value_cache, key_weight, value_weight):
    seqs, length, width = key_cache.shape
    depth = key_weight.shape[0]
    pairs = width // (2 * HD)
    operands = [message, queries, key_cache, value_cache, key_weight, value_weight]
    return pl.pallas_call(
        local_kernel,
        in_specs=[HBM] * 6,
        out_specs=[VMEM] * 5,
        out_shape=[
            jax.ShapeDtypeStruct((16, pairs // 2 * PAIR), BF16),
            jax.ShapeDtypeStruct((16, pairs // 2 * PAIR), BF16),
            jax.ShapeDtypeStruct((16, width), F32),
            jax.ShapeDtypeStruct((16, pairs // 2 * GROUP * HD), BF16),
            jax.ShapeDtypeStruct((24, 128), F32),
        ],
        scratch_shapes=[pltpu.VMEM((16, depth // 2 + 256), BF16)]
        + [pltpu.VMEM(o.shape, BF16) for o in operands[1:]]
        + [
            pltpu.SemaphoreType.DMA,
            pltpu.SemaphoreType.DMA((2,)),
            pltpu.SemaphoreType.DMA((2, 2)),
            pltpu.SemaphoreType.DMA((depth // CHUNK, 2)),
        ],
        compiler_params=pltpu.CompilerParams(vmem_limit_bytes=LOCAL_VMEM),
        cost_estimate=pl.CostEstimate(
            flops=4 * 64 * 256 * seqs * length * pairs + 4 * 16 * depth * width,
            bytes_accessed=4 * seqs * length * width + 4 * depth * width,
            transcendentals=64 * seqs * length * pairs,
        ),
        name="local",
    )(*operands)


def rank_kernel(n, rows, depth, *refs):
    base_ref, table_ref, own_ref, near_ref = refs[:4]
    tokens, (out_ref, *has) = refs[4 : 4 + n], refs[4 + n :]
    half = base_ref.shape[1] // 2
    place = lax.axis_index("dp")
    x = []
    for ref in tokens:
        part = ref[:, : depth // 2].astype(F32)
        x.append(jnp.concatenate([part[:8], part[8:]], 1))
    x = jnp.concatenate(x, 0).astype(BF16)
    down = jnp.concatenate(
        [ref[:, at : at + depth] for at in (0, depth) for ref in (own_ref, near_ref)], 0
    )
    products = lax.dot_general(x, down, NT, preferred_element_type=F32)
    products = jnp.concatenate([products, jnp.zeros_like(products)], 1)
    lane = lax.broadcasted_iota(jnp.int32, products.shape, 1)
    z = None
    for i in range(4):
        part = jnp.where(lane // 16 == i, products, 0.0)
        column = (place ^ (i % 2)) * rows + i // 2 * RANK
        part = pltpu.roll(part, (column + 128 - 16 * i) % 128, 1)
        z = part if z is None else z + part
    out_ref[:, :half] = base_ref[:, half:].astype(BF16)
    out_ref[:, half : half + 128] = split(table_ref[:8])
    for i in range(n):
        at = half + 128 * (i + 1)
        out_ref[:, at : at + 128] = split(z[8 * i : 8 * i + 8])
    for ref in has:
        here = place // 2 == lax.axis_index("tensor") % 2
        mine, far = (token[:, depth // 2 :].astype(F32) for token in tokens[:2])
        ref[:, : mine.shape[1]] = jnp.where(here, mine, far).astype(BF16)
        ref[:, mine.shape[1] :] = jnp.zeros((16, ref.shape[1] - mine.shape[1]), BF16)


def rank_products(rows, depth, columns, base, table, own, near, tokens):
    n = len(tokens)
    out_shape = [jax.ShapeDtypeStruct((16, base.shape[1] // 2 + 128 * (n + 1)), BF16)]
    if columns:
        out_shape.append(jax.ShapeDtypeStruct((16, columns), BF16))
    return pl.pallas_call(
        functools.partial(rank_kernel, n, rows, depth),
        in_specs=[VMEM] * (4 + n),
        out_specs=[VMEM] * len(out_shape),
        out_shape=out_shape,
        compiler_params=pltpu.CompilerParams(vmem_limit_bytes=32 * MEBI),
        name="rank_products",
    )(base, table, own, near, *tokens)


def broadcast_lane(tile, lane):
    return jnp.broadcast_to(tile[:, lane : lane + 1], tile.shape)


def combine_part_kernel(base_ref, mine_ref, theirs_ref, cache_ref, out_ref, *replies):
    half = base_ref.shape[1] // 2
    own = base_ref[:, :half] + theirs_ref[:, :half].astype(F32)
    out_ref[:, :half] = own.astype(BF16)
    sums = mine_ref[:, half:].astype(F32) + theirs_ref[:, half:].astype(F32)
    sums = split(sums[:8] + sums[8:])
    out_ref[:, half : half + 256] = sums[:, :256]
    out_ref[:, half + 256 :] = cache_ref[...]
    for i, ref in enumerate(replies):
        ref[...] = sums[:, 128 * (i + 2) : 128 * (i + 3)]


def combine_part(n, base, mine, theirs, cache):
    shapes = [(16, base.shape[1] // 2 + 256 + cache.shape[1])] + [(16, 128)] * n
    return pl.pallas_call(
        combine_part_kernel,
        in_specs=[VMEM] * 4,
        out_specs=[VMEM] * len(shapes),
        out_shape=[jax.ShapeDtypeStruct(shape, BF16) for shape in shapes],
        compiler_params=pltpu.CompilerParams(vmem_limit_bytes=32 * MEBI),
        name="combine_part",
    )(base, mine, theirs, cache)


def combine_cache_kernel(a_ref, b_ref, _, out_ref):
    lane = lax.broadcasted_iota(jnp.int32, (16, 128), 1)
    for p in range(out_ref.shape[1] // PAIR):
        end = slice(p * PAIR + GROUP * HD, (p + 1) * PAIR)
        a, b = a_ref[:, end].astype(F32), b_ref[:, end].astype(F32)
        top = jnp.maximum(a, b)
        fa = jnp.exp2(jnp.minimum(a - top, 0.0) * EXPONENT)
        fb = jnp.exp2(jnp.minimum(b - top, 0.0) * EXPONENT)
        total = fa * totals(a) + fb * totals(b)
        high = rounded(total)
        stats = jnp.where(lane < GROUP, top, 0.0)
        stats = jnp.where(lane // GROUP == 1, pltpu.roll(high, GROUP, 1), stats)
        stats = jnp.where(lane // GROUP == 2, pltpu.roll(total - high, 2 * GROUP, 1), stats)
        out_ref[:, end] = stats.astype(BF16)
        for g in range(GROUP):
            at = slice(p * PAIR + g * HD, p * PAIR + (g + 1) * HD)
            out_ref[:, at] = (
                broadcast_lane(fa, g) * a_ref[:, at].astype(F32)
                + broadcast_lane(fb, g) * b_ref[:, at].astype(F32)
            ).astype(BF16)


def totals(stats):
    return pltpu.roll(stats, 128 - GROUP, 1) + pltpu.roll(stats, 128 - 2 * GROUP, 1)


def combine_cache(a, b, earlier):
    return pl.pallas_call(
        combine_cache_kernel,
        in_specs=[VMEM] * 3,
        out_specs=VMEM,
        out_shape=jax.ShapeDtypeStruct(a.shape, BF16),
        compiler_params=pltpu.CompilerParams(vmem_limit_bytes=32 * MEBI),
        name="combine_cache",
    )(a, b, earlier)


def merge_kernel(n, paired, width_all, *refs):
    table_ref, qrot_ref, pa_ref, pb_ref = refs[:4]
    backs, (ua_ref, ub_ref, out_ref) = refs[4 : 4 + n], refs[4 + n :]
    pairs = qrot_ref.shape[1] // (GROUP * HD)
    width = pairs * 2 * HD
    cosine, sine = table_ref[8:16], table_ref[16:]
    head = width + 256
    sums = pa_ref[:, :head].astype(F32) + pb_ref[:, :head].astype(F32)
    tail = sums[:8, width : width + 256] + sums[8:, width : width + 256]
    squares, z = tail[:, :128], tail[:, 128:]
    for ref in backs:
        z = z + joined(ref[...])
    lane8 = lax.broadcasted_iota(jnp.int32, (8, 128), 1)
    z = jnp.concatenate(
        [jnp.where(lane8 < RANK, z, 0.0), jnp.where(lane8 < RANK, 0.0, z)], 0
    ).astype(BF16)
    adapted = []
    for ref in (ua_ref, ub_ref):
        ups = jnp.concatenate([ref[:, i : i + 128] for i in range(0, 16 * HD, 128)], 0)
        adapted.append(lax.dot_general(z, ups, NT, preferred_element_type=F32))
    if paired:
        even = lax.axis_index("dp") % 2 == 0
        a, b = adapted
        adapted = [jnp.where(even, a, b), jnp.where(even, b, a)]
    total = sums[:, :width] + jnp.concatenate(adapted, 1)
    scale = lax.rsqrt(squares / width_all + EPSILON)
    lane = lax.broadcasted_iota(jnp.int32, (16, 128), 1)
    step = lax.broadcasted_iota(jnp.int32, (16, 128), 0) % STEPS
    first = first_rows((8, 128))

    def of_step(tiles, j):
        return jnp.concatenate(
            [
                jnp.where(first, tile[j : j + 1], tile[STEPS + j : STEPS + j + 1])
                for tile in tiles
            ],
            0,
        )

    for p in range(pairs):
        new_keys, new_values = [], []
        for e in range(2):
            at = slice((2 * p + e) * HD, (2 * p + e + 1) * HD)
            new_keys.append(rounded(rotated(total[:8, at] * scale, cosine, sine)))
            new_values.append(rounded(total[8:, at] * scale))
            fresh = jnp.concatenate([new_keys[e], new_values[e]], 0)
            start = pairs * GROUP * HD + (2 * p + e) * HD
            out_ref[:, start : start + HD] = fresh.astype(BF16)
        keys = [of_step(new_keys, j) for j in range(STEPS)]
        values = [of_step(new_values, j) for j in range(STEPS)]
        scores = [jnp.zeros((16, 128), F32) for _ in range(STEPS)]
        for g in range(GROUP):
            q = qrot_ref[:, (p * GROUP + g) * HD : (p * GROUP + g + 1) * HD].astype(F32)
            for j in range(STEPS):
                dot = jnp.sum(q * keys[j], 1, keepdims=True)
                scores[j] = jnp.where(lane == g, dot, scores[j])
        scores = [jnp.where(j <= step, scores[j], MASKED_SCORE) for j in range(STEPS)]
        end = slice(head + p * PAIR + GROUP * HD, head + (p + 1) * PAIR)
        stats = [ref[:, end].astype(F32) for ref in (pa_ref, pb_ref)]
        top = functools.reduce(jnp.maximum, scores + stats)
        fresh = [rounded(jnp.exp2((scores[j] - top) * EXPONENT)) for j in range(STEPS)]
        factors = [jnp.exp2(jnp.minimum(s - top, 0.0) * EXPONENT) for s in stats]
        denom = functools.reduce(jnp.add, fresh)
        for factor, s in zip(factors, stats):
            denom = denom + factor * totals(s)
        inverse = 1.0 / denom
        coefficients = [c * inverse for c in fresh + factors]
        for g in range(GROUP):
            at = slice(head + p * PAIR + g * HD, head + p * PAIR + (g + 1) * HD)
            terms = values + [ref[:, at].astype(F32) for ref in (pa_ref, pb_ref)]
            tile = jnp.zeros((16, 128), F32)
            for c, term in zip(coefficients, terms):
                tile = tile + broadcast_lane(c, g) * term
            out_ref[:, (p * GROUP + g) * HD : (p * GROUP + g + 1) * HD] = tile.astype(BF16)


def merge(paired, width_all, table, qrot, parts, backs, ups):
    operands = [table, qrot, *parts, *backs, *ups]
    pairs = qrot.shape[1] // (GROUP * HD)
    return pl.pallas_call(
        functools.partial(merge_kernel, len(backs), paired, width_all),
        in_specs=[VMEM] * len(operands),
        out_specs=VMEM,
        out_shape=jax.ShapeDtypeStruct((16, pairs * (GROUP + 2) * HD), BF16),
        compiler_params=pltpu.CompilerParams(vmem_limit_bytes=32 * MEBI),
        name="merge",
    )(*operands)


def place_kernel(mine_ref, theirs_ref, keys_out, values_out, out_ref):
    pairs = mine_ref.shape[1] // ((GROUP + 2) * HD)
    for c, ref in enumerate((mine_ref, theirs_ref)):
        for p in range(pairs):
            pair = pair_at(c * pairs + p)
            tiles = ref[:, p * GROUP * HD : (p + 1) * GROUP * HD].astype(F32)
            size = GROUP * HD
            for e in range(2):
                at = pl.ds(pl.multiple_of((2 * pair + e) * size, size), size)
                for s in range(2):
                    rows = slice(8 * e + 4 * s, 8 * e + 4 * s + 4)
                    out_ref[s, :, at] = tiles[rows].astype(BF16)
            start = pairs * GROUP * HD + p * 2 * HD
            fresh = ref[:, start : start + 2 * HD].astype(F32)
            at = pl.ds(pl.multiple_of(pair * 2 * HD, 2 * HD), 2 * HD)
            for i, out in enumerate((keys_out, values_out)):
                for s in range(2):
                    rows = slice(8 * i + 4 * s, 8 * i + 4 * s + 4)
                    out[s, :, at] = fresh[rows].astype(BF16)


def place(width, mine, theirs):
    return pl.pallas_call(
        place_kernel,
        in_specs=[VMEM] * 2,
        out_specs=[VMEM] * 3,
        out_shape=[
            jax.ShapeDtypeStruct((2, STEPS, width), BF16),
            jax.ShapeDtypeStruct((2, STEPS, width), BF16),
            jax.ShapeDtypeStruct((2, STEPS, GROUP * width), BF16),
        ],
        compiler_params=pltpu.CompilerParams(vmem_limit_bytes=32 * MEBI),
        name="place",
    )(mine, theirs)


def swap(value, axis, n, distance):
    return lax.ppermute(value, axis, [(i, i ^ distance) for i in range(n)])


def shards(
    n_dp,
    n_tensor,
    hidden,
    norm_gain,
    queries,
    key_weight,
    value_weight,
    key_down,
    key_up,
    value_down,
    value_up,
    key_cache,
    value_cache,
    lengths,
):
    depth, width = key_weight.shape
    rows = key_down.shape[0]
    to_dp = lambda value, distance: swap(value, "dp", n_dp, distance)
    to_tensor = lambda value, distance: swap(value, "tensor", n_tensor, distance)
    partners = range(2, n_dp, 2)
    n = len(partners)
    paired = n_dp == 4

    down, tokens, own = pack(
        lengths, hidden, norm_gain, key_down, value_down, key_up, value_up
    )
    near = to_dp(down, 1)
    sent = [to_dp(tokens, d) for d in partners]
    keep, send, base, qrot, table = local(
        own, queries, key_cache, value_cache, key_weight, value_weight
    )
    received = to_tensor(send, 1)
    columns = UP_COLUMNS if paired else 0
    message, *has = rank_products(rows, depth, columns, base, table, down, near, [tokens, *sent])
    if paired:
        ups = [has[0], to_dp(has[0], 1)]
    else:
        ups = lax.all_gather(tokens[:, depth // 2 :], "dp")
        ups = ups.reshape(n_dp, 16, -1, 128).transpose(0, 2, 1, 3)
        ups = ups.reshape(2, 2, 16, 16, 128).transpose(0, 1, 3, 2, 4).reshape(2, 2, 16, -1)
        ups = lax.dynamic_index_in_dim(ups, lax.axis_index("tensor") % 2, 0, keepdims=False)
        ups = [ups[0], ups[1]]
    cache = combine_cache(keep, received, message)
    part, *replies = combine_part(n, base, message, to_tensor(message, 1), cache)
    part_far = to_tensor(part, 2)
    places = [(s, t) for s in range(n_dp) for t in range(n_tensor)]
    backs = []
    for reply, d in zip(replies, partners):
        for e in (0, 2):
            perm = [(s * n_tensor + t, (s ^ d) * n_tensor + (t ^ e)) for s, t in places]
            backs.append(lax.ppermute(reply, ("dp", "tensor"), perm))
    merged = merge(
        paired,
        float(depth * n_tensor),
        table,
        qrot,
        (part, part_far),
        backs,
        ups,
    )
    return place(width, merged, to_tensor(merged, 1))


def solution(mesh):
    body = functools.partial(shards, mesh.shape["dp"], mesh.shape["tensor"])
    return jax.shard_map(
        body,
        mesh=mesh,
        in_specs=(
            P(("groups", "dp"), None, "tensor"),
            P("tensor"),
            P(("groups", "dp"), None, None),
            P("tensor", None),
            P("tensor", None),
            P(("groups", "dp"), "tensor"),
            P(("groups", "dp"), None),
            P(("groups", "dp"), "tensor"),
            P(("groups", "dp"), None),
            P(("groups", "dp"), "tensor", None),
            P(("groups", "dp"), "tensor", None),
            P(("groups", "dp")),
        ),
        out_specs=(
            P(("groups", "dp"), None, None),
            P(("groups", "dp"), None, None),
            P(("groups", "dp"), None, None),
        ),
        check_vma=False,
    )
```
